32 devices in a mesh: dp: 8 (over z, x), tensor: 4 (over y, core).
Axes of the slice: x: 2, y: 2, z: 4, core: 2. Of those that a mesh axis runs over, the one named last changes fastest.
Arguments:
- token_ids: int32 [16384], P(('dp', 'tensor')), may hold values from 0 to 50271
- slot_perm: int32 [16384], P(('dp', 'tensor')), may hold values from 0 to 16383, each once
- seq_lengths: int32 [8, 8], P('dp'), may hold values from 1 to 512, 2048 in all within a row
- pair_index: int32 [64], P('dp'), may hold values from 0 to 63, as said below
- tok_table: float32 [50272, 1024], P('dp', 'tensor'), may hold values from -0.3125 to 0.3125
- tok_first: float32 [50272, 1024], P('dp', 'tensor'), may hold values from -2.2888184e-05 to 2.2888184e-05
- tok_second: float32 [50272, 1024], P('dp', 'tensor'), may hold values from 9.522163e-13 to 3.808865e-12
- pos_table: float32 [514, 1024], P(None, 'tensor'), may hold values from -0.3125 to 0.3125
- pos_first: float32 [514, 1024], P(None, 'tensor'), may hold values from -2.2888184e-05 to 2.2888184e-05
- pos_second: float32 [514, 1024], P(None, 'tensor'), may hold values from 9.522163e-13 to 3.808865e-12
- query_key_value_weight: float32 [1024, 3, 1024], P('dp', None, 'tensor'), may hold values from -0.1875 to 0.1875
- qkv_first: float32 [1024, 3, 1024], P('dp', None, 'tensor'), may hold values from -2.2888184e-05 to 2.2888184e-05
- qkv_second: float32 [1024, 3, 1024], P('dp', None, 'tensor'), may hold values from 9.522163e-13 to 3.808865e-12
- out_weight: float32 [1024, 1024], P('tensor', 'dp'), may hold values from -0.75 to 0.75
- out_first: float32 [1024, 1024], P('tensor', 'dp'), may hold values from -2.2888184e-05 to 2.2888184e-05
- out_second: float32 [1024, 1024], P('tensor', 'dp'), may hold values from 9.522163e-13 to 3.808865e-12
- up_weight: float32 [1024, 4, 1024], P('dp', None, 'tensor'), may hold values from -0.1875 to 0.1875
- up_first: float32 [1024, 4, 1024], P('dp', None, 'tensor'), may hold values from -2.2888184e-05 to 2.2888184e-05
- up_second: float32 [1024, 4, 1024], P('dp', None, 'tensor'), may hold values from 9.522163e-13 to 3.808865e-12
- down_weight: float32 [4, 1024, 1024], P(None, 'tensor', 'dp'), may hold values from -0.09375 to 0.09375
- down_first: float32 [4, 1024, 1024], P(None, 'tensor', 'dp'), may hold values from -2.2888184e-05 to 2.2888184e-05
- down_second: float32 [4, 1024, 1024], P(None, 'tensor', 'dp'), may hold values from 9.522163e-13 to 3.808865e-12
- head_weight: float32 [1024, 1024], replicated, may hold values from -0.1875 to 0.1875
- head_first: float32 [1024, 1024], replicated, may hold values from -2.2888184e-05 to 2.2888184e-05
- head_second: float32 [1024, 1024], replicated, may hold values from 9.522163e-13 to 3.808865e-12
- col_bias: float32 [6, 1024], P(None, 'tensor'), may hold values from -0.625 to 0.625
- col_first: float32 [6, 1024], P(None, 'tensor'), may hold values from -0.00010681152 to 0.00010681152
- col_second: float32 [6, 1024], P(None, 'tensor'), may hold values from 2.285319e-11 to 9.141276e-11
- row_params: float32 [8, 1024], replicated
- row_first: float32 [8, 1024], replicated, may hold values from -0.00010681152 to 0.00010681152
- row_second: float32 [8, 1024], replicated, may hold values from 2.285319e-11 to 9.141276e-11
Outputs:
- loss_sum: float32 [], replicated
- grad_norm: float32 [], replicated
- tok_table_new: float32 [50272, 1024], P('dp', 'tensor')
- tok_first_new: float32 [50272, 1024], P('dp', 'tensor')
- tok_second_new: float32 [50272, 1024], P('dp', 'tensor')
- pos_table_new: float32 [514, 1024], P(None, 'tensor')
- pos_first_new: float32 [514, 1024], P(None, 'tensor')
- pos_second_new: float32 [514, 1024], P(None, 'tensor')
- qkv_weight_new: float32 [1024, 3, 1024], P('dp', None, 'tensor')
- qkv_first_new: float32 [1024, 3, 1024], P('dp', None, 'tensor')
- qkv_second_new: float32 [1024, 3, 1024], P('dp', None, 'tensor')
- out_weight_new: float32 [1024, 1024], P('tensor', 'dp')
- out_first_new: float32 [1024, 1024], P('tensor', 'dp')
- out_second_new: float32 [1024, 1024], P('tensor', 'dp')
- up_weight_new: float32 [1024, 4, 1024], P('dp', None, 'tensor')
- up_first_new: float32 [1024, 4, 1024], P('dp', None, 'tensor')
- up_second_new: float32 [1024, 4, 1024], P('dp', None, 'tensor')
- down_weight_new: float32 [4, 1024, 1024], P(None, 'tensor', 'dp')
- down_first_new: float32 [4, 1024, 1024], P(None, 'tensor', 'dp')
- down_second_new: float32 [4, 1024, 1024], P(None, 'tensor', 'dp')
- head_weight_new: float32 [1024, 1024], replicated
- head_first_new: float32 [1024, 1024], replicated
- head_second_new: float32 [1024, 1024], replicated
- col_bias_new: float32 [6, 1024], P(None, 'tensor')
- col_first_new: float32 [6, 1024], P(None, 'tensor')
- col_second_new: float32 [6, 1024], P(None, 'tensor')
- row_params_new: float32 [8, 1024], replicated
- row_first_new: float32 [8, 1024], replicated
- row_second_new: float32 [8, 1024], replicated
The draws below stay inside these ranges and needn't reach their ends.
Inputs may be any that keep to these rules, and one draw needn't show every extreme that they name: pair_index[i] names a sequence other than i, in the order of pooled. `seq_lengths`: each group's 8 lengths add up to 2048. `slot_perm`: each arrival position once.
All inputs are finite; a program needn't handle non-finite values.
Results may differ from the reference program's by a relative error of at most 0.012.
The reference program's roundings to bfloat16 on the way count: a program that leaves them out, or rounds other values in their place, can miss the bound.
Values may be sent and summed in bfloat16 or wider, within the bound.
A program may use at most 256 MiB of HBM per device.

```python
import math
import jax
import jax.numpy as jnp
import numpy as np
from jax import lax

D = 1024
HEADS = 16
HEAD = 64
FF = 4096
VOCAB = 50272
MAXLEN = 512
STEP = 10
TOK_GRP = 2048
POSITIONS = 514
SEQS = 8
GROUPS = 8
TOKENS = 16384
NSEQ = 64


def draw_pair_index(key, part):
    key = jax.random.fold_in(key, 11)
    offsets = jax.random.randint(key, (NSEQ,), 1, NSEQ, dtype=jnp.int32)
    return (jnp.arange(NSEQ, dtype=jnp.int32) + offsets) % NSEQ


def draw_row_params(key, part):
    key = jax.random.fold_in(key, 12)
    key_gain, key_bias = jax.random.split(key)
    rising = 0.6 + 1.2 * jnp.arange(D, dtype=jnp.float32) / D
    gain_rows = rising[None, :] * (1.0 + 0.1 * jax.random.normal(key_gain, (3, D), jnp.float32))
    shifts = 0.1 * jax.random.normal(key_bias, (5, D), jnp.float32)
    return jnp.concatenate([gain_rows, shifts], axis=0)


def with_ends(entries, key, low, high):
    extent = entries.shape
    index_at = [jax.random.randint(jax.random.fold_in(key, axis), (), 0, extent[axis]) for axis in range(len(extent))]
    entries = entries.at[tuple(index_at)].set(low)
    longest = extent.index(max(extent))
    index_at[longest] = (index_at[longest] + 1) % extent[longest]
    return entries.at[tuple(index_at)].set(high)


def shard_levels(rng, shape, cuts, least, largest):
    def one(position, blocks):
        heights = jax.random.uniform(jax.random.fold_in(jax.random.fold_in(rng, 6), position), (blocks,), jnp.float32, least / len(cuts), largest / len(cuts))
        return jnp.repeat(jnp.exp(heights), shape[position] // blocks).reshape((-1,) + (1,) * (len(shape) - position - 1))

    level = one(*cuts[0])
    for cut in cuts[1:]:
        level = level * one(*cut)
    return level


def rank_bounds(amount, skew):
    weights = [(1 << 20) // math.isqrt(rank ** skew) + 1 for rank in range(1, amount + 1)]
    deviation = 1 + sum(weights) // (1 << 30)
    return np.cumsum(np.array([max(1, weight // deviation) for weight in weights]))


def ranked_ids(key, extent, amount, skew):
    grid = rank_bounds(amount, skew)
    ticket = jax.random.randint(jax.random.fold_in(key, 1), extent, 0, int(grid[amount - 1]))
    grade = jnp.searchsorted(jnp.asarray(grid, jnp.int32), ticket, side="right")
    return jax.random.permutation(jax.random.fold_in(key, 2), amount)[grade].astype(jnp.int32)


def split_up(amount, total, reach, slope):
    loads = [(1 << 20) // math.isqrt(rank ** slope) + 1 for rank in range(2, amount + 1)]
    surplus, holding = total - reach - (amount - 1), [1] * (amount - 1)
    while surplus > 0:
        candidates = [i for i in range(amount - 1) if holding[i] < reach]
        mass, remaining = sum([loads[i] for i in candidates]), surplus
        for i in candidates:
            addition = min(reach - holding[i], max(1, remaining * loads[i] // mass), surplus)
            holding[i] = holding[i] + addition
            surplus = surplus - addition
    return np.array([reach] + holding)


def ragged_sizes(rng, amount, total, bound, lean):
    if amount == 2:
        one = jax.random.randint(rng, (), max(1, total - bound), min(bound, total - 1) + 1)
        return jnp.stack([one, total - one])
    sizes = jnp.asarray(split_up(amount, total, bound, lean), jnp.int32)
    twos = (amount - 1) // 2
    giver, sink = sizes[1:1 + 2 * twos:2], sizes[2:2 + 2 * twos:2]
    slack = jnp.minimum(giver - 1, bound - sink)
    moved = jax.random.randint(jax.random.fold_in(rng, 1), (twos,), 0, 1 << 20) % (slack + 1)
    sizes = sizes.at[1:1 + 2 * twos:2].set(giver - moved).at[2:2 + 2 * twos:2].set(sink + moved)
    return sizes[jax.random.permutation(jax.random.fold_in(rng, 2), amount)]


def scatter_about(key, extent, deviation, reach, cuts=(), held_as=jnp.bfloat16):
    values = jax.random.normal(key, extent, jnp.float32) * deviation
    if len(cuts) > 0:
        values = shard_levels(key, extent, cuts, -0.22, 0.18) * values
    return jnp.clip(values, min=-reach, max=reach).astype(held_as)


def setup_inputs(seed: int = 0) -> dict:
    key_list = jax.random.split(jax.random.key(seed), 32)
    return {
        "token_ids": with_ends(ranked_ids(key_list[0], (TOKENS,), VOCAB, 2), jax.random.fold_in(key_list[0], 3), 0, VOCAB - 1).astype(jnp.int32),
        "slot_perm": jax.random.permutation(key_list[1], TOKENS).astype(jnp.int32),
        "seq_lengths": jax.vmap(lambda own: ragged_sizes(own, SEQS, TOK_GRP, MAXLEN, 2))(jax.random.split(key_list[2], GROUPS)).reshape((GROUPS, SEQS)).astype(jnp.int32),
        "pair_index": draw_pair_index(jax.random.fold_in(key_list[31], 71), 0),
        "tok_table": scatter_about(key_list[4], (VOCAB, D), 0.05, 0.3125, ((0, 8), (1, 4)), jnp.float32),
        "tok_first": scatter_about(key_list[5], (VOCAB, D), (0.03 / (D * (VOCAB + POSITIONS + 13 * D)) ** 0.5), 2.288818359375e-05, ((0, 8), (1, 4)), jnp.float32),
        "tok_second": jnp.clip(jnp.exp(math.log(3.808865115667581e-12) - 1.3862944 * jax.random.uniform(key_list[6], (VOCAB, D), jnp.float32) ** shard_levels(key_list[6], (VOCAB, D), ((0, 8), (1, 4)), -0.2, 0.2)), 9.522162789168953e-13, 3.808865115667581e-12),
        "pos_table": scatter_about(key_list[7], (POSITIONS, D), 0.05, 0.3125, ((1, 4),), jnp.float32),
        "pos_first": scatter_about(key_list[8], (POSITIONS, D), (0.03 / (D * (VOCAB + POSITIONS + 13 * D)) ** 0.5), 2.288818359375e-05, ((1, 4),), jnp.float32),
        "pos_second": jnp.clip(jnp.exp(math.log(3.808865115667581e-12) - 1.3862944 * jax.random.uniform(key_list[9], (POSITIONS, D), jnp.float32) ** shard_levels(key_list[9], (POSITIONS, D), ((1, 4),), -0.2, 0.2)), 9.522162789168953e-13, 3.808865115667581e-12),
        "query_key_value_weight": scatter_about(key_list[10], (D, 3, D), D ** -0.5, 0.1875, ((0, 8), (2, 4)), jnp.float32),
        "qkv_first": scatter_about(key_list[11], (D, 3, D), (0.03 / (D * (VOCAB + POSITIONS + 13 * D)) ** 0.5), 2.288818359375e-05, ((0, 8), (2, 4)), jnp.float32),
        "qkv_second": jnp.clip(jnp.exp(math.log(3.808865115667581e-12) - 1.3862944 * jax.random.uniform(key_list[12], (D, 3, D), jnp.float32) ** shard_levels(key_list[12], (D, 3, D), ((0, 8), (2, 4)), -0.2, 0.2)), 9.522162789168953e-13, 3.808865115667581e-12),
        "out_weight": scatter_about(key_list[13], (D, D), HEAD ** -0.5, 0.75, ((0, 4), (1, 8)), jnp.float32),
        "out_first": scatter_about(key_list[14], (D, D), (0.03 / (D * (VOCAB + POSITIONS + 13 * D)) ** 0.5), 2.288818359375e-05, ((0, 4), (1, 8)), jnp.float32),
        "out_second": jnp.clip(jnp.exp(math.log(3.808865115667581e-12) - 1.3862944 * jax.random.uniform(key_list[15], (D, D), jnp.float32) ** shard_levels(key_list[15], (D, D), ((0, 4), (1, 8)), -0.2, 0.2)), 9.522162789168953e-13, 3.808865115667581e-12),
        "up_weight": scatter_about(key_list[16], (D, FF // D, D), D ** -0.5, 0.1875, ((0, 8), (2, 4)), jnp.float32),
        "up_first": scatter_about(key_list[17], (D, FF // D, D), (0.03 / (D * (VOCAB + POSITIONS + 13 * D)) ** 0.5), 2.288818359375e-05, ((0, 8), (2, 4)), jnp.float32),
        "up_second": jnp.clip(jnp.exp(math.log(3.808865115667581e-12) - 1.3862944 * jax.random.uniform(key_list[18], (D, FF // D, D), jnp.float32) ** shard_levels(key_list[18], (D, FF // D, D), ((0, 8), (2, 4)), -0.2, 0.2)), 9.522162789168953e-13, 3.808865115667581e-12),
        "down_weight": scatter_about(key_list[19], (FF // D, D, D), FF ** -0.5, 0.09375, ((1, 4), (2, 8)), jnp.float32),
        "down_first": scatter_about(key_list[20], (FF // D, D, D), (0.03 / (D * (VOCAB + POSITIONS + 13 * D)) ** 0.5), 2.288818359375e-05, ((1, 4), (2, 8)), jnp.float32),
        "down_second": jnp.clip(jnp.exp(math.log(3.808865115667581e-12) - 1.3862944 * jax.random.uniform(key_list[21], (FF // D, D, D), jnp.float32) ** shard_levels(key_list[21], (FF // D, D, D), ((1, 4), (2, 8)), -0.2, 0.2)), 9.522162789168953e-13, 3.808865115667581e-12),
        "head_weight": scatter_about(key_list[22], (D, D), D ** -0.5, 0.1875, (), jnp.float32),
        "head_first": scatter_about(key_list[23], (D, D), (0.03 / (D * (VOCAB + POSITIONS + 13 * D)) ** 0.5), 2.288818359375e-05, (), jnp.float32),
        "head_second": jnp.clip(jnp.exp(jax.random.uniform(key_list[24], (D, D), jnp.float32, math.log(9.522162789168953e-13), math.log(3.808865115667581e-12))), 9.522162789168953e-13, 3.808865115667581e-12),
        "col_bias": scatter_about(key_list[25], (2 + FF // D, D), 0.1, 0.625, ((1, 4),), jnp.float32),
        "col_first": scatter_about(key_list[26], (2 + FF // D, D), (0.15 / (D * (VOCAB + POSITIONS + 13 * D)) ** 0.5), 0.00010681152, ((1, 4),), jnp.float32),
        "col_second": jnp.clip(jnp.exp(math.log(9.1412759306575e-11) - 1.3862944 * jax.random.uniform(key_list[27], (2 + FF // D, D), jnp.float32) ** shard_levels(key_list[27], (2 + FF // D, D), ((1, 4),), -0.2, 0.2)), 2.285318982664375e-11, 9.1412759306575e-11),
        "row_params": draw_row_params(jax.random.fold_in(key_list[31], 71), 0),
        "row_first": scatter_about(key_list[29], (8, D), (0.15 / (D * (VOCAB + POSITIONS + 13 * D)) ** 0.5), 0.00010681152, (), jnp.float32),
        "row_second": jnp.clip(jnp.exp(jax.random.uniform(key_list[30], (8, D), jnp.float32, math.log(2.285318982664375e-11), math.log(9.1412759306575e-11))), 2.285318982664375e-11, 9.1412759306575e-11),
    }


@jax.custom_vjp
def low(v):
    return lax.optimization_barrier(v.astype(jnp.bfloat16)).astype(jnp.float32)

@jax.custom_vjp
def low_back(v):
    return v

def low_keep(v):
    return (low(v), None)

def low_pass(kept, grad):
    return (grad,)

def back_keep(v):
    return (v, None)

def back_low(kept, grad):
    return (low(grad),)
low.defvjp(low_keep, low_pass)
low_back.defvjp(back_keep, back_low)
HIGHEST_MODE = lax.Precision.HIGHEST
LN_EPS = 1e-05
LOGIT_DIVISOR = 0.05
CLIP_NORM = 0.25
BETA_FIRST = 0.9
BETA_SECOND = 0.999
ADAM_EPS = 1e-08
RATE_MATRIX = 0.05
RATE_VECTOR = 0.5
DECAY_RATE = 0.01
MASK_FILL = -1e+30

def multiply_arrays(left_mat, right_mat):
    return jnp.dot(left_mat, right_mat, precision=HIGHEST_MODE, preferred_element_type=jnp.float32)

def norm_rows(values, gain_row, bias_row):
    center = values - lax.optimization_barrier(jnp.mean(values, axis=1, keepdims=True))
    inverse = lax.rsqrt(lax.optimization_barrier(jnp.mean(center * center, axis=1, keepdims=True)) + LN_EPS)
    return center * inverse * gain_row + bias_row

def seq_layout(lengths, slot_total):
    seq_ends = jnp.cumsum(lengths).astype(jnp.int32)
    starts = seq_ends - lengths
    slot_index = jnp.arange(slot_total, dtype=jnp.int32)
    member = (slot_index[:, None] >= starts[None, :]) & (slot_index[:, None] < seq_ends[None, :])
    seq_count = jnp.arange(lengths.shape[0], dtype=jnp.int32)
    seq_ids = lax.optimization_barrier(jnp.sum(jnp.where(member, seq_count[None, :], 0), axis=1)).astype(jnp.int32)
    positions = slot_index - lax.optimization_barrier(jnp.sum(jnp.where(member, starts[None, :], 0), axis=1)).astype(jnp.int32) + 2
    return (seq_ids, positions, member)

def contrast(vectors, pair_rows, first_row):
    anchors = pair_rows.shape[0]
    others = jnp.arange(vectors.shape[0], dtype=jnp.int32)
    own_ids = first_row + jnp.arange(anchors, dtype=jnp.int32)
    result = jnp.zeros((), jnp.float32)
    for fraction in (16, 4, 1):
        part_width = vectors.shape[1] // fraction
        prefix = vectors[:, :part_width]
        unit_length_entries = prefix * lax.rsqrt(lax.optimization_barrier(jnp.sum(prefix * prefix, axis=1, keepdims=True)) + 1e-06)
        reference_embedding = lax.dynamic_slice_in_dim(unit_length_entries, first_row, anchors, 0)
        cosine_logits = multiply_arrays(reference_embedding, unit_length_entries.T) / LOGIT_DIVISOR
        cosine_logits = jnp.where(own_ids[:, None] == others[None, :], MASK_FILL, cosine_logits)
        positive = lax.optimization_barrier(jnp.sum(jnp.where(pair_rows[:, None] == others[None, :], cosine_logits, 0.0), axis=1))
        result = result + jnp.sum(jax.nn.logsumexp(cosine_logits, axis=1) - positive)
    return result

def adam_step(weight, first_old, second_old, clipped, step_rate, decay_rate):
    first_new = BETA_FIRST * first_old + (1.0 - BETA_FIRST) * clipped
    second_new = BETA_SECOND * second_old + (1.0 - BETA_SECOND) * clipped * clipped
    first_hat = first_new / (1.0 - BETA_FIRST ** STEP)
    second_hat = second_new / (1.0 - BETA_SECOND ** STEP)
    weight_new = weight - step_rate * (first_hat / (jnp.sqrt(second_hat) + ADAM_EPS) + decay_rate * weight)
    return (weight_new, first_new, second_new)

def attend(query_rows, key_rows, value_rows, seq_ids):
    block_rows = MAXLEN
    block_count = query_rows.shape[0] // block_rows
    keys_pad = jnp.pad(key_rows, ((block_rows, block_rows), (0, 0), (0, 0)))
    values_pad = jnp.pad(value_rows, ((block_rows, block_rows), (0, 0), (0, 0)))
    seq_pad = jnp.pad(seq_ids, (block_rows, block_rows), constant_values=-1)

    def one_block(block_index):
        first_row = block_index * block_rows
        q_blk = lax.dynamic_slice_in_dim(query_rows, first_row, block_rows, 0)
        k_blk = lax.dynamic_slice_in_dim(keys_pad, first_row, 3 * block_rows, 0)
        v_blk = lax.dynamic_slice_in_dim(values_pad, first_row, 3 * block_rows, 0)
        q_seq = lax.dynamic_slice_in_dim(seq_ids, first_row, block_rows, 0)
        k_seq = lax.dynamic_slice_in_dim(seq_pad, first_row, 3 * block_rows, 0)
        scores = low_back(jnp.einsum('qhd,khd->hqk', q_blk, k_blk, precision=HIGHEST_MODE) * HEAD ** (-0.5))
        scores = jnp.where((q_seq[:, None] == k_seq[None, :])[None], scores, MASK_FILL)
        softmaxed = low(jax.nn.softmax(scores, axis=-1))
        return jnp.einsum('hqk,khd->qhd', softmaxed, v_blk, precision=HIGHEST_MODE)
    blocks_out = lax.map(jax.checkpoint(one_block), jnp.arange(block_count, dtype=jnp.int32))
    return blocks_out.reshape(query_rows.shape)

def group_pooled(emb_rows, seq_ids, member, lengths, layer_mats):
    qkv_mat, out_mat, up_mat, down_mat, col_vec, row_vec = layer_mats
    norm_first = norm_rows(emb_rows, row_vec[0], row_vec[3])
    qkv_bias = jnp.concatenate([col_vec[0], jnp.zeros_like(col_vec[0]), col_vec[1]])
    qkv_out = low(low_back(multiply_arrays(low(norm_first), qkv_mat.reshape(D, 3 * D)) + qkv_bias))
    qkv_out = qkv_out.reshape(-1, 3, HEADS, HEAD)
    attn_out = attend(qkv_out[:, 0], qkv_out[:, 1], qkv_out[:, 2], seq_ids)
    attn_out = low(low_back(attn_out.reshape(-1, D)))
    first_sum = norm_first + low_back(multiply_arrays(attn_out, out_mat) + row_vec[6])
    norm_second = norm_rows(first_sum, row_vec[1], row_vec[4])
    expansion_result = low_back(multiply_arrays(low(norm_second), up_mat.reshape(D, FF)) + col_vec[2:].reshape(FF))
    hidden = low(jax.nn.gelu(expansion_result, approximate=False))
    second_sum = norm_second + low_back(multiply_arrays(hidden, down_mat.reshape(FF, D)) + row_vec[7])
    norm_third = norm_rows(second_sum, row_vec[2], row_vec[5])
    return multiply_arrays(member.astype(jnp.float32).T, norm_third) / lengths.astype(jnp.float32)[:, None]

def forward_loss(params, slot_ids, seq_ids, positions, member, seq_lengths, pair_index):
    tok_mat, pos_mat, qkv_mat, out_mat, up_mat, down_mat, head_mat, col_vec, row_vec = params
    emb_rows = jnp.take(low(tok_mat), slot_ids, axis=0) + jnp.take(pos_mat, positions, axis=0)
    layer_mats = (low(qkv_mat), low(out_mat), low(up_mat), low(down_mat), col_vec, row_vec)

    def per_group(group_items):
        return group_pooled(group_items[0], group_items[1], group_items[2], group_items[3], layer_mats)
    pooled = lax.map(jax.checkpoint(per_group), (emb_rows.reshape(GROUPS, TOK_GRP, D), seq_ids, member, seq_lengths))
    vectors = multiply_arrays(low(pooled.reshape(NSEQ, D)), low(head_mat))
    return contrast(vectors, pair_index, 0)

def reference(token_ids, slot_perm, seq_lengths, pair_index, tok_table, tok_first, tok_second, pos_table, pos_first, pos_second, query_key_value_weight, qkv_first, qkv_second, out_weight, out_first, out_second, up_weight, up_first, up_second, down_weight, down_first, down_second, head_weight, head_first, head_second, col_bias, col_first, col_second, row_params, row_first, row_second):
    slot_ids = jnp.take(token_ids, slot_perm, axis=0)
    seq_ids, positions, member = jax.vmap(lambda lengths: seq_layout(lengths, TOK_GRP))(seq_lengths)
    params = (tok_table, pos_table, query_key_value_weight, out_weight, up_weight, down_weight, head_weight, col_bias, row_params)
    firsts = (tok_first, pos_first, qkv_first, out_first, up_first, down_first, head_first, col_first, row_first)
    seconds = (tok_second, pos_second, qkv_second, out_second, up_second, down_second, head_second, col_second, row_second)

    def loss_of(*weights_all):
        return forward_loss(weights_all, slot_ids, seq_ids, positions.reshape(-1), member, seq_lengths, pair_index)
    loss_val, loss_pull = jax.vjp(loss_of, *params)
    gradients = loss_pull(jnp.ones_like(loss_val))
    squares = sum((jnp.sum(grad_item * grad_item) for grad_item in gradients))
    grad_norm = jnp.sqrt(squares)
    clip_scale = jnp.minimum(1.0, CLIP_NORM / (grad_norm + 1e-06))
    results = []
    for item_index in range(9):
        step_rate = RATE_MATRIX if item_index < 7 else RATE_VECTOR
        decay_rate = DECAY_RATE if item_index < 7 else 0.0
        results.extend(adam_step(params[item_index], firsts[item_index], seconds[item_index], gradients[item_index] * clip_scale, step_rate, decay_rate))
    return (loss_val, grad_norm, results[0], results[1], results[2], results[3], results[4], results[5], results[6], results[7], results[8], results[9], results[10], results[11], results[12], results[13], results[14], results[15], results[16], results[17], results[18], results[19], results[20], results[21], results[22], results[23], results[24], results[25], results[26])
```

```python
from functools import partial

import jax
import jax.numpy as jnp
from jax import lax
from jax.experimental import pallas as pl
from jax.experimental.pallas import tpu as pltpu
from jax.sharding import PartitionSpec as P

D = 1024
HEAD = 64
MAXLEN = 512
STEP = 10


HIGHEST_MODE = lax.Precision.HIGHEST
LN_EPS = 1e-05
LOGIT_DIVISOR = 0.05
CLIP_NORM = 0.25
BETA_FIRST = 0.9
BETA_SECOND = 0.999
ADAM_EPS = 1e-08
RATE_MATRIX = 0.05
RATE_VECTOR = 0.5
DECAY_RATE = 0.01
MASK_FILL = -1e30


def multiply_arrays(left_mat, right_mat):
    return jnp.dot(left_mat, right_mat, preferred_element_type=jnp.float32)


def exact_multiply(left_mat, right_mat):
    return jnp.dot(left_mat, right_mat, precision=HIGHEST_MODE, preferred_element_type=jnp.float32)


def norm_rows(values, gain_row, bias_row):
    center = values - jnp.mean(values, axis=1, keepdims=True)
    inverse = lax.rsqrt(jnp.mean(center * center, axis=1, keepdims=True) + LN_EPS)
    return center * inverse * gain_row + bias_row


def norm_back(values, gain_row, bias_row, grad_rows):
    norm_pull = jax.vjp(norm_rows, values, gain_row, bias_row)[1]
    return norm_pull(grad_rows)


def seq_layout(lengths, slot_total):
    seq_ends = jnp.cumsum(lengths)
    starts = seq_ends - lengths
    slot_index = jnp.arange(slot_total, dtype=jnp.int32)
    member = (slot_index[:, None] >= starts[None, :]) & (slot_index[:, None] < seq_ends[None, :])
    seq_count = jnp.arange(lengths.shape[0], dtype=jnp.int32)
    seq_ids = jnp.sum(jnp.where(member, seq_count[None, :], 0), axis=1)
    positions = slot_index - jnp.sum(jnp.where(member, starts[None, :], 0), axis=1) + 2
    return (seq_ids, positions, member)


def adam_step(weight, first_old, second_old, clipped, step_rate, decay_rate):
    first_new = BETA_FIRST * first_old + (1.0 - BETA_FIRST) * clipped
    second_new = BETA_SECOND * second_old + (1.0 - BETA_SECOND) * clipped * clipped
    first_hat = first_new / (1.0 - BETA_FIRST**STEP)
    second_hat = second_new / (1.0 - BETA_SECOND**STEP)
    weight_new = weight - step_rate * (
        first_hat / (jnp.sqrt(second_hat) + ADAM_EPS) + decay_rate * weight
    )
    return (weight_new, first_new, second_new)


MESH_IDS = pl.DeviceIdType.MESH
VMEM_BYTES = 60 * 1024 * 1024


def in_vmem():
    return pl.BlockSpec(memory_space=pltpu.VMEM)


def greet(partners):
    barrier = pltpu.get_barrier_semaphore()
    for partner in partners:
        pl.semaphore_signal(barrier, inc=1, device_id=partner, device_id_type=MESH_IDS)
    pl.semaphore_wait(barrier, len(partners))


def remote(src, dst, send_sem, recv_sem, target):
    return pltpu.make_async_remote_copy(
        src_ref=src,
        dst_ref=dst,
        send_sem=send_sem,
        recv_sem=recv_sem,
        device_id=target,
        device_id_type=MESH_IDS,
    )


def comm_params(collective):
    return pltpu.CompilerParams(
        collective_id=collective, has_side_effects=True, vmem_limit_bytes=VMEM_BYTES
    )


def gather_all_kernel(groups, width, x_ref, o_ref, send, recv):
    total = groups * width
    me = lax.axis_index("dp") * width + lax.axis_index("tensor")

    def place(step):
        other = lax.rem(me + step, total)
        return (other // width, lax.rem(other, width))

    barrier = pltpu.get_barrier_semaphore()

    def hello(step, carry):
        pl.semaphore_signal(barrier, inc=1, device_id=place(step), device_id_type=MESH_IDS)
        return carry

    lax.fori_loop(1, total, hello, 0)
    pl.semaphore_wait(barrier, total - 1)

    def copy(step):
        return remote(x_ref, o_ref.at[me], send.at[step], recv.at[step], place(step))

    def begin(step, carry):
        copy(step).start()
        return carry

    def finish(step, carry):
        copy(step).wait()
        return carry

    lax.fori_loop(1, total, begin, 0)
    o_ref[me] = x_ref[...]
    lax.fori_loop(1, total, finish, 0)


def gather_all(block, collective):
    groups, width = lax.axis_size("dp"), lax.axis_size("tensor")
    total = groups * width
    return pl.pallas_call(
        partial(gather_all_kernel, groups, width),
        out_shape=jax.ShapeDtypeStruct((total,) + block.shape, block.dtype),
        in_specs=[in_vmem()],
        out_specs=in_vmem(),
        scratch_shapes=[pltpu.SemaphoreType.DMA((total,)), pltpu.SemaphoreType.DMA((total,))],
        compiler_params=comm_params(collective),
    )(block)


def swap_kernel(axis, count, x_ref, o_ref, send, recv):
    me = lax.axis_index(axis)
    others = [lax.rem(me + step, count) for step in range(1, count)]
    greet([{axis: other} for other in others])
    copies = [
        remote(x_ref.at[other], o_ref.at[me], send.at[i], recv.at[i], {axis: other})
        for i, other in enumerate(others)
    ]
    for copy in copies:
        copy.start()
    o_ref[me] = x_ref[me]
    for copy in copies:
        copy.wait()


def swap(blocks, axis, collective):
    count = lax.axis_size(axis)
    return pl.pallas_call(
        partial(swap_kernel, axis, count),
        out_shape=jax.ShapeDtypeStruct(blocks.shape, blocks.dtype),
        in_specs=[in_vmem()],
        out_specs=in_vmem(),
        scratch_shapes=[pltpu.SemaphoreType.DMA((count,)), pltpu.SemaphoreType.DMA((count,))],
        compiler_params=comm_params(collective),
    )(blocks)


CHUNKS = 4


def tensor_place(width):
    me = lax.axis_index("tensor")
    core = lax.rem(me, 2)
    row = me // 2
    mate = me + 1 - 2 * core
    return me, core, row, mate


def spread_kernel(width, x_ref, o_ref, far_send, far_recv, near_send, near_recv):
    me, core, row, mate = tensor_place(width)
    rows = width // 2
    height = x_ref.shape[0]
    size = height // CHUNKS
    peers = [lax.rem(row + step, rows) * 2 + core for step in range(1, rows)]
    greet([{"tensor": mate}] + [{"tensor": peer} for peer in peers])

    def span(owner, part):
        return pl.ds(pl.multiple_of(owner * height + part * size, size), size)

    far = [
        [
            remote(
                x_ref.at[pl.ds(part * size, size)],
                o_ref.at[span(me, part)],
                far_send.at[i, part],
                far_recv.at[i, part],
                {"tensor": peer},
            )
            for part in range(CHUNKS)
        ]
        for i, peer in enumerate(peers)
    ]
    for part in range(CHUNKS):
        for line in far:
            line[part].start()
    near = [
        remote(
            x_ref,
            o_ref.at[pl.ds(pl.multiple_of(me * height, height), height)],
            near_send.at[0, 0],
            near_recv.at[0, 0],
            {"tensor": mate},
        )
    ]
    near[0].start()
    o_ref[pl.ds(pl.multiple_of(me * height, height), height)] = x_ref[...]
    for part in range(CHUNKS):
        for i in range(rows - 1):
            far[i][part].wait_recv()
            source = lax.rem(row + rows - 1 - i, rows) * 2 + core
            onward = remote(
                o_ref.at[span(source, part)],
                o_ref.at[span(source, part)],
                near_send.at[i + 1, part],
                near_recv.at[i + 1, part],
                {"tensor": mate},
            )
            onward.start()
            near.append(onward)
    for copy in near:
        copy.wait()
    for line in far:
        for copy in line:
            copy.wait_send()


def spread(block, collective):
    width = lax.axis_size("tensor")
    rows = width // 2
    far = pltpu.SemaphoreType.DMA((rows, CHUNKS))
    return pl.pallas_call(
        partial(spread_kernel, width),
        out_shape=jax.ShapeDtypeStruct((width * block.shape[0],) + block.shape[1:], block.dtype),
        in_specs=[in_vmem()],
        out_specs=in_vmem(),
        scratch_shapes=[far, far, far, far],
        compiler_params=comm_params(collective),
    )(block)


def fold_kernel(width, p_ref, o_ref, near_buf, sum_buf, far_buf, near_send, near_recv, far_send, far_recv):
    me, core, row, mate = tensor_place(width)
    rows = width // 2
    height = o_ref.shape[0]
    size = height // CHUNKS
    peers = [lax.rem(row + step, rows) * 2 + core for step in range(1, rows)]
    greet([{"tensor": mate}] + [{"tensor": peer} for peer in peers])
    order = list(range(1, rows)) + [0]

    def span(owner, part):
        return pl.ds(pl.multiple_of(owner * height + part * size, size), size)

    near = {}
    for step in order:
        dest_row = lax.rem(row + step, rows)
        for part in range(CHUNKS):
            near[step, part] = remote(
                p_ref.at[span(dest_row * 2 + 1 - core, part)],
                near_buf.at[step, pl.ds(part * size, size)],
                near_send.at[step, part],
                near_recv.at[step, part],
                {"tensor": mate},
            )
            near[step, part].start()
    far = {}
    for step in range(1, rows):
        dest = lax.rem(row + step, rows) * 2 + core
        for part in range(CHUNKS):
            near[step, part].wait_recv()
            local = pl.ds(part * size, size)
            sum_buf[step - 1, local] = (
                p_ref[span(dest, part)].astype(jnp.float32)
                + near_buf[step, local].astype(jnp.float32)
            ).astype(jnp.bfloat16)
            far[step, part] = remote(
                sum_buf.at[step - 1, local],
                far_buf.at[step - 1, local],
                far_send.at[step - 1, part],
                far_recv.at[step - 1, part],
                {"tensor": dest},
            )
            far[step, part].start()
    for part in range(CHUNKS):
        near[0, part].wait_recv()
        local = pl.ds(part * size, size)
        o_ref[local] = p_ref[span(me, part)].astype(jnp.float32) + near_buf[0, local].astype(jnp.float32)
    for part in range(CHUNKS):
        local = pl.ds(part * size, size)
        for step in range(1, rows):
            far[step, part].wait_recv()
            o_ref[local] += far_buf[step - 1, local].astype(jnp.float32)
    for copy in list(near.values()) + list(far.values()):
        copy.wait_send()


def fold(parts, collective):
    width = lax.axis_size("tensor")
    rows = width // 2
    height, depth = parts.shape[0] // width, parts.shape[1]
    near = pltpu.SemaphoreType.DMA((rows, CHUNKS))
    return pl.pallas_call(
        partial(fold_kernel, width),
        out_shape=jax.ShapeDtypeStruct((height, depth), jnp.float32),
        in_specs=[in_vmem()],
        out_specs=in_vmem(),
        scratch_shapes=[
            pltpu.VMEM((rows, height, depth), jnp.bfloat16),
            pltpu.VMEM((max(rows - 1, 1), height, depth), jnp.bfloat16),
            pltpu.VMEM((max(rows - 1, 1), height, depth), jnp.bfloat16),
            near, near, near, near,
        ],
        compiler_params=comm_params(collective),
    )(parts)


def column_spread_kernel(width, x_ref, o_ref, far_send, far_recv, near_send, near_recv):
    me, core, row, mate = tensor_place(width)
    rows = width // 2
    height, depth = x_ref.shape
    size = height // CHUNKS
    peers = [lax.rem(row + step, rows) * 2 + core for step in range(1, rows)]
    greet([{"tensor": mate}] + [{"tensor": peer} for peer in peers])

    def lanes(owner):
        return pl.ds(pl.multiple_of(owner * depth, depth), depth)

    far = [
        [
            remote(
                x_ref.at[pl.ds(part * size, size)],
                o_ref.at[pl.ds(part * size, size), lanes(me)],
                far_send.at[i, part],
                far_recv.at[i, part],
                {"tensor": peer},
            )
            for part in range(CHUNKS)
        ]
        for i, peer in enumerate(peers)
    ]
    for part in range(CHUNKS):
        for line in far:
            line[part].start()
    near = [
        remote(x_ref, o_ref.at[:, lanes(me)], near_send.at[0, 0], near_recv.at[0, 0], {"tensor": mate})
    ]
    near[0].start()
    o_ref[:, lanes(me)] = x_ref[...]
    for part in range(CHUNKS):
        for i in range(rows - 1):
            far[i][part].wait_recv()
            source = lax.rem(row + rows - 1 - i, rows) * 2 + core
            window = o_ref.at[pl.ds(part * size, size), lanes(source)]
            onward = remote(
                window, window, near_send.at[i + 1, part], near_recv.at[i + 1, part], {"tensor": mate}
            )
            onward.start()
            near.append(onward)
    for copy in near:
        copy.wait()
    for line in far:
        for copy in line:
            copy.wait_send()


def column_spread(block, collective):
    width = lax.axis_size("tensor")
    far = pltpu.SemaphoreType.DMA((width // 2, CHUNKS))
    return pl.pallas_call(
        partial(column_spread_kernel, width),
        out_shape=jax.ShapeDtypeStruct((block.shape[0], width * block.shape[1]), block.dtype),
        in_specs=[in_vmem()],
        out_specs=in_vmem(),
        scratch_shapes=[far, far, far, far],
        compiler_params=comm_params(collective),
    )(block)


def sum_kernel(groups, width, keep, x_ref, o_ref, part_buf, sum_buf, all_buf, out_buf, *sems):
    dp_me, me = lax.axis_index("dp"), lax.axis_index("tensor")
    depth = part_buf.shape[2]
    mates = [lax.rem(me + step, width) for step in range(1, width)]
    peers = [lax.rem(dp_me + step, groups) for step in range(1, groups)]
    greet([{"tensor": mate} for mate in mates] + [{"dp": peer} for peer in peers])

    def lanes(owner):
        return pl.ds(pl.multiple_of(owner * depth, depth), depth)

    def run(copies):
        for copy in copies:
            copy.start()
        return copies

    first = run(
        [
            remote(x_ref.at[:, lanes(mate)], part_buf.at[me], sems[0].at[i], sems[1].at[i], {"tensor": mate})
            for i, mate in enumerate(mates)
        ]
    )
    part_buf[me] = x_ref[:, lanes(me)]
    for copy in first:
        copy.wait()
    sum_buf[...] = jnp.sum(part_buf[...], axis=0)
    second = run(
        [
            remote(sum_buf, all_buf.at[dp_me], sems[2].at[i], sems[3].at[i], {"dp": peer})
            for i, peer in enumerate(peers)
        ]
    )
    all_buf[dp_me] = sum_buf[...]
    for copy in second:
        copy.wait()
    if keep:
        out_buf[...] = all_buf[...]
    else:
        out_buf[0] = jnp.sum(all_buf[...], axis=0)
    third = run(
        [
            remote(out_buf, o_ref.at[:, :, lanes(me)], sems[4].at[i], sems[5].at[i], {"tensor": mate})
            for i, mate in enumerate(mates)
        ]
    )
    o_ref[:, :, lanes(me)] = out_buf[...]
    for copy in third:
        copy.wait()


def sum_all(block, keep, collective):
    groups, width = lax.axis_size("dp"), lax.axis_size("tensor")
    rows, depth = block.shape
    narrow = depth // width
    kept = groups if keep else 1
    near, far = pltpu.SemaphoreType.DMA((width,)), pltpu.SemaphoreType.DMA((groups,))
    return pl.pallas_call(
        partial(sum_kernel, groups, width, keep),
        out_shape=jax.ShapeDtypeStruct((kept, rows, depth), block.dtype),
        in_specs=[in_vmem()],
        out_specs=in_vmem(),
        scratch_shapes=[
            pltpu.VMEM((width, rows, narrow), block.dtype),
            pltpu.VMEM((rows, narrow), block.dtype),
            pltpu.VMEM((groups, rows, narrow), block.dtype),
            pltpu.VMEM((kept, rows, narrow), block.dtype),
            near, near, far, far, near, near,
        ],
        compiler_params=comm_params(collective),
    )(block)


def pad_keys(key_rows, value_rows, seq_ids):
    block_rows = MAXLEN
    keys_pad = jnp.pad(key_rows, ((block_rows, block_rows), (0, 0), (0, 0)))
    values_pad = jnp.pad(value_rows, ((block_rows, block_rows), (0, 0), (0, 0)))
    seq_pad = jnp.pad(seq_ids, (block_rows, block_rows), constant_values=-1)
    return (keys_pad, values_pad, seq_pad)


def score_block(q_blk, k_blk, q_seq, k_seq):
    scores = jnp.einsum(
        "qhd,khd->hqk", q_blk, k_blk, preferred_element_type=jnp.float32
    ) * HEAD ** (-0.5)
    return jnp.where((q_seq[:, None] == k_seq[None, :])[None], scores, MASK_FILL)


def attend(query_rows, key_rows, value_rows, seq_ids):
    block_rows = MAXLEN
    block_count = query_rows.shape[0] // block_rows
    keys_pad, values_pad, seq_pad = pad_keys(key_rows, value_rows, seq_ids)

    def one_block(block_index):
        first_row = block_index * block_rows
        q_blk = lax.dynamic_slice_in_dim(query_rows, first_row, block_rows, 0)
        k_blk = lax.dynamic_slice_in_dim(keys_pad, first_row, 3 * block_rows, 0)
        v_blk = lax.dynamic_slice_in_dim(values_pad, first_row, 3 * block_rows, 0)
        q_seq = lax.dynamic_slice_in_dim(seq_ids, first_row, block_rows, 0)
        k_seq = lax.dynamic_slice_in_dim(seq_pad, first_row, 3 * block_rows, 0)
        scores = score_block(q_blk, k_blk, q_seq, k_seq)
        row_top = jnp.max(scores, axis=-1, keepdims=True)
        weights = jnp.exp(scores - row_top)
        row_total = jnp.sum(weights, axis=-1, keepdims=True)
        softmaxed = (weights / row_total).astype(jnp.bfloat16)
        block_out = jnp.einsum("hqk,khd->qhd", softmaxed, v_blk, preferred_element_type=jnp.float32)
        return (block_out, row_top[..., 0] + jnp.log(row_total[..., 0]))

    blocks_out, log_total = lax.map(one_block, jnp.arange(block_count, dtype=jnp.int32))
    return (blocks_out.reshape(query_rows.shape), log_total)


def attend_back(query_rows, key_rows, value_rows, seq_ids, log_total, grad_out):
    block_rows = MAXLEN
    block_count = query_rows.shape[0] // block_rows
    keys_pad, values_pad, seq_pad = pad_keys(key_rows, value_rows, seq_ids)
    zeros_pad = jnp.zeros(keys_pad.shape, jnp.float32)
    scale_factor = HEAD ** (-0.5)

    def one_block(state_pair, block_index):
        key_grad, value_grad = state_pair
        first_row = block_index * block_rows
        q_blk = lax.dynamic_slice_in_dim(query_rows, first_row, block_rows, 0)
        g_blk = lax.dynamic_slice_in_dim(grad_out, first_row, block_rows, 0)
        k_blk = lax.dynamic_slice_in_dim(keys_pad, first_row, 3 * block_rows, 0)
        v_blk = lax.dynamic_slice_in_dim(values_pad, first_row, 3 * block_rows, 0)
        q_seq = lax.dynamic_slice_in_dim(seq_ids, first_row, block_rows, 0)
        k_seq = lax.dynamic_slice_in_dim(seq_pad, first_row, 3 * block_rows, 0)
        scores = score_block(q_blk, k_blk, q_seq, k_seq)
        softmaxed = jnp.exp(scores - log_total[block_index][:, :, None])
        prob_grad = jnp.einsum("qhd,khd->hqk", g_blk, v_blk, preferred_element_type=jnp.float32)
        inner = jnp.sum(softmaxed * prob_grad, axis=-1, keepdims=True)
        score_grad = (softmaxed * (prob_grad - inner)).astype(jnp.bfloat16)
        query_grad = (
            jnp.einsum("hqk,khd->qhd", score_grad, k_blk, preferred_element_type=jnp.float32)
            * scale_factor
        )
        key_part = (
            jnp.einsum("hqk,qhd->khd", score_grad, q_blk, preferred_element_type=jnp.float32)
            * scale_factor
        )
        value_part = jnp.einsum(
            "hqk,qhd->khd",
            softmaxed.astype(jnp.bfloat16),
            g_blk,
            preferred_element_type=jnp.float32,
        )
        key_grad = lax.dynamic_update_slice_in_dim(
            key_grad,
            lax.dynamic_slice_in_dim(key_grad, first_row, 3 * block_rows, 0) + key_part,
            first_row,
            0,
        )
        value_grad = lax.dynamic_update_slice_in_dim(
            value_grad,
            lax.dynamic_slice_in_dim(value_grad, first_row, 3 * block_rows, 0) + value_part,
            first_row,
            0,
        )
        return ((key_grad, value_grad), query_grad)

    (key_grad, value_grad), query_grad = lax.scan(
        one_block, (zeros_pad, zeros_pad), jnp.arange(block_count, dtype=jnp.int32)
    )
    return (
        query_grad.reshape(query_rows.shape),
        key_grad[block_rows:-block_rows],
        value_grad[block_rows:-block_rows],
    )


def layer_forward(emb_all, seq_ids, row_params, col_local, layer_mats):
    qkv_full, out_full, up_full, down_full = layer_mats
    col_width = qkv_full.shape[2]
    tok_dev = emb_all.shape[0] // lax.axis_size("tensor")
    first_moment_all = norm_rows(emb_all, row_params[0], row_params[3]).astype(jnp.bfloat16)
    emb_rows = lax.dynamic_slice_in_dim(emb_all, lax.axis_index("tensor") * tok_dev, tok_dev, 0)
    norm_first = norm_rows(emb_rows, row_params[0], row_params[3])
    qkv_bias = jnp.concatenate([col_local[0], jnp.zeros_like(col_local[0]), col_local[1]])
    qkv_out = (
        multiply_arrays(first_moment_all, qkv_full.reshape(D, 3 * col_width)) + qkv_bias
    ).astype(jnp.bfloat16)
    qkv_out = qkv_out.reshape(-1, 3, col_width // HEAD, HEAD)
    attn_out, log_total = attend(qkv_out[:, 0], qkv_out[:, 1], qkv_out[:, 2], seq_ids)
    attn_low = attn_out.reshape(-1, col_width).astype(jnp.bfloat16)
    first_sum = (
        norm_first
        + fold(multiply_arrays(attn_low, out_full).astype(jnp.bfloat16), 5)
        + row_params[6]
    )
    norm_second = norm_rows(first_sum, row_params[1], row_params[4])
    second_all = spread(norm_second.astype(jnp.bfloat16), 6)
    expansion_result = multiply_arrays(second_all, up_full.reshape(D, -1)) + col_local[2:].reshape(
        -1
    )
    hidden_low = jax.nn.gelu(expansion_result, approximate=False).astype(jnp.bfloat16)
    second_sum = (
        norm_second
        + fold(multiply_arrays(hidden_low, down_full.reshape(-1, D)).astype(jnp.bfloat16), 7)
        + row_params[7]
    )
    norm_third = norm_rows(second_sum, row_params[2], row_params[5])
    saved_vals = (
        emb_rows,
        first_moment_all,
        qkv_out,
        log_total,
        attn_low,
        first_sum,
        second_all,
        expansion_result,
        hidden_low,
        second_sum,
    )
    return (norm_third, saved_vals)


def layer_backward(grad_third, seq_ids, row_params, layer_mats, saved_vals):
    qkv_full, out_full, up_full, down_full = layer_mats
    (
        emb_rows,
        first_moment_all,
        qkv_out,
        log_total,
        attn_low,
        first_sum,
        second_all,
        expansion_result,
        hidden_low,
        second_sum,
    ) = saved_vals
    col_width = qkv_full.shape[2]
    grad_second, gain_c, shift_c = norm_back(second_sum, row_params[2], row_params[5], grad_third)
    mixed_low = grad_second.astype(jnp.bfloat16)
    mixed_all = spread(mixed_low, 10)
    down_grad = jnp.einsum("tf,td->fd", hidden_low, mixed_all, preferred_element_type=jnp.float32)
    hidden_grad = jnp.einsum(
        "td,fd->tf", mixed_all, down_full.reshape(-1, D), preferred_element_type=jnp.float32
    )
    gelu_pull = jax.vjp(partial(jax.nn.gelu, approximate=False), expansion_result)[1]
    up_low = gelu_pull(hidden_grad)[0].astype(jnp.bfloat16)
    up_grad = jnp.einsum("td,tf->df", second_all, up_low, preferred_element_type=jnp.float32)
    second_total = grad_second + fold(
        jnp.einsum(
            "tf,df->td", up_low, up_full.reshape(D, -1), preferred_element_type=jnp.float32
        ).astype(jnp.bfloat16),
        11,
    )
    grad_first, gain_b, shift_b = norm_back(first_sum, row_params[1], row_params[4], second_total)
    branch_low = grad_first.astype(jnp.bfloat16)
    branch_all = spread(branch_low, 12)
    out_grad = jnp.einsum("tc,td->cd", attn_low, branch_all, preferred_element_type=jnp.float32)
    attn_grad = jnp.einsum(
        "td,cd->tc", branch_all, out_full, preferred_element_type=jnp.float32
    ).astype(jnp.bfloat16)
    head_count = col_width // HEAD
    query_grad, key_grad, value_grad = attend_back(
        qkv_out[:, 0],
        qkv_out[:, 1],
        qkv_out[:, 2],
        seq_ids,
        log_total,
        attn_grad.reshape(-1, head_count, HEAD),
    )
    qkv_low = (
        jnp.stack([query_grad, key_grad, value_grad], 1)
        .astype(jnp.bfloat16)
        .reshape(-1, 3 * col_width)
    )
    qkv_grad = jnp.einsum(
        "td,tc->dc", first_moment_all, qkv_low, preferred_element_type=jnp.float32
    )
    first_total = grad_first + fold(
        jnp.einsum(
            "tc,dc->td", qkv_low, qkv_full.reshape(D, -1), preferred_element_type=jnp.float32
        ).astype(jnp.bfloat16),
        13,
    )
    emb_grad, gain_a, shift_a = norm_back(emb_rows, row_params[0], row_params[3], first_total)
    qkv_cols = jnp.sum(qkv_low.astype(jnp.float32), axis=0).reshape(3, col_width)
    up_cols = jnp.sum(up_low.astype(jnp.float32), axis=0).reshape(-1, col_width)
    col_grad = jnp.concatenate([qkv_cols[0:1], qkv_cols[2:3], up_cols], axis=0)
    row_grad = jnp.stack(
        [
            gain_a,
            gain_b,
            gain_c,
            shift_a,
            shift_b,
            shift_c,
            jnp.sum(branch_low.astype(jnp.float32), axis=0),
            jnp.sum(mixed_low.astype(jnp.float32), axis=0),
        ]
    )
    mats_grad = (
        qkv_grad.reshape(D, 3, col_width),
        out_grad,
        up_grad.reshape(D, -1, col_width),
        down_grad.reshape(-1, col_width, D),
    )
    return (emb_grad, mats_grad, col_grad, row_grad)


def plan_kernel(capacity, vocab_local, groups, perm_ref, low_ref, high_ref, slot_ref, list_ref, count_ref, id_buf, own_buf):
    slots = perm_ref.shape[1]
    table_rows = low_ref.shape[1]
    block = 128
    blocks = slots // block
    perm = perm_ref[...]
    high_part = perm // 128
    low_part = perm - high_part * 128
    chooser = (lax.broadcasted_iota(jnp.int32, (table_rows, slots), 0) == high_part).astype(
        jnp.float32
    ).astype(jnp.bfloat16)
    value = multiply_arrays(low_ref[...], chooser) + 256.0 * multiply_arrays(high_ref[...], chooser)
    lane_match = lax.broadcasted_iota(jnp.int32, (128, slots), 0) == low_part
    ids = jnp.sum(jnp.where(lane_match, value, 0.0), axis=0, keepdims=True)
    for b in range(blocks):
        id_buf[pl.ds(b * block, block), :] = jnp.broadcast_to(
            ids[:, b * block : (b + 1) * block], (block, block)
        ).T
    place = lax.broadcasted_iota(jnp.int32, (1, slots), 1).astype(jnp.float32)
    rows = lax.broadcasted_iota(jnp.int32, (block, 1), 0).astype(jnp.float32)

    def earliest(b, best):
        column = id_buf[pl.ds(pl.multiple_of(b * block, block), block), 0:1]
        index = rows + (b * block).astype(jnp.float32)
        found = jnp.where(column == ids, index, 1e9)
        return jnp.minimum(best, jnp.min(found, axis=0, keepdims=True))

    least = lax.fori_loop(0, blocks, earliest, jnp.full((1, slots), 1e9, jnp.float32))
    first = least == place
    owner = jnp.zeros((1, slots), jnp.float32)
    for index in range(1, groups):
        owner = owner + jnp.where(ids >= float(index * vocab_local), 1.0, 0.0)
    owner_rows = lax.broadcasted_iota(jnp.int32, (groups, slots), 0).astype(jnp.float32)
    marks = jnp.where(first & (owner == owner_rows), 1.0, 0.0)
    upper = jnp.where(
        lax.broadcasted_iota(jnp.int32, (block, block), 0)
        < lax.broadcasted_iota(jnp.int32, (block, block), 1),
        1.0,
        0.0,
    ).astype(jnp.bfloat16)
    running = jnp.zeros((groups, 1), jnp.float32)
    pieces = []
    for b in range(blocks):
        part = marks[:, b * block : (b + 1) * block]
        pieces.append(multiply_arrays(part.astype(jnp.bfloat16), upper) + running)
        running = running + jnp.sum(part, axis=1, keepdims=True)
    before = jnp.concatenate(pieces, axis=1)
    rank = jnp.sum(marks * before, axis=0, keepdims=True)
    own_slot = jnp.where(first & (rank < float(capacity)), owner * float(capacity) + rank, -1.0)
    for b in range(blocks):
        own_buf[pl.ds(b * block, block), :] = jnp.broadcast_to(
            own_slot[:, b * block : (b + 1) * block], (block, block)
        ).T
    width = list_ref.shape[1]
    target = lax.broadcasted_iota(jnp.int32, (1, width), 1).astype(jnp.float32)

    def settle(b, carry):
        slot, listed = carry
        window = pl.ds(pl.multiple_of(b * block, block), block)
        column, slot_column = id_buf[window, 0:1], own_buf[window, 0:1]
        slot = jnp.maximum(
            slot, jnp.max(jnp.where(column == ids, slot_column, -1.0), axis=0, keepdims=True)
        )
        listed = jnp.maximum(
            listed, jnp.max(jnp.where(slot_column == target, column, -1.0), axis=0, keepdims=True)
        )
        return (slot, listed)

    slot, listed = lax.fori_loop(
        0,
        blocks,
        settle,
        (jnp.full((1, slots), -1.0, jnp.float32), jnp.full((1, width), -1.0, jnp.float32)),
    )
    slot_ref[...] = slot.astype(jnp.int32)
    list_ref[...] = listed.astype(jnp.int32)
    count_ref[...] = jnp.broadcast_to(running, count_ref.shape).astype(jnp.int32)


def make_plan(perm, all_ids, capacity, vocab_local, groups):
    slots = perm.shape[0]
    table = all_ids.reshape(-1, 128).T
    high = table // 256
    low = table - high * 256
    return pl.pallas_call(
        partial(plan_kernel, capacity, vocab_local, groups),
        out_shape=[
            jax.ShapeDtypeStruct((1, slots), jnp.int32),
            jax.ShapeDtypeStruct((1, groups * capacity), jnp.int32),
            jax.ShapeDtypeStruct((groups, 128), jnp.int32),
        ],
        in_specs=[in_vmem()] * 3,
        out_specs=[in_vmem()] * 3,
        scratch_shapes=[pltpu.VMEM((slots, 128), jnp.float32), pltpu.VMEM((slots, 128), jnp.float32)],
        compiler_params=pltpu.CompilerParams(vmem_limit_bytes=VMEM_BYTES),
    )(perm[None], low.astype(jnp.bfloat16), high.astype(jnp.bfloat16))


def loss_kernel(pooled_ref, head_ref, pair_ref, loss_ref, low_ref, grad_ref, back_ref):
    total = pooled_ref.shape[0]
    low = pooled_ref[...].astype(jnp.bfloat16)
    low_ref[...] = low
    head_low = head_ref[...].astype(jnp.bfloat16)
    vectors = multiply_arrays(low, head_low)
    depth = vectors.shape[1]
    lane = lax.broadcasted_iota(jnp.int32, vectors.shape, 1)
    across = lax.broadcasted_iota(jnp.int32, (total, total), 1)
    diagonal = lax.broadcasted_iota(jnp.int32, (total, total), 0) == across
    chosen = across == pair_ref[...]
    loss = jnp.zeros((1, 1), jnp.float32)
    grads = jnp.zeros(vectors.shape, jnp.float32)

    def exact(left, right, dims):
        return lax.dot_general(
            left, right, (dims, ((), ())), precision=HIGHEST_MODE, preferred_element_type=jnp.float32
        )

    for fraction in (16, 4, 1):
        prefix = jnp.where(lane < depth // fraction, vectors, 0.0)
        inverse = lax.rsqrt(jnp.sum(prefix * prefix, axis=1, keepdims=True) + 1e-06)
        unit = prefix * inverse
        logits = exact(unit, unit, ((1,), (1,))) / LOGIT_DIVISOR
        logits = jnp.where(diagonal, MASK_FILL, logits)
        top = jnp.max(logits, axis=1, keepdims=True)
        weights = jnp.exp(logits - top)
        weight_sum = jnp.sum(weights, axis=1, keepdims=True)
        positive = jnp.sum(jnp.where(chosen, logits, 0.0), axis=1, keepdims=True)
        loss = loss + jnp.sum(jnp.log(weight_sum) + top - positive, keepdims=True)
        pull = weights / weight_sum - jnp.where(chosen, 1.0, 0.0)
        unit_grad = (exact(pull, unit, ((1,), (0,))) + exact(pull, unit, ((0,), (0,)))) / LOGIT_DIVISOR
        unit_grad = jnp.where(lane < depth // fraction, unit_grad, 0.0)
        inner = jnp.sum(unit_grad * prefix, axis=1, keepdims=True)
        grads = grads + inverse * unit_grad - prefix * (inverse * inverse * inverse * inner)
    loss_ref[...] = jnp.broadcast_to(loss, loss_ref.shape)
    grad_ref[...] = grads
    back_ref[...] = exact(grads, head_low.astype(jnp.float32), ((1,), (1,)))


def contrast_step(pooled, head_weight, pairs):
    total, depth = pooled.shape
    return pl.pallas_call(
        loss_kernel,
        out_shape=[
            jax.ShapeDtypeStruct((8, 128), jnp.float32),
            jax.ShapeDtypeStruct((total, depth), jnp.bfloat16),
            jax.ShapeDtypeStruct((total, depth), jnp.float32),
            jax.ShapeDtypeStruct((total, depth), jnp.float32),
        ],
        in_specs=[in_vmem()] * 3,
        out_specs=[in_vmem()] * 4,
        compiler_params=pltpu.CompilerParams(vmem_limit_bytes=VMEM_BYTES),
    )(pooled, head_weight, pairs[:, None])


CAPACITY = 256


def body(
    token_ids,
    slot_perm,
    seq_lengths,
    pair_index,
    tok_table,
    tok_first,
    tok_second,
    pos_table,
    pos_first,
    pos_second,
    query_key_value_weight,
    qkv_first,
    qkv_second,
    out_weight,
    out_first,
    out_second,
    up_weight,
    up_first,
    up_second,
    down_weight,
    down_first,
    down_second,
    head_weight,
    head_first,
    head_second,
    col_bias,
    col_first,
    col_second,
    row_params,
    row_first,
    row_second,
):
    groups = lax.axis_size("dp")
    tensor_count = lax.axis_size("tensor")
    group_index = lax.axis_index("dp")
    tensor_index = lax.axis_index("tensor")
    tok_dev = token_ids.shape[0]
    tok_grp = tok_dev * tensor_count
    col_width = pos_table.shape[1]
    vocab_local = tok_table.shape[0]
    column_start = tensor_index * col_width
    anchors = pair_index.shape[0]
    id_rows = tok_dev // 128
    block = jnp.concatenate(
        [
            token_ids.reshape(id_rows, 128),
            slot_perm.reshape(id_rows, 128),
            jnp.pad(pair_index, (0, 128 - anchors))[None],
            jnp.zeros((16 - 2 * id_rows - 1, 128), jnp.int32),
        ],
        axis=0,
    )
    gathered = gather_all(block, 1)
    all_ids = gathered[:, :id_rows].reshape(-1)
    pairs = gathered[:: tensor_count, 2 * id_rows, :anchors].reshape(-1)
    own_perm = lax.dynamic_slice_in_dim(
        gathered, group_index * tensor_count, tensor_count, 0
    )[:, id_rows : 2 * id_rows].reshape(-1)
    slot, listed, counts_out = make_plan(own_perm, all_ids, CAPACITY, vocab_local, groups)
    slot = slot[0]
    list_rows = CAPACITY // 128
    top_count = jnp.max(counts_out)
    request = jnp.concatenate(
        [
            listed.reshape(groups, list_rows, 128),
            jnp.broadcast_to(top_count, (groups, 8 - list_rows, 128)),
        ],
        axis=1,
    )
    asked = swap(request, "dp", 2)
    overflow = jnp.max(asked[:, list_rows]) > CAPACITY
    offset = group_index * vocab_local
    asked_rows = asked[:, :list_rows].reshape(-1) - offset
    asked_safe = jnp.clip(asked_rows, 0, vocab_local - 1)
    sent_rows = jnp.take(tok_table, asked_safe, axis=0).astype(jnp.bfloat16)
    got_rows = swap(sent_rows.reshape(groups, CAPACITY, col_width), "dp", 3).reshape(-1, col_width)
    chooser = (slot[:, None] == jnp.arange(groups * CAPACITY, dtype=jnp.int32)[None, :]).astype(
        jnp.bfloat16
    )
    lengths = seq_lengths[0]
    seq_ids, positions, member = seq_layout(lengths, tok_grp)

    def every_slot_id():
        every_perm = gathered[:, id_rows : 2 * id_rows].reshape(-1)
        return jnp.take(all_ids, every_perm, axis=0)

    def spread_wide():
        wanted = every_slot_id() - offset
        inside = (wanted >= 0) & (wanted < vocab_local)
        picked = jnp.take(
            tok_table.astype(jnp.bfloat16), jnp.clip(wanted, 0, vocab_local - 1), axis=0
        )
        return lax.psum_scatter(
            jnp.where(inside[:, None], picked, jnp.zeros((), jnp.bfloat16)),
            "dp",
            scatter_dimension=0,
            tiled=True,
        )

    tok_cols = lax.cond(
        overflow,
        spread_wide,
        lambda: multiply_arrays(chooser, got_rows).astype(jnp.bfloat16),
    )
    pos_full = lax.all_gather(pos_table, "tensor", axis=1, tiled=True)
    emb_all = column_spread(tok_cols, 4).astype(jnp.float32) + jnp.take(pos_full, positions, axis=0)
    layer_mats = (
        lax.all_gather(query_key_value_weight.astype(jnp.bfloat16), "dp", axis=0, tiled=True),
        lax.all_gather(out_weight.astype(jnp.bfloat16), "dp", axis=1, tiled=True),
        lax.all_gather(up_weight.astype(jnp.bfloat16), "dp", axis=0, tiled=True),
        lax.all_gather(down_weight.astype(jnp.bfloat16), "dp", axis=2, tiled=True),
    )
    norm_third, saved_vals = layer_forward(emb_all, seq_ids, row_params, col_bias, layer_mats)
    row_member = lax.dynamic_slice_in_dim(member, tensor_index * tok_dev, tok_dev, 0).astype(
        jnp.float32
    )
    counts = lengths.astype(jnp.float32)[:, None]
    pooled = sum_all(exact_multiply(row_member.T, norm_third) / counts, True, 9)
    loss_out, pooled_low, vec_grad, pooled_grad = contrast_step(
        pooled.reshape(-1, D), head_weight, pairs
    )
    head_sum = exact_multiply(pooled_low.astype(jnp.float32).T, vec_grad)
    own_grad = lax.dynamic_slice_in_dim(pooled_grad, group_index * anchors, anchors, 0)
    grad_third = exact_multiply(row_member, own_grad / counts)
    emb_grad, mats_grad, col_grad, row_grad = layer_backward(
        grad_third, seq_ids, row_params, layer_mats, saved_vals
    )
    cols_grad = swap(
        emb_grad.astype(jnp.bfloat16).reshape(tok_dev, tensor_count, col_width).swapaxes(0, 1),
        "tensor",
        14,
    ).reshape(tok_grp, col_width)
    pos_pick = (
        jnp.arange(pos_table.shape[0], dtype=jnp.int32)[:, None] == positions[None, :]
    ).astype(jnp.bfloat16)
    pos_grad = multiply_arrays(pos_pick, cols_grad)
    merged = jnp.einsum("kn,kc->nc", chooser, cols_grad, preferred_element_type=jnp.float32)
    back_rows = swap(merged.astype(jnp.bfloat16).reshape(groups, CAPACITY, col_width), "dp", 15)

    def add_wide():
        wanted = every_slot_id() - offset
        inside = (wanted >= 0) & (wanted < vocab_local)
        return (
            jnp.zeros(tok_table.shape, jnp.float32)
            .at[jnp.clip(wanted, 0, vocab_local - 1)]
            .add(
                jnp.where(
                    inside[:, None],
                    lax.all_gather(cols_grad, "dp", axis=0, tiled=True).astype(jnp.float32),
                    0.0,
                )
            )
        )

    def add_listed():
        return (
            jnp.zeros(tok_table.shape, jnp.float32)
            .at[jnp.where(asked_rows < 0, vocab_local, asked_rows)]
            .add(back_rows.reshape(-1, col_width).astype(jnp.float32), mode="drop")
        )

    tok_grad = lax.cond(overflow, add_wide, add_listed)
    qkv_part, out_part, up_part, down_part = mats_grad
    qkv_grad, out_grad, up_grad, down_grad = (
        lax.psum_scatter(qkv_part, "dp", scatter_dimension=0, tiled=True),
        lax.psum_scatter(out_part, "dp", scatter_dimension=1, tiled=True),
        lax.psum_scatter(up_part, "dp", scatter_dimension=0, tiled=True),
        lax.psum_scatter(down_part, "dp", scatter_dimension=2, tiled=True),
    )
    pos_own, col_own = lax.psum((pos_grad, col_grad), "dp")
    shared_squares = (jnp.sum(pos_own * pos_own) + jnp.sum(col_own * col_own)) / groups
    local_squares = (
        jnp.sum(tok_grad * tok_grad)
        + jnp.sum(qkv_grad * qkv_grad)
        + jnp.sum(out_grad * out_grad)
        + jnp.sum(up_grad * up_grad)
        + jnp.sum(down_grad * down_grad)
        + shared_squares
    )
    row_block = jnp.concatenate(
        [row_grad, jnp.pad(local_squares.reshape(1, 1), ((0, 7), (0, D - 1)))], axis=0
    )
    row_total = sum_all(row_block, False, 16)[0]
    row_sum = row_total[:8]
    squares = row_total[8, 0] + jnp.sum(row_sum * row_sum) + jnp.sum(head_sum * head_sum)
    grad_norm = jnp.sqrt(squares)
    clip_scale = jnp.minimum(1.0, CLIP_NORM / (grad_norm + 1e-06))
    tok_new = adam_step(
        tok_table, tok_first, tok_second, tok_grad * clip_scale, RATE_MATRIX, DECAY_RATE
    )
    pos_new = adam_step(
        pos_table, pos_first, pos_second, pos_own * clip_scale, RATE_MATRIX, DECAY_RATE
    )
    qkv_new = adam_step(
        query_key_value_weight,
        qkv_first,
        qkv_second,
        qkv_grad * clip_scale,
        RATE_MATRIX,
        DECAY_RATE,
    )
    out_new = adam_step(
        out_weight, out_first, out_second, out_grad * clip_scale, RATE_MATRIX, DECAY_RATE
    )
    up_new = adam_step(
        up_weight, up_first, up_second, up_grad * clip_scale, RATE_MATRIX, DECAY_RATE
    )
    down_new = adam_step(
        down_weight, down_first, down_second, down_grad * clip_scale, RATE_MATRIX, DECAY_RATE
    )
    head_new = adam_step(
        head_weight, head_first, head_second, head_sum * clip_scale, RATE_MATRIX, DECAY_RATE
    )
    col_new = adam_step(col_bias, col_first, col_second, col_own * clip_scale, RATE_VECTOR, 0.0)
    row_new = adam_step(row_params, row_first, row_second, row_sum * clip_scale, RATE_VECTOR, 0.0)
    return (loss_out[0, 0], grad_norm) + tok_new + pos_new + qkv_new + out_new + up_new + down_new + head_new + col_new + row_new


def solution(mesh):
    placed = (
        P(("dp", "tensor")),
        P(("dp", "tensor")),
        P("dp", None),
        P("dp"),
        P("dp", "tensor"),
        P("dp", "tensor"),
        P("dp", "tensor"),
        P(None, "tensor"),
        P(None, "tensor"),
        P(None, "tensor"),
        P("dp", None, "tensor"),
        P("dp", None, "tensor"),
        P("dp", None, "tensor"),
        P("tensor", "dp"),
        P("tensor", "dp"),
        P("tensor", "dp"),
        P("dp", None, "tensor"),
        P("dp", None, "tensor"),
        P("dp", None, "tensor"),
        P(None, "tensor", "dp"),
        P(None, "tensor", "dp"),
        P(None, "tensor", "dp"),
        P(),
        P(),
        P(),
        P(None, "tensor"),
        P(None, "tensor"),
        P(None, "tensor"),
        P(),
        P(),
        P(),
    )
    return jax.shard_map(
        body,
        mesh=mesh,
        in_specs=placed,
        out_specs=(
            P(),
            P(),
            P("dp", "tensor"),
            P("dp", "tensor"),
            P("dp", "tensor"),
            P(None, "tensor"),
            P(None, "tensor"),
            P(None, "tensor"),
            P("dp", None, "tensor"),
            P("dp", None, "tensor"),
            P("dp", None, "tensor"),
            P("tensor", "dp"),
            P("tensor", "dp"),
            P("tensor", "dp"),
            P("dp", None, "tensor"),
            P("dp", None, "tensor"),
            P("dp", None, "tensor"),
            P(None, "tensor", "dp"),
            P(None, "tensor", "dp"),
            P(None, "tensor", "dp"),
            P(),
            P(),
            P(),
            P(None, "tensor"),
            P(None, "tensor"),
            P(None, "tensor"),
            P(),
            P(),
            P(),
        ),
        check_vma=False,
    )
```

```python
from functools import partial

import jax
import jax.numpy as jnp
from jax import lax
from jax.experimental import pallas as pl
from jax.experimental.pallas import tpu as pltpu
from jax.sharding import PartitionSpec as P

D = 1024
HEAD = 64
MAXLEN = 512
STEP = 10


HIGHEST_MODE = lax.Precision.HIGHEST
LN_EPS = 1e-05
LOGIT_DIVISOR = 0.05
CLIP_NORM = 0.25
BETA_FIRST = 0.9
BETA_SECOND = 0.999
ADAM_EPS = 1e-08
RATE_MATRIX = 0.05
RATE_VECTOR = 0.5
DECAY_RATE = 0.01
MASK_FILL = -1e30


def multiply_arrays(left_mat, right_mat):
    return jnp.dot(left_mat, right_mat, preferred_element_type=jnp.float32)


def exact_multiply(left_mat, right_mat):
    return jnp.dot(left_mat, right_mat, precision=HIGHEST_MODE, preferred_element_type=jnp.float32)


def norm_rows(values, gain_row, bias_row):
    center = values - jnp.mean(values, axis=1, keepdims=True)
    inverse = lax.rsqrt(jnp.mean(center * center, axis=1, keepdims=True) + LN_EPS)
    return center * inverse * gain_row + bias_row


def norm_back(values, gain_row, bias_row, grad_rows):
    norm_pull = jax.vjp(norm_rows, values, gain_row, bias_row)[1]
    return norm_pull(grad_rows)


def seq_layout(lengths, slot_total):
    seq_ends = jnp.cumsum(lengths)
    starts = seq_ends - lengths
    slot_index = jnp.arange(slot_total, dtype=jnp.int32)
    member = (slot_index[:, None] >= starts[None, :]) & (slot_index[:, None] < seq_ends[None, :])
    seq_count = jnp.arange(lengths.shape[0], dtype=jnp.int32)
    seq_ids = jnp.sum(jnp.where(member, seq_count[None, :], 0), axis=1)
    positions = slot_index - jnp.sum(jnp.where(member, starts[None, :], 0), axis=1) + 2
    return (seq_ids, positions, member)


def adam_step(weight, first_old, second_old, clipped, step_rate, decay_rate):
    first_new = BETA_FIRST * first_old + (1.0 - BETA_FIRST) * clipped
    second_new = BETA_SECOND * second_old + (1.0 - BETA_SECOND) * clipped * clipped
    first_hat = first_new / (1.0 - BETA_FIRST**STEP)
    second_hat = second_new / (1.0 - BETA_SECOND**STEP)
    weight_new = weight - step_rate * (
        first_hat / (jnp.sqrt(second_hat) + ADAM_EPS) + decay_rate * weight
    )
    return (weight_new, first_new, second_new)


MESH_IDS = pl.DeviceIdType.MESH
VMEM_BYTES = 60 * 1024 * 1024
CHUNKS = 4
LINE = 4


def in_vmem():
    return pl.BlockSpec(memory_space=pltpu.VMEM)


def shaped(shape, dtype):
    return jax.ShapeDtypeStruct(tuple(shape), dtype)


def dma(*shape):
    return pltpu.SemaphoreType.DMA(shape)


def remote(src, dst, send_sem, recv_sem, target):
    return pltpu.make_async_remote_copy(
        src_ref=src,
        dst_ref=dst,
        send_sem=send_sem,
        recv_sem=recv_sem,
        device_id=target,
        device_id_type=MESH_IDS,
    )


def comm_params(collective):
    return pltpu.CompilerParams(
        collective_id=collective, has_side_effects=True, vmem_limit_bytes=VMEM_BYTES
    )


def exchange(collective, *tasks):
    def kernel(*refs):
        at = 0
        for attribute in ("ins", "outs", "scratch"):
            for task in tasks:
                size = len(getattr(task, attribute))
                setattr(task, attribute + "_refs", refs[at : at + size])
                at += size
        barrier = pltpu.get_barrier_semaphore()
        partners = [partner for task in tasks for partner in task.partners()]
        for partner in partners:
            pl.semaphore_signal(barrier, inc=1, device_id=partner, device_id_type=MESH_IDS)
        pl.semaphore_wait(barrier, len(partners))
        for task in tasks:
            task.begin()
        for task in tasks:
            task.middle()
        for task in tasks:
            task.end()

    results = pl.pallas_call(
        kernel,
        out_shape=[out for task in tasks for out in task.outs],
        in_specs=[in_vmem() for task in tasks for _ in task.ins],
        out_specs=[in_vmem() for task in tasks for _ in task.outs],
        scratch_shapes=[item for task in tasks for item in task.scratch],
        compiler_params=comm_params(collective),
    )(*[array for task in tasks for array in task.ins])
    return results[0] if len(results) == 1 else results


def tensor_place(width):
    me = lax.axis_index("tensor")
    core = lax.rem(me, 2)
    row = me // 2
    mate = me + 1 - 2 * core
    return (me, core, row, mate)


class Task:
    def begin(self):
        pass

    def middle(self):
        pass

    def end(self):
        pass


class Pair(Task):
    def __init__(self):
        self.width = lax.axis_size("tensor")
        self.rows = self.width // 2

    def partners(self):
        me, core, row, mate = tensor_place(self.width)
        return [{"tensor": mate}] + [
            {"tensor": lax.rem(row + step, self.rows) * 2 + core} for step in range(1, self.rows)
        ]


class Spread(Pair):
    def __init__(self, block, columns=False, chunks=CHUNKS):
        super().__init__()
        height, depth = block.shape
        self.columns, self.chunks = columns, chunks
        self.ins = (block,)
        whole = (height, self.width * depth) if columns else (self.width * height, depth)
        self.outs = (shaped(whole, block.dtype),)
        self.scratch = tuple(dma(self.rows, chunks) for _ in range(4))

    def window(self, owner, part=None):
        (x_ref,), (o_ref,) = self.ins_refs, self.outs_refs
        height, depth = x_ref.shape
        size = height // self.chunks
        if self.columns:
            lanes = pl.ds(pl.multiple_of(owner * depth, depth), depth)
            if part is None or self.chunks == 1:
                return o_ref.at[:, lanes]
            return o_ref.at[pl.ds(part * size, size), lanes]
        if part is None:
            return o_ref.at[pl.ds(pl.multiple_of(owner * height, height), height)]
        return o_ref.at[pl.ds(pl.multiple_of(owner * height + part * size, size), size)]

    def begin(self):
        (x_ref,) = self.ins_refs
        far_send, far_recv, near_send, near_recv = self.scratch_refs
        me, core, row, mate = tensor_place(self.width)
        size = x_ref.shape[0] // self.chunks
        self.far = {}
        for part in range(self.chunks):
            source = x_ref if self.chunks == 1 else x_ref.at[pl.ds(part * size, size)]
            for step in range(1, self.rows):
                copy = remote(
                    source,
                    self.window(me, part),
                    far_send.at[step, part],
                    far_recv.at[step, part],
                    {"tensor": lax.rem(row + step, self.rows) * 2 + core},
                )
                copy.start()
                self.far[step, part] = copy
        copy = remote(
            x_ref, self.window(me), near_send.at[0, 0], near_recv.at[0, 0], {"tensor": mate}
        )
        copy.start()
        self.near = [copy]
        self.window(me)[...] = x_ref[...]

    def middle(self):
        far_send, far_recv, near_send, near_recv = self.scratch_refs
        me, core, row, mate = tensor_place(self.width)
        for part in range(self.chunks):
            for step in range(1, self.rows):
                self.far[step, part].wait_recv()
                source = lax.rem(row + self.rows - step, self.rows) * 2 + core
                onward = remote(
                    self.window(source, part),
                    self.window(source, part),
                    near_send.at[step, part],
                    near_recv.at[step, part],
                    {"tensor": mate},
                )
                onward.start()
                self.near.append(onward)

    def end(self):
        for copy in self.near:
            copy.wait()
        for copy in self.far.values():
            copy.wait_send()


class Fold(Pair):
    def __init__(self, parts, chunks=CHUNKS):
        super().__init__()
        height, depth = parts.shape[0] // self.width, parts.shape[1]
        far_rows = max(self.rows - 1, 1)
        self.chunks = chunks
        self.ins = (parts,)
        self.outs = (shaped((height, depth), jnp.float32),)
        self.scratch = (
            pltpu.VMEM((self.rows, height, depth), jnp.bfloat16),
            pltpu.VMEM((far_rows, height, depth), jnp.bfloat16),
            pltpu.VMEM((far_rows, height, depth), jnp.bfloat16),
        ) + tuple(dma(self.rows, chunks) for _ in range(4))

    def span(self, owner, part):
        height = self.outs[0].shape[0]
        size = height // self.chunks
        return pl.ds(pl.multiple_of(owner * height + part * size, size), size)

    def local(self, part):
        size = self.outs[0].shape[0] // self.chunks
        return pl.ds(part * size, size)

    def begin(self):
        (p_ref,) = self.ins_refs
        near_buf, near_send, near_recv = self.scratch_refs[0], *self.scratch_refs[3:5]
        me, core, row, mate = tensor_place(self.width)
        self.near = {}
        for step in list(range(1, self.rows)) + [0]:
            dest_row = lax.rem(row + step, self.rows)
            for part in range(self.chunks):
                copy = remote(
                    p_ref.at[self.span(dest_row * 2 + 1 - core, part)],
                    near_buf.at[step, self.local(part)],
                    near_send.at[step, part],
                    near_recv.at[step, part],
                    {"tensor": mate},
                )
                copy.start()
                self.near[step, part] = copy

    def middle(self):
        (p_ref,), (o_ref,) = self.ins_refs, self.outs_refs
        near_buf, sum_buf, far_buf, near_send, near_recv, far_send, far_recv = self.scratch_refs
        me, core, row, mate = tensor_place(self.width)
        self.far = {}
        for step in range(1, self.rows):
            dest = lax.rem(row + step, self.rows) * 2 + core
            for part in range(self.chunks):
                local = self.local(part)
                self.near[step, part].wait_recv()
                sum_buf[step - 1, local] = (
                    p_ref[self.span(dest, part)].astype(jnp.float32)
                    + near_buf[step, local].astype(jnp.float32)
                ).astype(jnp.bfloat16)
                copy = remote(
                    sum_buf.at[step - 1, local],
                    far_buf.at[step - 1, local],
                    far_send.at[step - 1, part],
                    far_recv.at[step - 1, part],
                    {"tensor": dest},
                )
                copy.start()
                self.far[step, part] = copy
        for part in range(self.chunks):
            local = self.local(part)
            self.near[0, part].wait_recv()
            o_ref[local] = p_ref[self.span(me, part)].astype(jnp.float32) + near_buf[
                0, local
            ].astype(jnp.float32)

    def end(self):
        (o_ref,) = self.outs_refs
        far_buf = self.scratch_refs[2]
        for part in range(self.chunks):
            local = self.local(part)
            for step in range(1, self.rows):
                self.far[step, part].wait_recv()
                o_ref[local] += far_buf[step - 1, local].astype(jnp.float32)
        for copy in list(self.near.values()) + list(self.far.values()):
            copy.wait_send()


class Swap(Task):
    def __init__(self, blocks, axis):
        self.axis, self.count = axis, lax.axis_size(axis)
        self.ins = (blocks,)
        self.outs = (shaped(blocks.shape, blocks.dtype),)
        self.scratch = (dma(self.count), dma(self.count))

    def others(self):
        me = lax.axis_index(self.axis)
        return [lax.rem(me + step, self.count) for step in range(1, self.count)]

    def partners(self):
        return [{self.axis: other} for other in self.others()]

    def begin(self):
        (x_ref,), (o_ref,), (send, recv) = self.ins_refs, self.outs_refs, self.scratch_refs
        me = lax.axis_index(self.axis)
        self.copies = [
            remote(x_ref.at[other], o_ref.at[me], send.at[i], recv.at[i], {self.axis: other})
            for i, other in enumerate(self.others())
        ]
        for copy in self.copies:
            copy.start()
        o_ref[me] = x_ref[me]

    def end(self):
        for copy in self.copies:
            copy.wait()


class Gather(Swap):
    def __init__(self, block, axis):
        super().__init__(block, axis)
        self.outs = (shaped((self.count,) + block.shape, block.dtype),)

    def begin(self):
        (x_ref,), (o_ref,), (send, recv) = self.ins_refs, self.outs_refs, self.scratch_refs
        me = lax.axis_index(self.axis)
        self.copies = [
            remote(x_ref, o_ref.at[me], send.at[i], recv.at[i], {self.axis: other})
            for i, other in enumerate(self.others())
        ]
        for copy in self.copies:
            copy.start()
        o_ref[me] = x_ref[...]


class GridTask(Task):
    def __init__(self):
        self.cross = lax.axis_size("dp") // LINE

    def place(self):
        me = lax.axis_index("dp")
        return (me // self.cross, lax.rem(me, self.cross))


class ReduceCross(GridTask):
    def __init__(self, blocks):
        super().__init__()
        shape = blocks.shape[1:]
        self.blocks_shape = (LINE, self.cross) + shape
        self.ins = (blocks.reshape(self.blocks_shape),)
        self.outs = (shaped((LINE,) + shape, jnp.bfloat16),)
        others = max(self.cross - 1, 1)
        self.scratch = (
            pltpu.VMEM((others, LINE) + shape, jnp.bfloat16),
            dma(others, LINE),
            dma(others, LINE),
        )

    def targets(self):
        line, cross = self.place()
        return [lax.rem(cross + step, self.cross) for step in range(1, self.cross)]

    def partners(self):
        line, cross = self.place()
        return [{"dp": line * self.cross + other} for other in self.targets()]

    def begin(self):
        (x_ref,), (buf, send, recv) = self.ins_refs, self.scratch_refs
        line, cross = self.place()
        self.copies = []
        for i, other in enumerate(self.targets()):
            for z in range(LINE):
                copy = remote(
                    x_ref.at[z, other],
                    buf.at[i, z],
                    send.at[i, z],
                    recv.at[i, z],
                    {"dp": line * self.cross + other},
                )
                copy.start()
                self.copies.append(copy)

    def end(self):
        (x_ref,), (o_ref,), (buf, send, recv) = self.ins_refs, self.outs_refs, self.scratch_refs
        line, cross = self.place()
        for copy in self.copies:
            copy.wait()
        for z in range(LINE):
            total = x_ref[z, cross].astype(jnp.float32)
            for i in range(self.cross - 1):
                total = total + buf[i, z].astype(jnp.float32)
            o_ref[z] = total.astype(jnp.bfloat16)


class ReduceLine(GridTask):
    def __init__(self, blocks):
        super().__init__()
        shape = blocks.shape[1:]
        self.ins = (blocks,)
        self.outs = (shaped(shape, jnp.float32),)
        self.scratch = (pltpu.VMEM((LINE - 1,) + shape, jnp.bfloat16), dma(LINE - 1), dma(LINE - 1))

    def targets(self):
        line, cross = self.place()
        return [lax.rem(line + step, LINE) for step in range(1, LINE)]

    def partners(self):
        line, cross = self.place()
        return [{"dp": other * self.cross + cross} for other in self.targets()]

    def begin(self):
        (x_ref,), (buf, send, recv) = self.ins_refs, self.scratch_refs
        line, cross = self.place()
        self.copies = [
            remote(
                x_ref.at[other], buf.at[i], send.at[i], recv.at[i], {"dp": other * self.cross + cross}
            )
            for i, other in enumerate(self.targets())
        ]
        for copy in self.copies:
            copy.start()

    def end(self):
        (x_ref,), (o_ref,), (buf, send, recv) = self.ins_refs, self.outs_refs, self.scratch_refs
        line, cross = self.place()
        for copy in self.copies:
            copy.wait()
        total = x_ref[line].astype(jnp.float32)
        for i in range(LINE - 1):
            total = total + buf[i].astype(jnp.float32)
        o_ref[...] = total


class SumAll(Task):
    def __init__(self, block, keep):
        self.groups, self.width, self.keep = lax.axis_size("dp"), lax.axis_size("tensor"), keep
        rows, depth = block.shape
        self.narrow = narrow = depth // self.width
        kept = self.groups if keep else 1
        self.ins = (block,)
        self.outs = (shaped((kept, rows, depth), block.dtype),)
        near, far = dma(self.width), dma(self.groups)
        self.scratch = (
            pltpu.VMEM((self.width, rows, narrow), block.dtype),
            pltpu.VMEM((rows, narrow), block.dtype),
            pltpu.VMEM((self.groups, rows, narrow), block.dtype),
            pltpu.VMEM((kept, rows, narrow), block.dtype),
            near, near, far, far, near, near,
        )

    def mates(self):
        me = lax.axis_index("tensor")
        return [lax.rem(me + step, self.width) for step in range(1, self.width)]

    def peers(self):
        me = lax.axis_index("dp")
        return [lax.rem(me + step, self.groups) for step in range(1, self.groups)]

    def partners(self):
        return [{"tensor": mate} for mate in self.mates()] + [{"dp": peer} for peer in self.peers()]

    def lanes(self, owner):
        return pl.ds(pl.multiple_of(owner * self.narrow, self.narrow), self.narrow)

    def launch(self, copies):
        for copy in copies:
            copy.start()
        self.copies = copies

    def settle(self):
        for copy in self.copies:
            copy.wait()

    def begin(self):
        (x_ref,) = self.ins_refs
        part_buf, sems = self.scratch_refs[0], self.scratch_refs[4:]
        me = lax.axis_index("tensor")
        self.launch(
            [
                remote(
                    x_ref.at[:, self.lanes(mate)],
                    part_buf.at[me],
                    sems[0].at[i],
                    sems[1].at[i],
                    {"tensor": mate},
                )
                for i, mate in enumerate(self.mates())
            ]
        )
        part_buf[me] = x_ref[:, self.lanes(me)]

    def middle(self):
        (o_ref,) = self.outs_refs
        part_buf, sum_buf, all_buf, out_buf = self.scratch_refs[:4]
        sems = self.scratch_refs[4:]
        dp_me, me = lax.axis_index("dp"), lax.axis_index("tensor")
        self.settle()
        sum_buf[...] = jnp.sum(part_buf[...], axis=0)
        self.launch(
            [
                remote(sum_buf, all_buf.at[dp_me], sems[2].at[i], sems[3].at[i], {"dp": peer})
                for i, peer in enumerate(self.peers())
            ]
        )
        all_buf[dp_me] = sum_buf[...]
        self.settle()
        if self.keep:
            out_buf[...] = all_buf[...]
        else:
            out_buf[0] = jnp.sum(all_buf[...], axis=0)
        self.launch(
            [
                remote(
                    out_buf,
                    o_ref.at[:, :, self.lanes(me)],
                    sems[4].at[i],
                    sems[5].at[i],
                    {"tensor": mate},
                )
                for i, mate in enumerate(self.mates())
            ]
        )
        o_ref[:, :, self.lanes(me)] = out_buf[...]

    def end(self):
        self.settle()


def gather_all_kernel(groups, width, x_ref, o_ref, send, recv):
    total = groups * width
    me = lax.axis_index("dp") * width + lax.axis_index("tensor")

    def place(step):
        other = lax.rem(me + step, total)
        return (other // width, lax.rem(other, width))

    barrier = pltpu.get_barrier_semaphore()

    def hello(step, carry):
        pl.semaphore_signal(barrier, inc=1, device_id=place(step), device_id_type=MESH_IDS)
        return carry

    lax.fori_loop(1, total, hello, 0)
    pl.semaphore_wait(barrier, total - 1)

    def copy(step):
        return remote(x_ref, o_ref.at[me], send.at[step], recv.at[step], place(step))

    def begin(step, carry):
        copy(step).start()
        return carry

    def finish(step, carry):
        copy(step).wait()
        return carry

    lax.fori_loop(1, total, begin, 0)
    o_ref[me] = x_ref[...]
    lax.fori_loop(1, total, finish, 0)


def gather_all(block, collective):
    groups, width = lax.axis_size("dp"), lax.axis_size("tensor")
    total = groups * width
    return pl.pallas_call(
        partial(gather_all_kernel, groups, width),
        out_shape=jax.ShapeDtypeStruct((total,) + block.shape, block.dtype),
        in_specs=[in_vmem()],
        out_specs=in_vmem(),
        scratch_shapes=[pltpu.SemaphoreType.DMA((total,)), pltpu.SemaphoreType.DMA((total,))],
        compiler_params=comm_params(collective),
    )(block)


Q_BLOCK = 256
K_BLOCK = 256


def split_pair(wide):
    half = wide.shape[0] // 2
    upper = lax.broadcasted_iota(jnp.int32, wide.shape, 0) < half
    zero = jnp.zeros_like(wide)
    return jnp.concatenate([jnp.where(upper, wide, zero), jnp.where(upper, zero, wide)], axis=1)


def stack_pair(tall):
    half = tall.shape[1] // 2
    left = lax.broadcasted_iota(jnp.int32, tall.shape, 1) < half
    zero = jnp.zeros_like(tall)
    return jnp.concatenate([jnp.where(left, tall, zero), jnp.where(left, zero, tall)], axis=0)


def join_pair(wide):
    depth, columns = wide.shape
    upper = lax.broadcasted_iota(jnp.int32, (depth, columns // 2), 0) < depth // 2
    return jnp.where(upper, wide[:, : columns // 2], wide[:, columns // 2 :])


def turn(tile):
    return tile.astype(jnp.float32).T.astype(jnp.bfloat16)


def block_span(index, size):
    return pl.ds(pl.multiple_of(index * size, size), size)


def attend_kernel(low_ref, high_ref, qkv_ref, seq_col_ref, seq_row_ref, out_ref, log_ref, value_turned, scores):
    slots, columns = out_ref.shape
    pairs = columns // 128
    q_blocks, k_blocks = slots // Q_BLOCK, slots // K_BLOCK

    def turn_values(b, carry):
        rows = block_span(b, K_BLOCK)
        for pair in range(pairs):
            value_turned[pl.ds(pair * 128, 128), rows] = turn(
                qkv_ref[rows, pl.ds(2 * columns + pair * 128, 128)]
            )
        return carry

    lax.fori_loop(0, k_blocks, turn_values, 0)

    def one_block(q_index, carry):
        q_rows = block_span(q_index, Q_BLOCK)
        lowest, highest = low_ref[q_index], high_ref[q_index]
        seq_row = seq_row_ref[0:1, q_rows]
        seq_pair = jnp.concatenate([seq_row, seq_row], axis=1)
        queries = [
            split_pair(
                (qkv_ref[q_rows, pl.ds(pair * 128, 128)].astype(jnp.float32) * HEAD ** (-0.5))
                .T.astype(jnp.bfloat16)
            )
            for pair in range(pairs)
        ]

        def score(k_index, tops):
            k_rows = block_span(k_index, K_BLOCK)
            same = seq_col_ref[k_rows, 0:1] == seq_pair
            later = []
            for pair in range(pairs):
                keys = qkv_ref[k_rows, pl.ds(columns + pair * 128, 128)]
                value = jnp.where(same, multiply_arrays(keys, queries[pair]), MASK_FILL)
                scores[pair, k_index - lowest] = value
                later.append(jnp.maximum(tops[pair], jnp.max(value, axis=0, keepdims=True)))
            return tuple(later)

        start = tuple(jnp.full((1, 2 * Q_BLOCK), MASK_FILL, jnp.float32) for _ in range(pairs))
        tops = lax.fori_loop(lowest, highest, score, start)

        def mix(k_index, state):
            k_rows = block_span(k_index, K_BLOCK)
            later = []
            for pair in range(pairs):
                total, mixed = state[pair]
                weights = jnp.exp(scores[pair, k_index - lowest] - tops[pair])
                total = total + jnp.sum(weights, axis=0, keepdims=True)
                mixed = mixed + multiply_arrays(
                    value_turned[pl.ds(pair * 128, 128), k_rows], weights.astype(jnp.bfloat16)
                )
                later.append((total, mixed))
            return tuple(later)

        blank = tuple(
            (jnp.zeros((1, 2 * Q_BLOCK), jnp.float32), jnp.zeros((128, 2 * Q_BLOCK), jnp.float32))
            for _ in range(pairs)
        )
        final = lax.fori_loop(lowest, highest, mix, blank)
        for pair in range(pairs):
            total, mixed = final[pair]
            out_ref[q_rows, pl.ds(pair * 128, 128)] = join_pair(mixed / total).T.astype(jnp.bfloat16)
            logs = tops[pair] + jnp.log(total)
            log_ref[pl.ds(2 * pair, 1), q_rows] = logs[:, :Q_BLOCK]
            log_ref[pl.ds(2 * pair + 1, 1), q_rows] = logs[:, Q_BLOCK:]
        return carry

    lax.fori_loop(0, q_blocks, one_block, 0)


def block_bounds(lengths, slots):
    ends = jnp.cumsum(lengths)
    starts = ends - lengths
    first = jnp.arange(slots // Q_BLOCK, dtype=jnp.int32) * Q_BLOCK
    last = first + Q_BLOCK - 1
    lowest = jnp.max(
        jnp.where(starts[None, :] <= first[:, None], starts[None, :], 0), axis=1
    )
    highest = jnp.min(jnp.where(ends[None, :] > last[:, None], ends[None, :], slots), axis=1)
    return (lowest // K_BLOCK, (highest + K_BLOCK - 1) // K_BLOCK)


REACH = (2 * MAXLEN - 2) // K_BLOCK + Q_BLOCK // K_BLOCK + 1


def in_scalars():
    return pl.BlockSpec(memory_space=pltpu.SMEM)


def attend(qkv_out, seq_ids, bounds):
    slots, columns = qkv_out.shape[0], qkv_out.shape[1] // 3
    pairs = columns // 128
    return pl.pallas_call(
        attend_kernel,
        out_shape=[
            jax.ShapeDtypeStruct((slots, columns), jnp.bfloat16),
            jax.ShapeDtypeStruct((8, slots), jnp.float32),
        ],
        in_specs=[in_scalars(), in_scalars()] + [in_vmem()] * 3,
        out_specs=[in_vmem()] * 2,
        scratch_shapes=[
            pltpu.VMEM((columns, slots), jnp.bfloat16),
            pltpu.VMEM((pairs, REACH, K_BLOCK, 2 * Q_BLOCK), jnp.float32),
        ],
        compiler_params=pltpu.CompilerParams(vmem_limit_bytes=VMEM_BYTES),
    )(bounds[0], bounds[1], qkv_out, seq_ids[:, None], jnp.broadcast_to(seq_ids[None], (8, slots)))


def attend_back_kernel(
    low_ref, high_ref, qkv_ref, grad_ref, log_ref, seq_col_ref, seq_row_ref, out_ref,
    key_turned, probs, prob_grads, key_sum, value_sum,
):
    slots, columns = grad_ref.shape
    pairs = columns // 128
    q_blocks, k_blocks = slots // Q_BLOCK, slots // K_BLOCK

    def turn_keys(b, carry):
        rows = block_span(b, K_BLOCK)
        for pair in range(pairs):
            key_turned[pl.ds(pair * 128, 128), rows] = turn(
                qkv_ref[rows, pl.ds(columns + pair * 128, 128)]
            )
        key_sum[rows] = jnp.zeros((K_BLOCK, columns), jnp.float32)
        value_sum[rows] = jnp.zeros((K_BLOCK, columns), jnp.float32)
        return carry

    lax.fori_loop(0, k_blocks, turn_keys, 0)

    def one_block(q_index, carry):
        q_rows = block_span(q_index, Q_BLOCK)
        lowest, highest = low_ref[q_index], high_ref[q_index]
        seq_row = seq_row_ref[0:1, q_rows]
        seq_pair = jnp.concatenate([seq_row, seq_row], axis=1)
        scaled, queries, grads, turned, logs = [], [], [], [], []
        for pair in range(pairs):
            plain = qkv_ref[q_rows, pl.ds(pair * 128, 128)].astype(jnp.float32) * HEAD ** (-0.5)
            scaled.append(stack_pair(plain.astype(jnp.bfloat16)))
            queries.append(split_pair(plain.T.astype(jnp.bfloat16)))
            grad = grad_ref[q_rows, pl.ds(pair * 128, 128)]
            grads.append(stack_pair(grad))
            turned.append(split_pair(turn(grad)))
            logs.append(
                jnp.concatenate(
                    [log_ref[pl.ds(2 * pair, 1), q_rows], log_ref[pl.ds(2 * pair + 1, 1), q_rows]],
                    axis=1,
                )
            )

        def look(k_index, inners):
            k_rows = block_span(k_index, K_BLOCK)
            same = seq_col_ref[k_rows, 0:1] == seq_pair
            later = []
            for pair in range(pairs):
                keys = qkv_ref[k_rows, pl.ds(columns + pair * 128, 128)]
                values = qkv_ref[k_rows, pl.ds(2 * columns + pair * 128, 128)]
                logits = jnp.where(same, multiply_arrays(keys, queries[pair]), MASK_FILL)
                weights = jnp.exp(logits - logs[pair])
                weight_grad = multiply_arrays(values, turned[pair])
                probs[pair, k_index - lowest] = weights
                prob_grads[pair, k_index - lowest] = weight_grad
                value_sum[k_rows, pl.ds(pair * 128, 128)] += multiply_arrays(
                    weights.astype(jnp.bfloat16), grads[pair]
                )
                later.append(
                    inners[pair] + jnp.sum(weights * weight_grad, axis=0, keepdims=True)
                )
            return tuple(later)

        start = tuple(jnp.zeros((1, 2 * Q_BLOCK), jnp.float32) for _ in range(pairs))
        inners = lax.fori_loop(lowest, highest, look, start)

        def push(k_index, sums):
            k_rows = block_span(k_index, K_BLOCK)
            later = []
            for pair in range(pairs):
                slope = (
                    probs[pair, k_index - lowest]
                    * (prob_grads[pair, k_index - lowest] - inners[pair])
                ).astype(jnp.bfloat16)
                key_sum[k_rows, pl.ds(pair * 128, 128)] += multiply_arrays(slope, scaled[pair])
                later.append(
                    sums[pair] + multiply_arrays(key_turned[pl.ds(pair * 128, 128), k_rows], slope)
                )
            return tuple(later)

        blank = tuple(jnp.zeros((128, 2 * Q_BLOCK), jnp.float32) for _ in range(pairs))
        sums = lax.fori_loop(lowest, highest, push, blank)
        for pair in range(pairs):
            out_ref[q_rows, pl.ds(pair * 128, 128)] = (
                (join_pair(sums[pair]) * HEAD ** (-0.5)).T.astype(jnp.bfloat16)
            )
        return carry

    lax.fori_loop(0, q_blocks, one_block, 0)
    out_ref[:, columns : 2 * columns] = key_sum[...].astype(jnp.bfloat16)
    out_ref[:, 2 * columns :] = value_sum[...].astype(jnp.bfloat16)


def attend_back(qkv_out, attn_grad, log_total, seq_ids, bounds):
    slots, columns = attn_grad.shape
    pairs = columns // 128
    window = pltpu.VMEM((pairs, REACH, K_BLOCK, 2 * Q_BLOCK), jnp.float32)
    return pl.pallas_call(
        attend_back_kernel,
        out_shape=jax.ShapeDtypeStruct(qkv_out.shape, jnp.bfloat16),
        in_specs=[in_scalars(), in_scalars()] + [in_vmem()] * 5,
        out_specs=in_vmem(),
        scratch_shapes=[
            pltpu.VMEM((columns, slots), jnp.bfloat16),
            window,
            window,
            pltpu.VMEM((slots, columns), jnp.float32),
            pltpu.VMEM((slots, columns), jnp.float32),
        ],
        compiler_params=pltpu.CompilerParams(vmem_limit_bytes=VMEM_BYTES),
    )(
        bounds[0],
        bounds[1],
        qkv_out,
        attn_grad,
        log_total,
        seq_ids[:, None],
        jnp.broadcast_to(seq_ids[None], (8, slots)),
    )


def layer_forward(emb_all, seq_ids, bounds, row_params, col_local, layer_mats):
    qkv_full, out_full, up_full, down_full = layer_mats
    col_width = qkv_full.shape[2]
    tok_dev = emb_all.shape[0] // lax.axis_size("tensor")
    first_moment_all = norm_rows(emb_all, row_params[0], row_params[3]).astype(jnp.bfloat16)
    emb_rows = lax.dynamic_slice_in_dim(emb_all, lax.axis_index("tensor") * tok_dev, tok_dev, 0)
    norm_first = norm_rows(emb_rows, row_params[0], row_params[3])
    qkv_bias = jnp.concatenate([col_local[0], jnp.zeros_like(col_local[0]), col_local[1]])
    qkv_out = (
        multiply_arrays(first_moment_all, qkv_full.reshape(D, 3 * col_width)) + qkv_bias
    ).astype(jnp.bfloat16)
    attn_low, log_total = attend(qkv_out, seq_ids, bounds)
    first_sum = (
        norm_first
        + exchange(5, Fold(multiply_arrays(attn_low, out_full).astype(jnp.bfloat16)))
        + row_params[6]
    )
    norm_second = norm_rows(first_sum, row_params[1], row_params[4])
    second_all = exchange(6, Spread(norm_second.astype(jnp.bfloat16)))
    expansion_result = multiply_arrays(second_all, up_full.reshape(D, -1)) + col_local[2:].reshape(
        -1
    )
    hidden_low = jax.nn.gelu(expansion_result, approximate=False).astype(jnp.bfloat16)
    second_sum = (
        norm_second
        + exchange(
            7, Fold(multiply_arrays(hidden_low, down_full.reshape(-1, D)).astype(jnp.bfloat16))
        )
        + row_params[7]
    )
    norm_third = norm_rows(second_sum, row_params[2], row_params[5])
    saved_vals = (
        emb_rows,
        first_moment_all,
        qkv_out,
        log_total,
        attn_low,
        first_sum,
        second_all,
        expansion_result,
        hidden_low,
        second_sum,
    )
    return (norm_third, saved_vals)


def turned_grad(left_all, right_all):
    grad = jnp.einsum("td,tc->dc", left_all, right_all, preferred_element_type=jnp.float32)
    groups = lax.axis_size("dp")
    return grad.astype(jnp.bfloat16).reshape(groups, grad.shape[0] // groups, grad.shape[1])


def layer_backward(grad_third, seq_ids, bounds, row_params, layer_mats, saved_vals):
    qkv_full, out_full, up_full, down_full = layer_mats
    (
        emb_rows,
        first_moment_all,
        qkv_out,
        log_total,
        attn_low,
        first_sum,
        second_all,
        expansion_result,
        hidden_low,
        second_sum,
    ) = saved_vals
    col_width = qkv_full.shape[2]
    grad_second, gain_c, shift_c = norm_back(second_sum, row_params[2], row_params[5], grad_third)
    mixed_low = grad_second.astype(jnp.bfloat16)
    mixed_all = exchange(10, Spread(mixed_low))
    down_grad = turned_grad(mixed_all, hidden_low)
    hidden_grad = jnp.einsum(
        "td,fd->tf", mixed_all, down_full.reshape(-1, D), preferred_element_type=jnp.float32
    )
    gelu_pull = jax.vjp(partial(jax.nn.gelu, approximate=False), expansion_result)[1]
    up_low = gelu_pull(hidden_grad)[0].astype(jnp.bfloat16)
    up_grad = turned_grad(second_all, up_low)
    second_back = jnp.einsum(
        "tf,df->td", up_low, up_full.reshape(D, -1), preferred_element_type=jnp.float32
    ).astype(jnp.bfloat16)
    second_back, down_half = exchange(11, Fold(second_back), ReduceCross(down_grad))
    second_total = grad_second + second_back
    grad_first, gain_b, shift_b = norm_back(first_sum, row_params[1], row_params[4], second_total)
    branch_low = grad_first.astype(jnp.bfloat16)
    branch_all, down_sum, up_half = exchange(
        12, Spread(branch_low), ReduceLine(down_half), ReduceCross(up_grad)
    )
    out_grad = turned_grad(branch_all, attn_low)
    attn_grad = jnp.einsum(
        "td,cd->tc", branch_all, out_full, preferred_element_type=jnp.float32
    ).astype(jnp.bfloat16)
    qkv_low = attend_back(qkv_out, attn_grad, log_total, seq_ids, bounds)
    qkv_grad = turned_grad(first_moment_all, qkv_low)
    first_back = jnp.einsum(
        "tc,dc->td", qkv_low, qkv_full.reshape(D, -1), preferred_element_type=jnp.float32
    ).astype(jnp.bfloat16)
    first_back, up_sum, out_half, qkv_half = exchange(
        13, Fold(first_back), ReduceLine(up_half), ReduceCross(out_grad), ReduceCross(qkv_grad)
    )
    first_total = grad_first + first_back
    emb_grad, gain_a, shift_a = norm_back(emb_rows, row_params[0], row_params[3], first_total)
    qkv_cols = jnp.sum(qkv_low.astype(jnp.float32), axis=0).reshape(3, col_width)
    up_cols = jnp.sum(up_low.astype(jnp.float32), axis=0).reshape(-1, col_width)
    col_grad = jnp.concatenate([qkv_cols[0:1], qkv_cols[2:3], up_cols], axis=0)
    row_grad = jnp.stack(
        [
            gain_a,
            gain_b,
            gain_c,
            shift_a,
            shift_b,
            shift_c,
            jnp.sum(branch_low.astype(jnp.float32), axis=0),
            jnp.sum(mixed_low.astype(jnp.float32), axis=0),
        ]
    )
    return (emb_grad, (qkv_half, out_half, up_sum, down_sum), col_grad, row_grad)


def plan_kernel(capacity, vocab_local, groups, perm_ref, low_ref, high_ref, slot_ref, list_ref, count_ref, id_buf, own_buf):
    slots = perm_ref.shape[1]
    table_rows = low_ref.shape[1]
    block = 128
    blocks = slots // block
    perm = perm_ref[...]
    high_part = perm // 128
    low_part = perm - high_part * 128
    chooser = (lax.broadcasted_iota(jnp.int32, (table_rows, slots), 0) == high_part).astype(
        jnp.float32
    ).astype(jnp.bfloat16)
    value = multiply_arrays(low_ref[...], chooser) + 256.0 * multiply_arrays(high_ref[...], chooser)
    lane_match = lax.broadcasted_iota(jnp.int32, (128, slots), 0) == low_part
    ids = jnp.sum(jnp.where(lane_match, value, 0.0), axis=0, keepdims=True)
    for b in range(blocks):
        id_buf[pl.ds(b * block, block), :] = jnp.broadcast_to(
            ids[:, b * block : (b + 1) * block], (block, block)
        ).T
    place = lax.broadcasted_iota(jnp.int32, (1, slots), 1).astype(jnp.float32)
    rows = lax.broadcasted_iota(jnp.int32, (block, 1), 0).astype(jnp.float32)

    def earliest(b, best):
        column = id_buf[pl.ds(pl.multiple_of(b * block, block), block), 0:1]
        index = rows + (b * block).astype(jnp.float32)
        found = jnp.where(column == ids, index, 1e9)
        return jnp.minimum(best, jnp.min(found, axis=0, keepdims=True))

    least = lax.fori_loop(0, blocks, earliest, jnp.full((1, slots), 1e9, jnp.float32))
    first = least == place
    owner = jnp.zeros((1, slots), jnp.float32)
    for index in range(1, groups):
        owner = owner + jnp.where(ids >= float(index * vocab_local), 1.0, 0.0)
    owner_rows = lax.broadcasted_iota(jnp.int32, (groups, slots), 0).astype(jnp.float32)
    marks = jnp.where(first & (owner == owner_rows), 1.0, 0.0)
    upper = jnp.where(
        lax.broadcasted_iota(jnp.int32, (block, block), 0)
        < lax.broadcasted_iota(jnp.int32, (block, block), 1),
        1.0,
        0.0,
    ).astype(jnp.bfloat16)
    running = jnp.zeros((groups, 1), jnp.float32)
    pieces = []
    for b in range(blocks):
        part = marks[:, b * block : (b + 1) * block]
        pieces.append(multiply_arrays(part.astype(jnp.bfloat16), upper) + running)
        running = running + jnp.sum(part, axis=1, keepdims=True)
    before = jnp.concatenate(pieces, axis=1)
    rank = jnp.sum(marks * before, axis=0, keepdims=True)
    own_slot = jnp.where(first & (rank < float(capacity)), owner * float(capacity) + rank, -1.0)
    for b in range(blocks):
        own_buf[pl.ds(b * block, block), :] = jnp.broadcast_to(
            own_slot[:, b * block : (b + 1) * block], (block, block)
        ).T
    width = list_ref.shape[1]
    target = lax.broadcasted_iota(jnp.int32, (1, width), 1).astype(jnp.float32)

    def settle(b, carry):
        slot, listed = carry
        window = pl.ds(pl.multiple_of(b * block, block), block)
        column, slot_column = id_buf[window, 0:1], own_buf[window, 0:1]
        slot = jnp.maximum(
            slot, jnp.max(jnp.where(column == ids, slot_column, -1.0), axis=0, keepdims=True)
        )
        listed = jnp.maximum(
            listed, jnp.max(jnp.where(slot_column == target, column, -1.0), axis=0, keepdims=True)
        )
        return (slot, listed)

    slot, listed = lax.fori_loop(
        0,
        blocks,
        settle,
        (jnp.full((1, slots), -1.0, jnp.float32), jnp.full((1, width), -1.0, jnp.float32)),
    )
    slot_ref[...] = slot.astype(jnp.int32)
    list_ref[...] = listed.astype(jnp.int32)
    count_ref[...] = jnp.broadcast_to(running, count_ref.shape).astype(jnp.int32)


def make_plan(perm, all_ids, capacity, vocab_local, groups):
    slots = perm.shape[0]
    table = all_ids.reshape(-1, 128).T
    high = table // 256
    low = table - high * 256
    return pl.pallas_call(
        partial(plan_kernel, capacity, vocab_local, groups),
        out_shape=[
            jax.ShapeDtypeStruct((1, slots), jnp.int32),
            jax.ShapeDtypeStruct((1, groups * capacity), jnp.int32),
            jax.ShapeDtypeStruct((groups, 128), jnp.int32),
        ],
        in_specs=[in_vmem()] * 3,
        out_specs=[in_vmem()] * 3,
        scratch_shapes=[pltpu.VMEM((slots, 128), jnp.float32), pltpu.VMEM((slots, 128), jnp.float32)],
        compiler_params=pltpu.CompilerParams(vmem_limit_bytes=VMEM_BYTES),
    )(perm[None], low.astype(jnp.bfloat16), high.astype(jnp.bfloat16))


def loss_kernel(pooled_ref, head_ref, pair_ref, loss_ref, low_ref, grad_ref, back_ref):
    total = pooled_ref.shape[0]
    low = pooled_ref[...].astype(jnp.bfloat16)
    low_ref[...] = low
    head_low = head_ref[...].astype(jnp.bfloat16)
    vectors = multiply_arrays(low, head_low)
    depth = vectors.shape[1]
    lane = lax.broadcasted_iota(jnp.int32, vectors.shape, 1)
    across = lax.broadcasted_iota(jnp.int32, (total, total), 1)
    diagonal = lax.broadcasted_iota(jnp.int32, (total, total), 0) == across
    chosen = across == pair_ref[...]
    loss = jnp.zeros((1, 1), jnp.float32)
    grads = jnp.zeros(vectors.shape, jnp.float32)

    def exact(left, right, dims):
        return lax.dot_general(
            left, right, (dims, ((), ())), precision=HIGHEST_MODE, preferred_element_type=jnp.float32
        )

    for fraction in (16, 4, 1):
        prefix = jnp.where(lane < depth // fraction, vectors, 0.0)
        inverse = lax.rsqrt(jnp.sum(prefix * prefix, axis=1, keepdims=True) + 1e-06)
        unit = prefix * inverse
        logits = exact(unit, unit, ((1,), (1,))) / LOGIT_DIVISOR
        logits = jnp.where(diagonal, MASK_FILL, logits)
        top = jnp.max(logits, axis=1, keepdims=True)
        weights = jnp.exp(logits - top)
        weight_sum = jnp.sum(weights, axis=1, keepdims=True)
        positive = jnp.sum(jnp.where(chosen, logits, 0.0), axis=1, keepdims=True)
        loss = loss + jnp.sum(jnp.log(weight_sum) + top - positive, keepdims=True)
        pull = weights / weight_sum - jnp.where(chosen, 1.0, 0.0)
        unit_grad = (exact(pull, unit, ((1,), (0,))) + exact(pull, unit, ((0,), (0,)))) / LOGIT_DIVISOR
        unit_grad = jnp.where(lane < depth // fraction, unit_grad, 0.0)
        inner = jnp.sum(unit_grad * prefix, axis=1, keepdims=True)
        grads = grads + inverse * unit_grad - prefix * (inverse * inverse * inverse * inner)
    loss_ref[...] = jnp.broadcast_to(loss, loss_ref.shape)
    grad_ref[...] = grads
    back_ref[...] = exact(grads, head_low.astype(jnp.float32), ((1,), (1,)))


def contrast_step(pooled, head_weight, pairs):
    total, depth = pooled.shape
    return pl.pallas_call(
        loss_kernel,
        out_shape=[
            jax.ShapeDtypeStruct((8, 128), jnp.float32),
            jax.ShapeDtypeStruct((total, depth), jnp.bfloat16),
            jax.ShapeDtypeStruct((total, depth), jnp.float32),
            jax.ShapeDtypeStruct((total, depth), jnp.float32),
        ],
        in_specs=[in_vmem()] * 3,
        out_specs=[in_vmem()] * 4,
        compiler_params=pltpu.CompilerParams(vmem_limit_bytes=VMEM_BYTES),
    )(pooled, head_weight, pairs[:, None])


CAPACITY = 256


def body(
    token_ids,
    slot_perm,
    seq_lengths,
    pair_index,
    tok_table,
    tok_first,
    tok_second,
    pos_table,
    pos_first,
    pos_second,
    query_key_value_weight,
    qkv_first,
    qkv_second,
    out_weight,
    out_first,
    out_second,
    up_weight,
    up_first,
    up_second,
    down_weight,
    down_first,
    down_second,
    head_weight,
    head_first,
    head_second,
    col_bias,
    col_first,
    col_second,
    row_params,
    row_first,
    row_second,
):
    groups = lax.axis_size("dp")
    tensor_count = lax.axis_size("tensor")
    group_index = lax.axis_index("dp")
    tensor_index = lax.axis_index("tensor")
    tok_dev = token_ids.shape[0]
    tok_grp = tok_dev * tensor_count
    col_width = pos_table.shape[1]
    vocab_local = tok_table.shape[0]
    column_start = tensor_index * col_width
    anchors = pair_index.shape[0]
    id_rows = tok_dev // 128
    block = jnp.concatenate(
        [
            token_ids.reshape(id_rows, 128),
            slot_perm.reshape(id_rows, 128),
            jnp.pad(pair_index, (0, 128 - anchors))[None],
            jnp.zeros((16 - 2 * id_rows - 1, 128), jnp.int32),
        ],
        axis=0,
    )
    gathered = gather_all(block, 1)
    all_ids = gathered[:, :id_rows].reshape(-1)
    pairs = gathered[:: tensor_count, 2 * id_rows, :anchors].reshape(-1)
    own_perm = lax.dynamic_slice_in_dim(
        gathered, group_index * tensor_count, tensor_count, 0
    )[:, id_rows : 2 * id_rows].reshape(-1)
    slot, listed, counts_out = make_plan(own_perm, all_ids, CAPACITY, vocab_local, groups)
    slot = slot[0]
    list_rows = CAPACITY // 128
    top_count = jnp.max(counts_out)
    request = jnp.concatenate(
        [
            listed.reshape(groups, list_rows, 128),
            jnp.broadcast_to(top_count, (groups, 8 - list_rows, 128)),
        ],
        axis=1,
    )
    asked = exchange(2, Swap(request, "dp"))
    overflow = jnp.max(asked[:, list_rows]) > CAPACITY
    offset = group_index * vocab_local
    asked_rows = asked[:, :list_rows].reshape(-1) - offset
    asked_safe = jnp.clip(asked_rows, 0, vocab_local - 1)
    sent_rows = jnp.take(tok_table, asked_safe, axis=0).astype(jnp.bfloat16)
    got_rows, pos_full = exchange(
        3,
        Swap(sent_rows.reshape(groups, CAPACITY, col_width), "dp"),
        Spread(pos_table, columns=True, chunks=1),
    )
    got_rows = got_rows.reshape(-1, col_width)
    chooser = (slot[:, None] == jnp.arange(groups * CAPACITY, dtype=jnp.int32)[None, :]).astype(
        jnp.bfloat16
    )
    lengths = seq_lengths[0]
    seq_ids, positions, member = seq_layout(lengths, tok_grp)
    bounds = block_bounds(lengths, tok_grp)

    def every_slot_id():
        every_perm = gathered[:, id_rows : 2 * id_rows].reshape(-1)
        return jnp.take(all_ids, every_perm, axis=0)

    def spread_wide():
        wanted = every_slot_id() - offset
        inside = (wanted >= 0) & (wanted < vocab_local)
        picked = jnp.take(
            tok_table.astype(jnp.bfloat16), jnp.clip(wanted, 0, vocab_local - 1), axis=0
        )
        return lax.psum_scatter(
            jnp.where(inside[:, None], picked, jnp.zeros((), jnp.bfloat16)),
            "dp",
            scatter_dimension=0,
            tiled=True,
        )

    tok_cols = lax.cond(
        overflow,
        spread_wide,
        lambda: multiply_arrays(chooser, got_rows).astype(jnp.bfloat16),
    )
    emb_all = exchange(4, Spread(tok_cols, columns=True)).astype(jnp.float32) + jnp.take(pos_full, positions, axis=0)
    layer_mats = (
        lax.all_gather(query_key_value_weight.astype(jnp.bfloat16), "dp", axis=0, tiled=True),
        lax.all_gather(out_weight.astype(jnp.bfloat16), "dp", axis=1, tiled=True),
        lax.all_gather(up_weight.astype(jnp.bfloat16), "dp", axis=0, tiled=True),
        lax.all_gather(down_weight.astype(jnp.bfloat16), "dp", axis=2, tiled=True),
    )
    norm_third, saved_vals = layer_forward(emb_all, seq_ids, bounds, row_params, col_bias, layer_mats)
    row_member = lax.dynamic_slice_in_dim(member, tensor_index * tok_dev, tok_dev, 0).astype(
        jnp.float32
    )
    counts = lengths.astype(jnp.float32)[:, None]
    pooled = exchange(9, SumAll(exact_multiply(row_member.T, norm_third) / counts, True))
    loss_out, pooled_low, vec_grad, pooled_grad = contrast_step(
        pooled.reshape(-1, D), head_weight, pairs
    )
    head_sum = exact_multiply(pooled_low.astype(jnp.float32).T, vec_grad)
    own_grad = lax.dynamic_slice_in_dim(pooled_grad, group_index * anchors, anchors, 0)
    grad_third = exact_multiply(row_member, own_grad / counts)
    emb_grad, halves, col_grad, row_grad = layer_backward(
        grad_third, seq_ids, bounds, row_params, layer_mats, saved_vals
    )
    qkv_half, out_half, up_sum, down_sum = halves
    cols_grad, qkv_sum, out_sum = exchange(
        14,
        Swap(
            emb_grad.astype(jnp.bfloat16)
            .reshape(tok_dev, tensor_count, col_width)
            .swapaxes(0, 1),
            "tensor",
        ),
        ReduceLine(qkv_half),
        ReduceLine(out_half),
    )
    cols_grad = cols_grad.reshape(tok_grp, col_width)
    pos_pick = (
        jnp.arange(pos_table.shape[0], dtype=jnp.int32)[:, None] == positions[None, :]
    ).astype(jnp.bfloat16)
    pos_grad = multiply_arrays(pos_pick, cols_grad)
    shared = jnp.concatenate([pos_grad, col_grad], axis=0)
    shared_rows = -(-shared.shape[0] // (8 * groups)) * 8
    shared = jnp.pad(shared, ((0, shared_rows * groups - shared.shape[0]), (0, 0)))
    merged = jnp.einsum("kn,kc->nc", chooser, cols_grad, preferred_element_type=jnp.float32)
    back_rows, shared_parts = exchange(
        15,
        Swap(merged.astype(jnp.bfloat16).reshape(groups, CAPACITY, col_width), "dp"),
        Swap(shared.reshape(groups, shared_rows, col_width), "dp"),
    )
    shared_own = jnp.sum(shared_parts, axis=0)

    def add_wide():
        wanted = every_slot_id() - offset
        inside = (wanted >= 0) & (wanted < vocab_local)
        return (
            jnp.zeros(tok_table.shape, jnp.float32)
            .at[jnp.clip(wanted, 0, vocab_local - 1)]
            .add(
                jnp.where(
                    inside[:, None],
                    lax.all_gather(cols_grad, "dp", axis=0, tiled=True).astype(jnp.float32),
                    0.0,
                )
            )
        )

    def add_listed():
        return (
            jnp.zeros(tok_table.shape, jnp.float32)
            .at[jnp.where(asked_rows < 0, vocab_local, asked_rows)]
            .add(back_rows.reshape(-1, col_width).astype(jnp.float32), mode="drop")
        )

    tok_grad = lax.cond(overflow, add_wide, add_listed)
    qkv_grad = qkv_sum.reshape(query_key_value_weight.shape)
    out_grad = out_sum.T
    up_grad = up_sum.reshape(up_weight.shape)
    down_grad = down_sum.T.reshape(down_weight.shape)
    local_squares = (
        jnp.sum(tok_grad * tok_grad)
        + jnp.sum(qkv_grad * qkv_grad)
        + jnp.sum(out_grad * out_grad)
        + jnp.sum(up_grad * up_grad)
        + jnp.sum(down_grad * down_grad)
        + jnp.sum(shared_own * shared_own)
    )
    row_block = jnp.concatenate(
        [row_grad, jnp.pad(local_squares.reshape(1, 1), ((0, 7), (0, D - 1)))], axis=0
    )
    row_total, shared_sum = exchange(16, SumAll(row_block, False), Gather(shared_own, "dp"))
    row_total = row_total[0]
    shared_sum = shared_sum.reshape(-1, col_width)
    pos_own = shared_sum[: pos_table.shape[0]]
    col_own = shared_sum[pos_table.shape[0] : pos_table.shape[0] + col_bias.shape[0]]
    row_sum = row_total[:8]
    squares = row_total[8, 0] + jnp.sum(row_sum * row_sum) + jnp.sum(head_sum * head_sum)
    grad_norm = jnp.sqrt(squares)
    clip_scale = jnp.minimum(1.0, CLIP_NORM / (grad_norm + 1e-06))
    tok_new = adam_step(
        tok_table, tok_first, tok_second, tok_grad * clip_scale, RATE_MATRIX, DECAY_RATE
    )
    pos_new = adam_step(
        pos_table, pos_first, pos_second, pos_own * clip_scale, RATE_MATRIX, DECAY_RATE
    )
    qkv_new = adam_step(
        query_key_value_weight,
        qkv_first,
        qkv_second,
        qkv_grad * clip_scale,
        RATE_MATRIX,
        DECAY_RATE,
    )
    out_new = adam_step(
        out_weight, out_first, out_second, out_grad * clip_scale, RATE_MATRIX, DECAY_RATE
    )
    up_new = adam_step(
        up_weight, up_first, up_second, up_grad * clip_scale, RATE_MATRIX, DECAY_RATE
    )
    down_new = adam_step(
        down_weight, down_first, down_second, down_grad * clip_scale, RATE_MATRIX, DECAY_RATE
    )
    head_new = adam_step(
        head_weight, head_first, head_second, head_sum * clip_scale, RATE_MATRIX, DECAY_RATE
    )
    col_new = adam_step(col_bias, col_first, col_second, col_own * clip_scale, RATE_VECTOR, 0.0)
    row_new = adam_step(row_params, row_first, row_second, row_sum * clip_scale, RATE_VECTOR, 0.0)
    return (loss_out[0, 0], grad_norm) + tok_new + pos_new + qkv_new + out_new + up_new + down_new + head_new + col_new + row_new


def solution(mesh):
    placed = (
        P(("dp", "tensor")),
        P(("dp", "tensor")),
        P("dp", None),
        P("dp"),
        P("dp", "tensor"),
        P("dp", "tensor"),
        P("dp", "tensor"),
        P(None, "tensor"),
        P(None, "tensor"),
        P(None, "tensor"),
        P("dp", None, "tensor"),
        P("dp", None, "tensor"),
        P("dp", None, "tensor"),
        P("tensor", "dp"),
        P("tensor", "dp"),
        P("tensor", "dp"),
        P("dp", None, "tensor"),
        P("dp", None, "tensor"),
        P("dp", None, "tensor"),
        P(None, "tensor", "dp"),
        P(None, "tensor", "dp"),
        P(None, "tensor", "dp"),
        P(),
        P(),
        P(),
        P(None, "tensor"),
        P(None, "tensor"),
        P(None, "tensor"),
        P(),
        P(),
        P(),
    )
    return jax.shard_map(
        body,
        mesh=mesh,
        in_specs=placed,
        out_specs=(
            P(),
            P(),
            P("dp", "tensor"),
            P("dp", "tensor"),
            P("dp", "tensor"),
            P(None, "tensor"),
            P(None, "tensor"),
            P(None, "tensor"),
            P("dp", None, "tensor"),
            P("dp", None, "tensor"),
            P("dp", None, "tensor"),
            P("tensor", "dp"),
            P("tensor", "dp"),
            P("tensor", "dp"),
            P("dp", None, "tensor"),
            P("dp", None, "tensor"),
            P("dp", None, "tensor"),
            P(None, "tensor", "dp"),
            P(None, "tensor", "dp"),
            P(None, "tensor", "dp"),
            P(),
            P(),
            P(),
            P(None, "tensor"),
            P(None, "tensor"),
            P(None, "tensor"),
            P(),
            P(),
            P(),
        ),
        check_vma=False,
    )
```

```python
from functools import partial

import jax
import jax.numpy as jnp
from jax import lax
from jax.experimental import pallas as pl
from jax.experimental.pallas import tpu as pltpu
from jax.sharding import PartitionSpec as P

D = 1024
HEAD = 64
MAXLEN = 512
STEP = 10


HIGHEST_MODE = lax.Precision.HIGHEST
LN_EPS = 1e-05
LOGIT_DIVISOR = 0.05
CLIP_NORM = 0.25
BETA_FIRST = 0.9
BETA_SECOND = 0.999
ADAM_EPS = 1e-08
RATE_MATRIX = 0.05
RATE_VECTOR = 0.5
DECAY_RATE = 0.01
MASK_FILL = -1e30


def multiply_arrays(left_mat, right_mat):
    return jnp.dot(left_mat, right_mat, preferred_element_type=jnp.float32)


def exact_multiply(left_mat, right_mat):
    return jnp.dot(left_mat, right_mat, precision=HIGHEST_MODE, preferred_element_type=jnp.float32)


def norm_rows(values, gain_row, bias_row):
    center = values - jnp.mean(values, axis=1, keepdims=True)
    inverse = lax.rsqrt(jnp.mean(center * center, axis=1, keepdims=True) + LN_EPS)
    return center * inverse * gain_row + bias_row


def norm_back(values, gain_row, bias_row, grad_rows):
    norm_pull = jax.vjp(norm_rows, values, gain_row, bias_row)[1]
    return norm_pull(grad_rows)


def seq_layout(lengths, slot_total):
    seq_ends = jnp.cumsum(lengths)
    starts = seq_ends - lengths
    slot_index = jnp.arange(slot_total, dtype=jnp.int32)
    member = (slot_index[:, None] >= starts[None, :]) & (slot_index[:, None] < seq_ends[None, :])
    seq_count = jnp.arange(lengths.shape[0], dtype=jnp.int32)
    seq_ids = jnp.sum(jnp.where(member, seq_count[None, :], 0), axis=1)
    positions = slot_index - jnp.sum(jnp.where(member, starts[None, :], 0), axis=1) + 2
    return (seq_ids, positions, member)


def adam_step(weight, first_old, second_old, clipped, step_rate, decay_rate):
    first_new = BETA_FIRST * first_old + (1.0 - BETA_FIRST) * clipped
    second_new = BETA_SECOND * second_old + (1.0 - BETA_SECOND) * clipped * clipped
    first_hat = first_new / (1.0 - BETA_FIRST**STEP)
    second_hat = second_new / (1.0 - BETA_SECOND**STEP)
    weight_new = weight - step_rate * (
        first_hat / (jnp.sqrt(second_hat) + ADAM_EPS) + decay_rate * weight
    )
    return (weight_new, first_new, second_new)


MESH_IDS = pl.DeviceIdType.MESH
VMEM_BYTES = 60 * 1024 * 1024
CHUNKS = 4
LINE = 4


def in_vmem():
    return pl.BlockSpec(memory_space=pltpu.VMEM)


def shaped(shape, dtype):
    return jax.ShapeDtypeStruct(tuple(shape), dtype)


def dma(*shape):
    return pltpu.SemaphoreType.DMA(shape)


def remote(src, dst, send_sem, recv_sem, target):
    return pltpu.make_async_remote_copy(
        src_ref=src,
        dst_ref=dst,
        send_sem=send_sem,
        recv_sem=recv_sem,
        device_id=target,
        device_id_type=MESH_IDS,
    )


def comm_params(collective):
    return pltpu.CompilerParams(
        collective_id=collective, has_side_effects=True, vmem_limit_bytes=VMEM_BYTES
    )


def exchange(collective, *tasks):
    def kernel(*refs):
        at = 0
        for attribute in ("ins", "outs", "scratch"):
            for task in tasks:
                size = len(getattr(task, attribute))
                setattr(task, attribute + "_refs", refs[at : at + size])
                at += size
        barrier = pltpu.get_barrier_semaphore()
        pl.semaphore_wait(barrier, sum(task.hello(barrier) for task in tasks))
        for task in tasks:
            task.begin()
        for task in tasks:
            task.middle()
        for task in tasks:
            task.end()

    results = pl.pallas_call(
        kernel,
        out_shape=[out for task in tasks for out in task.outs],
        in_specs=[in_vmem() for task in tasks for _ in task.ins],
        out_specs=[in_vmem() for task in tasks for _ in task.outs],
        scratch_shapes=[item for task in tasks for item in task.scratch],
        compiler_params=comm_params(collective),
    )(*[array for task in tasks for array in task.ins])
    return results[0] if len(results) == 1 else results


def tensor_place(width):
    me = lax.axis_index("tensor")
    core = lax.rem(me, 2)
    row = me // 2
    mate = me + 1 - 2 * core
    return (me, core, row, mate)


class Task:
    def hello(self, barrier):
        partners = self.partners()
        for partner in partners:
            pl.semaphore_signal(barrier, inc=1, device_id=partner, device_id_type=MESH_IDS)
        return len(partners)

    def begin(self):
        pass

    def middle(self):
        pass

    def end(self):
        pass


class Pair(Task):
    def __init__(self):
        self.width = lax.axis_size("tensor")
        self.rows = self.width // 2

    def partners(self):
        me, core, row, mate = tensor_place(self.width)
        return [{"tensor": mate}] + [
            {"tensor": lax.rem(row + step, self.rows) * 2 + core} for step in range(1, self.rows)
        ]


class Spread(Pair):
    def __init__(self, block, columns=False, chunks=CHUNKS):
        super().__init__()
        height, depth = block.shape
        self.columns, self.chunks = columns, chunks
        self.ins = (block,)
        whole = (height, self.width * depth) if columns else (self.width * height, depth)
        self.outs = (shaped(whole, block.dtype),)
        self.scratch = tuple(dma(self.rows, chunks) for _ in range(4))

    def window(self, owner, part=None):
        (x_ref,), (o_ref,) = self.ins_refs, self.outs_refs
        height, depth = x_ref.shape
        size = height // self.chunks
        if self.columns:
            lanes = pl.ds(pl.multiple_of(owner * depth, depth), depth)
            if part is None or self.chunks == 1:
                return o_ref.at[:, lanes]
            return o_ref.at[pl.ds(part * size, size), lanes]
        if part is None:
            return o_ref.at[pl.ds(pl.multiple_of(owner * height, height), height)]
        return o_ref.at[pl.ds(pl.multiple_of(owner * height + part * size, size), size)]

    def begin(self):
        (x_ref,) = self.ins_refs
        far_send, far_recv, near_send, near_recv = self.scratch_refs
        me, core, row, mate = tensor_place(self.width)
        size = x_ref.shape[0] // self.chunks
        self.far = {}
        for part in range(self.chunks):
            source = x_ref if self.chunks == 1 else x_ref.at[pl.ds(part * size, size)]
            for step in range(1, self.rows):
                copy = remote(
                    source,
                    self.window(me, part),
                    far_send.at[step, part],
                    far_recv.at[step, part],
                    {"tensor": lax.rem(row + step, self.rows) * 2 + core},
                )
                copy.start()
                self.far[step, part] = copy
        copy = remote(
            x_ref, self.window(me), near_send.at[0, 0], near_recv.at[0, 0], {"tensor": mate}
        )
        copy.start()
        self.near = [copy]
        self.window(me)[...] = x_ref[...]

    def middle(self):
        far_send, far_recv, near_send, near_recv = self.scratch_refs
        me, core, row, mate = tensor_place(self.width)
        for part in range(self.chunks):
            for step in range(1, self.rows):
                self.far[step, part].wait_recv()
                source = lax.rem(row + self.rows - step, self.rows) * 2 + core
                onward = remote(
                    self.window(source, part),
                    self.window(source, part),
                    near_send.at[step, part],
                    near_recv.at[step, part],
                    {"tensor": mate},
                )
                onward.start()
                self.near.append(onward)

    def end(self):
        for copy in self.near:
            copy.wait()
        for copy in self.far.values():
            copy.wait_send()


class Fold(Pair):
    def __init__(self, parts, chunks=CHUNKS):
        super().__init__()
        height, depth = parts.shape[0] // self.width, parts.shape[1]
        far_rows = max(self.rows - 1, 1)
        self.chunks = chunks
        self.ins = (parts,)
        self.outs = (shaped((height, depth), jnp.float32),)
        self.scratch = (
            pltpu.VMEM((self.rows, height, depth), jnp.bfloat16),
            pltpu.VMEM((far_rows, height, depth), jnp.bfloat16),
            pltpu.VMEM((far_rows, height, depth), jnp.bfloat16),
        ) + tuple(dma(self.rows, chunks) for _ in range(4))

    def span(self, owner, part):
        height = self.outs[0].shape[0]
        size = height // self.chunks
        return pl.ds(pl.multiple_of(owner * height + part * size, size), size)

    def local(self, part):
        size = self.outs[0].shape[0] // self.chunks
        return pl.ds(part * size, size)

    def begin(self):
        (p_ref,) = self.ins_refs
        near_buf, near_send, near_recv = self.scratch_refs[0], *self.scratch_refs[3:5]
        me, core, row, mate = tensor_place(self.width)
        self.near = {}
        for step in list(range(1, self.rows)) + [0]:
            dest_row = lax.rem(row + step, self.rows)
            for part in range(self.chunks):
                copy = remote(
                    p_ref.at[self.span(dest_row * 2 + 1 - core, part)],
                    near_buf.at[step, self.local(part)],
                    near_send.at[step, part],
                    near_recv.at[step, part],
                    {"tensor": mate},
                )
                copy.start()
                self.near[step, part] = copy

    def middle(self):
        (p_ref,), (o_ref,) = self.ins_refs, self.outs_refs
        near_buf, sum_buf, far_buf, near_send, near_recv, far_send, far_recv = self.scratch_refs
        me, core, row, mate = tensor_place(self.width)
        self.far = {}
        for step in range(1, self.rows):
            dest = lax.rem(row + step, self.rows) * 2 + core
            for part in range(self.chunks):
                local = self.local(part)
                self.near[step, part].wait_recv()
                sum_buf[step - 1, local] = (
                    p_ref[self.span(dest, part)].astype(jnp.float32)
                    + near_buf[step, local].astype(jnp.float32)
                ).astype(jnp.bfloat16)
                copy = remote(
                    sum_buf.at[step - 1, local],
                    far_buf.at[step - 1, local],
                    far_send.at[step - 1, part],
                    far_recv.at[step - 1, part],
                    {"tensor": dest},
                )
                copy.start()
                self.far[step, part] = copy
        for part in range(self.chunks):
            local = self.local(part)
            self.near[0, part].wait_recv()
            o_ref[local] = p_ref[self.span(me, part)].astype(jnp.float32) + near_buf[
                0, local
            ].astype(jnp.float32)

    def end(self):
        (o_ref,) = self.outs_refs
        far_buf = self.scratch_refs[2]
        for part in range(self.chunks):
            local = self.local(part)
            for step in range(1, self.rows):
                self.far[step, part].wait_recv()
                o_ref[local] += far_buf[step - 1, local].astype(jnp.float32)
        for copy in list(self.near.values()) + list(self.far.values()):
            copy.wait_send()


class Swap(Task):
    def __init__(self, blocks, axis):
        self.axis, self.count = axis, lax.axis_size(axis)
        self.ins = (blocks,)
        self.outs = (shaped(blocks.shape, blocks.dtype),)
        self.scratch = (dma(self.count), dma(self.count))

    def others(self):
        me = lax.axis_index(self.axis)
        return [lax.rem(me + step, self.count) for step in range(1, self.count)]

    def partners(self):
        return [{self.axis: other} for other in self.others()]

    def begin(self):
        (x_ref,), (o_ref,), (send, recv) = self.ins_refs, self.outs_refs, self.scratch_refs
        me = lax.axis_index(self.axis)
        self.copies = [
            remote(x_ref.at[other], o_ref.at[me], send.at[i], recv.at[i], {self.axis: other})
            for i, other in enumerate(self.others())
        ]
        for copy in self.copies:
            copy.start()
        o_ref[me] = x_ref[me]

    def end(self):
        for copy in self.copies:
            copy.wait()


class Gather(Swap):
    def __init__(self, block, axis):
        super().__init__(block, axis)
        self.outs = (shaped((self.count,) + block.shape, block.dtype),)

    def begin(self):
        (x_ref,), (o_ref,), (send, recv) = self.ins_refs, self.outs_refs, self.scratch_refs
        me = lax.axis_index(self.axis)
        self.copies = [
            remote(x_ref, o_ref.at[me], send.at[i], recv.at[i], {self.axis: other})
            for i, other in enumerate(self.others())
        ]
        for copy in self.copies:
            copy.start()
        o_ref[me] = x_ref[...]


class GatherAll(Task):
    def __init__(self, block):
        self.width = lax.axis_size("tensor")
        self.total = total = lax.axis_size("dp") * self.width
        self.ins = (block,)
        self.outs = (shaped((total,) + block.shape, block.dtype),)
        self.scratch = (dma(total), dma(total))

    def me(self):
        return lax.axis_index("dp") * self.width + lax.axis_index("tensor")

    def place(self, step):
        other = lax.rem(self.me() + step, self.total)
        return (other // self.width, lax.rem(other, self.width))

    def copy(self, step):
        (x_ref,), (o_ref,), (send, recv) = self.ins_refs, self.outs_refs, self.scratch_refs
        return remote(x_ref, o_ref.at[self.me()], send.at[step], recv.at[step], self.place(step))

    def hello(self, barrier):
        def one(step, carry):
            pl.semaphore_signal(
                barrier, inc=1, device_id=self.place(step), device_id_type=MESH_IDS
            )
            return carry

        lax.fori_loop(1, self.total, one, 0)
        return self.total - 1

    def begin(self):
        def one(step, carry):
            self.copy(step).start()
            return carry

        lax.fori_loop(1, self.total, one, 0)
        self.outs_refs[0][self.me()] = self.ins_refs[0][...]

    def end(self):
        def one(step, carry):
            self.copy(step).wait()
            return carry

        lax.fori_loop(1, self.total, one, 0)


class GridTask(Task):
    def __init__(self):
        self.cross = lax.axis_size("dp") // LINE

    def place(self):
        me = lax.axis_index("dp")
        return (me // self.cross, lax.rem(me, self.cross))


class ReduceCross(GridTask):
    def __init__(self, blocks):
        super().__init__()
        shape = blocks.shape[1:]
        self.blocks_shape = (LINE, self.cross) + shape
        self.ins = (blocks.reshape(self.blocks_shape),)
        self.outs = (shaped((LINE,) + shape, jnp.bfloat16),)
        others = max(self.cross - 1, 1)
        self.scratch = (
            pltpu.VMEM((others, LINE) + shape, jnp.bfloat16),
            dma(others, LINE),
            dma(others, LINE),
        )

    def targets(self):
        line, cross = self.place()
        return [lax.rem(cross + step, self.cross) for step in range(1, self.cross)]

    def partners(self):
        line, cross = self.place()
        return [{"dp": line * self.cross + other} for other in self.targets()]

    def begin(self):
        (x_ref,), (buf, send, recv) = self.ins_refs, self.scratch_refs
        line, cross = self.place()
        self.copies = []
        for i, other in enumerate(self.targets()):
            for z in range(LINE):
                copy = remote(
                    x_ref.at[z, other],
                    buf.at[i, z],
                    send.at[i, z],
                    recv.at[i, z],
                    {"dp": line * self.cross + other},
                )
                copy.start()
                self.copies.append(copy)

    def end(self):
        (x_ref,), (o_ref,), (buf, send, recv) = self.ins_refs, self.outs_refs, self.scratch_refs
        line, cross = self.place()
        for copy in self.copies:
            copy.wait()
        for z in range(LINE):
            total = x_ref[z, cross].astype(jnp.float32)
            for i in range(self.cross - 1):
                total = total + buf[i, z].astype(jnp.float32)
            o_ref[z] = total.astype(jnp.bfloat16)


class SpreadLine(GridTask):
    def __init__(self, block):
        super().__init__()
        self.ins = (block,)
        self.outs = (shaped((LINE,) + block.shape, block.dtype),)
        self.scratch = (dma(LINE - 1), dma(LINE - 1))

    def targets(self):
        line, cross = self.place()
        return [lax.rem(line + step, LINE) for step in range(1, LINE)]

    def partners(self):
        line, cross = self.place()
        return [{"dp": other * self.cross + cross} for other in self.targets()]

    def begin(self):
        (x_ref,), (o_ref,), (send, recv) = self.ins_refs, self.outs_refs, self.scratch_refs
        line, cross = self.place()
        self.copies = [
            remote(x_ref, o_ref.at[line], send.at[i], recv.at[i], partner)
            for i, partner in enumerate(self.partners())
        ]
        for copy in self.copies:
            copy.start()
        o_ref[line] = x_ref[...]

    def end(self):
        for copy in self.copies:
            copy.wait()


class SpreadCross(GridTask):
    def __init__(self, blocks):
        super().__init__()
        self.ins = (blocks,)
        self.outs = (shaped((LINE, self.cross) + blocks.shape[1:], blocks.dtype),)
        others = max(self.cross - 1, 1)
        self.scratch = (dma(others, LINE), dma(others, LINE))

    def partners(self):
        line, cross = self.place()
        return [
            {"dp": line * self.cross + lax.rem(cross + step, self.cross)}
            for step in range(1, self.cross)
        ]

    def begin(self):
        (x_ref,), (o_ref,), (send, recv) = self.ins_refs, self.outs_refs, self.scratch_refs
        line, cross = self.place()
        self.copies = []
        for i, partner in enumerate(self.partners()):
            for z in range(LINE):
                copy = remote(x_ref.at[z], o_ref.at[z, cross], send.at[i, z], recv.at[i, z], partner)
                copy.start()
                self.copies.append(copy)
        for z in range(LINE):
            o_ref[z, cross] = x_ref[z]

    def end(self):
        for copy in self.copies:
            copy.wait()


class ReduceLine(GridTask):
    def __init__(self, blocks):
        super().__init__()
        shape = blocks.shape[1:]
        self.ins = (blocks,)
        self.outs = (shaped(shape, jnp.float32),)
        self.scratch = (pltpu.VMEM((LINE - 1,) + shape, jnp.bfloat16), dma(LINE - 1), dma(LINE - 1))

    def targets(self):
        line, cross = self.place()
        return [lax.rem(line + step, LINE) for step in range(1, LINE)]

    def partners(self):
        line, cross = self.place()
        return [{"dp": other * self.cross + cross} for other in self.targets()]

    def begin(self):
        (x_ref,), (buf, send, recv) = self.ins_refs, self.scratch_refs
        line, cross = self.place()
        self.copies = [
            remote(
                x_ref.at[other], buf.at[i], send.at[i], recv.at[i], {"dp": other * self.cross + cross}
            )
            for i, other in enumerate(self.targets())
        ]
        for copy in self.copies:
            copy.start()

    def end(self):
        (x_ref,), (o_ref,), (buf, send, recv) = self.ins_refs, self.outs_refs, self.scratch_refs
        line, cross = self.place()
        for copy in self.copies:
            copy.wait()
        total = x_ref[line].astype(jnp.float32)
        for i in range(LINE - 1):
            total = total + buf[i].astype(jnp.float32)
        o_ref[...] = total


class SumAll(Task):
    def __init__(self, block, keep):
        self.groups, self.width, self.keep = lax.axis_size("dp"), lax.axis_size("tensor"), keep
        rows, depth = block.shape
        self.narrow = narrow = depth // self.width
        kept = self.groups if keep else 1
        self.ins = (block,)
        self.outs = (shaped((kept, rows, depth), block.dtype),)
        near, far = dma(self.width), dma(self.groups)
        self.scratch = (
            pltpu.VMEM((self.width, rows, narrow), block.dtype),
            pltpu.VMEM((rows, narrow), block.dtype),
            pltpu.VMEM((self.groups, rows, narrow), block.dtype),
            pltpu.VMEM((kept, rows, narrow), block.dtype),
            near, near, far, far, near, near,
        )

    def mates(self):
        me = lax.axis_index("tensor")
        return [lax.rem(me + step, self.width) for step in range(1, self.width)]

    def peers(self):
        me = lax.axis_index("dp")
        return [lax.rem(me + step, self.groups) for step in range(1, self.groups)]

    def partners(self):
        return [{"tensor": mate} for mate in self.mates()] + [{"dp": peer} for peer in self.peers()]

    def lanes(self, owner):
        return pl.ds(pl.multiple_of(owner * self.narrow, self.narrow), self.narrow)

    def launch(self, copies):
        for copy in copies:
            copy.start()
        self.copies = copies

    def settle(self):
        for copy in self.copies:
            copy.wait()

    def begin(self):
        (x_ref,) = self.ins_refs
        part_buf, sems = self.scratch_refs[0], self.scratch_refs[4:]
        me = lax.axis_index("tensor")
        self.launch(
            [
                remote(
                    x_ref.at[:, self.lanes(mate)],
                    part_buf.at[me],
                    sems[0].at[i],
                    sems[1].at[i],
                    {"tensor": mate},
                )
                for i, mate in enumerate(self.mates())
            ]
        )
        part_buf[me] = x_ref[:, self.lanes(me)]

    def middle(self):
        (o_ref,) = self.outs_refs
        part_buf, sum_buf, all_buf, out_buf = self.scratch_refs[:4]
        sems = self.scratch_refs[4:]
        dp_me, me = lax.axis_index("dp"), lax.axis_index("tensor")
        self.settle()
        sum_buf[...] = jnp.sum(part_buf[...], axis=0)
        self.launch(
            [
                remote(sum_buf, all_buf.at[dp_me], sems[2].at[i], sems[3].at[i], {"dp": peer})
                for i, peer in enumerate(self.peers())
            ]
        )
        all_buf[dp_me] = sum_buf[...]
        self.settle()
        if self.keep:
            out_buf[...] = all_buf[...]
        else:
            out_buf[0] = jnp.sum(all_buf[...], axis=0)
        self.launch(
            [
                remote(
                    out_buf,
                    o_ref.at[:, :, self.lanes(me)],
                    sems[4].at[i],
                    sems[5].at[i],
                    {"tensor": mate},
                )
                for i, mate in enumerate(self.mates())
            ]
        )
        o_ref[:, :, self.lanes(me)] = out_buf[...]

    def end(self):
        self.settle()


Q_BLOCK = 256
K_BLOCK = 256


def split_pair(wide):
    half = wide.shape[0] // 2
    upper = lax.broadcasted_iota(jnp.int32, wide.shape, 0) < half
    zero = jnp.zeros_like(wide)
    return jnp.concatenate([jnp.where(upper, wide, zero), jnp.where(upper, zero, wide)], axis=1)


def stack_pair(tall):
    half = tall.shape[1] // 2
    left = lax.broadcasted_iota(jnp.int32, tall.shape, 1) < half
    zero = jnp.zeros_like(tall)
    return jnp.concatenate([jnp.where(left, tall, zero), jnp.where(left, zero, tall)], axis=0)


def join_pair(wide):
    depth, columns = wide.shape
    upper = lax.broadcasted_iota(jnp.int32, (depth, columns // 2), 0) < depth // 2
    return jnp.where(upper, wide[:, : columns // 2], wide[:, columns // 2 :])


def turn(tile):
    return tile.astype(jnp.float32).T.astype(jnp.bfloat16)


def block_span(index, size):
    return pl.ds(pl.multiple_of(index * size, size), size)


def attend_kernel(low_ref, high_ref, qkv_ref, seq_col_ref, seq_row_ref, out_ref, log_ref, value_turned, scores):
    slots, columns = out_ref.shape
    pairs = columns // 128
    q_blocks, k_blocks = slots // Q_BLOCK, slots // K_BLOCK

    def turn_values(b, carry):
        rows = block_span(b, K_BLOCK)
        for pair in range(pairs):
            value_turned[pl.ds(pair * 128, 128), rows] = turn(
                qkv_ref[rows, pl.ds(2 * columns + pair * 128, 128)]
            )
        return carry

    lax.fori_loop(0, k_blocks, turn_values, 0)

    def one_block(q_index, carry):
        q_rows = block_span(q_index, Q_BLOCK)
        lowest, highest = low_ref[q_index], high_ref[q_index]
        seq_row = seq_row_ref[0:1, q_rows]
        seq_pair = jnp.concatenate([seq_row, seq_row], axis=1)
        queries = [
            split_pair(
                (qkv_ref[q_rows, pl.ds(pair * 128, 128)].astype(jnp.float32) * HEAD ** (-0.5))
                .T.astype(jnp.bfloat16)
            )
            for pair in range(pairs)
        ]

        def score(k_index, tops):
            k_rows = block_span(k_index, K_BLOCK)
            same = seq_col_ref[k_rows, 0:1] == seq_pair
            later = []
            for pair in range(pairs):
                keys = qkv_ref[k_rows, pl.ds(columns + pair * 128, 128)]
                value = jnp.where(same, multiply_arrays(keys, queries[pair]), MASK_FILL)
                scores[pair, k_index - lowest] = value
                later.append(jnp.maximum(tops[pair], jnp.max(value, axis=0, keepdims=True)))
            return tuple(later)

        start = tuple(jnp.full((1, 2 * Q_BLOCK), MASK_FILL, jnp.float32) for _ in range(pairs))
        tops = lax.fori_loop(lowest, highest, score, start)

        def mix(k_index, state):
            k_rows = block_span(k_index, K_BLOCK)
            later = []
            for pair in range(pairs):
                total, mixed = state[pair]
                weights = jnp.exp(scores[pair, k_index - lowest] - tops[pair])
                total = total + jnp.sum(weights, axis=0, keepdims=True)
                mixed = mixed + multiply_arrays(
                    value_turned[pl.ds(pair * 128, 128), k_rows], weights.astype(jnp.bfloat16)
                )
                later.append((total, mixed))
            return tuple(later)

        blank = tuple(
            (jnp.zeros((1, 2 * Q_BLOCK), jnp.float32), jnp.zeros((128, 2 * Q_BLOCK), jnp.float32))
            for _ in range(pairs)
        )
        final = lax.fori_loop(lowest, highest, mix, blank)
        for pair in range(pairs):
            total, mixed = final[pair]
            out_ref[q_rows, pl.ds(pair * 128, 128)] = join_pair(mixed / total).T.astype(jnp.bfloat16)
            logs = tops[pair] + jnp.log(total)
            log_ref[pl.ds(2 * pair, 1), q_rows] = logs[:, :Q_BLOCK]
            log_ref[pl.ds(2 * pair + 1, 1), q_rows] = logs[:, Q_BLOCK:]
        return carry

    lax.fori_loop(0, q_blocks, one_block, 0)


def block_bounds(lengths, slots):
    ends = jnp.cumsum(lengths)
    starts = ends - lengths
    first = jnp.arange(slots // Q_BLOCK, dtype=jnp.int32) * Q_BLOCK
    last = first + Q_BLOCK - 1
    lowest = jnp.max(
        jnp.where(starts[None, :] <= first[:, None], starts[None, :], 0), axis=1
    )
    highest = jnp.min(jnp.where(ends[None, :] > last[:, None], ends[None, :], slots), axis=1)
    return (lowest // K_BLOCK, (highest + K_BLOCK - 1) // K_BLOCK)


REACH = (2 * MAXLEN - 2) // K_BLOCK + Q_BLOCK // K_BLOCK + 1


def in_scalars():
    return pl.BlockSpec(memory_space=pltpu.SMEM)


def attend(qkv_out, seq_ids, bounds):
    slots, columns = qkv_out.shape[0], qkv_out.shape[1] // 3
    pairs = columns // 128
    return pl.pallas_call(
        attend_kernel,
        out_shape=[
            jax.ShapeDtypeStruct((slots, columns), jnp.bfloat16),
            jax.ShapeDtypeStruct((8, slots), jnp.float32),
        ],
        in_specs=[in_scalars(), in_scalars()] + [in_vmem()] * 3,
        out_specs=[in_vmem()] * 2,
        scratch_shapes=[
            pltpu.VMEM((columns, slots), jnp.bfloat16),
            pltpu.VMEM((pairs, REACH, K_BLOCK, 2 * Q_BLOCK), jnp.float32),
        ],
        compiler_params=pltpu.CompilerParams(vmem_limit_bytes=VMEM_BYTES),
    )(bounds[0], bounds[1], qkv_out, seq_ids[:, None], jnp.broadcast_to(seq_ids[None], (8, slots)))


def attend_back_kernel(
    low_ref, high_ref, qkv_ref, grad_ref, log_ref, seq_col_ref, seq_row_ref, out_ref,
    key_turned, probs, prob_grads, key_sum, value_sum,
):
    slots, columns = grad_ref.shape
    pairs = columns // 128
    q_blocks, k_blocks = slots // Q_BLOCK, slots // K_BLOCK

    def turn_keys(b, carry):
        rows = block_span(b, K_BLOCK)
        for pair in range(pairs):
            key_turned[pl.ds(pair * 128, 128), rows] = turn(
                qkv_ref[rows, pl.ds(columns + pair * 128, 128)]
            )
        key_sum[rows] = jnp.zeros((K_BLOCK, columns), jnp.float32)
        value_sum[rows] = jnp.zeros((K_BLOCK, columns), jnp.float32)
        return carry

    lax.fori_loop(0, k_blocks, turn_keys, 0)

    def one_block(q_index, carry):
        q_rows = block_span(q_index, Q_BLOCK)
        lowest, highest = low_ref[q_index], high_ref[q_index]
        seq_row = seq_row_ref[0:1, q_rows]
        seq_pair = jnp.concatenate([seq_row, seq_row], axis=1)
        scaled, queries, grads, turned, logs = [], [], [], [], []
        for pair in range(pairs):
            plain = qkv_ref[q_rows, pl.ds(pair * 128, 128)].astype(jnp.float32) * HEAD ** (-0.5)
            scaled.append(stack_pair(plain.astype(jnp.bfloat16)))
            queries.append(split_pair(plain.T.astype(jnp.bfloat16)))
            grad = grad_ref[q_rows, pl.ds(pair * 128, 128)]
            grads.append(stack_pair(grad))
            turned.append(split_pair(turn(grad)))
            logs.append(
                jnp.concatenate(
                    [log_ref[pl.ds(2 * pair, 1), q_rows], log_ref[pl.ds(2 * pair + 1, 1), q_rows]],
                    axis=1,
                )
            )

        def look(k_index, inners):
            k_rows = block_span(k_index, K_BLOCK)
            same = seq_col_ref[k_rows, 0:1] == seq_pair
            later = []
            for pair in range(pairs):
                keys = qkv_ref[k_rows, pl.ds(columns + pair * 128, 128)]
                values = qkv_ref[k_rows, pl.ds(2 * columns + pair * 128, 128)]
                logits = jnp.where(same, multiply_arrays(keys, queries[pair]), MASK_FILL)
                weights = jnp.exp(logits - logs[pair])
                weight_grad = multiply_arrays(values, turned[pair])
                probs[pair, k_index - lowest] = weights
                prob_grads[pair, k_index - lowest] = weight_grad
                value_sum[k_rows, pl.ds(pair * 128, 128)] += multiply_arrays(
                    weights.astype(jnp.bfloat16), grads[pair]
                )
                later.append(
                    inners[pair] + jnp.sum(weights * weight_grad, axis=0, keepdims=True)
                )
            return tuple(later)

        start = tuple(jnp.zeros((1, 2 * Q_BLOCK), jnp.float32) for _ in range(pairs))
        inners = lax.fori_loop(lowest, highest, look, start)

        def push(k_index, sums):
            k_rows = block_span(k_index, K_BLOCK)
            later = []
            for pair in range(pairs):
                slope = (
                    probs[pair, k_index - lowest]
                    * (prob_grads[pair, k_index - lowest] - inners[pair])
                ).astype(jnp.bfloat16)
                key_sum[k_rows, pl.ds(pair * 128, 128)] += multiply_arrays(slope, scaled[pair])
                later.append(
                    sums[pair] + multiply_arrays(key_turned[pl.ds(pair * 128, 128), k_rows], slope)
                )
            return tuple(later)

        blank = tuple(jnp.zeros((128, 2 * Q_BLOCK), jnp.float32) for _ in range(pairs))
        sums = lax.fori_loop(lowest, highest, push, blank)
        for pair in range(pairs):
            out_ref[q_rows, pl.ds(pair * 128, 128)] = (
                (join_pair(sums[pair]) * HEAD ** (-0.5)).T.astype(jnp.bfloat16)
            )
        return carry

    lax.fori_loop(0, q_blocks, one_block, 0)
    out_ref[:, columns : 2 * columns] = key_sum[...].astype(jnp.bfloat16)
    out_ref[:, 2 * columns :] = value_sum[...].astype(jnp.bfloat16)


def attend_back(qkv_out, attn_grad, log_total, seq_ids, bounds):
    slots, columns = attn_grad.shape
    pairs = columns // 128
    window = pltpu.VMEM((pairs, REACH, K_BLOCK, 2 * Q_BLOCK), jnp.float32)
    return pl.pallas_call(
        attend_back_kernel,
        out_shape=jax.ShapeDtypeStruct(qkv_out.shape, jnp.bfloat16),
        in_specs=[in_scalars(), in_scalars()] + [in_vmem()] * 5,
        out_specs=in_vmem(),
        scratch_shapes=[
            pltpu.VMEM((columns, slots), jnp.bfloat16),
            window,
            window,
            pltpu.VMEM((slots, columns), jnp.float32),
            pltpu.VMEM((slots, columns), jnp.float32),
        ],
        compiler_params=pltpu.CompilerParams(vmem_limit_bytes=VMEM_BYTES),
    )(
        bounds[0],
        bounds[1],
        qkv_out,
        attn_grad,
        log_total,
        seq_ids[:, None],
        jnp.broadcast_to(seq_ids[None], (8, slots)),
    )


def gelu_parts(upper):
    distance = jnp.abs(upper) * 0.7071067811865476
    step = 1.0 / (1.0 + 0.3275911 * distance)
    bell = jnp.exp(-distance * distance)
    series = step * (
        0.254829592
        + step * (-0.284496736 + step * (1.421413741 + step * (-1.453152027 + step * 1.061405429)))
    )
    tail = 0.5 * series * bell
    share = jnp.where(upper >= 0.0, 1.0 - tail, tail)
    return (upper * share, share + upper * (bell * 0.3989422804014327))


def expand_kernel(rows_ref, weight_ref, bias_ref, hidden_ref, slope_ref):
    units = weight_ref.shape[1]
    rows = rows_ref[...]
    for first in range(0, units, 256):
        lanes = pl.ds(first, 256)
        upper = multiply_arrays(rows, weight_ref[:, lanes]) + bias_ref[:, lanes]
        hidden, slope = gelu_parts(upper)
        hidden_ref[:, lanes] = hidden.astype(jnp.bfloat16)
        slope_ref[:, lanes] = slope


def expand(rows, weight, bias):
    slots, depth = rows.shape
    units = weight.shape[1]
    tall = 256
    return pl.pallas_call(
        expand_kernel,
        grid=(slots // tall,),
        out_shape=[shaped((slots, units), jnp.bfloat16), shaped((slots, units), jnp.float32)],
        in_specs=[
            pl.BlockSpec((tall, depth), lambda i: (i, 0)),
            pl.BlockSpec((depth, units), lambda i: (0, 0)),
            pl.BlockSpec((1, units), lambda i: (0, 0)),
        ],
        out_specs=[
            pl.BlockSpec((tall, units), lambda i: (i, 0)),
            pl.BlockSpec((tall, units), lambda i: (i, 0)),
        ],
        compiler_params=pltpu.CompilerParams(vmem_limit_bytes=VMEM_BYTES),
    )(rows, weight, bias)


EMBED_ROWS = 128
MARGIN = 256


def embed_kernel(
    start_ref, span_ref, own_ref, tok_ref, pos_ref, seq_ref, row_ref, low_ref, emb_ref, norm_ref, padded
):
    slots = tok_ref.shape[0]
    blocks, own_blocks = slots // EMBED_ROWS, emb_ref.shape[0] // EMBED_ROWS
    padded[pl.ds(MARGIN, pos_ref.shape[0])] = pos_ref[...]
    gain, shift = row_ref[0:1], row_ref[3:4]

    def one_block(b, carry):
        rows = block_span(b, EMBED_ROWS)
        seq = seq_ref[rows, 0:1]

        def pick(s, placed):
            first = MARGIN + 2 + b * EMBED_ROWS - start_ref[s]
            base = first // 8
            window = padded[pl.ds(pl.multiple_of(base * 8, 8), EMBED_ROWS + 8)]
            window = pltpu.roll(window, EMBED_ROWS + 8 - (first - base * 8), 0)
            return jnp.where(seq == s, window[:EMBED_ROWS], placed)

        placed = lax.fori_loop(
            span_ref[0, b], span_ref[1, b], pick, jnp.zeros((EMBED_ROWS, tok_ref.shape[1]), jnp.float32)
        )
        emb = tok_ref[rows].astype(jnp.float32) + placed
        norm = norm_rows(emb, gain, shift)
        low_ref[rows] = norm.astype(jnp.bfloat16)
        own = b - own_ref[0] * own_blocks

        @pl.when((own >= 0) & (own < own_blocks))
        def _():
            own_rows = block_span(own, EMBED_ROWS)
            emb_ref[own_rows] = emb
            norm_ref[own_rows] = norm

        return carry

    lax.fori_loop(0, blocks, one_block, 0)


def embed(tok_all, pos_full, seq_ids, lengths, row_params):
    slots, depth = tok_all.shape
    own = slots // lax.axis_size("tensor")
    ends = jnp.cumsum(lengths)
    starts = ends - lengths
    first = jnp.arange(slots // EMBED_ROWS, dtype=jnp.int32) * EMBED_ROWS
    spans = jnp.stack(
        [
            jnp.sum((ends[None, :] <= first[:, None]).astype(jnp.int32), axis=1),
            jnp.sum((starts[None, :] < first[:, None] + EMBED_ROWS).astype(jnp.int32), axis=1),
        ]
    )
    return pl.pallas_call(
        embed_kernel,
        out_shape=[
            shaped((slots, depth), jnp.bfloat16),
            shaped((own, depth), jnp.float32),
            shaped((own, depth), jnp.float32),
        ],
        in_specs=[in_scalars()] * 3 + [in_vmem()] * 4,
        out_specs=[in_vmem()] * 3,
        scratch_shapes=[
            pltpu.VMEM((MARGIN + MAXLEN + EMBED_ROWS + 24, depth), jnp.float32)
        ],
        compiler_params=pltpu.CompilerParams(vmem_limit_bytes=VMEM_BYTES),
    )(
        starts,
        spans,
        lax.axis_index("tensor").astype(jnp.int32)[None],
        tok_all,
        pos_full,
        seq_ids[:, None],
        row_params,
    )


SCATTER_ROWS = 512


def scatter_kernel(index_ref, rows_ref, grad_ref, square_ref):
    first = pl.program_id(0) * SCATTER_ROWS
    slots = index_ref.shape[1]
    here = (
        lax.broadcasted_iota(jnp.int32, (SCATTER_ROWS, slots), 0) + first == index_ref[...]
    ).astype(jnp.float32)
    grad = multiply_arrays(here.astype(jnp.bfloat16), rows_ref[...])
    grad_ref[...] = grad

    @pl.when(pl.program_id(0) == 0)
    def _():
        square_ref[...] = jnp.zeros_like(square_ref)

    square_ref[...] += jnp.sum(
        (grad * grad).reshape(SCATTER_ROWS // 8, 8, grad.shape[1]), axis=0
    )


def scatter_rows(index, rows, height):
    slots, width = rows.shape
    grad, squares = pl.pallas_call(
        scatter_kernel,
        grid=(pl.cdiv(height, SCATTER_ROWS),),
        out_shape=[shaped((height, width), jnp.float32), shaped((8, width), jnp.float32)],
        in_specs=[
            pl.BlockSpec((1, slots), lambda i: (0, 0)),
            pl.BlockSpec((slots, width), lambda i: (0, 0)),
        ],
        out_specs=[
            pl.BlockSpec((SCATTER_ROWS, width), lambda i: (i, 0)),
            pl.BlockSpec((8, width), lambda i: (0, 0)),
        ],
        compiler_params=pltpu.CompilerParams(vmem_limit_bytes=VMEM_BYTES),
    )(index[None], rows)
    return (grad, jnp.sum(squares))


def layer_forward(embedded, seq_ids, bounds, row_params, col_local, layer_mats):
    first_moment_all, emb_rows, norm_first = embedded
    qkv_full, out_full, up_half, down_low = layer_mats
    col_width = col_local.shape[1]
    qkv_bias = jnp.concatenate([col_local[0], jnp.zeros_like(col_local[0]), col_local[1]])
    qkv_out = (multiply_arrays(first_moment_all, qkv_full) + qkv_bias).astype(jnp.bfloat16)
    attn_low, log_total = attend(qkv_out, seq_ids, bounds)
    first_back = jnp.einsum("tc,dc->td", attn_low, out_full, preferred_element_type=jnp.float32)
    first_branch, up_full, down_half = exchange(
        5, Fold(first_back.astype(jnp.bfloat16)), SpreadCross(up_half), SpreadLine(down_low)
    )
    up_full = up_full.reshape(D, -1)
    first_sum = norm_first + first_branch + row_params[6]
    norm_second = norm_rows(first_sum, row_params[1], row_params[4])
    second_all, down_full = exchange(
        6, Spread(norm_second.astype(jnp.bfloat16)), SpreadCross(down_half)
    )
    down_full = down_full.reshape(D, -1)
    hidden_low, slope = expand(second_all, up_full, col_local[2:].reshape(1, -1))
    second_back = jnp.einsum("tf,df->td", hidden_low, down_full, preferred_element_type=jnp.float32)
    second_sum = (
        norm_second + exchange(7, Fold(second_back.astype(jnp.bfloat16))) + row_params[7]
    )
    norm_third = norm_rows(second_sum, row_params[2], row_params[5])
    saved_vals = (
        emb_rows,
        first_moment_all,
        qkv_out,
        log_total,
        attn_low,
        first_sum,
        second_all,
        slope,
        hidden_low,
        second_sum,
    )
    return (norm_third, saved_vals, (qkv_full, out_full, up_full, down_full))


def turned_grad(left_all, right_all):
    grad = jnp.einsum("td,tc->dc", left_all, right_all, preferred_element_type=jnp.float32)
    groups = lax.axis_size("dp")
    return grad.astype(jnp.bfloat16).reshape(groups, grad.shape[0] // groups, grad.shape[1])


def layer_backward(grad_third, seq_ids, bounds, row_params, layer_mats, saved_vals):
    qkv_full, out_full, up_full, down_full = layer_mats
    (
        emb_rows,
        first_moment_all,
        qkv_out,
        log_total,
        attn_low,
        first_sum,
        second_all,
        slope,
        hidden_low,
        second_sum,
    ) = saved_vals
    col_width = out_full.shape[1]
    grad_second, gain_c, shift_c = norm_back(second_sum, row_params[2], row_params[5], grad_third)
    mixed_low = grad_second.astype(jnp.bfloat16)
    mixed_all = exchange(10, Spread(mixed_low))
    down_grad = turned_grad(mixed_all, hidden_low)
    up_low = (multiply_arrays(mixed_all, down_full) * slope).astype(jnp.bfloat16)
    up_grad = turned_grad(second_all, up_low)
    second_back = jnp.einsum(
        "tf,df->td", up_low, up_full, preferred_element_type=jnp.float32
    ).astype(jnp.bfloat16)
    second_back, down_half = exchange(11, Fold(second_back), ReduceCross(down_grad))
    second_total = grad_second + second_back
    grad_first, gain_b, shift_b = norm_back(first_sum, row_params[1], row_params[4], second_total)
    branch_low = grad_first.astype(jnp.bfloat16)
    branch_all, down_sum, up_half = exchange(
        12, Spread(branch_low), ReduceLine(down_half), ReduceCross(up_grad)
    )
    out_grad = turned_grad(branch_all, attn_low)
    attn_grad = multiply_arrays(branch_all, out_full).astype(jnp.bfloat16)
    qkv_low = attend_back(qkv_out, attn_grad, log_total, seq_ids, bounds)
    qkv_grad = turned_grad(first_moment_all, qkv_low)
    first_back = jnp.einsum(
        "tc,dc->td", qkv_low, qkv_full, preferred_element_type=jnp.float32
    ).astype(jnp.bfloat16)
    first_back, up_sum, out_half, qkv_half = exchange(
        13, Fold(first_back), ReduceLine(up_half), ReduceCross(out_grad), ReduceCross(qkv_grad)
    )
    first_total = grad_first + first_back
    emb_grad, gain_a, shift_a = norm_back(emb_rows, row_params[0], row_params[3], first_total)
    qkv_cols = jnp.sum(qkv_low.astype(jnp.float32), axis=0).reshape(3, col_width)
    up_cols = jnp.sum(up_low.astype(jnp.float32), axis=0).reshape(-1, col_width)
    col_grad = jnp.concatenate([qkv_cols[0:1], qkv_cols[2:3], up_cols], axis=0)
    row_grad = jnp.stack(
        [
            gain_a,
            gain_b,
            gain_c,
            shift_a,
            shift_b,
            shift_c,
            jnp.sum(branch_low.astype(jnp.float32), axis=0),
            jnp.sum(mixed_low.astype(jnp.float32), axis=0),
        ]
    )
    return (emb_grad, (qkv_half, out_half, up_sum, down_sum), col_grad, row_grad)


def plan_kernel(capacity, vocab_local, groups, perm_ref, low_ref, high_ref, slot_ref, list_ref, count_ref, id_buf, own_buf):
    slots = perm_ref.shape[1]
    table_rows = low_ref.shape[1]
    block = 128
    blocks = slots // block
    perm = perm_ref[...]
    high_part = perm // 128
    low_part = perm - high_part * 128
    chooser = (lax.broadcasted_iota(jnp.int32, (table_rows, slots), 0) == high_part).astype(
        jnp.float32
    ).astype(jnp.bfloat16)
    value = multiply_arrays(low_ref[...], chooser) + 256.0 * multiply_arrays(high_ref[...], chooser)
    lane_match = lax.broadcasted_iota(jnp.int32, (128, slots), 0) == low_part
    ids = jnp.sum(jnp.where(lane_match, value, 0.0), axis=0, keepdims=True)
    for b in range(blocks):
        id_buf[pl.ds(b * block, block), :] = jnp.broadcast_to(
            ids[:, b * block : (b + 1) * block], (block, block)
        ).T
    place = lax.broadcasted_iota(jnp.int32, (1, slots), 1).astype(jnp.float32)
    rows = lax.broadcasted_iota(jnp.int32, (block, 1), 0).astype(jnp.float32)

    def earliest(b, best):
        column = id_buf[pl.ds(pl.multiple_of(b * block, block), block), 0:1]
        index = rows + (b * block).astype(jnp.float32)
        found = jnp.where(column == ids, index, 1e9)
        return jnp.minimum(best, jnp.min(found, axis=0, keepdims=True))

    least = lax.fori_loop(0, blocks, earliest, jnp.full((1, slots), 1e9, jnp.float32))
    first = least == place
    owner = jnp.zeros((1, slots), jnp.float32)
    for index in range(1, groups):
        owner = owner + jnp.where(ids >= float(index * vocab_local), 1.0, 0.0)
    owner_rows = lax.broadcasted_iota(jnp.int32, (groups, slots), 0).astype(jnp.float32)
    marks = jnp.where(first & (owner == owner_rows), 1.0, 0.0)
    upper = jnp.where(
        lax.broadcasted_iota(jnp.int32, (block, block), 0)
        < lax.broadcasted_iota(jnp.int32, (block, block), 1),
        1.0,
        0.0,
    ).astype(jnp.bfloat16)
    running = jnp.zeros((groups, 1), jnp.float32)
    pieces = []
    for b in range(blocks):
        part = marks[:, b * block : (b + 1) * block]
        pieces.append(multiply_arrays(part.astype(jnp.bfloat16), upper) + running)
        running = running + jnp.sum(part, axis=1, keepdims=True)
    before = jnp.concatenate(pieces, axis=1)
    rank = jnp.sum(marks * before, axis=0, keepdims=True)
    own_slot = jnp.where(first & (rank < float(capacity)), owner * float(capacity) + rank, -1.0)
    for b in range(blocks):
        own_buf[pl.ds(b * block, block), :] = jnp.broadcast_to(
            own_slot[:, b * block : (b + 1) * block], (block, block)
        ).T
    width = list_ref.shape[1]
    target = lax.broadcasted_iota(jnp.int32, (1, width), 1).astype(jnp.float32)

    def settle(b, carry):
        slot, listed = carry
        window = pl.ds(pl.multiple_of(b * block, block), block)
        column, slot_column = id_buf[window, 0:1], own_buf[window, 0:1]
        slot = jnp.maximum(
            slot, jnp.max(jnp.where(column == ids, slot_column, -1.0), axis=0, keepdims=True)
        )
        listed = jnp.maximum(
            listed, jnp.max(jnp.where(slot_column == target, column, -1.0), axis=0, keepdims=True)
        )
        return (slot, listed)

    slot, listed = lax.fori_loop(
        0,
        blocks,
        settle,
        (jnp.full((1, slots), -1.0, jnp.float32), jnp.full((1, width), -1.0, jnp.float32)),
    )
    slot_ref[...] = slot.astype(jnp.int32)
    list_ref[...] = listed.astype(jnp.int32)
    count_ref[...] = jnp.broadcast_to(running, count_ref.shape).astype(jnp.int32)


def make_plan(perm, all_ids, capacity, vocab_local, groups):
    slots = perm.shape[0]
    table = all_ids.reshape(-1, 128).T
    high = table // 256
    low = table - high * 256
    return pl.pallas_call(
        partial(plan_kernel, capacity, vocab_local, groups),
        out_shape=[
            jax.ShapeDtypeStruct((1, slots), jnp.int32),
            jax.ShapeDtypeStruct((1, groups * capacity), jnp.int32),
            jax.ShapeDtypeStruct((groups, 128), jnp.int32),
        ],
        in_specs=[in_vmem()] * 3,
        out_specs=[in_vmem()] * 3,
        scratch_shapes=[pltpu.VMEM((slots, 128), jnp.float32), pltpu.VMEM((slots, 128), jnp.float32)],
        compiler_params=pltpu.CompilerParams(vmem_limit_bytes=VMEM_BYTES),
    )(perm[None], low.astype(jnp.bfloat16), high.astype(jnp.bfloat16))


def loss_kernel(pooled_ref, head_ref, pair_ref, loss_ref, low_ref, grad_ref, back_ref):
    total = pooled_ref.shape[0]
    low = pooled_ref[...].astype(jnp.bfloat16)
    low_ref[...] = low
    head_low = head_ref[...].astype(jnp.bfloat16)
    vectors = multiply_arrays(low, head_low)
    depth = vectors.shape[1]
    lane = lax.broadcasted_iota(jnp.int32, vectors.shape, 1)
    across = lax.broadcasted_iota(jnp.int32, (total, total), 1)
    diagonal = lax.broadcasted_iota(jnp.int32, (total, total), 0) == across
    chosen = across == pair_ref[...]
    loss = jnp.zeros((1, 1), jnp.float32)
    grads = jnp.zeros(vectors.shape, jnp.float32)

    def exact(left, right, dims):
        return lax.dot_general(
            left, right, (dims, ((), ())), precision=HIGHEST_MODE, preferred_element_type=jnp.float32
        )

    for fraction in (16, 4, 1):
        prefix = jnp.where(lane < depth // fraction, vectors, 0.0)
        inverse = lax.rsqrt(jnp.sum(prefix * prefix, axis=1, keepdims=True) + 1e-06)
        unit = prefix * inverse
        logits = exact(unit, unit, ((1,), (1,))) / LOGIT_DIVISOR
        logits = jnp.where(diagonal, MASK_FILL, logits)
        top = jnp.max(logits, axis=1, keepdims=True)
        weights = jnp.exp(logits - top)
        weight_sum = jnp.sum(weights, axis=1, keepdims=True)
        positive = jnp.sum(jnp.where(chosen, logits, 0.0), axis=1, keepdims=True)
        loss = loss + jnp.sum(jnp.log(weight_sum) + top - positive, keepdims=True)
        pull = weights / weight_sum - jnp.where(chosen, 1.0, 0.0)
        unit_grad = (exact(pull, unit, ((1,), (0,))) + exact(pull, unit, ((0,), (0,)))) / LOGIT_DIVISOR
        unit_grad = jnp.where(lane < depth // fraction, unit_grad, 0.0)
        inner = jnp.sum(unit_grad * prefix, axis=1, keepdims=True)
        grads = grads + inverse * unit_grad - prefix * (inverse * inverse * inverse * inner)
    loss_ref[...] = jnp.broadcast_to(loss, loss_ref.shape)
    grad_ref[...] = grads
    back_ref[...] = exact(grads, head_low.astype(jnp.float32), ((1,), (1,)))


def contrast_step(pooled, head_weight, pairs):
    total, depth = pooled.shape
    return pl.pallas_call(
        loss_kernel,
        out_shape=[
            jax.ShapeDtypeStruct((8, 128), jnp.float32),
            jax.ShapeDtypeStruct((total, depth), jnp.bfloat16),
            jax.ShapeDtypeStruct((total, depth), jnp.float32),
            jax.ShapeDtypeStruct((total, depth), jnp.float32),
        ],
        in_specs=[in_vmem()] * 3,
        out_specs=[in_vmem()] * 4,
        compiler_params=pltpu.CompilerParams(vmem_limit_bytes=VMEM_BYTES),
    )(pooled, head_weight, pairs[:, None])


CAPACITY = 192


def body(
    token_ids,
    slot_perm,
    seq_lengths,
    pair_index,
    tok_table,
    tok_first,
    tok_second,
    pos_table,
    pos_first,
    pos_second,
    query_key_value_weight,
    qkv_first,
    qkv_second,
    out_weight,
    out_first,
    out_second,
    up_weight,
    up_first,
    up_second,
    down_weight,
    down_first,
    down_second,
    head_weight,
    head_first,
    head_second,
    col_bias,
    col_first,
    col_second,
    row_params,
    row_first,
    row_second,
):
    groups = lax.axis_size("dp")
    tensor_count = lax.axis_size("tensor")
    group_index = lax.axis_index("dp")
    tensor_index = lax.axis_index("tensor")
    tok_dev = token_ids.shape[0]
    tok_grp = tok_dev * tensor_count
    col_width = pos_table.shape[1]
    vocab_local = tok_table.shape[0]
    column_start = tensor_index * col_width
    anchors = pair_index.shape[0]
    id_rows = tok_dev // 128
    block = jnp.concatenate(
        [
            token_ids.reshape(id_rows, 128),
            slot_perm.reshape(id_rows, 128),
            jnp.pad(pair_index, (0, 128 - anchors))[None],
            jnp.zeros((16 - 2 * id_rows - 1, 128), jnp.int32),
        ],
        axis=0,
    )
    qkv_low = query_key_value_weight.astype(jnp.bfloat16).reshape(-1, 3 * col_width)
    out_low = out_weight.T.astype(jnp.bfloat16)
    up_low = up_weight.astype(jnp.bfloat16).reshape(qkv_low.shape[0], -1)
    down_low = down_weight.reshape(-1, down_weight.shape[2]).T.astype(jnp.bfloat16)
    gathered, qkv_half = exchange(1, GatherAll(block), SpreadLine(qkv_low))
    all_ids = gathered[:, :id_rows].reshape(-1)
    pairs = gathered[:: tensor_count, 2 * id_rows, :anchors].reshape(-1)
    own_perm = lax.dynamic_slice_in_dim(
        gathered, group_index * tensor_count, tensor_count, 0
    )[:, id_rows : 2 * id_rows].reshape(-1)
    slot, listed, counts_out = make_plan(own_perm, all_ids, CAPACITY, vocab_local, groups)
    slot = slot[0]
    list_rows = -(-CAPACITY // 128)
    top_count = jnp.max(counts_out)
    request = jnp.concatenate(
        [
            jnp.pad(
                listed.reshape(groups, CAPACITY), ((0, 0), (0, list_rows * 128 - CAPACITY))
            ).reshape(groups, list_rows, 128),
            jnp.broadcast_to(top_count, (groups, 8 - list_rows, 128)),
        ],
        axis=1,
    )
    asked = exchange(2, Swap(request, "dp"))
    overflow = jnp.max(asked[:, list_rows]) > CAPACITY
    offset = group_index * vocab_local
    asked_rows = asked[:, :list_rows].reshape(groups, -1)[:, :CAPACITY].reshape(-1) - offset
    asked_safe = jnp.clip(asked_rows, 0, vocab_local - 1)
    sent_rows = jnp.take(tok_table, asked_safe, axis=0).astype(jnp.bfloat16)
    got_rows, pos_full, out_half = exchange(
        3,
        Swap(sent_rows.reshape(groups, CAPACITY, col_width), "dp"),
        Spread(pos_table, columns=True, chunks=1),
        SpreadLine(out_low),
    )
    got_rows = got_rows.reshape(-1, col_width)
    chooser = (slot[:, None] == jnp.arange(groups * CAPACITY, dtype=jnp.int32)[None, :]).astype(
        jnp.bfloat16
    )
    lengths = seq_lengths[0]
    seq_ids, positions, member = seq_layout(lengths, tok_grp)
    bounds = block_bounds(lengths, tok_grp)

    def every_slot_id():
        every_perm = gathered[:, id_rows : 2 * id_rows].reshape(-1)
        return jnp.take(all_ids, every_perm, axis=0)

    def spread_wide():
        wanted = every_slot_id() - offset
        inside = (wanted >= 0) & (wanted < vocab_local)
        picked = jnp.take(
            tok_table.astype(jnp.bfloat16), jnp.clip(wanted, 0, vocab_local - 1), axis=0
        )
        return lax.psum_scatter(
            jnp.where(inside[:, None], picked, jnp.zeros((), jnp.bfloat16)),
            "dp",
            scatter_dimension=0,
            tiled=True,
        )

    tok_cols = lax.cond(
        overflow,
        spread_wide,
        lambda: multiply_arrays(chooser, got_rows).astype(jnp.bfloat16),
    )
    tok_all, qkv_full, out_full, up_half = exchange(
        4,
        Spread(tok_cols, columns=True),
        SpreadCross(qkv_half),
        SpreadCross(out_half),
        SpreadLine(up_low),
    )
    layer_mats = (qkv_full.reshape(D, -1), out_full.reshape(D, -1), up_half, down_low)
    embedded = embed(tok_all, pos_full, seq_ids, lengths, row_params)
    norm_third, saved_vals, layer_mats = layer_forward(
        embedded, seq_ids, bounds, row_params, col_bias, layer_mats
    )
    row_member = lax.dynamic_slice_in_dim(member, tensor_index * tok_dev, tok_dev, 0).astype(
        jnp.float32
    )
    counts = lengths.astype(jnp.float32)[:, None]
    pooled = exchange(9, SumAll(exact_multiply(row_member.T, norm_third) / counts, True))
    loss_out, pooled_low, vec_grad, pooled_grad = contrast_step(
        pooled.reshape(-1, D), head_weight, pairs
    )
    head_sum = exact_multiply(pooled_low.astype(jnp.float32).T, vec_grad)
    own_grad = lax.dynamic_slice_in_dim(pooled_grad, group_index * anchors, anchors, 0)
    grad_third = exact_multiply(row_member, own_grad / counts)
    emb_grad, halves, col_grad, row_grad = layer_backward(
        grad_third, seq_ids, bounds, row_params, layer_mats, saved_vals
    )
    qkv_half, out_half, up_sum, down_sum = halves
    cols_grad, qkv_sum, out_sum = exchange(
        14,
        Swap(
            emb_grad.astype(jnp.bfloat16)
            .reshape(tok_dev, tensor_count, col_width)
            .swapaxes(0, 1),
            "tensor",
        ),
        ReduceLine(qkv_half),
        ReduceLine(out_half),
    )
    cols_grad = cols_grad.reshape(tok_grp, col_width)
    pos_pick = (
        jnp.arange(pos_table.shape[0], dtype=jnp.int32)[:, None] == positions[None, :]
    ).astype(jnp.bfloat16)
    pos_grad = multiply_arrays(pos_pick, cols_grad)
    shared = jnp.concatenate([pos_grad, col_grad], axis=0)
    shared_rows = -(-shared.shape[0] // (16 * groups)) * 16
    shared = jnp.pad(shared, ((0, shared_rows * groups - shared.shape[0]), (0, 0)))
    merged = jnp.einsum("kn,kc->nc", chooser, cols_grad, preferred_element_type=jnp.float32)
    back_rows, shared_parts = exchange(
        15,
        Swap(merged.astype(jnp.bfloat16).reshape(groups, CAPACITY, col_width), "dp"),
        Swap(shared.astype(jnp.bfloat16).reshape(groups, shared_rows, col_width), "dp"),
    )
    shared_own = jnp.sum(shared_parts.astype(jnp.float32), axis=0)

    def add_wide():
        wanted = every_slot_id() - offset
        inside = (wanted >= 0) & (wanted < vocab_local)
        grad = (
            jnp.zeros(tok_table.shape, jnp.float32)
            .at[jnp.clip(wanted, 0, vocab_local - 1)]
            .add(
                jnp.where(
                    inside[:, None],
                    lax.all_gather(cols_grad, "dp", axis=0, tiled=True).astype(jnp.float32),
                    0.0,
                )
            )
        )
        return (grad, jnp.sum(grad * grad))

    tok_grad, tok_squares = lax.cond(
        overflow,
        add_wide,
        lambda: scatter_rows(asked_rows, back_rows.reshape(-1, col_width), vocab_local),
    )
    qkv_grad = qkv_sum.reshape(query_key_value_weight.shape)
    out_grad = out_sum.T
    up_grad = up_sum.reshape(up_weight.shape)
    down_grad = down_sum.T.reshape(down_weight.shape)
    local_squares = (
        tok_squares
        + jnp.sum(qkv_grad * qkv_grad)
        + jnp.sum(out_grad * out_grad)
        + jnp.sum(up_grad * up_grad)
        + jnp.sum(down_grad * down_grad)
        + jnp.sum(shared_own * shared_own)
    )
    row_block = jnp.concatenate(
        [row_grad, jnp.pad(local_squares.reshape(1, 1), ((0, 7), (0, D - 1)))], axis=0
    )
    row_total, shared_sum = exchange(16, SumAll(row_block, False), Gather(shared_own, "dp"))
    row_total = row_total[0]
    shared_sum = shared_sum.reshape(-1, col_width)
    pos_own = shared_sum[: pos_table.shape[0]]
    col_own = shared_sum[pos_table.shape[0] : pos_table.shape[0] + col_bias.shape[0]]
    row_sum = row_total[:8]
    squares = row_total[8, 0] + jnp.sum(row_sum * row_sum) + jnp.sum(head_sum * head_sum)
    grad_norm = jnp.sqrt(squares)
    clip_scale = jnp.minimum(1.0, CLIP_NORM / (grad_norm + 1e-06))
    tok_new = adam_step(
        tok_table, tok_first, tok_second, tok_grad * clip_scale, RATE_MATRIX, DECAY_RATE
    )
    pos_new = adam_step(
        pos_table, pos_first, pos_second, pos_own * clip_scale, RATE_MATRIX, DECAY_RATE
    )
    qkv_new = adam_step(
        query_key_value_weight,
        qkv_first,
        qkv_second,
        qkv_grad * clip_scale,
        RATE_MATRIX,
        DECAY_RATE,
    )
    out_new = adam_step(
        out_weight, out_first, out_second, out_grad * clip_scale, RATE_MATRIX, DECAY_RATE
    )
    up_new = adam_step(
        up_weight, up_first, up_second, up_grad * clip_scale, RATE_MATRIX, DECAY_RATE
    )
    down_new = adam_step(
        down_weight, down_first, down_second, down_grad * clip_scale, RATE_MATRIX, DECAY_RATE
    )
    head_new = adam_step(
        head_weight, head_first, head_second, head_sum * clip_scale, RATE_MATRIX, DECAY_RATE
    )
    col_new = adam_step(col_bias, col_first, col_second, col_own * clip_scale, RATE_VECTOR, 0.0)
    row_new = adam_step(row_params, row_first, row_second, row_sum * clip_scale, RATE_VECTOR, 0.0)
    return (loss_out[0, 0], grad_norm) + tok_new + pos_new + qkv_new + out_new + up_new + down_new + head_new + col_new + row_new


def solution(mesh):
    placed = (
        P(("dp", "tensor")),
        P(("dp", "tensor")),
        P("dp", None),
        P("dp"),
        P("dp", "tensor"),
        P("dp", "tensor"),
        P("dp", "tensor"),
        P(None, "tensor"),
        P(None, "tensor"),
        P(None, "tensor"),
        P("dp", None, "tensor"),
        P("dp", None, "tensor"),
        P("dp", None, "tensor"),
        P("tensor", "dp"),
        P("tensor", "dp"),
        P("tensor", "dp"),
        P("dp", None, "tensor"),
        P("dp", None, "tensor"),
        P("dp", None, "tensor"),
        P(None, "tensor", "dp"),
        P(None, "tensor", "dp"),
        P(None, "tensor", "dp"),
        P(),
        P(),
        P(),
        P(None, "tensor"),
        P(None, "tensor"),
        P(None, "tensor"),
        P(),
        P(),
        P(),
    )
    return jax.shard_map(
        body,
        mesh=mesh,
        in_specs=placed,
        out_specs=(
            P(),
            P(),
            P("dp", "tensor"),
            P("dp", "tensor"),
            P("dp", "tensor"),
            P(None, "tensor"),
            P(None, "tensor"),
            P(None, "tensor"),
            P("dp", None, "tensor"),
            P("dp", None, "tensor"),
            P("dp", None, "tensor"),
            P("tensor", "dp"),
            P("tensor", "dp"),
            P("tensor", "dp"),
            P("dp", None, "tensor"),
            P("dp", None, "tensor"),
            P("dp", None, "tensor"),
            P(None, "tensor", "dp"),
            P(None, "tensor", "dp"),
            P(None, "tensor", "dp"),
            P(),
            P(),
            P(),
            P(None, "tensor"),
            P(None, "tensor"),
            P(None, "tensor"),
            P(),
            P(),
            P(),
        ),
        check_vma=False,
    )
```

```python
from functools import partial

import jax
import jax.numpy as jnp
from jax import lax
from jax.experimental import pallas as pl
from jax.experimental.pallas import tpu as pltpu
from jax.sharding import PartitionSpec as P

D = 1024
HEAD = 64
MAXLEN = 512
STEP = 10


HIGHEST_MODE = lax.Precision.HIGHEST
LN_EPS = 1e-05
LOGIT_DIVISOR = 0.05
CLIP_NORM = 0.25
BETA_FIRST = 0.9
BETA_SECOND = 0.999
ADAM_EPS = 1e-08
RATE_MATRIX = 0.05
RATE_VECTOR = 0.5
DECAY_RATE = 0.01
MASK_FILL = -1e30


def multiply_arrays(left_mat, right_mat):
    return jnp.dot(left_mat, right_mat, preferred_element_type=jnp.float32)


def exact_multiply(left_mat, right_mat):
    return jnp.dot(left_mat, right_mat, precision=HIGHEST_MODE, preferred_element_type=jnp.float32)


def norm_rows(values, gain_row, bias_row):
    center = values - jnp.mean(values, axis=1, keepdims=True)
    inverse = lax.rsqrt(jnp.mean(center * center, axis=1, keepdims=True) + LN_EPS)
    return center * inverse * gain_row + bias_row


def seq_layout(lengths, slot_total):
    seq_ends = jnp.cumsum(lengths)
    starts = seq_ends - lengths
    slot_index = jnp.arange(slot_total, dtype=jnp.int32)
    member = (slot_index[:, None] >= starts[None, :]) & (slot_index[:, None] < seq_ends[None, :])
    seq_count = jnp.arange(lengths.shape[0], dtype=jnp.int32)
    seq_ids = jnp.sum(jnp.where(member, seq_count[None, :], 0), axis=1)
    positions = slot_index - jnp.sum(jnp.where(member, starts[None, :], 0), axis=1) + 2
    return (seq_ids, positions, member)


def adam_step(weight, first_old, second_old, clipped, step_rate, decay_rate):
    first_new = BETA_FIRST * first_old + (1.0 - BETA_FIRST) * clipped
    second_new = BETA_SECOND * second_old + (1.0 - BETA_SECOND) * clipped * clipped
    first_hat = first_new / (1.0 - BETA_FIRST**STEP)
    second_hat = second_new / (1.0 - BETA_SECOND**STEP)
    weight_new = weight - step_rate * (
        first_hat / (jnp.sqrt(second_hat) + ADAM_EPS) + decay_rate * weight
    )
    return (weight_new, first_new, second_new)


MESH_IDS = pl.DeviceIdType.MESH
VMEM_BYTES = 60 * 1024 * 1024
CHUNKS = 4
LINE = 4


def in_vmem():
    return pl.BlockSpec(memory_space=pltpu.VMEM)


def shaped(shape, dtype):
    return jax.ShapeDtypeStruct(tuple(shape), dtype)


def dma(*shape):
    return pltpu.SemaphoreType.DMA(shape)


def remote(src, dst, send_sem, recv_sem, target):
    return pltpu.make_async_remote_copy(
        src_ref=src,
        dst_ref=dst,
        send_sem=send_sem,
        recv_sem=recv_sem,
        device_id=target,
        device_id_type=MESH_IDS,
    )


def comm_params(collective):
    return pltpu.CompilerParams(
        collective_id=collective, has_side_effects=True, vmem_limit_bytes=VMEM_BYTES
    )


def exchange(collective, *tasks):
    def kernel(*refs):
        at = 0
        for attribute in ("ins", "outs", "scratch"):
            for task in tasks:
                size = len(getattr(task, attribute))
                setattr(task, attribute + "_refs", refs[at : at + size])
                at += size
        barrier = pltpu.get_barrier_semaphore()
        pl.semaphore_wait(barrier, sum(task.hello(barrier) for task in tasks))
        for task in tasks:
            task.begin()
        for task in tasks:
            task.middle()
        for task in tasks:
            task.end()

    results = pl.pallas_call(
        kernel,
        out_shape=[out for task in tasks for out in task.outs],
        in_specs=[in_vmem() for task in tasks for _ in task.ins],
        out_specs=[in_vmem() for task in tasks for _ in task.outs],
        scratch_shapes=[item for task in tasks for item in task.scratch],
        compiler_params=comm_params(collective),
    )(*[array for task in tasks for array in task.ins])
    return results[0] if len(results) == 1 else results


def tensor_place(width):
    me = lax.axis_index("tensor")
    core = lax.rem(me, 2)
    row = me // 2
    mate = me + 1 - 2 * core
    return (me, core, row, mate)


class Task:
    def hello(self, barrier):
        partners = self.partners()
        for partner in partners:
            pl.semaphore_signal(barrier, inc=1, device_id=partner, device_id_type=MESH_IDS)
        return len(partners)

    def begin(self):
        pass

    def middle(self):
        pass

    def end(self):
        pass


class Pair(Task):
    def __init__(self):
        self.width = lax.axis_size("tensor")
        self.rows = self.width // 2

    def partners(self):
        me, core, row, mate = tensor_place(self.width)
        return [{"tensor": mate}] + [
            {"tensor": lax.rem(row + step, self.rows) * 2 + core} for step in range(1, self.rows)
        ]


class Spread(Pair):
    def __init__(self, block, columns=False, chunks=CHUNKS):
        super().__init__()
        height, depth = block.shape
        self.columns, self.chunks = columns, chunks
        self.ins = (block,)
        whole = (height, self.width * depth) if columns else (self.width * height, depth)
        self.outs = (shaped(whole, block.dtype),)
        self.scratch = tuple(dma(self.rows, chunks) for _ in range(4))

    def window(self, owner, part=None):
        (x_ref,), (o_ref,) = self.ins_refs, self.outs_refs
        height, depth = x_ref.shape
        size = height // self.chunks
        if self.columns:
            lanes = pl.ds(pl.multiple_of(owner * depth, depth), depth)
            if part is None or self.chunks == 1:
                return o_ref.at[:, lanes]
            return o_ref.at[pl.ds(part * size, size), lanes]
        if part is None:
            return o_ref.at[pl.ds(pl.multiple_of(owner * height, height), height)]
        return o_ref.at[pl.ds(pl.multiple_of(owner * height + part * size, size), size)]

    def begin(self):
        (x_ref,) = self.ins_refs
        far_send, far_recv, near_send, near_recv = self.scratch_refs
        me, core, row, mate = tensor_place(self.width)
        size = x_ref.shape[0] // self.chunks
        self.far = {}
        for part in range(self.chunks):
            source = x_ref if self.chunks == 1 else x_ref.at[pl.ds(part * size, size)]
            for step in range(1, self.rows):
                copy = remote(
                    source,
                    self.window(me, part),
                    far_send.at[step, part],
                    far_recv.at[step, part],
                    {"tensor": lax.rem(row + step, self.rows) * 2 + core},
                )
                copy.start()
                self.far[step, part] = copy
        copy = remote(
            x_ref, self.window(me), near_send.at[0, 0], near_recv.at[0, 0], {"tensor": mate}
        )
        copy.start()
        self.near = [copy]
        self.window(me)[...] = x_ref[...]

    def middle(self):
        far_send, far_recv, near_send, near_recv = self.scratch_refs
        me, core, row, mate = tensor_place(self.width)
        for part in range(self.chunks):
            for step in range(1, self.rows):
                self.far[step, part].wait_recv()
                source = lax.rem(row + self.rows - step, self.rows) * 2 + core
                onward = remote(
                    self.window(source, part),
                    self.window(source, part),
                    near_send.at[step, part],
                    near_recv.at[step, part],
                    {"tensor": mate},
                )
                onward.start()
                self.near.append(onward)

    def end(self):
        for copy in self.near:
            copy.wait()
        for copy in self.far.values():
            copy.wait_send()


class Fold(Pair):
    def __init__(self, parts, chunks=CHUNKS):
        super().__init__()
        height, depth = parts.shape[0] // self.width, parts.shape[1]
        far_rows = max(self.rows - 1, 1)
        self.chunks, self.height, self.depth = chunks, height, depth
        self.parts = parts
        self.fold_scratch = (
            pltpu.VMEM((self.rows, height, depth), jnp.bfloat16),
            pltpu.VMEM((far_rows, height, depth), jnp.bfloat16),
            pltpu.VMEM((far_rows, height, depth), jnp.bfloat16),
            pltpu.VMEM((height, depth), jnp.float32),
        ) + tuple(dma(self.rows, chunks) for _ in range(4))

    def span(self, owner, part):
        size = self.height // self.chunks
        return pl.ds(pl.multiple_of(owner * self.height + part * size, size), size)

    def local(self, part):
        size = self.height // self.chunks
        return pl.ds(part * size, size)

    def begin(self):
        p_ref = self.ins_refs[0]
        near_buf, near_send, near_recv = self.scratch_refs[0], *self.scratch_refs[4:6]
        me, core, row, mate = tensor_place(self.width)
        self.near = {}
        for step in list(range(1, self.rows)) + [0]:
            dest_row = lax.rem(row + step, self.rows)
            for part in range(self.chunks):
                copy = remote(
                    p_ref.at[self.span(dest_row * 2 + 1 - core, part)],
                    near_buf.at[step, self.local(part)],
                    near_send.at[step, part],
                    near_recv.at[step, part],
                    {"tensor": mate},
                )
                copy.start()
                self.near[step, part] = copy

    def middle(self):
        p_ref = self.ins_refs[0]
        near_buf, sum_buf, far_buf, total_buf = self.scratch_refs[:4]
        far_send, far_recv = self.scratch_refs[6:8]
        me, core, row, mate = tensor_place(self.width)
        self.far = {}
        for step in range(1, self.rows):
            dest = lax.rem(row + step, self.rows) * 2 + core
            for part in range(self.chunks):
                local = self.local(part)
                self.near[step, part].wait_recv()
                sum_buf[step - 1, local] = (
                    p_ref[self.span(dest, part)].astype(jnp.float32)
                    + near_buf[step, local].astype(jnp.float32)
                ).astype(jnp.bfloat16)
                copy = remote(
                    sum_buf.at[step - 1, local],
                    far_buf.at[step - 1, local],
                    far_send.at[step - 1, part],
                    far_recv.at[step - 1, part],
                    {"tensor": dest},
                )
                copy.start()
                self.far[step, part] = copy
        for part in range(self.chunks):
            local = self.local(part)
            self.near[0, part].wait_recv()
            total_buf[local] = p_ref[self.span(me, part)].astype(jnp.float32) + near_buf[
                0, local
            ].astype(jnp.float32)

    def folded(self, part):
        far_buf, total_buf = self.scratch_refs[2:4]
        local = self.local(part)
        total = total_buf[local]
        for step in range(1, self.rows):
            self.far[step, part].wait_recv()
            total = total + far_buf[step - 1, local].astype(jnp.float32)
        return total

    def settle_fold(self):
        for copy in list(self.near.values()) + list(self.far.values()):
            copy.wait_send()


class Relay:
    def relay_scratch(self):
        return (pltpu.VMEM((self.height, self.depth), jnp.bfloat16),) + tuple(
            dma(self.rows, self.chunks) for _ in range(4)
        )

    def relay_open(self, part, low):
        buf, far_send, far_recv, near_send, near_recv = self.scratch_refs[-5:]
        all_ref = self.outs_refs[0]
        me, core, row, mate = tensor_place(self.width)
        local = self.local(part)
        buf[local] = low
        if part == 0:
            self.sent, self.relay_near = {}, []
        for step in range(1, self.rows):
            copy = remote(
                buf.at[local],
                all_ref.at[self.span(me, part)],
                far_send.at[step, part],
                far_recv.at[step, part],
                {"tensor": lax.rem(row + step, self.rows) * 2 + core},
            )
            copy.start()
            self.sent[step, part] = copy
        copy = remote(
            buf.at[local],
            all_ref.at[self.span(me, part)],
            near_send.at[0, part],
            near_recv.at[0, part],
            {"tensor": mate},
        )
        copy.start()
        self.relay_near.append(copy)
        all_ref[self.span(me, part)] = low

    def relay_close(self):
        buf, far_send, far_recv, near_send, near_recv = self.scratch_refs[-5:]
        all_ref = self.outs_refs[0]
        me, core, row, mate = tensor_place(self.width)
        for part in range(self.chunks):
            for step in range(1, self.rows):
                self.sent[step, part].wait_recv()
                source = lax.rem(row + self.rows - step, self.rows) * 2 + core
                window = all_ref.at[self.span(source, part)]
                copy = remote(
                    window, window, near_send.at[step, part], near_recv.at[step, part], {"tensor": mate}
                )
                copy.start()
                self.relay_near.append(copy)
        for copy in self.relay_near:
            copy.wait()
        for copy in self.sent.values():
            copy.wait_send()


def split_three(values):
    pieces, rest = [], values
    for _ in range(3):
        pieces.append(rest.astype(jnp.bfloat16))
        rest = rest - pieces[-1].astype(jnp.float32)
    return pieces


def norm_pull(values, gain, grads):
    center = values - jnp.mean(values, axis=1, keepdims=True)
    inverse = lax.rsqrt(jnp.mean(center * center, axis=1, keepdims=True) + LN_EPS)
    unit = center * inverse
    scaled = grads * gain
    pull = inverse * (
        scaled
        - jnp.mean(scaled, axis=1, keepdims=True)
        - unit * jnp.mean(scaled * unit, axis=1, keepdims=True)
    )
    return (
        pull,
        jnp.sum(grads * unit, axis=0, keepdims=True),
        jnp.sum(grads, axis=0, keepdims=True),
    )


class FoldNormSpread(Relay, Fold):
    def __init__(self, parts, residual, row_params):
        super().__init__(parts)
        own = shaped((self.height, self.depth), jnp.float32)
        self.ins = (parts, residual, row_params)
        self.outs = (shaped(parts.shape, jnp.bfloat16), own, own)
        self.scratch = self.fold_scratch + self.relay_scratch()

    def end(self):
        p_ref, residual_ref, row_ref = self.ins_refs
        all_ref, sum_ref, norm_ref = self.outs_refs
        for part in range(self.chunks):
            local = self.local(part)
            total = residual_ref[local] + self.folded(part) + row_ref[6:7]
            sum_ref[local] = total
            norm = norm_rows(total, row_ref[1:2], row_ref[4:5])
            norm_ref[local] = norm
            self.relay_open(part, norm.astype(jnp.bfloat16))
        self.relay_close()
        self.settle_fold()


class FoldPullSpread(Relay, Fold):
    def __init__(self, parts, residual, values, row_params):
        super().__init__(parts)
        own = shaped((self.height, self.depth), jnp.float32)
        self.ins = (parts, residual, values, row_params)
        self.outs = (shaped(parts.shape, jnp.bfloat16), own, shaped((8, self.depth), jnp.float32))
        self.scratch = self.fold_scratch + self.relay_scratch()

    def end(self):
        p_ref, residual_ref, value_ref, row_ref = self.ins_refs
        all_ref, grad_ref, side_ref = self.outs_refs
        side_ref[...] = jnp.zeros_like(side_ref)
        for part in range(self.chunks):
            local = self.local(part)
            pull, gain, shift = norm_pull(
                value_ref[local], row_ref[1:2], residual_ref[local] + self.folded(part)
            )
            grad_ref[local] = pull
            low = pull.astype(jnp.bfloat16)
            self.relay_open(part, low)
            side_ref[0:1] += gain
            side_ref[1:2] += shift
            side_ref[2:3] += jnp.sum(low.astype(jnp.float32), axis=0, keepdims=True)
        self.relay_close()
        self.settle_fold()


class PullSpread(Relay, Pair):
    def __init__(self, pooled_grad, counts, members, values, row_params):
        super().__init__()
        self.height, self.depth = values.shape
        self.chunks = CHUNKS
        own = shaped(values.shape, jnp.float32)
        self.ins = (pooled_grad, counts, members, values, row_params)
        self.outs = (
            shaped((self.width * self.height, self.depth), jnp.bfloat16),
            own,
            shaped((8, self.depth), jnp.float32),
        )
        self.scratch = self.relay_scratch()

    span, local = Fold.span, Fold.local

    def begin(self):
        pooled_ref, count_ref, member_ref, value_ref, row_ref = self.ins_refs
        all_ref, grad_ref, side_ref = self.outs_refs
        side_ref[...] = jnp.zeros_like(side_ref)
        anchors = count_ref.shape[0]
        rows = block_span(lax.axis_index("dp"), anchors)
        pieces = jnp.concatenate(split_three(pooled_ref[rows] / count_ref[...]), axis=0)
        for part in range(self.chunks):
            local = self.local(part)
            grads = multiply_arrays(member_ref[local], pieces)
            pull, gain, shift = norm_pull(value_ref[local], row_ref[2:3], grads)
            grad_ref[local] = pull
            low = pull.astype(jnp.bfloat16)
            self.relay_open(part, low)
            side_ref[0:1] += gain
            side_ref[1:2] += shift
            side_ref[2:3] += jnp.sum(low.astype(jnp.float32), axis=0, keepdims=True)

    def end(self):
        self.relay_close()


class Swap(Task):
    def __init__(self, blocks, axis):
        self.axis, self.count = axis, lax.axis_size(axis)
        self.ins = (blocks,)
        self.outs = (shaped(blocks.shape, blocks.dtype),)
        self.scratch = (dma(self.count), dma(self.count))

    def others(self):
        me = lax.axis_index(self.axis)
        return [lax.rem(me + step, self.count) for step in range(1, self.count)]

    def partners(self):
        return [{self.axis: other} for other in self.others()]

    def begin(self):
        (x_ref,), (o_ref,), (send, recv) = self.ins_refs, self.outs_refs, self.scratch_refs
        me = lax.axis_index(self.axis)
        self.copies = [
            remote(x_ref.at[other], o_ref.at[me], send.at[i], recv.at[i], {self.axis: other})
            for i, other in enumerate(self.others())
        ]
        for copy in self.copies:
            copy.start()
        o_ref[me] = x_ref[me]

    def end(self):
        for copy in self.copies:
            copy.wait()


class Gather(Swap):
    def __init__(self, block, axis):
        super().__init__(block, axis)
        self.outs = (shaped((self.count,) + block.shape, block.dtype),)

    def begin(self):
        (x_ref,), (o_ref,), (send, recv) = self.ins_refs, self.outs_refs, self.scratch_refs
        me = lax.axis_index(self.axis)
        self.copies = [
            remote(x_ref, o_ref.at[me], send.at[i], recv.at[i], {self.axis: other})
            for i, other in enumerate(self.others())
        ]
        for copy in self.copies:
            copy.start()
        o_ref[me] = x_ref[...]


class GatherAll(Task):
    def __init__(self, block):
        self.width = lax.axis_size("tensor")
        self.total = total = lax.axis_size("dp") * self.width
        self.ins = (block,)
        self.outs = (shaped((total,) + block.shape, block.dtype),)
        self.scratch = (dma(total), dma(total))

    def me(self):
        return lax.axis_index("dp") * self.width + lax.axis_index("tensor")

    def place(self, step):
        other = lax.rem(self.me() + step, self.total)
        return (other // self.width, lax.rem(other, self.width))

    def copy(self, step):
        (x_ref,), (o_ref,), (send, recv) = self.ins_refs, self.outs_refs, self.scratch_refs
        return remote(x_ref, o_ref.at[self.me()], send.at[step], recv.at[step], self.place(step))

    def hello(self, barrier):
        def one(step, carry):
            pl.semaphore_signal(
                barrier, inc=1, device_id=self.place(step), device_id_type=MESH_IDS
            )
            return carry

        lax.fori_loop(1, self.total, one, 0)
        return self.total - 1

    def begin(self):
        def one(step, carry):
            self.copy(step).start()
            return carry

        lax.fori_loop(1, self.total, one, 0)
        self.outs_refs[0][self.me()] = self.ins_refs[0][...]

    def end(self):
        def one(step, carry):
            self.copy(step).wait()
            return carry

        lax.fori_loop(1, self.total, one, 0)


class FoldPool(Fold):
    def __init__(self, parts, residual, members, counts, row_params):
        super().__init__(parts)
        anchors = members.shape[0]
        self.total = SumAll(shaped((anchors, self.depth), jnp.float32), True)
        self.ins = (parts, residual, members, counts, row_params)
        self.outs = (shaped((self.height, self.depth), jnp.float32),) + self.total.outs
        self.scratch = (
            self.fold_scratch
            + (pltpu.VMEM((anchors, self.depth), jnp.float32),)
            + self.total.scratch
        )

    def hello(self, barrier):
        return super().hello(barrier) + self.total.hello(barrier)

    def end(self):
        p_ref, residual_ref, member_ref, count_ref, row_ref = self.ins_refs
        sum_ref = self.outs_refs[0]
        at = len(self.fold_scratch)
        pooled = self.scratch_refs[at]
        size = self.height // self.chunks
        parts = []
        for part in range(self.chunks):
            local = self.local(part)
            total = residual_ref[local] + self.folded(part) + row_ref[7:8]
            sum_ref[local] = total
            norm = norm_rows(total, row_ref[2:3], row_ref[5:6])
            member = member_ref[:, part * size : (part + 1) * size]
            for piece in split_three(norm):
                parts.append(multiply_arrays(member, piece))
        pooled[...] = sum(parts[1:], parts[0]) / count_ref[...]
        total = self.total
        total.ins_refs, total.outs_refs = (pooled,), self.outs_refs[1:]
        total.scratch_refs = self.scratch_refs[at + 1 :]
        total.begin()
        total.middle()
        total.end()
        self.settle_fold()


class FoldPullSwap(Fold):
    def __init__(self, parts, residual, values, row_params):
        super().__init__(parts)
        self.narrow = self.depth // self.width
        self.ins = (parts, residual, values, row_params)
        self.outs = (
            shaped((self.width, self.height, self.narrow), jnp.bfloat16),
            shaped((8, self.depth), jnp.float32),
        )
        self.scratch = self.fold_scratch + (
            pltpu.VMEM((self.height, self.depth), jnp.bfloat16),
            dma(self.width, self.chunks),
            dma(self.width, self.chunks),
        )

    def partners(self):
        me = lax.axis_index("tensor")
        return [{"tensor": lax.rem(me + step, self.width)} for step in range(1, self.width)]

    def end(self):
        p_ref, residual_ref, value_ref, row_ref = self.ins_refs
        cols_ref, side_ref = self.outs_refs
        buf, send, recv = self.scratch_refs[-3:]
        side_ref[...] = jnp.zeros_like(side_ref)
        me = lax.axis_index("tensor")

        def lanes(owner):
            return pl.ds(pl.multiple_of(owner * self.narrow, self.narrow), self.narrow)

        copies = []
        for part in range(self.chunks):
            local = self.local(part)
            pull, gain, shift = norm_pull(
                value_ref[local], row_ref[0:1], residual_ref[local] + self.folded(part)
            )
            buf[local] = pull.astype(jnp.bfloat16)
            for step in range(1, self.width):
                other = lax.rem(me + step, self.width)
                copy = remote(
                    buf.at[local, lanes(other)],
                    cols_ref.at[me, local],
                    send.at[step, part],
                    recv.at[step, part],
                    {"tensor": other},
                )
                copy.start()
                copies.append(copy)
            cols_ref[me, local] = buf[local, lanes(me)]
            side_ref[0:1] += gain
            side_ref[1:2] += shift
        for copy in copies:
            copy.wait()
        self.settle_fold()


def eight_rows(values):
    return jnp.sum(values.reshape(values.shape[0] // 8, 8, values.shape[1]), axis=0)


class GridTask(Task):
    def __init__(self):
        self.cross = lax.axis_size("dp") // LINE

    def place(self):
        me = lax.axis_index("dp")
        return (me // self.cross, lax.rem(me, self.cross))


class ReduceCross(GridTask):
    def __init__(self, blocks):
        super().__init__()
        shape = blocks.shape[1:]
        self.blocks_shape = (LINE, self.cross) + shape
        self.ins = (blocks.reshape(self.blocks_shape),)
        self.outs = (shaped((LINE,) + shape, jnp.bfloat16),)
        others = max(self.cross - 1, 1)
        self.scratch = (
            pltpu.VMEM((others, LINE) + shape, jnp.bfloat16),
            dma(others, LINE),
            dma(others, LINE),
        )

    def targets(self):
        line, cross = self.place()
        return [lax.rem(cross + step, self.cross) for step in range(1, self.cross)]

    def partners(self):
        line, cross = self.place()
        return [{"dp": line * self.cross + other} for other in self.targets()]

    def begin(self):
        (x_ref,), (buf, send, recv) = self.ins_refs, self.scratch_refs
        line, cross = self.place()
        self.copies = []
        for i, other in enumerate(self.targets()):
            for z in range(LINE):
                copy = remote(
                    x_ref.at[z, other],
                    buf.at[i, z],
                    send.at[i, z],
                    recv.at[i, z],
                    {"dp": line * self.cross + other},
                )
                copy.start()
                self.copies.append(copy)

    def end(self):
        (x_ref,), (o_ref,), (buf, send, recv) = self.ins_refs, self.outs_refs, self.scratch_refs
        line, cross = self.place()
        for copy in self.copies:
            copy.wait()
        for z in range(LINE):
            total = x_ref[z, cross].astype(jnp.float32)
            for i in range(self.cross - 1):
                total = total + buf[i, z].astype(jnp.float32)
            o_ref[z] = total.astype(jnp.bfloat16)


class SpreadLine(GridTask):
    def __init__(self, block):
        super().__init__()
        self.ins = (block,)
        self.outs = (shaped((LINE,) + block.shape, block.dtype),)
        self.scratch = (dma(LINE - 1), dma(LINE - 1))

    def targets(self):
        line, cross = self.place()
        return [lax.rem(line + step, LINE) for step in range(1, LINE)]

    def partners(self):
        line, cross = self.place()
        return [{"dp": other * self.cross + cross} for other in self.targets()]

    def begin(self):
        (x_ref,), (o_ref,), (send, recv) = self.ins_refs, self.outs_refs, self.scratch_refs
        line, cross = self.place()
        self.copies = [
            remote(x_ref, o_ref.at[line], send.at[i], recv.at[i], partner)
            for i, partner in enumerate(self.partners())
        ]
        for copy in self.copies:
            copy.start()
        o_ref[line] = x_ref[...]

    def end(self):
        for copy in self.copies:
            copy.wait()


class Chain(Task):
    def __init__(self, first, second):
        self.first, self.second = first, second
        self.ins = first.ins
        self.outs = first.outs + second.outs
        self.scratch = first.scratch + second.scratch

    def hello(self, barrier):
        return self.first.hello(barrier) + self.second.hello(barrier)

    def begin(self):
        outs, scratch = len(self.first.outs), len(self.first.scratch)
        self.first.ins_refs, self.first.outs_refs = self.ins_refs, self.outs_refs[:outs]
        self.first.scratch_refs = self.scratch_refs[:scratch]
        self.second.ins_refs, self.second.outs_refs = self.outs_refs[:outs], self.outs_refs[outs:]
        self.second.scratch_refs = self.scratch_refs[scratch:]
        self.first.begin()

    def middle(self):
        self.first.end()
        self.second.begin()

    def end(self):
        self.second.end()


class Later(Task):
    def __init__(self, task):
        self.task = task
        self.ins, self.outs, self.scratch = task.ins, task.outs, task.scratch

    def hello(self, barrier):
        return self.task.hello(barrier)

    def middle(self):
        task = self.task
        task.ins_refs, task.outs_refs = self.ins_refs, self.outs_refs
        task.scratch_refs = self.scratch_refs
        task.begin()

    def end(self):
        self.task.end()


def reduce_grid(blocks):
    first = ReduceCross(blocks)
    return Chain(first, ReduceLine(first.outs[0]))


def spread_grid(block):
    first = SpreadLine(block)
    return Chain(first, SpreadCross(first.outs[0]))


class SpreadCross(GridTask):
    def __init__(self, blocks):
        super().__init__()
        self.ins = (blocks,)
        self.outs = (shaped((LINE, self.cross) + blocks.shape[1:], blocks.dtype),)
        others = max(self.cross - 1, 1)
        self.scratch = (dma(others, LINE), dma(others, LINE))

    def partners(self):
        line, cross = self.place()
        return [
            {"dp": line * self.cross + lax.rem(cross + step, self.cross)}
            for step in range(1, self.cross)
        ]

    def begin(self):
        (x_ref,), (o_ref,), (send, recv) = self.ins_refs, self.outs_refs, self.scratch_refs
        line, cross = self.place()
        self.copies = []
        for i, partner in enumerate(self.partners()):
            for z in range(LINE):
                copy = remote(x_ref.at[z], o_ref.at[z, cross], send.at[i, z], recv.at[i, z], partner)
                copy.start()
                self.copies.append(copy)
        for z in range(LINE):
            o_ref[z, cross] = x_ref[z]

    def end(self):
        for copy in self.copies:
            copy.wait()


class GatherGrid(GridTask):
    def __init__(self, block):
        super().__init__()
        self.ins = (block,)
        self.outs = (shaped((LINE, self.cross) + block.shape, block.dtype),)
        others = max(self.cross - 1, 1)
        self.scratch = (dma(LINE - 1), dma(LINE - 1), dma(others, LINE), dma(others, LINE))

    def lines(self):
        line, cross = self.place()
        return [
            {"dp": lax.rem(line + step, LINE) * self.cross + cross} for step in range(1, LINE)
        ]

    def crosses(self):
        line, cross = self.place()
        return [
            {"dp": line * self.cross + lax.rem(cross + step, self.cross)}
            for step in range(1, self.cross)
        ]

    def partners(self):
        return self.lines() + self.crosses()

    def begin(self):
        (x_ref,), (o_ref,), sems = self.ins_refs, self.outs_refs, self.scratch_refs
        line, cross = self.place()
        self.copies = [
            remote(x_ref, o_ref.at[line, cross], sems[0].at[i], sems[1].at[i], partner)
            for i, partner in enumerate(self.lines())
        ]
        for copy in self.copies:
            copy.start()
        o_ref[line, cross] = x_ref[...]

    def middle(self):
        (o_ref,), sems = self.outs_refs, self.scratch_refs
        line, cross = self.place()
        for copy in self.copies:
            copy.wait()
        self.copies = []
        for i, partner in enumerate(self.crosses()):
            for z in range(LINE):
                window = o_ref.at[z, cross]
                copy = remote(window, window, sems[2].at[i, z], sems[3].at[i, z], partner)
                copy.start()
                self.copies.append(copy)

    def end(self):
        for copy in self.copies:
            copy.wait()


class ReduceLine(GridTask):
    def __init__(self, blocks):
        super().__init__()
        shape = blocks.shape[1:]
        self.ins = (blocks,)
        self.outs = (shaped(shape, jnp.float32), shaped((8, shape[1]), jnp.float32))
        self.scratch = (pltpu.VMEM((LINE - 1,) + shape, jnp.bfloat16), dma(LINE - 1), dma(LINE - 1))

    def targets(self):
        line, cross = self.place()
        return [lax.rem(line + step, LINE) for step in range(1, LINE)]

    def partners(self):
        line, cross = self.place()
        return [{"dp": other * self.cross + cross} for other in self.targets()]

    def begin(self):
        (x_ref,), (buf, send, recv) = self.ins_refs, self.scratch_refs
        line, cross = self.place()
        self.copies = [
            remote(
                x_ref.at[other], buf.at[i], send.at[i], recv.at[i], {"dp": other * self.cross + cross}
            )
            for i, other in enumerate(self.targets())
        ]
        for copy in self.copies:
            copy.start()

    def end(self):
        (x_ref,), (o_ref, square_ref) = self.ins_refs, self.outs_refs
        buf = self.scratch_refs[0]
        line, cross = self.place()
        for copy in self.copies:
            copy.wait()
        total = x_ref[line].astype(jnp.float32)
        for i in range(LINE - 1):
            total = total + buf[i].astype(jnp.float32)
        o_ref[...] = total
        square_ref[...] = eight_rows(total * total)


class SumAll(Task):
    def __init__(self, block, keep):
        self.groups, self.width, self.keep = lax.axis_size("dp"), lax.axis_size("tensor"), keep
        rows, depth = block.shape
        self.narrow = narrow = depth // self.width
        kept = self.groups if keep else 1
        self.ins = (block,)
        self.outs = (shaped((kept, rows, depth), block.dtype),)
        near, far = dma(self.width), dma(self.groups)
        self.scratch = (
            pltpu.VMEM((self.width, rows, narrow), block.dtype),
            pltpu.VMEM((rows, narrow), block.dtype),
            pltpu.VMEM((self.groups, rows, narrow), block.dtype),
            pltpu.VMEM((kept, rows, narrow), block.dtype),
            near, near, far, far, near, near,
        )

    def mates(self):
        me = lax.axis_index("tensor")
        return [lax.rem(me + step, self.width) for step in range(1, self.width)]

    def peers(self):
        me = lax.axis_index("dp")
        return [lax.rem(me + step, self.groups) for step in range(1, self.groups)]

    def partners(self):
        return [{"tensor": mate} for mate in self.mates()] + [{"dp": peer} for peer in self.peers()]

    def lanes(self, owner):
        return pl.ds(pl.multiple_of(owner * self.narrow, self.narrow), self.narrow)

    def launch(self, copies):
        for copy in copies:
            copy.start()
        self.copies = copies

    def settle(self):
        for copy in self.copies:
            copy.wait()

    def begin(self):
        (x_ref,) = self.ins_refs
        part_buf, sems = self.scratch_refs[0], self.scratch_refs[4:]
        me = lax.axis_index("tensor")
        self.launch(
            [
                remote(
                    x_ref.at[:, self.lanes(mate)],
                    part_buf.at[me],
                    sems[0].at[i],
                    sems[1].at[i],
                    {"tensor": mate},
                )
                for i, mate in enumerate(self.mates())
            ]
        )
        part_buf[me] = x_ref[:, self.lanes(me)]

    def middle(self):
        (o_ref,) = self.outs_refs
        part_buf, sum_buf, all_buf, out_buf = self.scratch_refs[:4]
        sems = self.scratch_refs[4:]
        dp_me, me = lax.axis_index("dp"), lax.axis_index("tensor")
        self.settle()
        sum_buf[...] = jnp.sum(part_buf[...], axis=0)
        self.launch(
            [
                remote(sum_buf, all_buf.at[dp_me], sems[2].at[i], sems[3].at[i], {"dp": peer})
                for i, peer in enumerate(self.peers())
            ]
        )
        all_buf[dp_me] = sum_buf[...]
        self.settle()
        if self.keep:
            out_buf[...] = all_buf[...]
        else:
            out_buf[0] = jnp.sum(all_buf[...], axis=0)
        self.launch(
            [
                remote(
                    out_buf,
                    o_ref.at[:, :, self.lanes(me)],
                    sems[4].at[i],
                    sems[5].at[i],
                    {"tensor": mate},
                )
                for i, mate in enumerate(self.mates())
            ]
        )
        o_ref[:, :, self.lanes(me)] = out_buf[...]

    def end(self):
        self.settle()


Q_BLOCK = 256
K_BLOCK = 256


def split_pair(wide):
    half = wide.shape[0] // 2
    upper = lax.broadcasted_iota(jnp.int32, wide.shape, 0) < half
    zero = jnp.zeros_like(wide)
    return jnp.concatenate([jnp.where(upper, wide, zero), jnp.where(upper, zero, wide)], axis=1)


def stack_pair(tall):
    half = tall.shape[1] // 2
    left = lax.broadcasted_iota(jnp.int32, tall.shape, 1) < half
    zero = jnp.zeros_like(tall)
    return jnp.concatenate([jnp.where(left, tall, zero), jnp.where(left, zero, tall)], axis=0)


def join_pair(wide):
    depth, columns = wide.shape
    upper = lax.broadcasted_iota(jnp.int32, (depth, columns // 2), 0) < depth // 2
    return jnp.where(upper, wide[:, : columns // 2], wide[:, columns // 2 :])


def turn(tile):
    return tile.astype(jnp.float32).T.astype(jnp.bfloat16)


def block_span(index, size):
    return pl.ds(pl.multiple_of(index * size, size), size)


def attend_kernel(low_ref, high_ref, qkv_ref, seq_col_ref, seq_row_ref, out_ref, log_ref, value_turned, scores):
    slots, columns = out_ref.shape
    pairs = columns // 128
    q_blocks, k_blocks = slots // Q_BLOCK, slots // K_BLOCK

    def turn_values(b, carry):
        rows = block_span(b, K_BLOCK)
        for pair in range(pairs):
            value_turned[pl.ds(pair * 128, 128), rows] = turn(
                qkv_ref[rows, pl.ds(2 * columns + pair * 128, 128)]
            )
        return carry

    lax.fori_loop(0, k_blocks, turn_values, 0)

    def one_block(q_index, carry):
        q_rows = block_span(q_index, Q_BLOCK)
        lowest, highest = low_ref[q_index], high_ref[q_index]
        seq_row = seq_row_ref[0:1, q_rows]
        seq_pair = jnp.concatenate([seq_row, seq_row], axis=1)
        queries = [
            split_pair(
                (qkv_ref[q_rows, pl.ds(pair * 128, 128)].astype(jnp.float32) * HEAD ** (-0.5))
                .T.astype(jnp.bfloat16)
            )
            for pair in range(pairs)
        ]

        def score(k_index, tops):
            k_rows = block_span(k_index, K_BLOCK)
            same = seq_col_ref[k_rows, 0:1] == seq_pair
            later = []
            for pair in range(pairs):
                keys = qkv_ref[k_rows, pl.ds(columns + pair * 128, 128)]
                value = jnp.where(same, multiply_arrays(keys, queries[pair]), MASK_FILL)
                scores[pair, k_index - lowest] = value
                later.append(jnp.maximum(tops[pair], jnp.max(value, axis=0, keepdims=True)))
            return tuple(later)

        start = tuple(jnp.full((1, 2 * Q_BLOCK), MASK_FILL, jnp.float32) for _ in range(pairs))
        tops = lax.fori_loop(lowest, highest, score, start)

        def mix(k_index, state):
            k_rows = block_span(k_index, K_BLOCK)
            later = []
            for pair in range(pairs):
                total, mixed = state[pair]
                weights = jnp.exp(scores[pair, k_index - lowest] - tops[pair])
                total = total + jnp.sum(weights, axis=0, keepdims=True)
                mixed = mixed + multiply_arrays(
                    value_turned[pl.ds(pair * 128, 128), k_rows], weights.astype(jnp.bfloat16)
                )
                later.append((total, mixed))
            return tuple(later)

        blank = tuple(
            (jnp.zeros((1, 2 * Q_BLOCK), jnp.float32), jnp.zeros((128, 2 * Q_BLOCK), jnp.float32))
            for _ in range(pairs)
        )
        final = lax.fori_loop(lowest, highest, mix, blank)
        for pair in range(pairs):
            total, mixed = final[pair]
            out_ref[q_rows, pl.ds(pair * 128, 128)] = join_pair(mixed / total).T.astype(jnp.bfloat16)
            logs = tops[pair] + jnp.log(total)
            log_ref[pl.ds(2 * pair, 1), q_rows] = logs[:, :Q_BLOCK]
            log_ref[pl.ds(2 * pair + 1, 1), q_rows] = logs[:, Q_BLOCK:]
        return carry

    lax.fori_loop(0, q_blocks, one_block, 0)


def block_bounds(lengths, slots):
    ends = jnp.cumsum(lengths)
    starts = ends - lengths
    first = jnp.arange(slots // Q_BLOCK, dtype=jnp.int32) * Q_BLOCK
    last = first + Q_BLOCK - 1
    lowest = jnp.max(
        jnp.where(starts[None, :] <= first[:, None], starts[None, :], 0), axis=1
    )
    highest = jnp.min(jnp.where(ends[None, :] > last[:, None], ends[None, :], slots), axis=1)
    return (lowest // K_BLOCK, (highest + K_BLOCK - 1) // K_BLOCK)


REACH = (2 * MAXLEN - 2) // K_BLOCK + Q_BLOCK // K_BLOCK + 1


def in_scalars():
    return pl.BlockSpec(memory_space=pltpu.SMEM)


def attend(qkv_out, seq_ids, bounds):
    slots, columns = qkv_out.shape[0], qkv_out.shape[1] // 3
    pairs = columns // 128
    return pl.pallas_call(
        attend_kernel,
        out_shape=[
            jax.ShapeDtypeStruct((slots, columns), jnp.bfloat16),
            jax.ShapeDtypeStruct((8, slots), jnp.float32),
        ],
        in_specs=[in_scalars(), in_scalars()] + [in_vmem()] * 3,
        out_specs=[in_vmem()] * 2,
        scratch_shapes=[
            pltpu.VMEM((columns, slots), jnp.bfloat16),
            pltpu.VMEM((pairs, REACH, K_BLOCK, 2 * Q_BLOCK), jnp.float32),
        ],
        compiler_params=pltpu.CompilerParams(vmem_limit_bytes=VMEM_BYTES),
    )(bounds[0], bounds[1], qkv_out, seq_ids[:, None], jnp.broadcast_to(seq_ids[None], (8, slots)))


def attend_back_kernel(
    low_ref, high_ref, qkv_ref, grad_ref, log_ref, seq_col_ref, seq_row_ref, out_ref,
    key_turned, probs, prob_grads, key_sum, value_sum,
):
    slots, columns = grad_ref.shape
    pairs = columns // 128
    q_blocks, k_blocks = slots // Q_BLOCK, slots // K_BLOCK

    def turn_keys(b, carry):
        rows = block_span(b, K_BLOCK)
        for pair in range(pairs):
            key_turned[pl.ds(pair * 128, 128), rows] = turn(
                qkv_ref[rows, pl.ds(columns + pair * 128, 128)]
            )
        key_sum[rows] = jnp.zeros((K_BLOCK, columns), jnp.float32)
        value_sum[rows] = jnp.zeros((K_BLOCK, columns), jnp.float32)
        return carry

    lax.fori_loop(0, k_blocks, turn_keys, 0)

    def one_block(q_index, carry):
        q_rows = block_span(q_index, Q_BLOCK)
        lowest, highest = low_ref[q_index], high_ref[q_index]
        seq_row = seq_row_ref[0:1, q_rows]
        seq_pair = jnp.concatenate([seq_row, seq_row], axis=1)
        scaled, queries, grads, turned, logs = [], [], [], [], []
        for pair in range(pairs):
            plain = qkv_ref[q_rows, pl.ds(pair * 128, 128)].astype(jnp.float32) * HEAD ** (-0.5)
            scaled.append(stack_pair(plain.astype(jnp.bfloat16)))
            queries.append(split_pair(plain.T.astype(jnp.bfloat16)))
            grad = grad_ref[q_rows, pl.ds(pair * 128, 128)]
            grads.append(stack_pair(grad))
            turned.append(split_pair(turn(grad)))
            logs.append(
                jnp.concatenate(
                    [log_ref[pl.ds(2 * pair, 1), q_rows], log_ref[pl.ds(2 * pair + 1, 1), q_rows]],
                    axis=1,
                )
            )

        def look(k_index, inners):
            k_rows = block_span(k_index, K_BLOCK)
            same = seq_col_ref[k_rows, 0:1] == seq_pair
            later = []
            for pair in range(pairs):
                keys = qkv_ref[k_rows, pl.ds(columns + pair * 128, 128)]
                values = qkv_ref[k_rows, pl.ds(2 * columns + pair * 128, 128)]
                logits = jnp.where(same, multiply_arrays(keys, queries[pair]), MASK_FILL)
                weights = jnp.exp(logits - logs[pair])
                weight_grad = multiply_arrays(values, turned[pair])
                probs[pair, k_index - lowest] = weights
                prob_grads[pair, k_index - lowest] = weight_grad
                value_sum[k_rows, pl.ds(pair * 128, 128)] += multiply_arrays(
                    weights.astype(jnp.bfloat16), grads[pair]
                )
                later.append(
                    inners[pair] + jnp.sum(weights * weight_grad, axis=0, keepdims=True)
                )
            return tuple(later)

        start = tuple(jnp.zeros((1, 2 * Q_BLOCK), jnp.float32) for _ in range(pairs))
        inners = lax.fori_loop(lowest, highest, look, start)

        def push(k_index, sums):
            k_rows = block_span(k_index, K_BLOCK)
            later = []
            for pair in range(pairs):
                slope = (
                    probs[pair, k_index - lowest]
                    * (prob_grads[pair, k_index - lowest] - inners[pair])
                ).astype(jnp.bfloat16)
                key_sum[k_rows, pl.ds(pair * 128, 128)] += multiply_arrays(slope, scaled[pair])
                later.append(
                    sums[pair] + multiply_arrays(key_turned[pl.ds(pair * 128, 128), k_rows], slope)
                )
            return tuple(later)

        blank = tuple(jnp.zeros((128, 2 * Q_BLOCK), jnp.float32) for _ in range(pairs))
        sums = lax.fori_loop(lowest, highest, push, blank)
        for pair in range(pairs):
            out_ref[q_rows, pl.ds(pair * 128, 128)] = (
                (join_pair(sums[pair]) * HEAD ** (-0.5)).T.astype(jnp.bfloat16)
            )
        return carry

    lax.fori_loop(0, q_blocks, one_block, 0)
    out_ref[:, columns : 2 * columns] = key_sum[...].astype(jnp.bfloat16)
    out_ref[:, 2 * columns :] = value_sum[...].astype(jnp.bfloat16)


def attend_back(qkv_out, attn_grad, log_total, seq_ids, bounds):
    slots, columns = attn_grad.shape
    pairs = columns // 128
    window = pltpu.VMEM((pairs, REACH, K_BLOCK, 2 * Q_BLOCK), jnp.float32)
    return pl.pallas_call(
        attend_back_kernel,
        out_shape=jax.ShapeDtypeStruct(qkv_out.shape, jnp.bfloat16),
        in_specs=[in_scalars(), in_scalars()] + [in_vmem()] * 5,
        out_specs=in_vmem(),
        scratch_shapes=[
            pltpu.VMEM((columns, slots), jnp.bfloat16),
            window,
            window,
            pltpu.VMEM((slots, columns), jnp.float32),
            pltpu.VMEM((slots, columns), jnp.float32),
        ],
        compiler_params=pltpu.CompilerParams(vmem_limit_bytes=VMEM_BYTES),
    )(
        bounds[0],
        bounds[1],
        qkv_out,
        attn_grad,
        log_total,
        seq_ids[:, None],
        jnp.broadcast_to(seq_ids[None], (8, slots)),
    )


def gelu_parts(upper):
    distance = jnp.abs(upper) * 0.7071067811865476
    step = 1.0 / (1.0 + 0.3275911 * distance)
    bell = jnp.exp(-distance * distance)
    series = step * (
        0.254829592
        + step * (-0.284496736 + step * (1.421413741 + step * (-1.453152027 + step * 1.061405429)))
    )
    tail = 0.5 * series * bell
    share = jnp.where(upper >= 0.0, 1.0 - tail, tail)
    return (upper * share, share + upper * (bell * 0.3989422804014327))


def expand_kernel(rows_ref, weight_ref, bias_ref, hidden_ref, slope_ref):
    units = weight_ref.shape[1]
    rows = rows_ref[...]
    for first in range(0, units, 256):
        lanes = pl.ds(first, 256)
        upper = multiply_arrays(rows, weight_ref[:, lanes]) + bias_ref[:, lanes]
        hidden, slope = gelu_parts(upper)
        hidden_ref[:, lanes] = hidden.astype(jnp.bfloat16)
        slope_ref[:, lanes] = slope


def expand(rows, weight, bias):
    slots, depth = rows.shape
    units = weight.shape[1]
    tall = 256
    return pl.pallas_call(
        expand_kernel,
        grid=(slots // tall,),
        out_shape=[shaped((slots, units), jnp.bfloat16), shaped((slots, units), jnp.float32)],
        in_specs=[
            pl.BlockSpec((tall, depth), lambda i: (i, 0)),
            pl.BlockSpec((depth, units), lambda i: (0, 0)),
            pl.BlockSpec((1, units), lambda i: (0, 0)),
        ],
        out_specs=[
            pl.BlockSpec((tall, units), lambda i: (i, 0)),
            pl.BlockSpec((tall, units), lambda i: (i, 0)),
        ],
        compiler_params=pltpu.CompilerParams(vmem_limit_bytes=VMEM_BYTES),
    )(rows, weight, bias)


EMBED_ROWS = 128
EMBED_PART = 16
MARGIN = 256


def embed_kernel(
    start_ref, span_ref, own_ref, tok_ref, pos_ref, seq_ref, row_ref, low_ref, emb_ref, norm_ref,
    padded, placed, normed,
):
    slots = tok_ref.shape[0]
    blocks, own_blocks = slots // EMBED_ROWS, emb_ref.shape[0] // EMBED_ROWS
    padded[pl.ds(MARGIN, pos_ref.shape[0])] = pos_ref[...]
    gain, shift = row_ref[0:1], row_ref[3:4]

    def one_block(b, carry):
        rows = block_span(b, EMBED_ROWS)
        seq = seq_ref[rows, 0:1]

        def pick(s, state):
            first = MARGIN + 2 + b * EMBED_ROWS - start_ref[s]
            base = first // 8
            shift = EMBED_PART + 8 - (first - base * 8)
            for at in range(0, EMBED_ROWS, EMBED_PART):
                window = padded[pl.ds(pl.multiple_of(base * 8 + at, 8), EMBED_PART + 8)]
                window = pltpu.roll(window, shift, 0)[:EMBED_PART]
                local = pl.ds(at, EMBED_PART)
                placed[local] = jnp.where(seq[at : at + EMBED_PART] == s, window, placed[local])
            return state

        lax.fori_loop(span_ref[0, b], span_ref[1, b], pick, 0)
        own = b - own_ref[0] * own_blocks
        kept = (own >= 0) & (own < own_blocks)
        own_first = jnp.where(kept, own, 0) * EMBED_ROWS
        for at in range(0, EMBED_ROWS, EMBED_PART):
            local = pl.ds(pl.multiple_of(b * EMBED_ROWS + at, EMBED_PART), EMBED_PART)
            emb = tok_ref[local].astype(jnp.float32) + placed[pl.ds(at, EMBED_PART)]
            norm = norm_rows(emb, gain, shift)
            low_ref[local] = norm.astype(jnp.bfloat16)
            placed[pl.ds(at, EMBED_PART)] = emb
            normed[pl.ds(at, EMBED_PART)] = norm

        @pl.when(kept)
        def _():
            own_rows = pl.ds(pl.multiple_of(own_first, EMBED_ROWS), EMBED_ROWS)
            emb_ref[own_rows] = placed[...]
            norm_ref[own_rows] = normed[...]

        return carry

    lax.fori_loop(0, blocks, one_block, 0)


def embed(tok_all, pos_full, seq_ids, lengths, row_params):
    slots, depth = tok_all.shape
    own = slots // lax.axis_size("tensor")
    ends = jnp.cumsum(lengths)
    starts = ends - lengths
    first = jnp.arange(slots // EMBED_ROWS, dtype=jnp.int32) * EMBED_ROWS
    spans = jnp.stack(
        [
            jnp.sum((ends[None, :] <= first[:, None]).astype(jnp.int32), axis=1),
            jnp.sum((starts[None, :] < first[:, None] + EMBED_ROWS).astype(jnp.int32), axis=1),
        ]
    )
    return pl.pallas_call(
        embed_kernel,
        out_shape=[
            shaped((slots, depth), jnp.bfloat16),
            shaped((own, depth), jnp.float32),
            shaped((own, depth), jnp.float32),
        ],
        in_specs=[in_scalars()] * 3 + [in_vmem()] * 4,
        out_specs=[in_vmem()] * 3,
        scratch_shapes=[
            pltpu.VMEM((MARGIN + MAXLEN + EMBED_ROWS + 24, depth), jnp.float32),
            pltpu.VMEM((EMBED_ROWS, depth), jnp.float32),
            pltpu.VMEM((EMBED_ROWS, depth), jnp.float32),
        ],
        compiler_params=pltpu.CompilerParams(vmem_limit_bytes=VMEM_BYTES),
    )(
        starts,
        spans,
        lax.axis_index("tensor").astype(jnp.int32)[None],
        tok_all,
        pos_full,
        seq_ids[:, None],
        row_params,
    )


SCATTER_ROWS = 512


def scatter_kernel(index_ref, rows_ref, grad_ref, square_ref):
    first = pl.program_id(0) * SCATTER_ROWS
    slots = index_ref.shape[1]
    here = (
        lax.broadcasted_iota(jnp.int32, (SCATTER_ROWS, slots), 0) + first == index_ref[...]
    ).astype(jnp.float32)
    grad = multiply_arrays(here.astype(jnp.bfloat16), rows_ref[...])
    grad_ref[...] = grad

    @pl.when(pl.program_id(0) == 0)
    def _():
        square_ref[...] = jnp.zeros_like(square_ref)

    square_ref[...] += eight_rows(grad * grad)


def scatter_rows(index, rows, height):
    slots, width = rows.shape
    return pl.pallas_call(
        scatter_kernel,
        grid=(pl.cdiv(height, SCATTER_ROWS),),
        out_shape=[shaped((height, width), jnp.float32), shaped((8, width), jnp.float32)],
        in_specs=[
            pl.BlockSpec((1, slots), lambda i: (0, 0)),
            pl.BlockSpec((slots, width), lambda i: (0, 0)),
        ],
        out_specs=[
            pl.BlockSpec((SCATTER_ROWS, width), lambda i: (i, 0)),
            pl.BlockSpec((8, width), lambda i: (0, 0)),
        ],
        compiler_params=pltpu.CompilerParams(vmem_limit_bytes=VMEM_BYTES),
    )(index[None], rows)


def layer_forward(embedded, seq_ids, bounds, members, counts, row_params, col_local, layer_mats):
    first_moment_all, emb_rows, norm_first = embedded
    qkv_full, out_full, up_half, down_low = layer_mats
    col_width = col_local.shape[1]
    qkv_bias = jnp.concatenate([col_local[0], jnp.zeros_like(col_local[0]), col_local[1]])
    qkv_out = (multiply_arrays(first_moment_all, qkv_full) + qkv_bias).astype(jnp.bfloat16)
    attn_low, log_total = attend(qkv_out, seq_ids, bounds)
    first_back = jnp.einsum("tc,dc->td", attn_low, out_full, preferred_element_type=jnp.float32)
    second_all, first_sum, norm_second, up_full, _, down_full = exchange(
        5,
        FoldNormSpread(first_back.astype(jnp.bfloat16), norm_first, row_params),
        SpreadCross(up_half),
        spread_grid(down_low),
    )
    up_full = up_full.reshape(D, -1)
    down_full = down_full.reshape(D, -1)
    hidden_low, slope = expand(second_all, up_full, col_local[2:].reshape(1, -1))
    second_back = jnp.einsum("tf,df->td", hidden_low, down_full, preferred_element_type=jnp.float32)
    second_sum, pooled = exchange(
        7, FoldPool(second_back.astype(jnp.bfloat16), norm_second, members, counts, row_params)
    )
    saved_vals = (
        emb_rows,
        first_moment_all,
        qkv_out,
        log_total,
        attn_low,
        first_sum,
        second_all,
        slope,
        hidden_low,
        second_sum,
    )
    return (pooled, saved_vals, (qkv_full, out_full, up_full, down_full))


def turned_grad(left_all, right_all):
    grad = jnp.einsum("td,tc->dc", left_all, right_all, preferred_element_type=jnp.float32)
    groups = lax.axis_size("dp")
    return grad.astype(jnp.bfloat16).reshape(groups, grad.shape[0] // groups, grad.shape[1])


def layer_backward(pooled_grad, counts, members, seq_ids, bounds, row_params, layer_mats, saved_vals):
    qkv_full, out_full, up_full, down_full = layer_mats
    (
        emb_rows,
        first_moment_all,
        qkv_out,
        log_total,
        attn_low,
        first_sum,
        second_all,
        slope,
        hidden_low,
        second_sum,
    ) = saved_vals
    col_width = out_full.shape[1]
    mixed_all, grad_second, side_c = exchange(
        10, PullSpread(pooled_grad, counts, jnp.tile(members.T, (1, 3)), second_sum, row_params)
    )
    down_grad = turned_grad(mixed_all, hidden_low)
    up_low = (multiply_arrays(mixed_all, down_full) * slope).astype(jnp.bfloat16)
    up_grad = turned_grad(second_all, up_low)
    second_back = jnp.einsum(
        "tf,df->td", up_low, up_full, preferred_element_type=jnp.float32
    ).astype(jnp.bfloat16)
    branch_all, grad_first, side_b, _, down_sum, down_squares, up_half = exchange(
        11,
        FoldPullSpread(second_back, grad_second, first_sum, row_params),
        reduce_grid(down_grad),
        Later(ReduceCross(up_grad)),
    )
    out_grad = turned_grad(branch_all, attn_low)
    attn_grad = multiply_arrays(branch_all, out_full).astype(jnp.bfloat16)
    qkv_low = attend_back(qkv_out, attn_grad, log_total, seq_ids, bounds)
    qkv_grad = turned_grad(first_moment_all, qkv_low)
    first_back = jnp.einsum(
        "tc,dc->td", qkv_low, qkv_full, preferred_element_type=jnp.float32
    ).astype(jnp.bfloat16)
    cols_grad, side_a, up_sum, up_squares, _, out_sum, out_squares, _, qkv_sum, qkv_squares = exchange(
        13,
        FoldPullSwap(first_back, grad_first, emb_rows, row_params),
        ReduceLine(up_half),
        reduce_grid(out_grad),
        reduce_grid(qkv_grad),
    )
    qkv_cols = jnp.sum(qkv_low.astype(jnp.float32), axis=0).reshape(3, col_width)
    up_cols = jnp.sum(up_low.astype(jnp.float32), axis=0).reshape(-1, col_width)
    col_grad = jnp.concatenate([qkv_cols[0:1], qkv_cols[2:3], up_cols], axis=0)
    row_grad = jnp.concatenate(
        [
            side_a[0:1],
            side_b[0:1],
            side_c[0:1],
            side_a[1:2],
            side_b[1:2],
            side_c[1:2],
            side_b[2:3],
            side_c[2:3],
        ]
    )
    return (
        cols_grad,
        (qkv_sum, out_sum, up_sum, down_sum),
        (qkv_squares, out_squares, up_squares + down_squares),
        col_grad,
        row_grad,
    )


def plan_kernel(capacity, vocab_local, groups, perm_ref, low_ref, high_ref, slot_ref, ask_ref, id_buf, own_buf):
    slots = perm_ref.shape[1]
    table_rows = low_ref.shape[1]
    block = 128
    blocks = slots // block
    perm = perm_ref[...]
    high_part = perm // 128
    low_part = perm - high_part * 128
    chooser = (lax.broadcasted_iota(jnp.int32, (table_rows, slots), 0) == high_part).astype(
        jnp.float32
    ).astype(jnp.bfloat16)
    value = multiply_arrays(low_ref[...], chooser) + 256.0 * multiply_arrays(high_ref[...], chooser)
    lane_match = lax.broadcasted_iota(jnp.int32, (128, slots), 0) == low_part
    ids = jnp.sum(jnp.where(lane_match, value, 0.0), axis=0, keepdims=True)
    for b in range(blocks):
        id_buf[pl.ds(b * block, block), :] = jnp.broadcast_to(
            ids[:, b * block : (b + 1) * block], (block, block)
        ).T
    place = lax.broadcasted_iota(jnp.int32, (1, slots), 1).astype(jnp.float32)
    rows = lax.broadcasted_iota(jnp.int32, (block, 1), 0).astype(jnp.float32)

    def earliest(b, best):
        column = id_buf[pl.ds(pl.multiple_of(b * block, block), block), 0:1]
        index = rows + (b * block).astype(jnp.float32)
        found = jnp.where(column == ids, index, 1e9)
        return jnp.minimum(best, jnp.min(found, axis=0, keepdims=True))

    least = lax.fori_loop(0, blocks, earliest, jnp.full((1, slots), 1e9, jnp.float32))
    first = least == place
    owner = jnp.zeros((1, slots), jnp.float32)
    for index in range(1, groups):
        owner = owner + jnp.where(ids >= float(index * vocab_local), 1.0, 0.0)
    owner_rows = lax.broadcasted_iota(jnp.int32, (groups, slots), 0).astype(jnp.float32)
    marks = jnp.where(first & (owner == owner_rows), 1.0, 0.0)
    upper = jnp.where(
        lax.broadcasted_iota(jnp.int32, (block, block), 0)
        < lax.broadcasted_iota(jnp.int32, (block, block), 1),
        1.0,
        0.0,
    ).astype(jnp.bfloat16)
    running = jnp.zeros((groups, 1), jnp.float32)
    pieces = []
    for b in range(blocks):
        part = marks[:, b * block : (b + 1) * block]
        pieces.append(multiply_arrays(part.astype(jnp.bfloat16), upper) + running)
        running = running + jnp.sum(part, axis=1, keepdims=True)
    before = jnp.concatenate(pieces, axis=1)
    rank = jnp.sum(marks * before, axis=0, keepdims=True)
    own_slot = jnp.where(first & (rank < float(capacity)), owner * float(capacity) + rank, -1.0)
    for b in range(blocks):
        own_buf[pl.ds(b * block, block), :] = jnp.broadcast_to(
            own_slot[:, b * block : (b + 1) * block], (block, block)
        ).T
    list_rows = -(-capacity // 128)
    stride = list_rows * 128
    width = groups * stride
    index = lax.broadcasted_iota(jnp.int32, (1, width), 1)
    target = (index // stride * capacity + lax.rem(index, stride)).astype(jnp.float32)
    target = jnp.where(lax.rem(index, stride) < capacity, target, -2.0)

    def settle(b, carry):
        slot, listed = carry
        window = pl.ds(pl.multiple_of(b * block, block), block)
        column, slot_column = id_buf[window, 0:1], own_buf[window, 0:1]
        slot = jnp.maximum(
            slot, jnp.max(jnp.where(column == ids, slot_column, -1.0), axis=0, keepdims=True)
        )
        listed = jnp.maximum(
            listed, jnp.max(jnp.where(slot_column == target, column, -1.0), axis=0, keepdims=True)
        )
        return (slot, listed)

    slot, listed = lax.fori_loop(
        0,
        blocks,
        settle,
        (jnp.full((1, slots), -1.0, jnp.float32), jnp.full((1, width), -1.0, jnp.float32)),
    )
    slot_ref[...] = slot.astype(jnp.int32)
    listed = listed.astype(jnp.int32)
    most = jnp.max(running, axis=0, keepdims=True).astype(jnp.int32)
    for group in range(groups):
        for row in range(list_rows):
            first_lane = group * stride + row * 128
            ask_ref[group, row : row + 1] = listed[:, first_lane : first_lane + 128]
        ask_ref[group, list_rows:] = jnp.broadcast_to(most, (8 - list_rows, 128))


def make_plan(perm, all_ids, capacity, vocab_local, groups):
    slots = perm.shape[0]
    table = all_ids.reshape(-1, 128).T
    high = table // 256
    low = table - high * 256
    return pl.pallas_call(
        partial(plan_kernel, capacity, vocab_local, groups),
        out_shape=[
            jax.ShapeDtypeStruct((1, slots), jnp.int32),
            jax.ShapeDtypeStruct((groups, 8, 128), jnp.int32),
        ],
        in_specs=[in_vmem()] * 3,
        out_specs=[in_vmem()] * 2,
        scratch_shapes=[pltpu.VMEM((slots, 128), jnp.float32), pltpu.VMEM((slots, 128), jnp.float32)],
        compiler_params=pltpu.CompilerParams(vmem_limit_bytes=VMEM_BYTES),
    )(perm[None], low.astype(jnp.bfloat16), high.astype(jnp.bfloat16))


def loss_kernel(pooled_ref, head_ref, pair_ref, loss_ref, low_ref, grad_ref, back_ref):
    total = pooled_ref.shape[0]
    low = pooled_ref[...].astype(jnp.bfloat16)
    low_ref[...] = low
    head_low = head_ref[...].astype(jnp.bfloat16)
    vectors = multiply_arrays(low, head_low)
    depth = vectors.shape[1]
    lane = lax.broadcasted_iota(jnp.int32, vectors.shape, 1)
    across = lax.broadcasted_iota(jnp.int32, (total, total), 1)
    diagonal = lax.broadcasted_iota(jnp.int32, (total, total), 0) == across
    chosen = across == pair_ref[...]
    loss = jnp.zeros((1, 1), jnp.float32)
    grads = jnp.zeros(vectors.shape, jnp.float32)

    def exact(left, right, dims):
        return lax.dot_general(
            left, right, (dims, ((), ())), precision=HIGHEST_MODE, preferred_element_type=jnp.float32
        )

    for fraction in (16, 4, 1):
        prefix = jnp.where(lane < depth // fraction, vectors, 0.0)
        inverse = lax.rsqrt(jnp.sum(prefix * prefix, axis=1, keepdims=True) + 1e-06)
        unit = prefix * inverse
        logits = exact(unit, unit, ((1,), (1,))) / LOGIT_DIVISOR
        logits = jnp.where(diagonal, MASK_FILL, logits)
        top = jnp.max(logits, axis=1, keepdims=True)
        weights = jnp.exp(logits - top)
        weight_sum = jnp.sum(weights, axis=1, keepdims=True)
        positive = jnp.sum(jnp.where(chosen, logits, 0.0), axis=1, keepdims=True)
        loss = loss + jnp.sum(jnp.log(weight_sum) + top - positive, keepdims=True)
        pull = weights / weight_sum - jnp.where(chosen, 1.0, 0.0)
        unit_grad = (exact(pull, unit, ((1,), (0,))) + exact(pull, unit, ((0,), (0,)))) / LOGIT_DIVISOR
        unit_grad = jnp.where(lane < depth // fraction, unit_grad, 0.0)
        inner = jnp.sum(unit_grad * prefix, axis=1, keepdims=True)
        grads = grads + inverse * unit_grad - prefix * (inverse * inverse * inverse * inner)
    low_wide = low.astype(jnp.float32)
    head_squares = jnp.sum(
        exact(low_wide, low_wide, ((1,), (1,))) * exact(grads, grads, ((1,), (1,))), keepdims=True
    )
    line = lax.broadcasted_iota(jnp.int32, loss_ref.shape, 0)
    loss_ref[...] = jnp.where(line == 0, loss, head_squares)
    grad_ref[...] = grads
    pieces, rest = [], grads
    for _ in range(3):
        pieces.append(rest.astype(jnp.bfloat16))
        rest = rest - pieces[-1].astype(jnp.float32)
    product = lax.dot_general(
        jnp.concatenate(pieces, axis=0),
        head_low,
        (((1,), (1,)), ((), ())),
        preferred_element_type=jnp.float32,
    )
    back_ref[...] = product[:total] + product[total : 2 * total] + product[2 * total :]


def contrast_step(pooled, head_weight, pairs):
    total, depth = pooled.shape
    return pl.pallas_call(
        loss_kernel,
        out_shape=[
            jax.ShapeDtypeStruct((8, 128), jnp.float32),
            jax.ShapeDtypeStruct((total, depth), jnp.bfloat16),
            jax.ShapeDtypeStruct((total, depth), jnp.float32),
            jax.ShapeDtypeStruct((total, depth), jnp.float32),
        ],
        in_specs=[in_vmem()] * 3,
        out_specs=[in_vmem()] * 4,
        compiler_params=pltpu.CompilerParams(vmem_limit_bytes=VMEM_BYTES),
    )(pooled, head_weight, pairs[:, None])


CAPACITY = 192


def body(
    token_ids,
    slot_perm,
    seq_lengths,
    pair_index,
    tok_table,
    tok_first,
    tok_second,
    pos_table,
    pos_first,
    pos_second,
    query_key_value_weight,
    qkv_first,
    qkv_second,
    out_weight,
    out_first,
    out_second,
    up_weight,
    up_first,
    up_second,
    down_weight,
    down_first,
    down_second,
    head_weight,
    head_first,
    head_second,
    col_bias,
    col_first,
    col_second,
    row_params,
    row_first,
    row_second,
):
    groups = lax.axis_size("dp")
    tensor_count = lax.axis_size("tensor")
    group_index = lax.axis_index("dp")
    tensor_index = lax.axis_index("tensor")
    tok_dev = token_ids.shape[0]
    tok_grp = tok_dev * tensor_count
    col_width = pos_table.shape[1]
    vocab_local = tok_table.shape[0]
    column_start = tensor_index * col_width
    anchors = pair_index.shape[0]
    id_rows = tok_dev // 128
    block = jnp.concatenate(
        [
            token_ids.reshape(id_rows, 128),
            jnp.pad(pair_index, (0, 128 - anchors))[None],
            jnp.zeros((7 - id_rows, 128), jnp.int32),
        ],
        axis=0,
    )
    perm_block = jnp.pad(slot_perm.reshape(id_rows, 128), ((0, 8 - id_rows), (0, 0)))
    qkv_low = query_key_value_weight.astype(jnp.bfloat16).reshape(-1, 3 * col_width)
    out_low = out_weight.T.astype(jnp.bfloat16)
    up_low = up_weight.astype(jnp.bfloat16).reshape(qkv_low.shape[0], -1)
    down_low = down_weight.reshape(-1, down_weight.shape[2]).T.astype(jnp.bfloat16)
    gathered, perms, out_half = exchange(
        1, GatherAll(block), Gather(perm_block, "tensor"), SpreadLine(out_low)
    )
    all_ids = gathered[:, :id_rows].reshape(-1)
    pairs = gathered[::tensor_count, id_rows, :anchors].reshape(-1)
    own_perm = perms[:, :id_rows].reshape(-1)
    slot, request = make_plan(own_perm, all_ids, CAPACITY, vocab_local, groups)
    slot = slot[0]
    list_rows = -(-CAPACITY // 128)
    asked = exchange(2, Swap(request, "dp"))
    overflow = jnp.max(asked[:, list_rows]) > CAPACITY
    offset = group_index * vocab_local
    asked_rows = asked[:, :list_rows].reshape(groups, -1)[:, :CAPACITY].reshape(-1) - offset
    asked_safe = jnp.clip(asked_rows, 0, vocab_local - 1)
    sent_rows = jnp.take(tok_table, asked_safe, axis=0).astype(jnp.bfloat16)
    got_rows, pos_full, qkv_half, out_full = exchange(
        3,
        Swap(sent_rows.reshape(groups, CAPACITY, col_width), "dp"),
        Spread(pos_table, columns=True, chunks=1),
        SpreadLine(qkv_low),
        SpreadCross(out_half),
    )
    got_rows = got_rows.reshape(-1, col_width)

    def chooser(slots):
        places = jnp.arange(groups * CAPACITY, dtype=jnp.int32)
        return (slots[:, None] == places[None, :]).astype(jnp.bfloat16)

    lengths = seq_lengths[0]
    seq_ids, positions, member = seq_layout(lengths, tok_grp)
    bounds = block_bounds(lengths, tok_grp)

    def every_slot_id():
        every_perm = lax.all_gather(slot_perm, ("dp", "tensor"), axis=0, tiled=True)
        return jnp.take(all_ids, every_perm, axis=0)

    def spread_wide():
        wanted = every_slot_id() - offset
        inside = (wanted >= 0) & (wanted < vocab_local)
        picked = jnp.take(
            tok_table.astype(jnp.bfloat16), jnp.clip(wanted, 0, vocab_local - 1), axis=0
        )
        return lax.psum_scatter(
            jnp.where(inside[:, None], picked, jnp.zeros((), jnp.bfloat16)),
            "dp",
            scatter_dimension=0,
            tiled=True,
        )

    tok_cols = lax.cond(
        overflow,
        spread_wide,
        lambda: multiply_arrays(chooser(slot), got_rows).astype(jnp.bfloat16),
    )
    tok_all, qkv_full, up_half = exchange(
        4,
        Spread(tok_cols, columns=True),
        SpreadCross(qkv_half),
        SpreadLine(up_low),
    )
    layer_mats = (qkv_full.reshape(D, -1), out_full.reshape(D, -1), up_half, down_low)
    embedded = embed(tok_all, pos_full, seq_ids, lengths, row_params)
    members = lax.dynamic_slice_in_dim(member, tensor_index * tok_dev, tok_dev, 0).T.astype(
        jnp.bfloat16
    )
    counts = lengths.astype(jnp.float32)[:, None]
    pooled, saved_vals, layer_mats = layer_forward(
        embedded, seq_ids, bounds, members, counts, row_params, col_bias, layer_mats
    )
    loss_out, pooled_low, vec_grad, pooled_grad = contrast_step(
        pooled.reshape(-1, D), head_weight, pairs
    )
    head_sum = exact_multiply(pooled_low.astype(jnp.float32).T, vec_grad)
    cols_grad, sums, grid_squares, col_grad, row_grad = layer_backward(
        pooled_grad, counts, members, seq_ids, bounds, row_params, layer_mats, saved_vals
    )
    qkv_sum, out_sum, up_sum, down_sum = sums
    qkv_squares, out_squares, wide_squares = grid_squares
    cols_grad = cols_grad.reshape(tok_grp, col_width)
    pos_pick = (
        jnp.arange(pos_table.shape[0], dtype=jnp.int32)[:, None] == positions[None, :]
    ).astype(jnp.bfloat16)
    pos_grad = multiply_arrays(pos_pick, cols_grad)
    shared = jnp.concatenate([pos_grad, col_grad], axis=0)
    shared_rows = -(-shared.shape[0] // (16 * groups)) * 16
    shared = jnp.pad(shared, ((0, shared_rows * groups - shared.shape[0]), (0, 0)))
    merged = jnp.einsum(
        "kn,kc->nc",
        chooser(lax.optimization_barrier(slot)),
        cols_grad,
        preferred_element_type=jnp.float32,
    )
    back_rows, shared_parts = exchange(
        15,
        Swap(merged.astype(jnp.bfloat16).reshape(groups, CAPACITY, col_width), "dp"),
        Swap(shared.astype(jnp.bfloat16).reshape(groups, shared_rows, col_width), "dp"),
    )
    shared_own = jnp.sum(shared_parts.astype(jnp.float32), axis=0)

    def add_wide():
        wanted = every_slot_id() - offset
        inside = (wanted >= 0) & (wanted < vocab_local)
        grad = (
            jnp.zeros(tok_table.shape, jnp.float32)
            .at[jnp.clip(wanted, 0, vocab_local - 1)]
            .add(
                jnp.where(
                    inside[:, None],
                    lax.all_gather(cols_grad, "dp", axis=0, tiled=True).astype(jnp.float32),
                    0.0,
                )
            )
        )
        squares = jnp.sum(grad * grad, axis=0, keepdims=True)
        return (grad, jnp.pad(squares, ((0, 7), (0, 0))))

    tok_grad, tok_squares = lax.cond(
        overflow,
        add_wide,
        lambda: tuple(scatter_rows(asked_rows, back_rows.reshape(-1, col_width), vocab_local)),
    )
    qkv_grad = qkv_sum.reshape(query_key_value_weight.shape)
    out_grad = lax.optimization_barrier(out_sum.T)
    up_grad = up_sum.reshape(up_weight.shape)
    down_grad = lax.optimization_barrier(down_sum.T.reshape(down_weight.shape))
    def widen(*parts):
        joined = jnp.concatenate(parts, axis=1)
        return jnp.pad(joined, ((0, 0), (0, D - joined.shape[1])))

    square_rows = (
        widen(wide_squares)
        + widen(qkv_squares, out_squares)
        + widen(tok_squares, eight_rows(shared_own * shared_own))
    )
    row_block = jnp.concatenate([row_grad, square_rows], axis=0)
    row_total, shared_sum = exchange(16, SumAll(row_block, False), GatherGrid(shared_own.astype(jnp.bfloat16)))
    row_total = row_total[0]
    shared_sum = shared_sum.reshape(-1, col_width).astype(jnp.float32)
    pos_own = shared_sum[: pos_table.shape[0]]
    col_own = shared_sum[pos_table.shape[0] : pos_table.shape[0] + col_bias.shape[0]]
    row_sum = row_total[:8]
    squares = jnp.sum(row_total[8:]) + jnp.sum(row_sum * row_sum) + loss_out[1, 0]
    grad_norm = jnp.sqrt(squares)
    clip_scale = jnp.minimum(1.0, CLIP_NORM / (grad_norm + 1e-06))
    tok_new = adam_step(
        tok_table, tok_first, tok_second, tok_grad * clip_scale, RATE_MATRIX, DECAY_RATE
    )
    pos_new = adam_step(
        pos_table, pos_first, pos_second, pos_own * clip_scale, RATE_MATRIX, DECAY_RATE
    )
    qkv_new = adam_step(
        query_key_value_weight,
        qkv_first,
        qkv_second,
        qkv_grad * clip_scale,
        RATE_MATRIX,
        DECAY_RATE,
    )
    out_new = adam_step(
        out_weight, out_first, out_second, out_grad * clip_scale, RATE_MATRIX, DECAY_RATE
    )
    up_new = adam_step(
        up_weight, up_first, up_second, up_grad * clip_scale, RATE_MATRIX, DECAY_RATE
    )
    down_new = adam_step(
        down_weight, down_first, down_second, down_grad * clip_scale, RATE_MATRIX, DECAY_RATE
    )
    head_new = adam_step(
        head_weight, head_first, head_second, head_sum * clip_scale, RATE_MATRIX, DECAY_RATE
    )
    col_new = adam_step(col_bias, col_first, col_second, col_own * clip_scale, RATE_VECTOR, 0.0)
    row_new = adam_step(row_params, row_first, row_second, row_sum * clip_scale, RATE_VECTOR, 0.0)
    return (loss_out[0, 0], grad_norm) + tok_new + pos_new + qkv_new + out_new + up_new + down_new + head_new + col_new + row_new


def solution(mesh):
    placed = (
        P(("dp", "tensor")),
        P(("dp", "tensor")),
        P("dp", None),
        P("dp"),
        P("dp", "tensor"),
        P("dp", "tensor"),
        P("dp", "tensor"),
        P(None, "tensor"),
        P(None, "tensor"),
        P(None, "tensor"),
        P("dp", None, "tensor"),
        P("dp", None, "tensor"),
        P("dp", None, "tensor"),
        P("tensor", "dp"),
        P("tensor", "dp"),
        P("tensor", "dp"),
        P("dp", None, "tensor"),
        P("dp", None, "tensor"),
        P("dp", None, "tensor"),
        P(None, "tensor", "dp"),
        P(None, "tensor", "dp"),
        P(None, "tensor", "dp"),
        P(),
        P(),
        P(),
        P(None, "tensor"),
        P(None, "tensor"),
        P(None, "tensor"),
        P(),
        P(),
        P(),
    )
    return jax.shard_map(
        body,
        mesh=mesh,
        in_specs=placed,
        out_specs=(
            P(),
            P(),
            P("dp", "tensor"),
            P("dp", "tensor"),
            P("dp", "tensor"),
            P(None, "tensor"),
            P(None, "tensor"),
            P(None, "tensor"),
            P("dp", None, "tensor"),
            P("dp", None, "tensor"),
            P("dp", None, "tensor"),
            P("tensor", "dp"),
            P("tensor", "dp"),
            P("tensor", "dp"),
            P("dp", None, "tensor"),
            P("dp", None, "tensor"),
            P("dp", None, "tensor"),
            P(None, "tensor", "dp"),
            P(None, "tensor", "dp"),
            P(None, "tensor", "dp"),
            P(),
            P(),
            P(),
            P(None, "tensor"),
            P(None, "tensor"),
            P(None, "tensor"),
            P(),
            P(),
            P(),
        ),
        check_vma=False,
    )
```

```python
from functools import partial

import jax
import jax.numpy as jnp
from jax import lax
from jax.experimental import pallas as pl
from jax.experimental.pallas import tpu as pltpu
from jax.sharding import PartitionSpec as P

D = 1024
HEAD = 64
MAXLEN = 512
STEP = 10


HIGHEST_MODE = lax.Precision.HIGHEST
LN_EPS = 1e-05
LOGIT_DIVISOR = 0.05
CLIP_NORM = 0.25
BETA_FIRST = 0.9
BETA_SECOND = 0.999
ADAM_EPS = 1e-08
RATE_MATRIX = 0.05
RATE_VECTOR = 0.5
DECAY_RATE = 0.01
MASK_FILL = -1e30


def multiply_arrays(left_mat, right_mat):
    return jnp.dot(left_mat, right_mat, preferred_element_type=jnp.float32)


def exact_multiply(left_mat, right_mat):
    return jnp.dot(left_mat, right_mat, precision=HIGHEST_MODE, preferred_element_type=jnp.float32)


def norm_rows(values, gain_row, bias_row):
    center = values - jnp.mean(values, axis=1, keepdims=True)
    inverse = lax.rsqrt(jnp.mean(center * center, axis=1, keepdims=True) + LN_EPS)
    return center * inverse * gain_row + bias_row


def seq_layout(lengths, slot_total):
    seq_ends = jnp.cumsum(lengths)
    starts = seq_ends - lengths
    slot_index = jnp.arange(slot_total, dtype=jnp.int32)
    member = (slot_index[:, None] >= starts[None, :]) & (slot_index[:, None] < seq_ends[None, :])
    seq_count = jnp.arange(lengths.shape[0], dtype=jnp.int32)
    seq_ids = jnp.sum(jnp.where(member, seq_count[None, :], 0), axis=1)
    positions = slot_index - jnp.sum(jnp.where(member, starts[None, :], 0), axis=1) + 2
    return (seq_ids, positions, member)


def adam_step(weight, first_old, second_old, clipped, step_rate, decay_rate):
    first_new = BETA_FIRST * first_old + (1.0 - BETA_FIRST) * clipped
    second_new = BETA_SECOND * second_old + (1.0 - BETA_SECOND) * clipped * clipped
    first_hat = first_new / (1.0 - BETA_FIRST**STEP)
    second_hat = second_new / (1.0 - BETA_SECOND**STEP)
    weight_new = weight - step_rate * (
        first_hat / (jnp.sqrt(second_hat) + ADAM_EPS) + decay_rate * weight
    )
    return (weight_new, first_new, second_new)


MESH_IDS = pl.DeviceIdType.MESH
SPARE_BYTES = 6 * 1024 * 1024
CHUNKS = 4
LINE = 4


def in_vmem():
    return pl.BlockSpec(memory_space=pltpu.VMEM)


def shaped(shape, dtype):
    return jax.ShapeDtypeStruct(tuple(shape), dtype)


def dma(*shape):
    return pltpu.SemaphoreType.DMA(shape)


def remote(src, dst, send_sem, recv_sem, target):
    return pltpu.make_async_remote_copy(
        src_ref=src,
        dst_ref=dst,
        send_sem=send_sem,
        recv_sem=recv_sem,
        device_id=target,
        device_id_type=MESH_IDS,
    )


def room(*items):
    total = 0
    for item in items:
        size = 0
        if item.dtype == jnp.bfloat16:
            size = 2
        elif item.dtype == jnp.float32 or item.dtype == jnp.int32:
            size = 4
        for extent in item.shape[:-1]:
            size = size * extent
        total = total + size * (-(-item.shape[-1] // 128) * 128)
    return total + SPARE_BYTES


def comm_params(collective, limit):
    return pltpu.CompilerParams(
        collective_id=collective, has_side_effects=True, vmem_limit_bytes=limit
    )


def exchange(collective, *tasks):
    def kernel(*refs):
        at = 0
        for attribute in ("ins", "outs", "scratch"):
            for task in tasks:
                size = len(getattr(task, attribute))
                setattr(task, attribute + "_refs", refs[at : at + size])
                at += size
        barrier = pltpu.get_barrier_semaphore()
        pl.semaphore_wait(barrier, sum(task.hello(barrier) for task in tasks))
        for task in tasks:
            task.begin()
        for task in tasks:
            task.middle()
        for task in tasks:
            task.late()
        for task in tasks[1:]:
            task.end()
        tasks[0].end()

    results = pl.pallas_call(
        kernel,
        out_shape=[out for task in tasks for out in task.outs],
        in_specs=[in_vmem() for task in tasks for _ in task.ins],
        out_specs=[in_vmem() for task in tasks for _ in task.outs],
        scratch_shapes=[item for task in tasks for item in task.scratch],
        compiler_params=comm_params(
            collective,
            room(*[item for task in tasks for item in task.ins + task.outs + task.scratch]),
        ),
    )(*[array for task in tasks for array in task.ins])
    return results[0] if len(results) == 1 else results


def tensor_place(width):
    me = lax.axis_index("tensor")
    core = lax.rem(me, 2)
    row = me // 2
    mate = me + 1 - 2 * core
    return (me, core, row, mate)


class Task:
    def hello(self, barrier):
        partners = self.partners()
        for partner in partners:
            pl.semaphore_signal(barrier, inc=1, device_id=partner, device_id_type=MESH_IDS)
        return len(partners)

    def begin(self):
        pass

    def middle(self):
        pass

    def late(self):
        pass

    def end(self):
        pass


class Pair(Task):
    def __init__(self):
        self.width = lax.axis_size("tensor")
        self.rows = self.width // 2

    def partners(self):
        me, core, row, mate = tensor_place(self.width)
        return [{"tensor": mate}] + [
            {"tensor": lax.rem(row + step, self.rows) * 2 + core} for step in range(1, self.rows)
        ]


class Spread(Pair):
    def __init__(self, block, columns=False, chunks=CHUNKS):
        super().__init__()
        height, depth = block.shape
        self.columns, self.chunks = columns, chunks
        self.ins = (block,)
        whole = (height, self.width * depth) if columns else (self.width * height, depth)
        self.outs = (shaped(whole, block.dtype),)
        self.scratch = tuple(dma(self.rows, chunks) for _ in range(4))

    def window(self, owner, part=None):
        (x_ref,), (o_ref,) = self.ins_refs, self.outs_refs
        height, depth = x_ref.shape
        size = height // self.chunks
        if self.columns:
            lanes = pl.ds(pl.multiple_of(owner * depth, depth), depth)
            if part is None or self.chunks == 1:
                return o_ref.at[:, lanes]
            return o_ref.at[pl.ds(part * size, size), lanes]
        if part is None:
            return o_ref.at[pl.ds(pl.multiple_of(owner * height, height), height)]
        return o_ref.at[pl.ds(pl.multiple_of(owner * height + part * size, size), size)]

    def begin(self):
        (x_ref,) = self.ins_refs
        far_send, far_recv, near_send, near_recv = self.scratch_refs
        me, core, row, mate = tensor_place(self.width)
        size = x_ref.shape[0] // self.chunks
        self.far = {}
        for part in range(self.chunks):
            source = x_ref if self.chunks == 1 else x_ref.at[pl.ds(part * size, size)]
            for step in range(1, self.rows):
                copy = remote(
                    source,
                    self.window(me, part),
                    far_send.at[step, part],
                    far_recv.at[step, part],
                    {"tensor": lax.rem(row + step, self.rows) * 2 + core},
                )
                copy.start()
                self.far[step, part] = copy
        copy = remote(
            x_ref, self.window(me), near_send.at[0, 0], near_recv.at[0, 0], {"tensor": mate}
        )
        copy.start()
        self.near = [copy]
        self.window(me)[...] = x_ref[...]

    def middle(self):
        far_send, far_recv, near_send, near_recv = self.scratch_refs
        me, core, row, mate = tensor_place(self.width)
        for part in range(self.chunks):
            for step in range(1, self.rows):
                self.far[step, part].wait_recv()
                source = lax.rem(row + self.rows - step, self.rows) * 2 + core
                onward = remote(
                    self.window(source, part),
                    self.window(source, part),
                    near_send.at[step, part],
                    near_recv.at[step, part],
                    {"tensor": mate},
                )
                onward.start()
                self.near.append(onward)

    def end(self):
        for copy in self.near:
            copy.wait()
        for copy in self.far.values():
            copy.wait_send()


class Fold(Pair):
    def __init__(self, parts, chunks=CHUNKS):
        super().__init__()
        height, depth = parts.shape[0] // self.width, parts.shape[1]
        far_rows = max(self.rows - 1, 1)
        self.chunks, self.height, self.depth = chunks, height, depth
        self.parts = parts
        self.fold_scratch = (
            pltpu.VMEM((self.rows, height, depth), jnp.bfloat16),
            pltpu.VMEM((far_rows, height, depth), jnp.bfloat16),
            pltpu.VMEM((far_rows, height, depth), jnp.bfloat16),
            pltpu.VMEM((height, depth), jnp.float32),
        ) + tuple(dma(self.rows, chunks) for _ in range(4))

    def span(self, owner, part):
        size = self.height // self.chunks
        return pl.ds(pl.multiple_of(owner * self.height + part * size, size), size)

    def local(self, part):
        size = self.height // self.chunks
        return pl.ds(part * size, size)

    def begin(self):
        p_ref = self.ins_refs[0]
        near_buf, near_send, near_recv = self.scratch_refs[0], *self.scratch_refs[4:6]
        me, core, row, mate = tensor_place(self.width)
        self.near = {}
        for step in list(range(1, self.rows)) + [0]:
            dest_row = lax.rem(row + step, self.rows)
            for part in range(self.chunks):
                copy = remote(
                    p_ref.at[self.span(dest_row * 2 + 1 - core, part)],
                    near_buf.at[step, self.local(part)],
                    near_send.at[step, part],
                    near_recv.at[step, part],
                    {"tensor": mate},
                )
                copy.start()
                self.near[step, part] = copy

    def middle(self):
        p_ref = self.ins_refs[0]
        near_buf, sum_buf, far_buf, total_buf = self.scratch_refs[:4]
        far_send, far_recv = self.scratch_refs[6:8]
        me, core, row, mate = tensor_place(self.width)
        self.far = {}
        for step in range(1, self.rows):
            dest = lax.rem(row + step, self.rows) * 2 + core
            for part in range(self.chunks):
                local = self.local(part)
                self.near[step, part].wait_recv()
                sum_buf[step - 1, local] = (
                    p_ref[self.span(dest, part)].astype(jnp.float32)
                    + near_buf[step, local].astype(jnp.float32)
                ).astype(jnp.bfloat16)
                copy = remote(
                    sum_buf.at[step - 1, local],
                    far_buf.at[step - 1, local],
                    far_send.at[step - 1, part],
                    far_recv.at[step - 1, part],
                    {"tensor": dest},
                )
                copy.start()
                self.far[step, part] = copy
        for part in range(self.chunks):
            local = self.local(part)
            self.near[0, part].wait_recv()
            total_buf[local] = p_ref[self.span(me, part)].astype(jnp.float32) + near_buf[
                0, local
            ].astype(jnp.float32)

    def folded(self, part):
        far_buf, total_buf = self.scratch_refs[2:4]
        local = self.local(part)
        total = total_buf[local]
        for step in range(1, self.rows):
            self.far[step, part].wait_recv()
            total = total + far_buf[step - 1, local].astype(jnp.float32)
        return total

    def settle_fold(self):
        for copy in list(self.near.values()) + list(self.far.values()):
            copy.wait_send()


class Relay:
    def relay_scratch(self):
        return (pltpu.VMEM((self.height, self.depth), jnp.bfloat16),) + tuple(
            dma(self.rows, self.chunks) for _ in range(4)
        )

    def relay_open(self, part, low):
        buf, far_send, far_recv, near_send, near_recv = self.scratch_refs[-5:]
        all_ref = self.outs_refs[0]
        me, core, row, mate = tensor_place(self.width)
        local = self.local(part)
        buf[local] = low
        if part == 0:
            self.sent, self.relay_near = {}, []
        for step in range(1, self.rows):
            copy = remote(
                buf.at[local],
                all_ref.at[self.span(me, part)],
                far_send.at[step, part],
                far_recv.at[step, part],
                {"tensor": lax.rem(row + step, self.rows) * 2 + core},
            )
            copy.start()
            self.sent[step, part] = copy
        copy = remote(
            buf.at[local],
            all_ref.at[self.span(me, part)],
            near_send.at[0, part],
            near_recv.at[0, part],
            {"tensor": mate},
        )
        copy.start()
        self.relay_near.append(copy)
        all_ref[self.span(me, part)] = low

    def relay_close(self):
        buf, far_send, far_recv, near_send, near_recv = self.scratch_refs[-5:]
        all_ref = self.outs_refs[0]
        me, core, row, mate = tensor_place(self.width)
        for part in range(self.chunks):
            for step in range(1, self.rows):
                self.sent[step, part].wait_recv()
                source = lax.rem(row + self.rows - step, self.rows) * 2 + core
                window = all_ref.at[self.span(source, part)]
                copy = remote(
                    window, window, near_send.at[step, part], near_recv.at[step, part], {"tensor": mate}
                )
                copy.start()
                self.relay_near.append(copy)
        for copy in self.relay_near:
            copy.wait()
        for copy in self.sent.values():
            copy.wait_send()


def split_three(values):
    pieces, rest = [], values
    for _ in range(3):
        pieces.append(rest.astype(jnp.bfloat16))
        rest = rest - pieces[-1].astype(jnp.float32)
    return pieces


def norm_pull(values, gain, grads):
    center = values - jnp.mean(values, axis=1, keepdims=True)
    inverse = lax.rsqrt(jnp.mean(center * center, axis=1, keepdims=True) + LN_EPS)
    unit = center * inverse
    scaled = grads * gain
    pull = inverse * (
        scaled
        - jnp.mean(scaled, axis=1, keepdims=True)
        - unit * jnp.mean(scaled * unit, axis=1, keepdims=True)
    )
    return (
        pull,
        jnp.sum(grads * unit, axis=0, keepdims=True),
        jnp.sum(grads, axis=0, keepdims=True),
    )


class FoldNormSpread(Relay, Fold):
    def __init__(self, parts, residual, row_params):
        super().__init__(parts)
        own = shaped((self.height, self.depth), jnp.float32)
        self.ins = (parts, residual, row_params)
        self.outs = (shaped(parts.shape, jnp.bfloat16), own, own)
        self.scratch = self.fold_scratch + self.relay_scratch()

    def late(self):
        p_ref, residual_ref, row_ref = self.ins_refs
        all_ref, sum_ref, norm_ref = self.outs_refs
        for part in range(self.chunks):
            local = self.local(part)
            total = residual_ref[local] + self.folded(part) + row_ref[6:7]
            sum_ref[local] = total
            norm = norm_rows(total, row_ref[1:2], row_ref[4:5])
            norm_ref[local] = norm
            self.relay_open(part, norm.astype(jnp.bfloat16))

    def end(self):
        self.relay_close()
        self.settle_fold()


class FoldPullSpread(Relay, Fold):
    def __init__(self, parts, residual, values, row_params):
        super().__init__(parts)
        own = shaped((self.height, self.depth), jnp.float32)
        self.ins = (parts, residual, values, row_params)
        self.outs = (shaped(parts.shape, jnp.bfloat16), own, shaped((8, self.depth), jnp.float32))
        self.scratch = self.fold_scratch + self.relay_scratch()

    def late(self):
        p_ref, residual_ref, value_ref, row_ref = self.ins_refs
        all_ref, grad_ref, side_ref = self.outs_refs
        side_ref[...] = jnp.zeros_like(side_ref)
        for part in range(self.chunks):
            local = self.local(part)
            pull, gain, shift = norm_pull(
                value_ref[local], row_ref[1:2], residual_ref[local] + self.folded(part)
            )
            grad_ref[local] = pull
            low = pull.astype(jnp.bfloat16)
            self.relay_open(part, low)
            side_ref[0:1] += gain
            side_ref[1:2] += shift
            side_ref[2:3] += jnp.sum(low.astype(jnp.float32), axis=0, keepdims=True)

    def end(self):
        self.relay_close()
        self.settle_fold()


class PullSpread(Relay, Pair):
    def __init__(self, pooled_grad, counts, members, values, row_params):
        super().__init__()
        self.height, self.depth = values.shape
        self.chunks = CHUNKS
        own = shaped(values.shape, jnp.float32)
        self.ins = (pooled_grad, counts, members, values, row_params)
        self.outs = (
            shaped((self.width * self.height, self.depth), jnp.bfloat16),
            own,
            shaped((8, self.depth), jnp.float32),
        )
        self.scratch = self.relay_scratch()

    span, local = Fold.span, Fold.local

    def begin(self):
        pooled_ref, count_ref, member_ref, value_ref, row_ref = self.ins_refs
        all_ref, grad_ref, side_ref = self.outs_refs
        side_ref[...] = jnp.zeros_like(side_ref)
        anchors = count_ref.shape[0]
        rows = block_span(lax.axis_index("dp"), anchors)
        pieces = jnp.concatenate(split_three(pooled_ref[rows] / count_ref[...]), axis=0)
        for part in range(self.chunks):
            local = self.local(part)
            grads = multiply_arrays(member_ref[local], pieces)
            pull, gain, shift = norm_pull(value_ref[local], row_ref[2:3], grads)
            grad_ref[local] = pull
            low = pull.astype(jnp.bfloat16)
            self.relay_open(part, low)
            side_ref[0:1] += gain
            side_ref[1:2] += shift
            side_ref[2:3] += jnp.sum(low.astype(jnp.float32), axis=0, keepdims=True)

    def end(self):
        self.relay_close()


class Swap(Task):
    def __init__(self, blocks, axis):
        self.axis, self.count = axis, lax.axis_size(axis)
        self.ins = (blocks,)
        self.outs = (shaped(blocks.shape, blocks.dtype),)
        self.scratch = (dma(self.count), dma(self.count))

    def others(self):
        me = lax.axis_index(self.axis)
        return [lax.rem(me + step, self.count) for step in range(1, self.count)]

    def partners(self):
        return [{self.axis: other} for other in self.others()]

    def begin(self):
        (x_ref,), (o_ref,), (send, recv) = self.ins_refs, self.outs_refs, self.scratch_refs
        me = lax.axis_index(self.axis)
        self.copies = [
            remote(x_ref.at[other], o_ref.at[me], send.at[i], recv.at[i], {self.axis: other})
            for i, other in enumerate(self.others())
        ]
        for copy in self.copies:
            copy.start()
        o_ref[me] = x_ref[me]

    def end(self):
        for copy in self.copies:
            copy.wait()


class Gather(Swap):
    def __init__(self, block, axis):
        super().__init__(block, axis)
        self.outs = (shaped((self.count,) + block.shape, block.dtype),)

    def begin(self):
        (x_ref,), (o_ref,), (send, recv) = self.ins_refs, self.outs_refs, self.scratch_refs
        me = lax.axis_index(self.axis)
        self.copies = [
            remote(x_ref, o_ref.at[me], send.at[i], recv.at[i], {self.axis: other})
            for i, other in enumerate(self.others())
        ]
        for copy in self.copies:
            copy.start()
        o_ref[me] = x_ref[...]


class GatherAll(Task):
    def __init__(self, block):
        self.width = lax.axis_size("tensor")
        self.total = total = lax.axis_size("dp") * self.width
        self.ins = (block,)
        self.outs = (shaped((total,) + block.shape, block.dtype),)
        self.scratch = (dma(total), dma(total))

    def me(self):
        return lax.axis_index("dp") * self.width + lax.axis_index("tensor")

    def place(self, step):
        other = lax.rem(self.me() + step, self.total)
        return (other // self.width, lax.rem(other, self.width))

    def copy(self, step):
        (x_ref,), (o_ref,), (send, recv) = self.ins_refs, self.outs_refs, self.scratch_refs
        return remote(x_ref, o_ref.at[self.me()], send.at[step], recv.at[step], self.place(step))

    def hello(self, barrier):
        def one(step, carry):
            pl.semaphore_signal(
                barrier, inc=1, device_id=self.place(step), device_id_type=MESH_IDS
            )
            return carry

        lax.fori_loop(1, self.total, one, 0)
        return self.total - 1

    def begin(self):
        def one(step, carry):
            self.copy(step).start()
            return carry

        lax.fori_loop(1, self.total, one, 0)
        self.outs_refs[0][self.me()] = self.ins_refs[0][...]

    def end(self):
        def one(step, carry):
            self.copy(step).wait()
            return carry

        lax.fori_loop(1, self.total, one, 0)


class FoldPool(Fold):
    def __init__(self, parts, residual, members, counts, row_params):
        super().__init__(parts)
        anchors = members.shape[0]
        self.total = SumAll(shaped((anchors, self.depth), jnp.float32), True)
        self.ins = (parts, residual, members, counts, row_params)
        self.outs = (shaped((self.height, self.depth), jnp.float32),) + self.total.outs
        self.scratch = (
            self.fold_scratch
            + (pltpu.VMEM((anchors, self.depth), jnp.float32),)
            + self.total.scratch
        )

    def hello(self, barrier):
        return super().hello(barrier) + self.total.hello(barrier)

    def end(self):
        p_ref, residual_ref, member_ref, count_ref, row_ref = self.ins_refs
        sum_ref = self.outs_refs[0]
        at = len(self.fold_scratch)
        pooled = self.scratch_refs[at]
        size = self.height // self.chunks
        parts = []
        for part in range(self.chunks):
            local = self.local(part)
            total = residual_ref[local] + self.folded(part) + row_ref[7:8]
            sum_ref[local] = total
            norm = norm_rows(total, row_ref[2:3], row_ref[5:6])
            member = member_ref[:, part * size : (part + 1) * size]
            for piece in split_three(norm):
                parts.append(multiply_arrays(member, piece))
        pooled[...] = sum(parts[1:], parts[0]) / count_ref[...]
        total = self.total
        total.ins_refs, total.outs_refs = (pooled,), self.outs_refs[1:]
        total.scratch_refs = self.scratch_refs[at + 1 :]
        total.begin()
        total.middle()
        total.end()
        self.settle_fold()


class FoldPullSwap(Fold):
    def __init__(self, parts, residual, values, row_params):
        super().__init__(parts)
        self.narrow = self.depth // self.width
        self.ins = (parts, residual, values, row_params)
        self.outs = (
            shaped((self.width, self.height, self.narrow), jnp.bfloat16),
            shaped((8, self.depth), jnp.float32),
        )
        self.scratch = self.fold_scratch + (
            pltpu.VMEM((self.height, self.depth), jnp.bfloat16),
            dma(self.width, self.chunks),
            dma(self.width, self.chunks),
        )

    def partners(self):
        me = lax.axis_index("tensor")
        return [{"tensor": lax.rem(me + step, self.width)} for step in range(1, self.width)]

    def late(self):
        p_ref, residual_ref, value_ref, row_ref = self.ins_refs
        cols_ref, side_ref = self.outs_refs
        buf, send, recv = self.scratch_refs[-3:]
        side_ref[...] = jnp.zeros_like(side_ref)
        me = lax.axis_index("tensor")

        def lanes(owner):
            return pl.ds(pl.multiple_of(owner * self.narrow, self.narrow), self.narrow)

        copies = []
        for part in range(self.chunks):
            local = self.local(part)
            pull, gain, shift = norm_pull(
                value_ref[local], row_ref[0:1], residual_ref[local] + self.folded(part)
            )
            buf[local] = pull.astype(jnp.bfloat16)
            for step in range(1, self.width):
                other = lax.rem(me + step, self.width)
                copy = remote(
                    buf.at[local, lanes(other)],
                    cols_ref.at[me, local],
                    send.at[step, part],
                    recv.at[step, part],
                    {"tensor": other},
                )
                copy.start()
                copies.append(copy)
            cols_ref[me, local] = buf[local, lanes(me)]
            side_ref[0:1] += gain
            side_ref[1:2] += shift
        self.copies = copies

    def end(self):
        for copy in self.copies:
            copy.wait()
        self.settle_fold()


def eight_rows(values):
    return jnp.sum(values.reshape(values.shape[0] // 8, 8, values.shape[1]), axis=0)


class GridTask(Task):
    def __init__(self):
        self.cross = lax.axis_size("dp") // LINE

    def place(self):
        me = lax.axis_index("dp")
        return (me // self.cross, lax.rem(me, self.cross))


class ReduceCross(GridTask):
    def __init__(self, blocks):
        super().__init__()
        shape = blocks.shape[1:]
        self.blocks_shape = (LINE, self.cross) + shape
        self.ins = (blocks.reshape(self.blocks_shape),)
        self.outs = (shaped((LINE,) + shape, jnp.bfloat16),)
        others = max(self.cross - 1, 1)
        self.scratch = (
            pltpu.VMEM((others, LINE) + shape, jnp.bfloat16),
            dma(others, LINE),
            dma(others, LINE),
        )

    def targets(self):
        line, cross = self.place()
        return [lax.rem(cross + step, self.cross) for step in range(1, self.cross)]

    def partners(self):
        line, cross = self.place()
        return [{"dp": line * self.cross + other} for other in self.targets()]

    def begin(self):
        (x_ref,), (buf, send, recv) = self.ins_refs, self.scratch_refs
        line, cross = self.place()
        self.copies = []
        for i, other in enumerate(self.targets()):
            for z in range(LINE):
                copy = remote(
                    x_ref.at[z, other],
                    buf.at[i, z],
                    send.at[i, z],
                    recv.at[i, z],
                    {"dp": line * self.cross + other},
                )
                copy.start()
                self.copies.append(copy)

    def end(self):
        (x_ref,), (o_ref,), (buf, send, recv) = self.ins_refs, self.outs_refs, self.scratch_refs
        line, cross = self.place()
        for copy in self.copies:
            copy.wait()
        for z in range(LINE):
            total = x_ref[z, cross].astype(jnp.float32)
            for i in range(self.cross - 1):
                total = total + buf[i, z].astype(jnp.float32)
            o_ref[z] = total.astype(jnp.bfloat16)


class SpreadLine(GridTask):
    def __init__(self, block):
        super().__init__()
        self.ins = (block,)
        self.outs = (shaped((LINE,) + block.shape, block.dtype),)
        self.scratch = (dma(LINE - 1), dma(LINE - 1))

    def targets(self):
        line, cross = self.place()
        return [lax.rem(line + step, LINE) for step in range(1, LINE)]

    def partners(self):
        line, cross = self.place()
        return [{"dp": other * self.cross + cross} for other in self.targets()]

    def begin(self):
        (x_ref,), (o_ref,), (send, recv) = self.ins_refs, self.outs_refs, self.scratch_refs
        line, cross = self.place()
        self.copies = [
            remote(x_ref, o_ref.at[line], send.at[i], recv.at[i], partner)
            for i, partner in enumerate(self.partners())
        ]
        for copy in self.copies:
            copy.start()
        o_ref[line] = x_ref[...]

    def end(self):
        for copy in self.copies:
            copy.wait()


class Chain(Task):
    def __init__(self, first, second):
        self.first, self.second = first, second
        self.ins = first.ins
        self.outs = first.outs + second.outs
        self.scratch = first.scratch + second.scratch

    def hello(self, barrier):
        return self.first.hello(barrier) + self.second.hello(barrier)

    def begin(self):
        outs, scratch = len(self.first.outs), len(self.first.scratch)
        self.first.ins_refs, self.first.outs_refs = self.ins_refs, self.outs_refs[:outs]
        self.first.scratch_refs = self.scratch_refs[:scratch]
        self.second.ins_refs, self.second.outs_refs = self.outs_refs[:outs], self.outs_refs[outs:]
        self.second.scratch_refs = self.scratch_refs[scratch:]
        self.first.begin()

    def middle(self):
        self.first.end()
        self.second.begin()

    def end(self):
        self.second.end()


class Later(Task):
    def __init__(self, task):
        self.task = task
        self.ins, self.outs, self.scratch = task.ins, task.outs, task.scratch

    def hello(self, barrier):
        return self.task.hello(barrier)

    def middle(self):
        task = self.task
        task.ins_refs, task.outs_refs = self.ins_refs, self.outs_refs
        task.scratch_refs = self.scratch_refs
        task.begin()

    def end(self):
        self.task.end()


def reduce_grid(blocks, **form):
    first = ReduceCross(blocks)
    return Chain(first, ReduceLine(first.outs[0], **form))


def spread_grid(block):
    first = SpreadLine(block)
    return Chain(first, SpreadCross(first.outs[0]))


class SpreadCross(GridTask):
    def __init__(self, *pieces):
        super().__init__()
        self.ins = pieces
        self.tall, depth = pieces[0].shape[1:]
        count = len(pieces)
        self.outs = (shaped((LINE, self.cross, self.tall * count, depth), pieces[0].dtype),)
        others = max(self.cross - 1, 1)
        self.scratch = (dma(others, LINE, count), dma(others, LINE, count))

    def partners(self):
        line, cross = self.place()
        return [
            {"dp": line * self.cross + lax.rem(cross + step, self.cross)}
            for step in range(1, self.cross)
        ]

    def begin(self):
        (o_ref,), (send, recv) = self.outs_refs, self.scratch_refs
        line, cross = self.place()
        self.copies = []
        for p, x_ref in enumerate(self.ins_refs):
            rows = pl.ds(p * self.tall, self.tall)
            for i, partner in enumerate(self.partners()):
                for z in range(LINE):
                    copy = remote(
                        x_ref.at[z],
                        o_ref.at[z, cross, rows],
                        send.at[i, z, p],
                        recv.at[i, z, p],
                        partner,
                    )
                    copy.start()
                    self.copies.append(copy)
            for z in range(LINE):
                o_ref[z, cross, rows] = x_ref[z]

    def end(self):
        for copy in self.copies:
            copy.wait()


class GatherGrid(GridTask):
    def __init__(self, block):
        super().__init__()
        self.ins = (block,)
        self.outs = (shaped((LINE, self.cross) + block.shape, block.dtype),)
        others = max(self.cross - 1, 1)
        self.scratch = (dma(LINE - 1), dma(LINE - 1), dma(others, LINE), dma(others, LINE))

    def lines(self):
        line, cross = self.place()
        return [
            {"dp": lax.rem(line + step, LINE) * self.cross + cross} for step in range(1, LINE)
        ]

    def crosses(self):
        line, cross = self.place()
        return [
            {"dp": line * self.cross + lax.rem(cross + step, self.cross)}
            for step in range(1, self.cross)
        ]

    def partners(self):
        return self.lines() + self.crosses()

    def begin(self):
        (x_ref,), (o_ref,), sems = self.ins_refs, self.outs_refs, self.scratch_refs
        line, cross = self.place()
        self.copies = [
            remote(x_ref, o_ref.at[line, cross], sems[0].at[i], sems[1].at[i], partner)
            for i, partner in enumerate(self.lines())
        ]
        for copy in self.copies:
            copy.start()
        o_ref[line, cross] = x_ref[...]

    def middle(self):
        (o_ref,), sems = self.outs_refs, self.scratch_refs
        line, cross = self.place()
        for copy in self.copies:
            copy.wait()
        self.copies = []
        for i, partner in enumerate(self.crosses()):
            for z in range(LINE):
                window = o_ref.at[z, cross]
                copy = remote(window, window, sems[2].at[i, z], sems[3].at[i, z], partner)
                copy.start()
                self.copies.append(copy)

    def end(self):
        for copy in self.copies:
            copy.wait()


class ReduceLine(GridTask):
    def __init__(self, blocks, slabs=1, turned=False):
        super().__init__()
        shape = blocks.shape[1:]
        self.slabs, self.turned = slabs, turned
        self.ins = (blocks,)
        result = shape[::-1] if turned else shape
        if slabs > 1:
            result = (slabs, shape[0], shape[1] // slabs)
        self.outs = (shaped(result, jnp.float32), shaped((8, shape[1]), jnp.float32))
        self.scratch = (pltpu.VMEM((LINE - 1,) + shape, jnp.bfloat16), dma(LINE - 1), dma(LINE - 1))

    def targets(self):
        line, cross = self.place()
        return [lax.rem(line + step, LINE) for step in range(1, LINE)]

    def partners(self):
        line, cross = self.place()
        return [{"dp": other * self.cross + cross} for other in self.targets()]

    def begin(self):
        (x_ref,), (buf, send, recv) = self.ins_refs, self.scratch_refs
        line, cross = self.place()
        self.copies = [
            remote(
                x_ref.at[other], buf.at[i], send.at[i], recv.at[i], {"dp": other * self.cross + cross}
            )
            for i, other in enumerate(self.targets())
        ]
        for copy in self.copies:
            copy.start()

    def end(self):
        (x_ref,), (o_ref, square_ref) = self.ins_refs, self.outs_refs
        buf = self.scratch_refs[0]
        line, cross = self.place()
        for copy in self.copies:
            copy.wait()
        total = x_ref[line].astype(jnp.float32)
        for i in range(LINE - 1):
            total = total + buf[i].astype(jnp.float32)
        square_ref[...] = eight_rows(total * total)
        if self.turned:
            o_ref[...] = total.T
        elif self.slabs > 1:
            narrow = total.shape[1] // self.slabs
            for slab in range(self.slabs):
                o_ref[slab] = total[:, slab * narrow : (slab + 1) * narrow]
        else:
            o_ref[...] = total


class SumAll(Task):
    def __init__(self, block, keep):
        self.groups, self.width, self.keep = lax.axis_size("dp"), lax.axis_size("tensor"), keep
        rows, depth = block.shape
        self.narrow = narrow = depth // self.width
        kept = self.groups if keep else 1
        self.ins = (block,)
        self.outs = (shaped((kept, rows, depth), block.dtype),)
        near, far = dma(self.width), dma(self.groups)
        self.scratch = (
            pltpu.VMEM((self.width, rows, narrow), block.dtype),
            pltpu.VMEM((rows, narrow), block.dtype),
            pltpu.VMEM((self.groups, rows, narrow), block.dtype),
            pltpu.VMEM((kept, rows, narrow), block.dtype),
            near, near, far, far, near, near,
        )

    def mates(self):
        me = lax.axis_index("tensor")
        return [lax.rem(me + step, self.width) for step in range(1, self.width)]

    def peers(self):
        me = lax.axis_index("dp")
        return [lax.rem(me + step, self.groups) for step in range(1, self.groups)]

    def partners(self):
        return [{"tensor": mate} for mate in self.mates()] + [{"dp": peer} for peer in self.peers()]

    def lanes(self, owner):
        return pl.ds(pl.multiple_of(owner * self.narrow, self.narrow), self.narrow)

    def launch(self, copies):
        for copy in copies:
            copy.start()
        self.copies = copies

    def settle(self):
        for copy in self.copies:
            copy.wait()

    def begin(self):
        (x_ref,) = self.ins_refs
        part_buf, sems = self.scratch_refs[0], self.scratch_refs[4:]
        me = lax.axis_index("tensor")
        self.launch(
            [
                remote(
                    x_ref.at[:, self.lanes(mate)],
                    part_buf.at[me],
                    sems[0].at[i],
                    sems[1].at[i],
                    {"tensor": mate},
                )
                for i, mate in enumerate(self.mates())
            ]
        )
        part_buf[me] = x_ref[:, self.lanes(me)]

    def middle(self):
        (o_ref,) = self.outs_refs
        part_buf, sum_buf, all_buf, out_buf = self.scratch_refs[:4]
        sems = self.scratch_refs[4:]
        dp_me, me = lax.axis_index("dp"), lax.axis_index("tensor")
        self.settle()
        sum_buf[...] = jnp.sum(part_buf[...], axis=0)
        self.launch(
            [
                remote(sum_buf, all_buf.at[dp_me], sems[2].at[i], sems[3].at[i], {"dp": peer})
                for i, peer in enumerate(self.peers())
            ]
        )
        all_buf[dp_me] = sum_buf[...]
        self.settle()
        if self.keep:
            out_buf[...] = all_buf[...]
        else:
            out_buf[0] = jnp.sum(all_buf[...], axis=0)
        self.launch(
            [
                remote(
                    out_buf,
                    o_ref.at[:, :, self.lanes(me)],
                    sems[4].at[i],
                    sems[5].at[i],
                    {"tensor": mate},
                )
                for i, mate in enumerate(self.mates())
            ]
        )
        o_ref[:, :, self.lanes(me)] = out_buf[...]

    def end(self):
        self.settle()


Q_BLOCK = 256
K_BLOCK = 256


def split_pair(wide):
    half = wide.shape[0] // 2
    upper = lax.broadcasted_iota(jnp.int32, wide.shape, 0) < half
    zero = jnp.zeros_like(wide)
    return jnp.concatenate([jnp.where(upper, wide, zero), jnp.where(upper, zero, wide)], axis=1)


def stack_pair(tall):
    half = tall.shape[1] // 2
    left = lax.broadcasted_iota(jnp.int32, tall.shape, 1) < half
    zero = jnp.zeros_like(tall)
    return jnp.concatenate([jnp.where(left, tall, zero), jnp.where(left, zero, tall)], axis=0)


def join_pair(wide):
    depth, columns = wide.shape
    upper = lax.broadcasted_iota(jnp.int32, (depth, columns // 2), 0) < depth // 2
    return jnp.where(upper, wide[:, : columns // 2], wide[:, columns // 2 :])


def turn(tile):
    return tile.astype(jnp.float32).T.astype(jnp.bfloat16)


def block_span(index, size):
    return pl.ds(pl.multiple_of(index * size, size), size)


def attend_kernel(low_ref, high_ref, qkv_ref, seq_col_ref, seq_row_ref, out_ref, log_ref, value_turned, scores):
    slots, columns = out_ref.shape
    pairs = columns // 128
    q_blocks, k_blocks = slots // Q_BLOCK, slots // K_BLOCK

    def turn_values(b, carry):
        rows = block_span(b, K_BLOCK)
        for pair in range(pairs):
            value_turned[pl.ds(pair * 128, 128), rows] = turn(
                qkv_ref[rows, pl.ds(2 * columns + pair * 128, 128)]
            )
        return carry

    lax.fori_loop(0, k_blocks, turn_values, 0)

    def one_block(q_index, carry):
        q_rows = block_span(q_index, Q_BLOCK)
        lowest, highest = low_ref[q_index], high_ref[q_index]
        seq_row = seq_row_ref[0:1, q_rows]
        seq_pair = jnp.concatenate([seq_row, seq_row], axis=1)
        queries = [
            split_pair(
                (qkv_ref[q_rows, pl.ds(pair * 128, 128)].astype(jnp.float32) * HEAD ** (-0.5))
                .T.astype(jnp.bfloat16)
            )
            for pair in range(pairs)
        ]

        def score(k_index, tops):
            k_rows = block_span(k_index, K_BLOCK)
            same = seq_col_ref[k_rows, 0:1] == seq_pair
            later = []
            for pair in range(pairs):
                keys = qkv_ref[k_rows, pl.ds(columns + pair * 128, 128)]
                value = jnp.where(same, multiply_arrays(keys, queries[pair]), MASK_FILL)
                scores[pair, k_index - lowest] = value
                later.append(jnp.maximum(tops[pair], jnp.max(value, axis=0, keepdims=True)))
            return tuple(later)

        start = tuple(jnp.full((1, 2 * Q_BLOCK), MASK_FILL, jnp.float32) for _ in range(pairs))
        tops = lax.fori_loop(lowest, highest, score, start)

        def mix(k_index, state):
            k_rows = block_span(k_index, K_BLOCK)
            later = []
            for pair in range(pairs):
                total, mixed = state[pair]
                weights = jnp.exp(scores[pair, k_index - lowest] - tops[pair])
                total = total + jnp.sum(weights, axis=0, keepdims=True)
                mixed = mixed + multiply_arrays(
                    value_turned[pl.ds(pair * 128, 128), k_rows], weights.astype(jnp.bfloat16)
                )
                later.append((total, mixed))
            return tuple(later)

        blank = tuple(
            (jnp.zeros((1, 2 * Q_BLOCK), jnp.float32), jnp.zeros((128, 2 * Q_BLOCK), jnp.float32))
            for _ in range(pairs)
        )
        final = lax.fori_loop(lowest, highest, mix, blank)
        for pair in range(pairs):
            total, mixed = final[pair]
            out_ref[q_rows, pl.ds(pair * 128, 128)] = join_pair(mixed / total).T.astype(jnp.bfloat16)
            logs = tops[pair] + jnp.log(total)
            log_ref[pl.ds(2 * pair, 1), q_rows] = logs[:, :Q_BLOCK]
            log_ref[pl.ds(2 * pair + 1, 1), q_rows] = logs[:, Q_BLOCK:]
        return carry

    lax.fori_loop(0, q_blocks, one_block, 0)


def block_bounds(lengths, slots):
    ends = jnp.cumsum(lengths)
    starts = ends - lengths
    first = jnp.arange(slots // Q_BLOCK, dtype=jnp.int32) * Q_BLOCK
    last = first + Q_BLOCK - 1
    lowest = jnp.max(
        jnp.where(starts[None, :] <= first[:, None], starts[None, :], 0), axis=1
    )
    highest = jnp.min(jnp.where(ends[None, :] > last[:, None], ends[None, :], slots), axis=1)
    return (lowest // K_BLOCK, (highest + K_BLOCK - 1) // K_BLOCK)


REACH = (2 * MAXLEN - 2) // K_BLOCK + Q_BLOCK // K_BLOCK + 1


def in_scalars():
    return pl.BlockSpec(memory_space=pltpu.SMEM)


def attend(qkv_out, seq_ids, bounds):
    slots, columns = qkv_out.shape[0], qkv_out.shape[1] // 3
    pairs = columns // 128
    return pl.pallas_call(
        attend_kernel,
        out_shape=[
            jax.ShapeDtypeStruct((slots, columns), jnp.bfloat16),
            jax.ShapeDtypeStruct((8, slots), jnp.float32),
        ],
        in_specs=[in_scalars(), in_scalars()] + [in_vmem()] * 3,
        out_specs=[in_vmem()] * 2,
        scratch_shapes=[
            pltpu.VMEM((columns, slots), jnp.bfloat16),
            pltpu.VMEM((pairs, REACH, K_BLOCK, 2 * Q_BLOCK), jnp.float32),
        ],
        compiler_params=pltpu.CompilerParams(vmem_limit_bytes=20 * 1024 * 1024),
    )(bounds[0], bounds[1], qkv_out, seq_ids[:, None], jnp.broadcast_to(seq_ids[None], (8, slots)))


def attend_back_kernel(
    low_ref, high_ref, qkv_ref, grad_ref, log_ref, seq_col_ref, seq_row_ref, out_ref,
    key_turned, probs, prob_grads, key_sum, value_sum,
):
    slots, columns = grad_ref.shape
    pairs = columns // 128
    q_blocks, k_blocks = slots // Q_BLOCK, slots // K_BLOCK

    def turn_keys(b, carry):
        rows = block_span(b, K_BLOCK)
        for pair in range(pairs):
            key_turned[pl.ds(pair * 128, 128), rows] = turn(
                qkv_ref[rows, pl.ds(columns + pair * 128, 128)]
            )
        key_sum[rows] = jnp.zeros((K_BLOCK, columns), jnp.float32)
        value_sum[rows] = jnp.zeros((K_BLOCK, columns), jnp.float32)
        return carry

    lax.fori_loop(0, k_blocks, turn_keys, 0)

    def one_block(q_index, carry):
        q_rows = block_span(q_index, Q_BLOCK)
        lowest, highest = low_ref[q_index], high_ref[q_index]
        seq_row = seq_row_ref[0:1, q_rows]
        seq_pair = jnp.concatenate([seq_row, seq_row], axis=1)
        scaled, queries, grads, turned, logs = [], [], [], [], []
        for pair in range(pairs):
            plain = qkv_ref[q_rows, pl.ds(pair * 128, 128)].astype(jnp.float32) * HEAD ** (-0.5)
            scaled.append(stack_pair(plain.astype(jnp.bfloat16)))
            queries.append(split_pair(plain.T.astype(jnp.bfloat16)))
            grad = grad_ref[q_rows, pl.ds(pair * 128, 128)]
            grads.append(stack_pair(grad))
            turned.append(split_pair(turn(grad)))
            logs.append(
                jnp.concatenate(
                    [log_ref[pl.ds(2 * pair, 1), q_rows], log_ref[pl.ds(2 * pair + 1, 1), q_rows]],
                    axis=1,
                )
            )

        def look(k_index, inners):
            k_rows = block_span(k_index, K_BLOCK)
            same = seq_col_ref[k_rows, 0:1] == seq_pair
            later = []
            for pair in range(pairs):
                keys = qkv_ref[k_rows, pl.ds(columns + pair * 128, 128)]
                values = qkv_ref[k_rows, pl.ds(2 * columns + pair * 128, 128)]
                logits = jnp.where(same, multiply_arrays(keys, queries[pair]), MASK_FILL)
                weights = jnp.exp(logits - logs[pair])
                weight_grad = multiply_arrays(values, turned[pair])
                probs[pair, k_index - lowest] = weights
                prob_grads[pair, k_index - lowest] = weight_grad
                value_sum[k_rows, pl.ds(pair * 128, 128)] += multiply_arrays(
                    weights.astype(jnp.bfloat16), grads[pair]
                )
                later.append(
                    inners[pair] + jnp.sum(weights * weight_grad, axis=0, keepdims=True)
                )
            return tuple(later)

        start = tuple(jnp.zeros((1, 2 * Q_BLOCK), jnp.float32) for _ in range(pairs))
        inners = lax.fori_loop(lowest, highest, look, start)

        def push(k_index, sums):
            k_rows = block_span(k_index, K_BLOCK)
            later = []
            for pair in range(pairs):
                slope = (
                    probs[pair, k_index - lowest]
                    * (prob_grads[pair, k_index - lowest] - inners[pair])
                ).astype(jnp.bfloat16)
                key_sum[k_rows, pl.ds(pair * 128, 128)] += multiply_arrays(slope, scaled[pair])
                later.append(
                    sums[pair] + multiply_arrays(key_turned[pl.ds(pair * 128, 128), k_rows], slope)
                )
            return tuple(later)

        blank = tuple(jnp.zeros((128, 2 * Q_BLOCK), jnp.float32) for _ in range(pairs))
        sums = lax.fori_loop(lowest, highest, push, blank)
        for pair in range(pairs):
            out_ref[q_rows, pl.ds(pair * 128, 128)] = (
                (join_pair(sums[pair]) * HEAD ** (-0.5)).T.astype(jnp.bfloat16)
            )
        return carry

    lax.fori_loop(0, q_blocks, one_block, 0)
    out_ref[:, columns : 2 * columns] = key_sum[...].astype(jnp.bfloat16)
    out_ref[:, 2 * columns :] = value_sum[...].astype(jnp.bfloat16)


def attend_back(qkv_out, attn_grad, log_total, seq_ids, bounds):
    slots, columns = attn_grad.shape
    pairs = columns // 128
    window = pltpu.VMEM((pairs, REACH, K_BLOCK, 2 * Q_BLOCK), jnp.float32)
    return pl.pallas_call(
        attend_back_kernel,
        out_shape=jax.ShapeDtypeStruct(qkv_out.shape, jnp.bfloat16),
        in_specs=[in_scalars(), in_scalars()] + [in_vmem()] * 5,
        out_specs=in_vmem(),
        scratch_shapes=[
            pltpu.VMEM((columns, slots), jnp.bfloat16),
            window,
            window,
            pltpu.VMEM((slots, columns), jnp.float32),
            pltpu.VMEM((slots, columns), jnp.float32),
        ],
        compiler_params=pltpu.CompilerParams(vmem_limit_bytes=36 * 1024 * 1024),
    )(
        bounds[0],
        bounds[1],
        qkv_out,
        attn_grad,
        log_total,
        seq_ids[:, None],
        jnp.broadcast_to(seq_ids[None], (8, slots)),
    )


def gelu_parts(upper):
    distance = jnp.abs(upper) * 0.7071067811865476
    step = 1.0 / (1.0 + 0.3275911 * distance)
    bell = jnp.exp(-distance * distance)
    series = step * (
        0.254829592
        + step * (-0.284496736 + step * (1.421413741 + step * (-1.453152027 + step * 1.061405429)))
    )
    tail = 0.5 * series * bell
    share = jnp.where(upper >= 0.0, 1.0 - tail, tail)
    return (upper * share, share + upper * (bell * 0.3989422804014327))


def expand_kernel(rows_ref, weight_ref, bias_ref, hidden_ref, slope_ref):
    units = weight_ref.shape[1]
    rows = rows_ref[...]
    for first in range(0, units, 256):
        lanes = pl.ds(first, 256)
        upper = multiply_arrays(rows, weight_ref[:, lanes]) + bias_ref[:, lanes]
        hidden, slope = gelu_parts(upper)
        hidden_ref[:, lanes] = hidden.astype(jnp.bfloat16)
        slope_ref[:, lanes] = slope


def expand(rows, weight, bias):
    slots, depth = rows.shape
    units = weight.shape[1]
    tall = 256
    return pl.pallas_call(
        expand_kernel,
        grid=(slots // tall,),
        out_shape=[shaped((slots, units), jnp.bfloat16), shaped((slots, units), jnp.float32)],
        in_specs=[
            pl.BlockSpec((tall, depth), lambda i: (i, 0)),
            pl.BlockSpec((depth, units), lambda i: (0, 0)),
            pl.BlockSpec((1, units), lambda i: (0, 0)),
        ],
        out_specs=[
            pl.BlockSpec((tall, units), lambda i: (i, 0)),
            pl.BlockSpec((tall, units), lambda i: (i, 0)),
        ],
        compiler_params=pltpu.CompilerParams(vmem_limit_bytes=16 * 1024 * 1024),
    )(rows, weight, bias)


EMBED_ROWS = 128
EMBED_PART = 16
MARGIN = 256


def embed_kernel(
    start_ref, span_ref, own_ref, tok_ref, pos_ref, seq_ref, row_ref, low_ref, emb_ref, norm_ref,
    padded, placed, normed,
):
    slots = tok_ref.shape[0]
    blocks, own_blocks = slots // EMBED_ROWS, emb_ref.shape[0] // EMBED_ROWS
    padded[pl.ds(MARGIN, pos_ref.shape[0])] = pos_ref[...]
    gain, shift = row_ref[0:1], row_ref[3:4]

    def one_block(b, carry):
        rows = block_span(b, EMBED_ROWS)
        seq = seq_ref[rows, 0:1]

        def pick(s, state):
            first = MARGIN + 2 + b * EMBED_ROWS - start_ref[s]
            base = first // 8
            shift = EMBED_PART + 8 - (first - base * 8)
            for at in range(0, EMBED_ROWS, EMBED_PART):
                window = padded[pl.ds(pl.multiple_of(base * 8 + at, 8), EMBED_PART + 8)]
                window = pltpu.roll(window, shift, 0)[:EMBED_PART]
                local = pl.ds(at, EMBED_PART)
                placed[local] = jnp.where(seq[at : at + EMBED_PART] == s, window, placed[local])
            return state

        lax.fori_loop(span_ref[0, b], span_ref[1, b], pick, 0)
        own = b - own_ref[0] * own_blocks
        kept = (own >= 0) & (own < own_blocks)
        own_first = jnp.where(kept, own, 0) * EMBED_ROWS
        for at in range(0, EMBED_ROWS, EMBED_PART):
            local = pl.ds(pl.multiple_of(b * EMBED_ROWS + at, EMBED_PART), EMBED_PART)
            emb = tok_ref[local].astype(jnp.float32) + placed[pl.ds(at, EMBED_PART)]
            norm = norm_rows(emb, gain, shift)
            low_ref[local] = norm.astype(jnp.bfloat16)
            placed[pl.ds(at, EMBED_PART)] = emb
            normed[pl.ds(at, EMBED_PART)] = norm

        @pl.when(kept)
        def _():
            own_rows = pl.ds(pl.multiple_of(own_first, EMBED_ROWS), EMBED_ROWS)
            emb_ref[own_rows] = placed[...]
            norm_ref[own_rows] = normed[...]

        return carry

    lax.fori_loop(0, blocks, one_block, 0)


def embed(tok_all, pos_full, seq_ids, lengths, row_params):
    slots, depth = tok_all.shape
    own = slots // lax.axis_size("tensor")
    ends = jnp.cumsum(lengths)
    starts = ends - lengths
    first = jnp.arange(slots // EMBED_ROWS, dtype=jnp.int32) * EMBED_ROWS
    spans = jnp.stack(
        [
            jnp.sum((ends[None, :] <= first[:, None]).astype(jnp.int32), axis=1),
            jnp.sum((starts[None, :] < first[:, None] + EMBED_ROWS).astype(jnp.int32), axis=1),
        ]
    )
    return pl.pallas_call(
        embed_kernel,
        out_shape=[
            shaped((slots, depth), jnp.bfloat16),
            shaped((own, depth), jnp.float32),
            shaped((own, depth), jnp.float32),
        ],
        in_specs=[in_scalars()] * 3 + [in_vmem()] * 4,
        out_specs=[in_vmem()] * 3,
        scratch_shapes=[
            pltpu.VMEM((MARGIN + MAXLEN + EMBED_ROWS + 24, depth), jnp.float32),
            pltpu.VMEM((EMBED_ROWS, depth), jnp.float32),
            pltpu.VMEM((EMBED_ROWS, depth), jnp.float32),
        ],
        compiler_params=pltpu.CompilerParams(vmem_limit_bytes=28 * 1024 * 1024),
    )(
        starts,
        spans,
        lax.axis_index("tensor").astype(jnp.int32)[None],
        tok_all,
        pos_full,
        seq_ids[:, None],
        row_params,
    )


SCATTER_ROWS = 512


def scatter_kernel(index_ref, rows_ref, grad_ref, square_ref):
    first = pl.program_id(0) * SCATTER_ROWS
    slots = index_ref.shape[1]
    here = (
        lax.broadcasted_iota(jnp.int32, (SCATTER_ROWS, slots), 0) + first == index_ref[...]
    ).astype(jnp.float32)
    grad = multiply_arrays(here.astype(jnp.bfloat16), rows_ref[...])
    grad_ref[...] = grad

    @pl.when(pl.program_id(0) == 0)
    def _():
        square_ref[...] = jnp.zeros_like(square_ref)

    square_ref[...] += eight_rows(grad * grad)


def scatter_rows(index, rows, height):
    slots, width = rows.shape
    return pl.pallas_call(
        scatter_kernel,
        grid=(pl.cdiv(height, SCATTER_ROWS),),
        out_shape=[shaped((height, width), jnp.float32), shaped((8, width), jnp.float32)],
        in_specs=[
            pl.BlockSpec((1, slots), lambda i: (0, 0)),
            pl.BlockSpec((slots, width), lambda i: (0, 0)),
        ],
        out_specs=[
            pl.BlockSpec((SCATTER_ROWS, width), lambda i: (i, 0)),
            pl.BlockSpec((8, width), lambda i: (0, 0)),
        ],
        compiler_params=pltpu.CompilerParams(vmem_limit_bytes=20 * 1024 * 1024),
    )(index[None], rows)


def layer_forward(embedded, seq_ids, bounds, members, counts, row_params, col_local, layer_mats):
    first_moment_all, emb_rows, norm_first = embedded
    qkv_full, out_full, up_half, down_low = layer_mats
    col_width = col_local.shape[1]
    qkv_bias = jnp.concatenate([col_local[0], jnp.zeros_like(col_local[0]), col_local[1]])
    qkv_out = (multiply_arrays(first_moment_all, qkv_full) + qkv_bias).astype(jnp.bfloat16)
    attn_low, log_total = attend(qkv_out, seq_ids, bounds)
    first_back = jnp.einsum("tc,dc->td", attn_low, out_full, preferred_element_type=jnp.float32)
    second_all, first_sum, norm_second, up_full, _, down_full = exchange(
        5,
        FoldNormSpread(first_back.astype(jnp.bfloat16), norm_first, row_params),
        SpreadCross(up_half),
        spread_grid(down_low),
    )
    up_full = up_full.reshape(D, -1)
    down_full = down_full.reshape(D, -1)
    hidden_low, slope = expand(second_all, up_full, col_local[2:].reshape(1, -1))
    second_back = jnp.einsum("tf,df->td", hidden_low, down_full, preferred_element_type=jnp.float32)
    second_sum, pooled = exchange(
        7, FoldPool(second_back.astype(jnp.bfloat16), norm_second, members, counts, row_params)
    )
    saved_vals = (
        emb_rows,
        first_moment_all,
        qkv_out,
        log_total,
        attn_low,
        first_sum,
        second_all,
        slope,
        hidden_low,
        second_sum,
    )
    return (pooled, saved_vals, (qkv_full, out_full, up_full, down_full))


def turned_grad(left_all, right_all):
    grad = jnp.einsum("td,tc->dc", left_all, right_all, preferred_element_type=jnp.float32)
    groups = lax.axis_size("dp")
    return grad.astype(jnp.bfloat16).reshape(groups, grad.shape[0] // groups, grad.shape[1])


def layer_backward(pooled_grad, counts, members, seq_ids, bounds, row_params, layer_mats, saved_vals):
    qkv_full, out_full, up_full, down_full = layer_mats
    (
        emb_rows,
        first_moment_all,
        qkv_out,
        log_total,
        attn_low,
        first_sum,
        second_all,
        slope,
        hidden_low,
        second_sum,
    ) = saved_vals
    col_width = out_full.shape[1]
    mixed_all, grad_second, side_c = exchange(
        10, PullSpread(pooled_grad, counts, jnp.tile(members.T, (1, 3)), second_sum, row_params)
    )
    down_grad = turned_grad(mixed_all, hidden_low)
    up_low = (multiply_arrays(mixed_all, down_full) * slope).astype(jnp.bfloat16)
    up_grad = turned_grad(second_all, up_low)
    second_back = jnp.einsum(
        "tf,df->td", up_low, up_full, preferred_element_type=jnp.float32
    ).astype(jnp.bfloat16)
    branch_all, grad_first, side_b, _, down_sum, down_squares, up_half = exchange(
        11,
        FoldPullSpread(second_back, grad_second, first_sum, row_params),
        reduce_grid(down_grad, turned=True),
        Later(ReduceCross(up_grad)),
    )
    out_grad = turned_grad(branch_all, attn_low)
    attn_grad = multiply_arrays(branch_all, out_full).astype(jnp.bfloat16)
    qkv_low = attend_back(qkv_out, attn_grad, log_total, seq_ids, bounds)
    qkv_grad = turned_grad(first_moment_all, qkv_low)
    first_back = jnp.einsum(
        "tc,dc->td", qkv_low, qkv_full, preferred_element_type=jnp.float32
    ).astype(jnp.bfloat16)
    cols_grad, side_a, up_sum, up_squares, _, out_sum, out_squares, _, qkv_sum, qkv_squares = exchange(
        13,
        FoldPullSwap(first_back, grad_first, emb_rows, row_params),
        ReduceLine(up_half),
        reduce_grid(out_grad, turned=True),
        reduce_grid(qkv_grad, slabs=3),
    )
    qkv_cols = jnp.sum(qkv_low.astype(jnp.float32), axis=0).reshape(3, col_width)
    up_cols = jnp.sum(up_low.astype(jnp.float32), axis=0).reshape(-1, col_width)
    col_grad = jnp.concatenate([qkv_cols[0:1], qkv_cols[2:3], up_cols], axis=0)
    row_grad = jnp.concatenate(
        [
            side_a[0:1],
            side_b[0:1],
            side_c[0:1],
            side_a[1:2],
            side_b[1:2],
            side_c[1:2],
            side_b[2:3],
            side_c[2:3],
        ]
    )
    return (
        cols_grad,
        (qkv_sum, out_sum, up_sum, down_sum),
        (qkv_squares, out_squares, up_squares + down_squares),
        col_grad,
        row_grad,
    )


def plan_kernel(capacity, vocab_local, groups, perm_ref, low_ref, high_ref, pair_ref, slot_ref, ask_ref, id_buf, own_buf):
    slots = perm_ref.shape[1]
    table_rows = low_ref.shape[1]
    block = 128
    blocks = slots // block
    perm = perm_ref[...]
    high_part = perm // 128
    low_part = perm - high_part * 128
    chooser = (lax.broadcasted_iota(jnp.int32, (table_rows, slots), 0) == high_part).astype(
        jnp.float32
    ).astype(jnp.bfloat16)
    value = multiply_arrays(low_ref[...], chooser) + 256.0 * multiply_arrays(high_ref[...], chooser)
    lane_match = lax.broadcasted_iota(jnp.int32, (128, slots), 0) == low_part
    ids = jnp.sum(jnp.where(lane_match, value, 0.0), axis=0, keepdims=True)
    for b in range(blocks):
        id_buf[pl.ds(b * block, block), :] = jnp.broadcast_to(
            ids[:, b * block : (b + 1) * block], (block, block)
        ).T
    place = lax.broadcasted_iota(jnp.int32, (1, slots), 1).astype(jnp.float32)
    rows = lax.broadcasted_iota(jnp.int32, (block, 1), 0).astype(jnp.float32)

    def earliest(b, best):
        column = id_buf[pl.ds(pl.multiple_of(b * block, block), block), 0:1]
        index = rows + (b * block).astype(jnp.float32)
        found = jnp.where(column == ids, index, 1e9)
        return jnp.minimum(best, jnp.min(found, axis=0, keepdims=True))

    least = lax.fori_loop(0, blocks, earliest, jnp.full((1, slots), 1e9, jnp.float32))
    first = least == place
    owner = jnp.zeros((1, slots), jnp.float32)
    for index in range(1, groups):
        owner = owner + jnp.where(ids >= float(index * vocab_local), 1.0, 0.0)
    owner_rows = lax.broadcasted_iota(jnp.int32, (groups, slots), 0).astype(jnp.float32)
    marks = jnp.where(first & (owner == owner_rows), 1.0, 0.0)
    upper = jnp.where(
        lax.broadcasted_iota(jnp.int32, (block, block), 0)
        < lax.broadcasted_iota(jnp.int32, (block, block), 1),
        1.0,
        0.0,
    ).astype(jnp.bfloat16)
    running = jnp.zeros((groups, 1), jnp.float32)
    pieces = []
    for b in range(blocks):
        part = marks[:, b * block : (b + 1) * block]
        pieces.append(multiply_arrays(part.astype(jnp.bfloat16), upper) + running)
        running = running + jnp.sum(part, axis=1, keepdims=True)
    before = jnp.concatenate(pieces, axis=1)
    rank = jnp.sum(marks * before, axis=0, keepdims=True)
    own_slot = jnp.where(first & (rank < float(capacity)), owner * float(capacity) + rank, -1.0)
    for b in range(blocks):
        own_buf[pl.ds(b * block, block), :] = jnp.broadcast_to(
            own_slot[:, b * block : (b + 1) * block], (block, block)
        ).T
    list_rows = -(-capacity // 128)
    stride = list_rows * 128
    width = groups * stride
    index = lax.broadcasted_iota(jnp.int32, (1, width), 1)
    target = (index // stride * capacity + lax.rem(index, stride)).astype(jnp.float32)
    target = jnp.where(lax.rem(index, stride) < capacity, target, -2.0)

    def settle(b, carry):
        slot, listed = carry
        window = pl.ds(pl.multiple_of(b * block, block), block)
        column, slot_column = id_buf[window, 0:1], own_buf[window, 0:1]
        slot = jnp.maximum(
            slot, jnp.max(jnp.where(column == ids, slot_column, -1.0), axis=0, keepdims=True)
        )
        listed = jnp.maximum(
            listed, jnp.max(jnp.where(slot_column == target, column, -1.0), axis=0, keepdims=True)
        )
        return (slot, listed)

    slot, listed = lax.fori_loop(
        0,
        blocks,
        settle,
        (jnp.full((1, slots), -1.0, jnp.float32), jnp.full((1, width), -1.0, jnp.float32)),
    )
    slot_ref[...] = slot.astype(jnp.int32)
    listed = listed.astype(jnp.int32)
    most = jnp.max(running, axis=0, keepdims=True).astype(jnp.int32)
    for group in range(groups):
        for row in range(list_rows):
            first_lane = group * stride + row * 128
            ask_ref[group, row : row + 1] = listed[:, first_lane : first_lane + 128]
        ask_ref[group, list_rows : list_rows + 1] = pair_ref[...]
        ask_ref[group, list_rows + 1 :] = jnp.broadcast_to(most, (7 - list_rows, 128))


def make_plan(perm, all_ids, pair_row, capacity, vocab_local, groups):
    slots = perm.shape[0]
    table = all_ids.reshape(-1, 128).T
    high = table // 256
    low = table - high * 256
    return pl.pallas_call(
        partial(plan_kernel, capacity, vocab_local, groups),
        out_shape=[
            jax.ShapeDtypeStruct((1, slots), jnp.int32),
            jax.ShapeDtypeStruct((groups, 8, 128), jnp.int32),
        ],
        in_specs=[in_vmem()] * 4,
        out_specs=[in_vmem()] * 2,
        scratch_shapes=[pltpu.VMEM((slots, 128), jnp.float32), pltpu.VMEM((slots, 128), jnp.float32)],
        compiler_params=pltpu.CompilerParams(vmem_limit_bytes=16 * 1024 * 1024),
    )(perm[None], low.astype(jnp.bfloat16), high.astype(jnp.bfloat16), pair_row)


def loss_kernel(pooled_ref, head_ref, pair_ref, loss_ref, low_ref, grad_ref, back_ref):
    total = pooled_ref.shape[0]
    low = pooled_ref[...].astype(jnp.bfloat16)
    low_ref[...] = low
    head_low = head_ref[...].astype(jnp.bfloat16)
    vectors = multiply_arrays(low, head_low)
    depth = vectors.shape[1]
    lane = lax.broadcasted_iota(jnp.int32, vectors.shape, 1)
    across = lax.broadcasted_iota(jnp.int32, (total, total), 1)
    diagonal = lax.broadcasted_iota(jnp.int32, (total, total), 0) == across
    chosen = across == pair_ref[...]
    loss = jnp.zeros((1, 1), jnp.float32)
    grads = jnp.zeros(vectors.shape, jnp.float32)

    def exact(left, right, dims):
        return lax.dot_general(
            left, right, (dims, ((), ())), precision=HIGHEST_MODE, preferred_element_type=jnp.float32
        )

    for fraction in (16, 4, 1):
        prefix = jnp.where(lane < depth // fraction, vectors, 0.0)
        inverse = lax.rsqrt(jnp.sum(prefix * prefix, axis=1, keepdims=True) + 1e-06)
        unit = prefix * inverse
        logits = exact(unit, unit, ((1,), (1,))) / LOGIT_DIVISOR
        logits = jnp.where(diagonal, MASK_FILL, logits)
        top = jnp.max(logits, axis=1, keepdims=True)
        weights = jnp.exp(logits - top)
        weight_sum = jnp.sum(weights, axis=1, keepdims=True)
        positive = jnp.sum(jnp.where(chosen, logits, 0.0), axis=1, keepdims=True)
        loss = loss + jnp.sum(jnp.log(weight_sum) + top - positive, keepdims=True)
        pull = weights / weight_sum - jnp.where(chosen, 1.0, 0.0)
        unit_grad = (exact(pull, unit, ((1,), (0,))) + exact(pull, unit, ((0,), (0,)))) / LOGIT_DIVISOR
        unit_grad = jnp.where(lane < depth // fraction, unit_grad, 0.0)
        inner = jnp.sum(unit_grad * prefix, axis=1, keepdims=True)
        grads = grads + inverse * unit_grad - prefix * (inverse * inverse * inverse * inner)
    low_wide = low.astype(jnp.float32)
    head_squares = jnp.sum(
        exact(low_wide, low_wide, ((1,), (1,))) * exact(grads, grads, ((1,), (1,))), keepdims=True
    )
    line = lax.broadcasted_iota(jnp.int32, loss_ref.shape, 0)
    loss_ref[...] = jnp.where(line == 0, loss, head_squares)
    grad_ref[...] = grads
    pieces, rest = [], grads
    for _ in range(3):
        pieces.append(rest.astype(jnp.bfloat16))
        rest = rest - pieces[-1].astype(jnp.float32)
    product = lax.dot_general(
        jnp.concatenate(pieces, axis=0),
        head_low,
        (((1,), (1,)), ((), ())),
        preferred_element_type=jnp.float32,
    )
    back_ref[...] = product[:total] + product[total : 2 * total] + product[2 * total :]


def contrast_step(pooled, head_weight, pairs):
    total, depth = pooled.shape
    return pl.pallas_call(
        loss_kernel,
        out_shape=[
            jax.ShapeDtypeStruct((8, 128), jnp.float32),
            jax.ShapeDtypeStruct((total, depth), jnp.bfloat16),
            jax.ShapeDtypeStruct((total, depth), jnp.float32),
            jax.ShapeDtypeStruct((total, depth), jnp.float32),
        ],
        in_specs=[in_vmem()] * 3,
        out_specs=[in_vmem()] * 4,
        compiler_params=pltpu.CompilerParams(vmem_limit_bytes=20 * 1024 * 1024),
    )(pooled, head_weight, pairs[:, None])


CAPACITY = 192


def body(
    token_ids,
    slot_perm,
    seq_lengths,
    pair_index,
    tok_table,
    tok_first,
    tok_second,
    pos_table,
    pos_first,
    pos_second,
    query_key_value_weight,
    qkv_first,
    qkv_second,
    out_weight,
    out_first,
    out_second,
    up_weight,
    up_first,
    up_second,
    down_weight,
    down_first,
    down_second,
    head_weight,
    head_first,
    head_second,
    col_bias,
    col_first,
    col_second,
    row_params,
    row_first,
    row_second,
):
    groups = lax.axis_size("dp")
    tensor_count = lax.axis_size("tensor")
    group_index = lax.axis_index("dp")
    tensor_index = lax.axis_index("tensor")
    tok_dev = token_ids.shape[0]
    tok_grp = tok_dev * tensor_count
    col_width = pos_table.shape[1]
    vocab_local = tok_table.shape[0]
    column_start = tensor_index * col_width
    anchors = pair_index.shape[0]
    id_rows = tok_dev // 128
    pair_row = jnp.pad(pair_index, (0, 128 - anchors))[None]
    qkv_low = jnp.concatenate(
        [query_key_value_weight[:, third] for third in range(3)], axis=1
    ).astype(jnp.bfloat16)
    out_low = out_weight.T.astype(jnp.bfloat16)
    up_low = up_weight.astype(jnp.bfloat16).reshape(qkv_low.shape[0], -1)
    down_low = down_weight.reshape(-1, down_weight.shape[2]).T.astype(jnp.bfloat16)
    half = qkv_low.shape[0] // 2
    gathered, perms, qkv_first_half = exchange(
        1,
        GatherAll(token_ids.reshape(id_rows, 128)),
        Gather(slot_perm.reshape(id_rows, 128), "tensor"),
        SpreadLine(qkv_low[:half]),
    )
    all_ids = gathered.reshape(-1)
    own_perm = perms.reshape(-1)
    slot, request = make_plan(own_perm, all_ids, pair_row, CAPACITY, vocab_local, groups)
    slot = slot[0]
    list_rows = -(-CAPACITY // 128)
    asked = exchange(2, Swap(request, "dp"))
    pairs = asked[:, list_rows, :anchors].reshape(-1)
    overflow = jnp.max(asked[:, list_rows + 1]) > CAPACITY
    offset = group_index * vocab_local
    asked_rows = asked[:, :list_rows].reshape(groups, -1)[:, :CAPACITY].reshape(-1) - offset
    asked_safe = jnp.clip(asked_rows, 0, vocab_local - 1)
    sent_rows = jnp.take(tok_table, asked_safe, axis=0).astype(jnp.bfloat16)
    got_rows, pos_full, qkv_second_half = exchange(
        3,
        Swap(sent_rows.reshape(groups, CAPACITY, col_width), "dp"),
        Spread(pos_table, columns=True, chunks=1),
        SpreadLine(qkv_low[half:]),
    )
    got_rows = got_rows.reshape(-1, col_width)

    def chooser(slots):
        places = jnp.arange(groups * CAPACITY, dtype=jnp.int32)
        return (slots[:, None] == places[None, :]).astype(jnp.bfloat16)

    lengths = seq_lengths[0]
    seq_ids, positions, member = seq_layout(lengths, tok_grp)
    bounds = block_bounds(lengths, tok_grp)

    def every_slot_id():
        every_perm = lax.all_gather(slot_perm, ("dp", "tensor"), axis=0, tiled=True)
        return jnp.take(all_ids, every_perm, axis=0)

    def spread_wide():
        wanted = every_slot_id() - offset
        inside = (wanted >= 0) & (wanted < vocab_local)
        picked = jnp.take(
            tok_table.astype(jnp.bfloat16), jnp.clip(wanted, 0, vocab_local - 1), axis=0
        )
        return lax.psum_scatter(
            jnp.where(inside[:, None], picked, jnp.zeros((), jnp.bfloat16)),
            "dp",
            scatter_dimension=0,
            tiled=True,
        )

    tok_cols = lax.cond(
        overflow,
        spread_wide,
        lambda: multiply_arrays(chooser(slot), got_rows).astype(jnp.bfloat16),
    )
    tok_all, _, out_full, qkv_full, up_half = exchange(
        4,
        Spread(tok_cols, columns=True),
        spread_grid(out_low),
        SpreadCross(qkv_first_half, qkv_second_half),
        SpreadLine(up_low),
    )
    layer_mats = (qkv_full.reshape(D, -1), out_full.reshape(D, -1), up_half, down_low)
    embedded = embed(tok_all, pos_full, seq_ids, lengths, row_params)
    members = lax.dynamic_slice_in_dim(member, tensor_index * tok_dev, tok_dev, 0).T.astype(
        jnp.bfloat16
    )
    counts = lengths.astype(jnp.float32)[:, None]
    pooled, saved_vals, layer_mats = layer_forward(
        embedded, seq_ids, bounds, members, counts, row_params, col_bias, layer_mats
    )
    loss_out, pooled_low, vec_grad, pooled_grad = contrast_step(
        pooled.reshape(-1, D), head_weight, pairs
    )
    head_sum = exact_multiply(pooled_low.astype(jnp.float32).T, vec_grad)
    cols_grad, sums, grid_squares, col_grad, row_grad = layer_backward(
        pooled_grad, counts, members, seq_ids, bounds, row_params, layer_mats, saved_vals
    )
    qkv_sum, out_sum, up_sum, down_sum = sums
    qkv_squares, out_squares, wide_squares = grid_squares
    cols_grad = cols_grad.reshape(tok_grp, col_width)
    pos_pick = (
        jnp.arange(pos_table.shape[0], dtype=jnp.int32)[:, None] == positions[None, :]
    ).astype(jnp.bfloat16)
    pos_grad = multiply_arrays(pos_pick, cols_grad)
    shared = jnp.concatenate([pos_grad, col_grad], axis=0)
    shared_rows = -(-shared.shape[0] // (16 * groups)) * 16
    shared = jnp.pad(shared, ((0, shared_rows * groups - shared.shape[0]), (0, 0)))
    merged = jnp.einsum(
        "kn,kc->nc",
        chooser(lax.optimization_barrier(slot)),
        cols_grad,
        preferred_element_type=jnp.float32,
    )
    back_rows, _, shared_own, shared_squares = exchange(
        15,
        Swap(merged.astype(jnp.bfloat16).reshape(groups, CAPACITY, col_width), "dp"),
        reduce_grid(shared.astype(jnp.bfloat16).reshape(groups, shared_rows, col_width)),
    )

    def add_wide():
        wanted = every_slot_id() - offset
        inside = (wanted >= 0) & (wanted < vocab_local)
        grad = (
            jnp.zeros(tok_table.shape, jnp.float32)
            .at[jnp.clip(wanted, 0, vocab_local - 1)]
            .add(
                jnp.where(
                    inside[:, None],
                    lax.all_gather(cols_grad, "dp", axis=0, tiled=True).astype(jnp.float32),
                    0.0,
                )
            )
        )
        squares = jnp.sum(grad * grad, axis=0, keepdims=True)
        return (grad, jnp.pad(squares, ((0, 7), (0, 0))))

    tok_grad, tok_squares = lax.cond(
        overflow,
        add_wide,
        lambda: tuple(scatter_rows(asked_rows, back_rows.reshape(-1, col_width), vocab_local)),
    )
    up_grad = up_sum.reshape(up_weight.shape)
    down_grad = down_sum.reshape(down_weight.shape)

    def widen(*parts):
        joined = jnp.concatenate(parts, axis=1)
        return jnp.pad(joined, ((0, 0), (0, D - joined.shape[1])))

    square_rows = (
        widen(wide_squares)
        + widen(qkv_squares, out_squares)
        + widen(tok_squares, shared_squares)
    )
    row_block = jnp.concatenate([row_grad, square_rows], axis=0)
    row_total, shared_sum = exchange(16, SumAll(row_block, False), GatherGrid(shared_own.astype(jnp.bfloat16)))
    row_total = row_total[0]
    shared_sum = shared_sum.reshape(-1, col_width).astype(jnp.float32)
    pos_own = shared_sum[: pos_table.shape[0]]
    col_own = shared_sum[pos_table.shape[0] : pos_table.shape[0] + col_bias.shape[0]]
    row_sum = row_total[:8]
    squares = jnp.sum(row_total[8:]) + jnp.sum(row_sum * row_sum) + loss_out[1, 0]
    grad_norm = jnp.sqrt(squares)
    clip_scale = jnp.minimum(1.0, CLIP_NORM / (grad_norm + 1e-06))
    tok_new = adam_step(
        tok_table, tok_first, tok_second, tok_grad * clip_scale, RATE_MATRIX, DECAY_RATE
    )
    pos_new = adam_step(
        pos_table, pos_first, pos_second, pos_own * clip_scale, RATE_MATRIX, DECAY_RATE
    )
    qkv_new = adam_step(
        query_key_value_weight.swapaxes(0, 1),
        qkv_first.swapaxes(0, 1),
        qkv_second.swapaxes(0, 1),
        qkv_sum * clip_scale,
        RATE_MATRIX,
        DECAY_RATE,
    )
    qkv_new = tuple(item.swapaxes(0, 1) for item in qkv_new)
    out_new = adam_step(
        out_weight, out_first, out_second, out_sum * clip_scale, RATE_MATRIX, DECAY_RATE
    )
    up_new = adam_step(
        up_weight, up_first, up_second, up_grad * clip_scale, RATE_MATRIX, DECAY_RATE
    )
    down_new = adam_step(
        down_weight, down_first, down_second, down_grad * clip_scale, RATE_MATRIX, DECAY_RATE
    )
    head_new = adam_step(
        head_weight, head_first, head_second, head_sum * clip_scale, RATE_MATRIX, DECAY_RATE
    )
    col_new = adam_step(col_bias, col_first, col_second, col_own * clip_scale, RATE_VECTOR, 0.0)
    row_new = adam_step(row_params, row_first, row_second, row_sum * clip_scale, RATE_VECTOR, 0.0)
    return (loss_out[0, 0], grad_norm) + tok_new + pos_new + qkv_new + out_new + up_new + down_new + head_new + col_new + row_new


def solution(mesh):
    placed = (
        P(("dp", "tensor")),
        P(("dp", "tensor")),
        P("dp", None),
        P("dp"),
        P("dp", "tensor"),
        P("dp", "tensor"),
        P("dp", "tensor"),
        P(None, "tensor"),
        P(None, "tensor"),
        P(None, "tensor"),
        P("dp", None, "tensor"),
        P("dp", None, "tensor"),
        P("dp", None, "tensor"),
        P("tensor", "dp"),
        P("tensor", "dp"),
        P("tensor", "dp"),
        P("dp", None, "tensor"),
        P("dp", None, "tensor"),
        P("dp", None, "tensor"),
        P(None, "tensor", "dp"),
        P(None, "tensor", "dp"),
        P(None, "tensor", "dp"),
        P(),
        P(),
        P(),
        P(None, "tensor"),
        P(None, "tensor"),
        P(None, "tensor"),
        P(),
        P(),
        P(),
    )
    return jax.shard_map(
        body,
        mesh=mesh,
        in_specs=placed,
        out_specs=(
            P(),
            P(),
            P("dp", "tensor"),
            P("dp", "tensor"),
            P("dp", "tensor"),
            P(None, "tensor"),
            P(None, "tensor"),
            P(None, "tensor"),
            P("dp", None, "tensor"),
            P("dp", None, "tensor"),
            P("dp", None, "tensor"),
            P("tensor", "dp"),
            P("tensor", "dp"),
            P("tensor", "dp"),
            P("dp", None, "tensor"),
            P("dp", None, "tensor"),
            P("dp", None, "tensor"),
            P(None, "tensor", "dp"),
            P(None, "tensor", "dp"),
            P(None, "tensor", "dp"),
            P(),
            P(),
            P(),
            P(None, "tensor"),
            P(None, "tensor"),
            P(None, "tensor"),
            P(),
            P(),
            P(),
        ),
        check_vma=False,
    )
```

```python
from functools import partial

import jax
import jax.numpy as jnp
from jax import lax
from jax.experimental import pallas as pl
from jax.experimental.pallas import tpu as pltpu
from jax.sharding import PartitionSpec as P

D = 1024
HEAD = 64
MAXLEN = 512
STEP = 10


HIGHEST_MODE = lax.Precision.HIGHEST
LN_EPS = 1e-05
LOGIT_DIVISOR = 0.05
CLIP_NORM = 0.25
BETA_FIRST = 0.9
BETA_SECOND = 0.999
ADAM_EPS = 1e-08
RATE_MATRIX = 0.05
RATE_VECTOR = 0.5
DECAY_RATE = 0.01
MASK_FILL = -1e30


def multiply_arrays(left_mat, right_mat):
    return jnp.dot(left_mat, right_mat, preferred_element_type=jnp.float32)


def exact_multiply(left_mat, right_mat):
    return jnp.dot(left_mat, right_mat, precision=HIGHEST_MODE, preferred_element_type=jnp.float32)


def norm_rows(values, gain_row, bias_row):
    center = values - jnp.mean(values, axis=1, keepdims=True)
    inverse = lax.rsqrt(jnp.mean(center * center, axis=1, keepdims=True) + LN_EPS)
    return center * inverse * gain_row + bias_row


def seq_layout(lengths, slot_total):
    seq_ends = jnp.cumsum(lengths)
    starts = seq_ends - lengths
    slot_index = jnp.arange(slot_total, dtype=jnp.int32)
    member = (slot_index[:, None] >= starts[None, :]) & (slot_index[:, None] < seq_ends[None, :])
    seq_count = jnp.arange(lengths.shape[0], dtype=jnp.int32)
    seq_ids = jnp.sum(jnp.where(member, seq_count[None, :], 0), axis=1)
    positions = slot_index - jnp.sum(jnp.where(member, starts[None, :], 0), axis=1) + 2
    return (seq_ids, positions, member)


def adam_step(weight, first_old, second_old, clipped, step_rate, decay_rate):
    first_new = BETA_FIRST * first_old + (1.0 - BETA_FIRST) * clipped
    second_new = BETA_SECOND * second_old + (1.0 - BETA_SECOND) * clipped * clipped
    first_hat = first_new / (1.0 - BETA_FIRST**STEP)
    second_hat = second_new / (1.0 - BETA_SECOND**STEP)
    weight_new = weight - step_rate * (
        first_hat / (jnp.sqrt(second_hat) + ADAM_EPS) + decay_rate * weight
    )
    return (weight_new, first_new, second_new)


MESH_IDS = pl.DeviceIdType.MESH
SPARE_BYTES = 6 * 1024 * 1024
CHUNKS = 4
LINE = 4


def in_vmem():
    return pl.BlockSpec(memory_space=pltpu.VMEM)


def shaped(shape, dtype):
    return jax.ShapeDtypeStruct(tuple(shape), dtype)


def dma(*shape):
    return pltpu.SemaphoreType.DMA(shape)


def remote(src, dst, send_sem, recv_sem, target):
    return pltpu.make_async_remote_copy(
        src_ref=src,
        dst_ref=dst,
        send_sem=send_sem,
        recv_sem=recv_sem,
        device_id=target,
        device_id_type=MESH_IDS,
    )


def room(*items):
    total = 0
    for item in items:
        size = 0
        if item.dtype == jnp.bfloat16:
            size = 2
        elif item.dtype == jnp.float32 or item.dtype == jnp.int32:
            size = 4
        for extent in item.shape[:-1]:
            size = size * extent
        total = total + size * (-(-item.shape[-1] // 128) * 128)
    return total + SPARE_BYTES


def comm_params(collective, limit):
    return pltpu.CompilerParams(
        collective_id=collective, has_side_effects=True, vmem_limit_bytes=limit
    )


def exchange(collective, *tasks):
    def kernel(*refs):
        at = 0
        for attribute in ("ins", "outs", "scratch"):
            for task in tasks:
                size = len(getattr(task, attribute))
                setattr(task, attribute + "_refs", refs[at : at + size])
                at += size
        barrier = pltpu.get_barrier_semaphore()
        pl.semaphore_wait(barrier, sum(task.hello(barrier) for task in tasks))
        for task in tasks:
            task.begin()
        for task in tasks:
            task.middle()
        for task in tasks:
            task.late()
        for task in tasks[1:]:
            task.end()
        tasks[0].end()

    results = pl.pallas_call(
        kernel,
        out_shape=[out for task in tasks for out in task.outs],
        in_specs=[in_vmem() for task in tasks for _ in task.ins],
        out_specs=[in_vmem() for task in tasks for _ in task.outs],
        scratch_shapes=[item for task in tasks for item in task.scratch],
        compiler_params=comm_params(
            collective,
            room(*[item for task in tasks for item in task.ins + task.outs + task.scratch]),
        ),
    )(*[array for task in tasks for array in task.ins])
    return results[0] if len(results) == 1 else results


def tensor_place(width):
    me = lax.axis_index("tensor")
    core = lax.rem(me, 2)
    row = me // 2
    mate = me + 1 - 2 * core
    return (me, core, row, mate)


class Task:
    def hello(self, barrier):
        partners = self.partners()
        for partner in partners:
            pl.semaphore_signal(barrier, inc=1, device_id=partner, device_id_type=MESH_IDS)
        return len(partners)

    def begin(self):
        pass

    def middle(self):
        pass

    def late(self):
        pass

    def end(self):
        pass


class Pair(Task):
    def __init__(self):
        self.width = lax.axis_size("tensor")
        self.rows = self.width // 2

    def partners(self):
        me, core, row, mate = tensor_place(self.width)
        return [{"tensor": mate}] + [
            {"tensor": lax.rem(row + step, self.rows) * 2 + core} for step in range(1, self.rows)
        ]


class Spread(Pair):
    def __init__(self, block, columns=False, chunks=CHUNKS):
        super().__init__()
        height, depth = block.shape
        self.columns, self.chunks = columns, chunks
        self.ins = (block,)
        whole = (height, self.width * depth) if columns else (self.width * height, depth)
        self.outs = (shaped(whole, block.dtype),)
        self.scratch = tuple(dma(self.rows, chunks) for _ in range(4))

    def window(self, owner, part=None):
        (x_ref,), (o_ref,) = self.ins_refs, self.outs_refs
        height, depth = x_ref.shape
        size = height // self.chunks
        if self.columns:
            lanes = pl.ds(pl.multiple_of(owner * depth, depth), depth)
            if part is None or self.chunks == 1:
                return o_ref.at[:, lanes]
            return o_ref.at[pl.ds(part * size, size), lanes]
        if part is None:
            return o_ref.at[pl.ds(pl.multiple_of(owner * height, height), height)]
        return o_ref.at[pl.ds(pl.multiple_of(owner * height + part * size, size), size)]

    def begin(self):
        (x_ref,) = self.ins_refs
        far_send, far_recv, near_send, near_recv = self.scratch_refs
        me, core, row, mate = tensor_place(self.width)
        size = x_ref.shape[0] // self.chunks
        self.far = {}
        for part in range(self.chunks):
            source = x_ref if self.chunks == 1 else x_ref.at[pl.ds(part * size, size)]
            for step in range(1, self.rows):
                copy = remote(
                    source,
                    self.window(me, part),
                    far_send.at[step, part],
                    far_recv.at[step, part],
                    {"tensor": lax.rem(row + step, self.rows) * 2 + core},
                )
                copy.start()
                self.far[step, part] = copy
        copy = remote(
            x_ref, self.window(me), near_send.at[0, 0], near_recv.at[0, 0], {"tensor": mate}
        )
        copy.start()
        self.near = [copy]
        self.window(me)[...] = x_ref[...]

    def middle(self):
        far_send, far_recv, near_send, near_recv = self.scratch_refs
        me, core, row, mate = tensor_place(self.width)
        for part in range(self.chunks):
            for step in range(1, self.rows):
                self.far[step, part].wait_recv()
                source = lax.rem(row + self.rows - step, self.rows) * 2 + core
                onward = remote(
                    self.window(source, part),
                    self.window(source, part),
                    near_send.at[step, part],
                    near_recv.at[step, part],
                    {"tensor": mate},
                )
                onward.start()
                self.near.append(onward)

    def end(self):
        for copy in self.near:
            copy.wait()
        for copy in self.far.values():
            copy.wait_send()


class Fold(Pair):
    def __init__(self, parts, chunks=CHUNKS):
        super().__init__()
        height, depth = parts.shape[0] // self.width, parts.shape[1]
        far_rows = max(self.rows - 1, 1)
        self.chunks, self.height, self.depth = chunks, height, depth
        self.parts = parts
        self.fold_scratch = (
            pltpu.VMEM((self.rows, height, depth), jnp.bfloat16),
            pltpu.VMEM((far_rows, height, depth), jnp.bfloat16),
            pltpu.VMEM((far_rows, height, depth), jnp.bfloat16),
            pltpu.VMEM((height, depth), jnp.float32),
        ) + tuple(dma(self.rows, chunks) for _ in range(4))

    def span(self, owner, part):
        size = self.height // self.chunks
        return pl.ds(pl.multiple_of(owner * self.height + part * size, size), size)

    def local(self, part):
        size = self.height // self.chunks
        return pl.ds(part * size, size)

    def begin(self):
        p_ref = self.ins_refs[0]
        near_buf, near_send, near_recv = self.scratch_refs[0], *self.scratch_refs[4:6]
        me, core, row, mate = tensor_place(self.width)
        self.near = {}
        for step in list(range(1, self.rows)) + [0]:
            dest_row = lax.rem(row + step, self.rows)
            for part in range(self.chunks):
                copy = remote(
                    p_ref.at[self.span(dest_row * 2 + 1 - core, part)],
                    near_buf.at[step, self.local(part)],
                    near_send.at[step, part],
                    near_recv.at[step, part],
                    {"tensor": mate},
                )
                copy.start()
                self.near[step, part] = copy

    def middle(self):
        p_ref = self.ins_refs[0]
        near_buf, sum_buf, far_buf, total_buf = self.scratch_refs[:4]
        far_send, far_recv = self.scratch_refs[6:8]
        me, core, row, mate = tensor_place(self.width)
        self.far = {}
        for step in range(1, self.rows):
            dest = lax.rem(row + step, self.rows) * 2 + core
            for part in range(self.chunks):
                local = self.local(part)
                self.near[step, part].wait_recv()
                sum_buf[step - 1, local] = (
                    p_ref[self.span(dest, part)].astype(jnp.float32)
                    + near_buf[step, local].astype(jnp.float32)
                ).astype(jnp.bfloat16)
                copy = remote(
                    sum_buf.at[step - 1, local],
                    far_buf.at[step - 1, local],
                    far_send.at[step - 1, part],
                    far_recv.at[step - 1, part],
                    {"tensor": dest},
                )
                copy.start()
                self.far[step, part] = copy
        for part in range(self.chunks):
            local = self.local(part)
            self.near[0, part].wait_recv()
            total_buf[local] = p_ref[self.span(me, part)].astype(jnp.float32) + near_buf[
                0, local
            ].astype(jnp.float32)

    def folded(self, part):
        far_buf, total_buf = self.scratch_refs[2:4]
        local = self.local(part)
        total = total_buf[local]
        for step in range(1, self.rows):
            self.far[step, part].wait_recv()
            total = total + far_buf[step - 1, local].astype(jnp.float32)
        return total

    def settle_fold(self):
        for copy in list(self.near.values()) + list(self.far.values()):
            copy.wait_send()


class Relay:
    def relay_scratch(self):
        return (pltpu.VMEM((self.height, self.depth), jnp.bfloat16),) + tuple(
            dma(self.rows, self.chunks) for _ in range(4)
        )

    def relay_open(self, part, low):
        buf, far_send, far_recv, near_send, near_recv = self.scratch_refs[-5:]
        all_ref = self.outs_refs[0]
        me, core, row, mate = tensor_place(self.width)
        local = self.local(part)
        buf[local] = low
        if part == 0:
            self.sent, self.relay_near = {}, []
        for step in range(1, self.rows):
            copy = remote(
                buf.at[local],
                all_ref.at[self.span(me, part)],
                far_send.at[step, part],
                far_recv.at[step, part],
                {"tensor": lax.rem(row + step, self.rows) * 2 + core},
            )
            copy.start()
            self.sent[step, part] = copy
        copy = remote(
            buf.at[local],
            all_ref.at[self.span(me, part)],
            near_send.at[0, part],
            near_recv.at[0, part],
            {"tensor": mate},
        )
        copy.start()
        self.relay_near.append(copy)
        all_ref[self.span(me, part)] = low

    def relay_close(self):
        buf, far_send, far_recv, near_send, near_recv = self.scratch_refs[-5:]
        all_ref = self.outs_refs[0]
        me, core, row, mate = tensor_place(self.width)
        for part in range(self.chunks):
            for step in range(1, self.rows):
                self.sent[step, part].wait_recv()
                source = lax.rem(row + self.rows - step, self.rows) * 2 + core
                window = all_ref.at[self.span(source, part)]
                copy = remote(
                    window, window, near_send.at[step, part], near_recv.at[step, part], {"tensor": mate}
                )
                copy.start()
                self.relay_near.append(copy)
        for copy in self.relay_near:
            copy.wait()
        for copy in self.sent.values():
            copy.wait_send()


def split_three(values):
    pieces, rest = [], values
    for _ in range(3):
        pieces.append(rest.astype(jnp.bfloat16))
        rest = rest - pieces[-1].astype(jnp.float32)
    return pieces


def norm_pull(values, gain, grads):
    center = values - jnp.mean(values, axis=1, keepdims=True)
    inverse = lax.rsqrt(jnp.mean(center * center, axis=1, keepdims=True) + LN_EPS)
    unit = center * inverse
    scaled = grads * gain
    pull = inverse * (
        scaled
        - jnp.mean(scaled, axis=1, keepdims=True)
        - unit * jnp.mean(scaled * unit, axis=1, keepdims=True)
    )
    return (
        pull,
        jnp.sum(grads * unit, axis=0, keepdims=True),
        jnp.sum(grads, axis=0, keepdims=True),
    )


class FoldNormSpread(Relay, Fold):
    def __init__(self, parts, residual, row_params):
        super().__init__(parts)
        own = shaped((self.height, self.depth), jnp.float32)
        self.ins = (parts, residual, row_params)
        self.outs = (shaped(parts.shape, jnp.bfloat16), own, own)
        self.scratch = self.fold_scratch + self.relay_scratch()

    def late(self):
        p_ref, residual_ref, row_ref = self.ins_refs
        all_ref, sum_ref, norm_ref = self.outs_refs
        for part in range(self.chunks):
            local = self.local(part)
            total = residual_ref[local] + self.folded(part) + row_ref[6:7]
            sum_ref[local] = total
            norm = norm_rows(total, row_ref[1:2], row_ref[4:5])
            norm_ref[local] = norm
            self.relay_open(part, norm.astype(jnp.bfloat16))

    def end(self):
        self.relay_close()
        self.settle_fold()


class FoldPullSpread(Relay, Fold):
    def __init__(self, parts, residual, values, row_params):
        super().__init__(parts)
        own = shaped((self.height, self.depth), jnp.float32)
        self.ins = (parts, residual, values, row_params)
        self.outs = (shaped(parts.shape, jnp.bfloat16), own, shaped((8, self.depth), jnp.float32))
        self.scratch = self.fold_scratch + self.relay_scratch()

    def late(self):
        p_ref, residual_ref, value_ref, row_ref = self.ins_refs
        all_ref, grad_ref, side_ref = self.outs_refs
        side_ref[...] = jnp.zeros_like(side_ref)
        for part in range(self.chunks):
            local = self.local(part)
            pull, gain, shift = norm_pull(
                value_ref[local], row_ref[1:2], residual_ref[local] + self.folded(part)
            )
            grad_ref[local] = pull
            low = pull.astype(jnp.bfloat16)
            self.relay_open(part, low)
            side_ref[0:1] += gain
            side_ref[1:2] += shift
            side_ref[2:3] += jnp.sum(low.astype(jnp.float32), axis=0, keepdims=True)

    def end(self):
        self.relay_close()
        self.settle_fold()


class PullSpread(Relay, Pair):
    def __init__(self, pooled_grad, counts, members, values, row_params):
        super().__init__()
        self.height, self.depth = values.shape
        self.chunks = CHUNKS
        own = shaped(values.shape, jnp.float32)
        self.ins = (pooled_grad, counts, members, values, row_params)
        self.outs = (
            shaped((self.width * self.height, self.depth), jnp.bfloat16),
            own,
            shaped((8, self.depth), jnp.float32),
        )
        self.scratch = self.relay_scratch()

    span, local = Fold.span, Fold.local

    def begin(self):
        pooled_ref, count_ref, member_ref, value_ref, row_ref = self.ins_refs
        all_ref, grad_ref, side_ref = self.outs_refs
        side_ref[...] = jnp.zeros_like(side_ref)
        anchors = count_ref.shape[0]
        rows = block_span(lax.axis_index("dp"), anchors)
        pieces = jnp.concatenate(split_three(pooled_ref[rows] / count_ref[...]), axis=0)
        for part in range(self.chunks):
            local = self.local(part)
            grads = multiply_arrays(member_ref[local], pieces)
            pull, gain, shift = norm_pull(value_ref[local], row_ref[2:3], grads)
            grad_ref[local] = pull
            low = pull.astype(jnp.bfloat16)
            self.relay_open(part, low)
            side_ref[0:1] += gain
            side_ref[1:2] += shift
            side_ref[2:3] += jnp.sum(low.astype(jnp.float32), axis=0, keepdims=True)

    def end(self):
        self.relay_close()


class Swap(Task):
    def __init__(self, blocks, axis):
        self.axis, self.count = axis, lax.axis_size(axis)
        self.ins = (blocks,)
        self.outs = (shaped(blocks.shape, blocks.dtype),)
        self.scratch = (dma(self.count), dma(self.count))

    def others(self):
        me = lax.axis_index(self.axis)
        return [lax.rem(me + step, self.count) for step in range(1, self.count)]

    def partners(self):
        return [{self.axis: other} for other in self.others()]

    def begin(self):
        (x_ref,), (o_ref,), (send, recv) = self.ins_refs, self.outs_refs, self.scratch_refs
        me = lax.axis_index(self.axis)
        self.copies = [
            remote(x_ref.at[other], o_ref.at[me], send.at[i], recv.at[i], {self.axis: other})
            for i, other in enumerate(self.others())
        ]
        for copy in self.copies:
            copy.start()
        o_ref[me] = x_ref[me]

    def end(self):
        for copy in self.copies:
            copy.wait()


class Gather(Swap):
    def __init__(self, block, axis):
        super().__init__(block, axis)
        self.outs = (shaped((self.count,) + block.shape, block.dtype),)

    def begin(self):
        (x_ref,), (o_ref,), (send, recv) = self.ins_refs, self.outs_refs, self.scratch_refs
        me = lax.axis_index(self.axis)
        self.copies = [
            remote(x_ref, o_ref.at[me], send.at[i], recv.at[i], {self.axis: other})
            for i, other in enumerate(self.others())
        ]
        for copy in self.copies:
            copy.start()
        o_ref[me] = x_ref[...]


class GatherAll(Task):
    def __init__(self, block):
        self.width = lax.axis_size("tensor")
        self.total = total = lax.axis_size("dp") * self.width
        self.ins = (block,)
        self.outs = (shaped((total,) + block.shape, block.dtype),)
        self.scratch = (dma(total), dma(total))

    def me(self):
        return lax.axis_index("dp") * self.width + lax.axis_index("tensor")

    def place(self, step):
        other = lax.rem(self.me() + step, self.total)
        return (other // self.width, lax.rem(other, self.width))

    def copy(self, step):
        (x_ref,), (o_ref,), (send, recv) = self.ins_refs, self.outs_refs, self.scratch_refs
        return remote(x_ref, o_ref.at[self.me()], send.at[step], recv.at[step], self.place(step))

    def hello(self, barrier):
        def one(step, carry):
            pl.semaphore_signal(
                barrier, inc=1, device_id=self.place(step), device_id_type=MESH_IDS
            )
            return carry

        lax.fori_loop(1, self.total, one, 0)
        return self.total - 1

    def begin(self):
        def one(step, carry):
            self.copy(step).start()
            return carry

        lax.fori_loop(1, self.total, one, 0)
        self.outs_refs[0][self.me()] = self.ins_refs[0][...]

    def end(self):
        def one(step, carry):
            self.copy(step).wait()
            return carry

        lax.fori_loop(1, self.total, one, 0)


class FoldPool(Fold):
    def __init__(self, parts, residual, members, counts, row_params):
        super().__init__(parts)
        anchors = members.shape[0]
        self.total = SumAll(shaped((anchors, self.depth), jnp.float32), True)
        self.ins = (parts, residual, members, counts, row_params)
        self.outs = (shaped((self.height, self.depth), jnp.float32),) + self.total.outs
        self.scratch = (
            self.fold_scratch
            + (pltpu.VMEM((anchors, self.depth), jnp.float32),)
            + self.total.scratch
        )

    def hello(self, barrier):
        return super().hello(barrier) + self.total.hello(barrier)

    def end(self):
        p_ref, residual_ref, member_ref, count_ref, row_ref = self.ins_refs
        sum_ref = self.outs_refs[0]
        at = len(self.fold_scratch)
        pooled = self.scratch_refs[at]
        size = self.height // self.chunks
        parts = []
        for part in range(self.chunks):
            local = self.local(part)
            total = residual_ref[local] + self.folded(part) + row_ref[7:8]
            sum_ref[local] = total
            norm = norm_rows(total, row_ref[2:3], row_ref[5:6])
            member = member_ref[:, part * size : (part + 1) * size]
            for piece in split_three(norm):
                parts.append(multiply_arrays(member, piece))
        pooled[...] = sum(parts[1:], parts[0]) / count_ref[...]
        total = self.total
        total.ins_refs, total.outs_refs = (pooled,), self.outs_refs[1:]
        total.scratch_refs = self.scratch_refs[at + 1 :]
        total.begin()
        total.middle()
        total.end()
        self.settle_fold()


class FoldPullSwap(Fold):
    def __init__(self, parts, residual, values, row_params):
        super().__init__(parts)
        self.narrow = self.depth // self.width
        self.ins = (parts, residual, values, row_params)
        self.outs = (
            shaped((self.width, self.height, self.narrow), jnp.bfloat16),
            shaped((8, self.depth), jnp.float32),
        )
        self.scratch = self.fold_scratch + (
            pltpu.VMEM((self.height, self.depth), jnp.bfloat16),
            dma(self.width, self.chunks),
            dma(self.width, self.chunks),
        )

    def partners(self):
        me = lax.axis_index("tensor")
        return [{"tensor": lax.rem(me + step, self.width)} for step in range(1, self.width)]

    def late(self):
        p_ref, residual_ref, value_ref, row_ref = self.ins_refs
        cols_ref, side_ref = self.outs_refs
        buf, send, recv = self.scratch_refs[-3:]
        side_ref[...] = jnp.zeros_like(side_ref)
        me = lax.axis_index("tensor")

        def lanes(owner):
            return pl.ds(pl.multiple_of(owner * self.narrow, self.narrow), self.narrow)

        copies = []
        for part in range(self.chunks):
            local = self.local(part)
            pull, gain, shift = norm_pull(
                value_ref[local], row_ref[0:1], residual_ref[local] + self.folded(part)
            )
            buf[local] = pull.astype(jnp.bfloat16)
            for step in range(1, self.width):
                other = lax.rem(me + step, self.width)
                copy = remote(
                    buf.at[local, lanes(other)],
                    cols_ref.at[me, local],
                    send.at[step, part],
                    recv.at[step, part],
                    {"tensor": other},
                )
                copy.start()
                copies.append(copy)
            cols_ref[me, local] = buf[local, lanes(me)]
            side_ref[0:1] += gain
            side_ref[1:2] += shift
        self.copies = copies

    def end(self):
        for copy in self.copies:
            copy.wait()
        self.settle_fold()


def eight_rows(values):
    return jnp.sum(values.reshape(values.shape[0] // 8, 8, values.shape[1]), axis=0)


class GridTask(Task):
    def __init__(self):
        self.cross = lax.axis_size("dp") // LINE

    def place(self):
        me = lax.axis_index("dp")
        return (me // self.cross, lax.rem(me, self.cross))


class ReduceCross(GridTask):
    def __init__(self, blocks):
        super().__init__()
        shape = blocks.shape[1:]
        self.blocks_shape = (LINE, self.cross) + shape
        self.ins = (blocks.reshape(self.blocks_shape),)
        self.outs = (shaped((LINE,) + shape, jnp.bfloat16),)
        others = max(self.cross - 1, 1)
        self.scratch = (
            pltpu.VMEM((others, LINE) + shape, jnp.bfloat16),
            dma(others, LINE),
            dma(others, LINE),
        )

    def targets(self):
        line, cross = self.place()
        return [lax.rem(cross + step, self.cross) for step in range(1, self.cross)]

    def partners(self):
        line, cross = self.place()
        return [{"dp": line * self.cross + other} for other in self.targets()]

    def begin(self):
        (x_ref,), (buf, send, recv) = self.ins_refs, self.scratch_refs
        line, cross = self.place()
        self.copies = []
        for i, other in enumerate(self.targets()):
            for z in range(LINE):
                copy = remote(
                    x_ref.at[z, other],
                    buf.at[i, z],
                    send.at[i, z],
                    recv.at[i, z],
                    {"dp": line * self.cross + other},
                )
                copy.start()
                self.copies.append(copy)

    def end(self):
        (x_ref,), (o_ref,), (buf, send, recv) = self.ins_refs, self.outs_refs, self.scratch_refs
        line, cross = self.place()
        for copy in self.copies:
            copy.wait()
        for z in range(LINE):
            total = x_ref[z, cross].astype(jnp.float32)
            for i in range(self.cross - 1):
                total = total + buf[i, z].astype(jnp.float32)
            o_ref[z] = total.astype(jnp.bfloat16)


class SpreadLine(GridTask):
    def __init__(self, block):
        super().__init__()
        self.ins = (block,)
        self.outs = (shaped((LINE,) + block.shape, block.dtype),)
        self.scratch = (dma(LINE - 1), dma(LINE - 1))

    def targets(self):
        line, cross = self.place()
        return [lax.rem(line + step, LINE) for step in range(1, LINE)]

    def partners(self):
        line, cross = self.place()
        return [{"dp": other * self.cross + cross} for other in self.targets()]

    def begin(self):
        (x_ref,), (o_ref,), (send, recv) = self.ins_refs, self.outs_refs, self.scratch_refs
        line, cross = self.place()
        self.copies = [
            remote(x_ref, o_ref.at[line], send.at[i], recv.at[i], partner)
            for i, partner in enumerate(self.partners())
        ]
        for copy in self.copies:
            copy.start()
        o_ref[line] = x_ref[...]

    def end(self):
        for copy in self.copies:
            copy.wait()


class Chain(Task):
    def __init__(self, first, second):
        self.first, self.second = first, second
        self.ins = first.ins
        self.outs = first.outs + second.outs
        self.scratch = first.scratch + second.scratch

    def hello(self, barrier):
        return self.first.hello(barrier) + self.second.hello(barrier)

    def begin(self):
        outs, scratch = len(self.first.outs), len(self.first.scratch)
        self.first.ins_refs, self.first.outs_refs = self.ins_refs, self.outs_refs[:outs]
        self.first.scratch_refs = self.scratch_refs[:scratch]
        self.second.ins_refs, self.second.outs_refs = self.outs_refs[:outs], self.outs_refs[outs:]
        self.second.scratch_refs = self.scratch_refs[scratch:]
        self.first.begin()

    def middle(self):
        self.first.end()
        self.second.begin()

    def end(self):
        self.second.end()


class Later(Task):
    def __init__(self, task):
        self.task = task
        self.ins, self.outs, self.scratch = task.ins, task.outs, task.scratch

    def hello(self, barrier):
        return self.task.hello(barrier)

    def middle(self):
        task = self.task
        task.ins_refs, task.outs_refs = self.ins_refs, self.outs_refs
        task.scratch_refs = self.scratch_refs
        task.begin()

    def end(self):
        self.task.end()


def reduce_grid(blocks, **form):
    first = ReduceCross(blocks)
    return Chain(first, ReduceLine(first.outs[0], **form))


def spread_grid(block):
    first = SpreadLine(block)
    return Chain(first, SpreadCross(first.outs[0]))


class SpreadCross(GridTask):
    def __init__(self, *pieces):
        super().__init__()
        self.ins = pieces
        self.tall, depth = pieces[0].shape[1:]
        count = len(pieces)
        self.outs = (shaped((LINE, self.cross, self.tall * count, depth), pieces[0].dtype),)
        others = max(self.cross - 1, 1)
        self.scratch = (dma(others, LINE, count), dma(others, LINE, count))

    def partners(self):
        line, cross = self.place()
        return [
            {"dp": line * self.cross + lax.rem(cross + step, self.cross)}
            for step in range(1, self.cross)
        ]

    def begin(self):
        (o_ref,), (send, recv) = self.outs_refs, self.scratch_refs
        line, cross = self.place()
        self.copies = []
        for p, x_ref in enumerate(self.ins_refs):
            rows = pl.ds(p * self.tall, self.tall)
            for i, partner in enumerate(self.partners()):
                for z in range(LINE):
                    copy = remote(
                        x_ref.at[z],
                        o_ref.at[z, cross, rows],
                        send.at[i, z, p],
                        recv.at[i, z, p],
                        partner,
                    )
                    copy.start()
                    self.copies.append(copy)
            for z in range(LINE):
                o_ref[z, cross, rows] = x_ref[z]

    def end(self):
        for copy in self.copies:
            copy.wait()


class GatherGrid(GridTask):
    def __init__(self, block):
        super().__init__()
        self.ins = (block,)
        self.outs = (shaped((LINE, self.cross) + block.shape, block.dtype),)
        others = max(self.cross - 1, 1)
        self.scratch = (dma(LINE - 1), dma(LINE - 1), dma(others, LINE), dma(others, LINE))

    def lines(self):
        line, cross = self.place()
        return [
            {"dp": lax.rem(line + step, LINE) * self.cross + cross} for step in range(1, LINE)
        ]

    def crosses(self):
        line, cross = self.place()
        return [
            {"dp": line * self.cross + lax.rem(cross + step, self.cross)}
            for step in range(1, self.cross)
        ]

    def partners(self):
        return self.lines() + self.crosses()

    def begin(self):
        (x_ref,), (o_ref,), sems = self.ins_refs, self.outs_refs, self.scratch_refs
        line, cross = self.place()
        self.copies = [
            remote(x_ref, o_ref.at[line, cross], sems[0].at[i], sems[1].at[i], partner)
            for i, partner in enumerate(self.lines())
        ]
        for copy in self.copies:
            copy.start()
        o_ref[line, cross] = x_ref[...]

    def middle(self):
        (o_ref,), sems = self.outs_refs, self.scratch_refs
        line, cross = self.place()
        for copy in self.copies:
            copy.wait()
        self.copies = []
        for i, partner in enumerate(self.crosses()):
            for z in range(LINE):
                window = o_ref.at[z, cross]
                copy = remote(window, window, sems[2].at[i, z], sems[3].at[i, z], partner)
                copy.start()
                self.copies.append(copy)

    def end(self):
        for copy in self.copies:
            copy.wait()


class ReduceLine(GridTask):
    def __init__(self, blocks, slabs=1, turned=False):
        super().__init__()
        shape = blocks.shape[1:]
        self.slabs, self.turned = slabs, turned
        self.ins = (blocks,)
        result = shape[::-1] if turned else shape
        if slabs > 1:
            result = (slabs, shape[0], shape[1] // slabs)
        self.outs = (shaped(result, jnp.float32), shaped((8, shape[1]), jnp.float32))
        self.scratch = (pltpu.VMEM((LINE - 1,) + shape, jnp.bfloat16), dma(LINE - 1), dma(LINE - 1))

    def targets(self):
        line, cross = self.place()
        return [lax.rem(line + step, LINE) for step in range(1, LINE)]

    def partners(self):
        line, cross = self.place()
        return [{"dp": other * self.cross + cross} for other in self.targets()]

    def begin(self):
        (x_ref,), (buf, send, recv) = self.ins_refs, self.scratch_refs
        line, cross = self.place()
        self.copies = [
            remote(
                x_ref.at[other], buf.at[i], send.at[i], recv.at[i], {"dp": other * self.cross + cross}
            )
            for i, other in enumerate(self.targets())
        ]
        for copy in self.copies:
            copy.start()

    def end(self):
        (x_ref,), (o_ref, square_ref) = self.ins_refs, self.outs_refs
        buf = self.scratch_refs[0]
        line, cross = self.place()
        for copy in self.copies:
            copy.wait()
        total = x_ref[line].astype(jnp.float32)
        for i in range(LINE - 1):
            total = total + buf[i].astype(jnp.float32)
        square_ref[...] = eight_rows(total * total)
        if self.turned:
            o_ref[...] = total.T
        elif self.slabs > 1:
            narrow = total.shape[1] // self.slabs
            for slab in range(self.slabs):
                o_ref[slab] = total[:, slab * narrow : (slab + 1) * narrow]
        else:
            o_ref[...] = total


class SumAll(Task):
    def __init__(self, block, keep):
        self.groups, self.width, self.keep = lax.axis_size("dp"), lax.axis_size("tensor"), keep
        rows, depth = block.shape
        self.narrow = narrow = depth // self.width
        kept = self.groups if keep else 1
        self.ins = (block,)
        self.outs = (shaped((kept, rows, depth), block.dtype),)
        near, far = dma(self.width), dma(self.groups)
        self.scratch = (
            pltpu.VMEM((self.width, rows, narrow), block.dtype),
            pltpu.VMEM((rows, narrow), block.dtype),
            pltpu.VMEM((self.groups, rows, narrow), block.dtype),
            pltpu.VMEM((kept, rows, narrow), block.dtype),
            near, near, far, far, near, near,
        )

    def mates(self):
        me = lax.axis_index("tensor")
        return [lax.rem(me + step, self.width) for step in range(1, self.width)]

    def peers(self):
        me = lax.axis_index("dp")
        return [lax.rem(me + step, self.groups) for step in range(1, self.groups)]

    def partners(self):
        return [{"tensor": mate} for mate in self.mates()] + [{"dp": peer} for peer in self.peers()]

    def lanes(self, owner):
        return pl.ds(pl.multiple_of(owner * self.narrow, self.narrow), self.narrow)

    def launch(self, copies):
        for copy in copies:
            copy.start()
        self.copies = copies

    def settle(self):
        for copy in self.copies:
            copy.wait()

    def begin(self):
        (x_ref,) = self.ins_refs
        part_buf, sems = self.scratch_refs[0], self.scratch_refs[4:]
        me = lax.axis_index("tensor")
        self.launch(
            [
                remote(
                    x_ref.at[:, self.lanes(mate)],
                    part_buf.at[me],
                    sems[0].at[i],
                    sems[1].at[i],
                    {"tensor": mate},
                )
                for i, mate in enumerate(self.mates())
            ]
        )
        part_buf[me] = x_ref[:, self.lanes(me)]

    def middle(self):
        (o_ref,) = self.outs_refs
        part_buf, sum_buf, all_buf, out_buf = self.scratch_refs[:4]
        sems = self.scratch_refs[4:]
        dp_me, me = lax.axis_index("dp"), lax.axis_index("tensor")
        self.settle()
        sum_buf[...] = jnp.sum(part_buf[...], axis=0)
        self.launch(
            [
                remote(sum_buf, all_buf.at[dp_me], sems[2].at[i], sems[3].at[i], {"dp": peer})
                for i, peer in enumerate(self.peers())
            ]
        )
        all_buf[dp_me] = sum_buf[...]
        self.settle()
        if self.keep:
            out_buf[...] = all_buf[...]
        else:
            out_buf[0] = jnp.sum(all_buf[...], axis=0)
        self.launch(
            [
                remote(
                    out_buf,
                    o_ref.at[:, :, self.lanes(me)],
                    sems[4].at[i],
                    sems[5].at[i],
                    {"tensor": mate},
                )
                for i, mate in enumerate(self.mates())
            ]
        )
        o_ref[:, :, self.lanes(me)] = out_buf[...]

    def end(self):
        self.settle()


Q_BLOCK = 256
K_BLOCK = 128


def split_pair(wide):
    half = wide.shape[0] // 2
    upper = lax.broadcasted_iota(jnp.int32, wide.shape, 0) < half
    zero = jnp.zeros_like(wide)
    return jnp.concatenate([jnp.where(upper, wide, zero), jnp.where(upper, zero, wide)], axis=1)


def stack_pair(tall):
    half = tall.shape[1] // 2
    left = lax.broadcasted_iota(jnp.int32, tall.shape, 1) < half
    zero = jnp.zeros_like(tall)
    return jnp.concatenate([jnp.where(left, tall, zero), jnp.where(left, zero, tall)], axis=0)


def join_pair(wide):
    depth, columns = wide.shape
    upper = lax.broadcasted_iota(jnp.int32, (depth, columns // 2), 0) < depth // 2
    return jnp.where(upper, wide[:, : columns // 2], wide[:, columns // 2 :])


def turn(tile):
    return tile.astype(jnp.float32).T.astype(jnp.bfloat16)


def block_span(index, size):
    return pl.ds(pl.multiple_of(index * size, size), size)


def attend_kernel(low_ref, high_ref, qkv_ref, seq_col_ref, seq_row_ref, out_ref, log_ref, value_turned, scores):
    slots, columns = out_ref.shape
    pairs = columns // 128
    q_blocks, k_blocks = slots // Q_BLOCK, slots // K_BLOCK

    def turn_values(b, carry):
        rows = block_span(b, K_BLOCK)
        for pair in range(pairs):
            value_turned[pl.ds(pair * 128, 128), rows] = turn(
                qkv_ref[rows, pl.ds(2 * columns + pair * 128, 128)]
            )
        return carry

    lax.fori_loop(0, k_blocks, turn_values, 0)

    def one_block(q_index, carry):
        q_rows = block_span(q_index, Q_BLOCK)
        lowest, highest = low_ref[q_index], high_ref[q_index]
        seq_row = seq_row_ref[0:1, q_rows]
        seq_pair = jnp.concatenate([seq_row, seq_row], axis=1)
        queries = [
            split_pair(
                (qkv_ref[q_rows, pl.ds(pair * 128, 128)].astype(jnp.float32) * HEAD ** (-0.5))
                .T.astype(jnp.bfloat16)
            )
            for pair in range(pairs)
        ]

        def score(k_index, tops):
            k_rows = block_span(k_index, K_BLOCK)
            same = seq_col_ref[k_rows, 0:1] == seq_pair
            later = []
            for pair in range(pairs):
                keys = qkv_ref[k_rows, pl.ds(columns + pair * 128, 128)]
                value = jnp.where(same, multiply_arrays(keys, queries[pair]), MASK_FILL)
                scores[pair, k_index - lowest] = value
                later.append(jnp.maximum(tops[pair], jnp.max(value, axis=0, keepdims=True)))
            return tuple(later)

        start = tuple(jnp.full((1, 2 * Q_BLOCK), MASK_FILL, jnp.float32) for _ in range(pairs))
        tops = lax.fori_loop(lowest, highest, score, start)

        def mix(k_index, state):
            k_rows = block_span(k_index, K_BLOCK)
            later = []
            for pair in range(pairs):
                total, mixed = state[pair]
                weights = jnp.exp(scores[pair, k_index - lowest] - tops[pair])
                total = total + jnp.sum(weights, axis=0, keepdims=True)
                mixed = mixed + multiply_arrays(
                    value_turned[pl.ds(pair * 128, 128), k_rows], weights.astype(jnp.bfloat16)
                )
                later.append((total, mixed))
            return tuple(later)

        blank = tuple(
            (jnp.zeros((1, 2 * Q_BLOCK), jnp.float32), jnp.zeros((128, 2 * Q_BLOCK), jnp.float32))
            for _ in range(pairs)
        )
        final = lax.fori_loop(lowest, highest, mix, blank)
        for pair in range(pairs):
            total, mixed = final[pair]
            out_ref[q_rows, pl.ds(pair * 128, 128)] = join_pair(mixed / total).T.astype(jnp.bfloat16)
            logs = tops[pair] + jnp.log(total)
            log_ref[pl.ds(2 * pair, 1), q_rows] = logs[:, :Q_BLOCK]
            log_ref[pl.ds(2 * pair + 1, 1), q_rows] = logs[:, Q_BLOCK:]
        return carry

    lax.fori_loop(0, q_blocks, one_block, 0)


def block_bounds(lengths, slots):
    ends = jnp.cumsum(lengths)
    starts = ends - lengths
    first = jnp.arange(slots // Q_BLOCK, dtype=jnp.int32) * Q_BLOCK
    last = first + Q_BLOCK - 1
    lowest = jnp.max(
        jnp.where(starts[None, :] <= first[:, None], starts[None, :], 0), axis=1
    )
    highest = jnp.min(jnp.where(ends[None, :] > last[:, None], ends[None, :], slots), axis=1)
    return (lowest // K_BLOCK, (highest + K_BLOCK - 1) // K_BLOCK)


REACH = (2 * MAXLEN - 2) // K_BLOCK + Q_BLOCK // K_BLOCK + 1


def in_scalars():
    return pl.BlockSpec(memory_space=pltpu.SMEM)


def attend(qkv_out, seq_ids, bounds):
    slots, columns = qkv_out.shape[0], qkv_out.shape[1] // 3
    pairs = columns // 128
    return pl.pallas_call(
        attend_kernel,
        out_shape=[
            jax.ShapeDtypeStruct((slots, columns), jnp.bfloat16),
            jax.ShapeDtypeStruct((8, slots), jnp.float32),
        ],
        in_specs=[in_scalars(), in_scalars()] + [in_vmem()] * 3,
        out_specs=[in_vmem()] * 2,
        scratch_shapes=[
            pltpu.VMEM((columns, slots), jnp.bfloat16),
            pltpu.VMEM((pairs, REACH, K_BLOCK, 2 * Q_BLOCK), jnp.float32),
        ],
        compiler_params=pltpu.CompilerParams(vmem_limit_bytes=20 * 1024 * 1024),
    )(bounds[0], bounds[1], qkv_out, seq_ids[:, None], jnp.broadcast_to(seq_ids[None], (8, slots)))


def attend_back_kernel(
    low_ref, high_ref, qkv_ref, grad_ref, log_ref, seq_col_ref, seq_row_ref, out_ref,
    key_turned, probs, prob_grads, key_sum, value_sum,
):
    slots, columns = grad_ref.shape
    pairs = columns // 128
    q_blocks, k_blocks = slots // Q_BLOCK, slots // K_BLOCK

    def turn_keys(b, carry):
        rows = block_span(b, K_BLOCK)
        for pair in range(pairs):
            key_turned[pl.ds(pair * 128, 128), rows] = turn(
                qkv_ref[rows, pl.ds(columns + pair * 128, 128)]
            )
        key_sum[rows] = jnp.zeros((K_BLOCK, columns), jnp.float32)
        value_sum[rows] = jnp.zeros((K_BLOCK, columns), jnp.float32)
        return carry

    lax.fori_loop(0, k_blocks, turn_keys, 0)

    def one_block(q_index, carry):
        q_rows = block_span(q_index, Q_BLOCK)
        lowest, highest = low_ref[q_index], high_ref[q_index]
        seq_row = seq_row_ref[0:1, q_rows]
        seq_pair = jnp.concatenate([seq_row, seq_row], axis=1)
        scaled, queries, grads, turned, logs = [], [], [], [], []
        for pair in range(pairs):
            plain = qkv_ref[q_rows, pl.ds(pair * 128, 128)].astype(jnp.float32) * HEAD ** (-0.5)
            scaled.append(stack_pair(plain.astype(jnp.bfloat16)))
            queries.append(split_pair(plain.T.astype(jnp.bfloat16)))
            grad = grad_ref[q_rows, pl.ds(pair * 128, 128)]
            grads.append(stack_pair(grad))
            turned.append(split_pair(turn(grad)))
            logs.append(
                jnp.concatenate(
                    [log_ref[pl.ds(2 * pair, 1), q_rows], log_ref[pl.ds(2 * pair + 1, 1), q_rows]],
                    axis=1,
                )
            )

        def look(k_index, inners):
            k_rows = block_span(k_index, K_BLOCK)
            same = seq_col_ref[k_rows, 0:1] == seq_pair
            later = []
            for pair in range(pairs):
                keys = qkv_ref[k_rows, pl.ds(columns + pair * 128, 128)]
                values = qkv_ref[k_rows, pl.ds(2 * columns + pair * 128, 128)]
                logits = jnp.where(same, multiply_arrays(keys, queries[pair]), MASK_FILL)
                weights = jnp.exp(logits - logs[pair])
                weight_grad = multiply_arrays(values, turned[pair])
                probs[pair, k_index - lowest] = weights
                prob_grads[pair, k_index - lowest] = weight_grad
                value_sum[k_rows, pl.ds(pair * 128, 128)] += multiply_arrays(
                    weights.astype(jnp.bfloat16), grads[pair]
                )
                later.append(
                    inners[pair] + jnp.sum(weights * weight_grad, axis=0, keepdims=True)
                )
            return tuple(later)

        start = tuple(jnp.zeros((1, 2 * Q_BLOCK), jnp.float32) for _ in range(pairs))
        inners = lax.fori_loop(lowest, highest, look, start)

        def push(k_index, sums):
            k_rows = block_span(k_index, K_BLOCK)
            later = []
            for pair in range(pairs):
                slope = (
                    probs[pair, k_index - lowest]
                    * (prob_grads[pair, k_index - lowest] - inners[pair])
                ).astype(jnp.bfloat16)
                key_sum[k_rows, pl.ds(pair * 128, 128)] += multiply_arrays(slope, scaled[pair])
                later.append(
                    sums[pair] + multiply_arrays(key_turned[pl.ds(pair * 128, 128), k_rows], slope)
                )
            return tuple(later)

        blank = tuple(jnp.zeros((128, 2 * Q_BLOCK), jnp.float32) for _ in range(pairs))
        sums = lax.fori_loop(lowest, highest, push, blank)
        for pair in range(pairs):
            out_ref[q_rows, pl.ds(pair * 128, 128)] = (
                (join_pair(sums[pair]) * HEAD ** (-0.5)).T.astype(jnp.bfloat16)
            )
        return carry

    lax.fori_loop(0, q_blocks, one_block, 0)
    out_ref[:, columns : 2 * columns] = key_sum[...].astype(jnp.bfloat16)
    out_ref[:, 2 * columns :] = value_sum[...].astype(jnp.bfloat16)


def attend_back(qkv_out, attn_grad, log_total, seq_ids, bounds):
    slots, columns = attn_grad.shape
    pairs = columns // 128
    window = pltpu.VMEM((pairs, REACH, K_BLOCK, 2 * Q_BLOCK), jnp.float32)
    return pl.pallas_call(
        attend_back_kernel,
        out_shape=jax.ShapeDtypeStruct(qkv_out.shape, jnp.bfloat16),
        in_specs=[in_scalars(), in_scalars()] + [in_vmem()] * 5,
        out_specs=in_vmem(),
        scratch_shapes=[
            pltpu.VMEM((columns, slots), jnp.bfloat16),
            window,
            window,
            pltpu.VMEM((slots, columns), jnp.float32),
            pltpu.VMEM((slots, columns), jnp.float32),
        ],
        compiler_params=pltpu.CompilerParams(vmem_limit_bytes=36 * 1024 * 1024),
    )(
        bounds[0],
        bounds[1],
        qkv_out,
        attn_grad,
        log_total,
        seq_ids[:, None],
        jnp.broadcast_to(seq_ids[None], (8, slots)),
    )


def gelu_parts(upper):
    distance = jnp.abs(upper) * 0.7071067811865476
    step = 1.0 / (1.0 + 0.3275911 * distance)
    bell = jnp.exp(-distance * distance)
    series = step * (
        0.254829592
        + step * (-0.284496736 + step * (1.421413741 + step * (-1.453152027 + step * 1.061405429)))
    )
    tail = 0.5 * series * bell
    share = jnp.where(upper >= 0.0, 1.0 - tail, tail)
    return (upper * share, share + upper * (bell * 0.3989422804014327))


def expand_kernel(rows_ref, weight_ref, bias_ref, hidden_ref, slope_ref):
    units = weight_ref.shape[1]
    rows = rows_ref[...]
    for first in range(0, units, 256):
        lanes = pl.ds(first, 256)
        upper = multiply_arrays(rows, weight_ref[:, lanes]) + bias_ref[:, lanes]
        hidden, slope = gelu_parts(upper)
        hidden_ref[:, lanes] = hidden.astype(jnp.bfloat16)
        slope_ref[:, lanes] = slope


def expand(rows, weight, bias):
    slots, depth = rows.shape
    units = weight.shape[1]
    tall = 512
    return pl.pallas_call(
        expand_kernel,
        grid=(slots // tall,),
        out_shape=[shaped((slots, units), jnp.bfloat16), shaped((slots, units), jnp.float32)],
        in_specs=[
            pl.BlockSpec((tall, depth), lambda i: (i, 0)),
            pl.BlockSpec((depth, units), lambda i: (0, 0)),
            pl.BlockSpec((1, units), lambda i: (0, 0)),
        ],
        out_specs=[
            pl.BlockSpec((tall, units), lambda i: (i, 0)),
            pl.BlockSpec((tall, units), lambda i: (i, 0)),
        ],
        compiler_params=pltpu.CompilerParams(vmem_limit_bytes=20 * 1024 * 1024),
    )(rows, weight, bias)


EMBED_ROWS = 128
EMBED_PART = 16
MARGIN = 256


def embed_kernel(
    start_ref, span_ref, own_ref, tok_ref, pos_ref, seq_ref, row_ref, low_ref, emb_ref, norm_ref,
    padded, placed, normed,
):
    slots = tok_ref.shape[0]
    blocks, own_blocks = slots // EMBED_ROWS, emb_ref.shape[0] // EMBED_ROWS
    padded[pl.ds(MARGIN, pos_ref.shape[0])] = pos_ref[...]
    gain, shift = row_ref[0:1], row_ref[3:4]

    def one_block(b, carry):
        rows = block_span(b, EMBED_ROWS)
        seq = seq_ref[rows, 0:1]

        def pick(s, state):
            first = MARGIN + 2 + b * EMBED_ROWS - start_ref[s]
            base = first // 8
            shift = EMBED_PART + 8 - (first - base * 8)
            for at in range(0, EMBED_ROWS, EMBED_PART):
                window = padded[pl.ds(pl.multiple_of(base * 8 + at, 8), EMBED_PART + 8)]
                window = pltpu.roll(window, shift, 0)[:EMBED_PART]
                local = pl.ds(at, EMBED_PART)
                placed[local] = jnp.where(seq[at : at + EMBED_PART] == s, window, placed[local])
            return state

        lax.fori_loop(span_ref[0, b], span_ref[1, b], pick, 0)
        own = b - own_ref[0] * own_blocks
        kept = (own >= 0) & (own < own_blocks)
        own_first = jnp.where(kept, own, 0) * EMBED_ROWS
        for at in range(0, EMBED_ROWS, EMBED_PART):
            local = pl.ds(pl.multiple_of(b * EMBED_ROWS + at, EMBED_PART), EMBED_PART)
            emb = tok_ref[local].astype(jnp.float32) + placed[pl.ds(at, EMBED_PART)]
            norm = norm_rows(emb, gain, shift)
            low_ref[local] = norm.astype(jnp.bfloat16)
            placed[pl.ds(at, EMBED_PART)] = emb
            normed[pl.ds(at, EMBED_PART)] = norm

        @pl.when(kept)
        def _():
            own_rows = pl.ds(pl.multiple_of(own_first, EMBED_ROWS), EMBED_ROWS)
            emb_ref[own_rows] = placed[...]
            norm_ref[own_rows] = normed[...]

        return carry

    lax.fori_loop(0, blocks, one_block, 0)


def embed(tok_all, pos_full, seq_ids, lengths, row_params):
    slots, depth = tok_all.shape
    own = slots // lax.axis_size("tensor")
    ends = jnp.cumsum(lengths)
    starts = ends - lengths
    first = jnp.arange(slots // EMBED_ROWS, dtype=jnp.int32) * EMBED_ROWS
    spans = jnp.stack(
        [
            jnp.sum((ends[None, :] <= first[:, None]).astype(jnp.int32), axis=1),
            jnp.sum((starts[None, :] < first[:, None] + EMBED_ROWS).astype(jnp.int32), axis=1),
        ]
    )
    return pl.pallas_call(
        embed_kernel,
        out_shape=[
            shaped((slots, depth), jnp.bfloat16),
            shaped((own, depth), jnp.float32),
            shaped((own, depth), jnp.float32),
        ],
        in_specs=[in_scalars()] * 3 + [in_vmem()] * 4,
        out_specs=[in_vmem()] * 3,
        scratch_shapes=[
            pltpu.VMEM((MARGIN + MAXLEN + EMBED_ROWS + 24, depth), jnp.float32),
            pltpu.VMEM((EMBED_ROWS, depth), jnp.float32),
            pltpu.VMEM((EMBED_ROWS, depth), jnp.float32),
        ],
        compiler_params=pltpu.CompilerParams(vmem_limit_bytes=28 * 1024 * 1024),
    )(
        starts,
        spans,
        lax.axis_index("tensor").astype(jnp.int32)[None],
        tok_all,
        pos_full,
        seq_ids[:, None],
        row_params,
    )


SCATTER_ROWS = 512


def scatter_kernel(index_ref, rows_ref, grad_ref, square_ref):
    first = pl.program_id(0) * SCATTER_ROWS
    slots = index_ref.shape[1]
    here = (
        lax.broadcasted_iota(jnp.int32, (SCATTER_ROWS, slots), 0) + first == index_ref[...]
    ).astype(jnp.float32)
    grad = multiply_arrays(here.astype(jnp.bfloat16), rows_ref[...])
    grad_ref[...] = grad

    @pl.when(pl.program_id(0) == 0)
    def _():
        square_ref[...] = jnp.zeros_like(square_ref)

    square_ref[...] += eight_rows(grad * grad)


def scatter_rows(index, rows, height):
    slots, width = rows.shape
    return pl.pallas_call(
        scatter_kernel,
        grid=(pl.cdiv(height, SCATTER_ROWS),),
        out_shape=[shaped((height, width), jnp.float32), shaped((8, width), jnp.float32)],
        in_specs=[
            pl.BlockSpec((1, slots), lambda i: (0, 0)),
            pl.BlockSpec((slots, width), lambda i: (0, 0)),
        ],
        out_specs=[
            pl.BlockSpec((SCATTER_ROWS, width), lambda i: (i, 0)),
            pl.BlockSpec((8, width), lambda i: (0, 0)),
        ],
        compiler_params=pltpu.CompilerParams(vmem_limit_bytes=20 * 1024 * 1024),
    )(index[None], rows)


def layer_forward(embedded, seq_ids, bounds, members, counts, row_params, col_local, layer_mats):
    first_moment_all, emb_rows, norm_first = embedded
    qkv_full, out_full, up_half, down_low = layer_mats
    col_width = col_local.shape[1]
    qkv_bias = jnp.concatenate([col_local[0], jnp.zeros_like(col_local[0]), col_local[1]])
    qkv_out = (multiply_arrays(first_moment_all, qkv_full) + qkv_bias).astype(jnp.bfloat16)
    attn_low, log_total = attend(qkv_out, seq_ids, bounds)
    first_back = jnp.einsum("tc,dc->td", attn_low, out_full, preferred_element_type=jnp.float32)
    second_all, first_sum, norm_second, up_full, _, down_full = exchange(
        5,
        FoldNormSpread(first_back.astype(jnp.bfloat16), norm_first, row_params),
        SpreadCross(up_half),
        spread_grid(down_low),
    )
    up_full = up_full.reshape(D, -1)
    down_full = down_full.reshape(D, -1)
    hidden_low, slope = expand(second_all, up_full, col_local[2:].reshape(1, -1))
    second_back = jnp.einsum("tf,df->td", hidden_low, down_full, preferred_element_type=jnp.float32)
    second_sum, pooled = exchange(
        7, FoldPool(second_back.astype(jnp.bfloat16), norm_second, members, counts, row_params)
    )
    saved_vals = (
        emb_rows,
        first_moment_all,
        qkv_out,
        log_total,
        attn_low,
        first_sum,
        second_all,
        slope,
        hidden_low,
        second_sum,
    )
    return (pooled, saved_vals, (qkv_full, out_full, up_full, down_full))


def turned_grad(left_all, right_all):
    grad = jnp.einsum("td,tc->dc", left_all, right_all, preferred_element_type=jnp.float32)
    groups = lax.axis_size("dp")
    return grad.astype(jnp.bfloat16).reshape(groups, grad.shape[0] // groups, grad.shape[1])


def layer_backward(pooled_grad, counts, members, seq_ids, bounds, row_params, layer_mats, saved_vals):
    qkv_full, out_full, up_full, down_full = layer_mats
    (
        emb_rows,
        first_moment_all,
        qkv_out,
        log_total,
        attn_low,
        first_sum,
        second_all,
        slope,
        hidden_low,
        second_sum,
    ) = saved_vals
    col_width = out_full.shape[1]
    mixed_all, grad_second, side_c = exchange(
        10, PullSpread(pooled_grad, counts, jnp.tile(members.T, (1, 3)), second_sum, row_params)
    )
    down_grad = turned_grad(mixed_all, hidden_low)
    up_low = (multiply_arrays(mixed_all, down_full) * slope).astype(jnp.bfloat16)
    up_grad = turned_grad(second_all, up_low)
    second_back = jnp.einsum(
        "tf,df->td", up_low, up_full, preferred_element_type=jnp.float32
    ).astype(jnp.bfloat16)
    branch_all, grad_first, side_b, _, down_sum, down_squares, up_half = exchange(
        11,
        FoldPullSpread(second_back, grad_second, first_sum, row_params),
        reduce_grid(down_grad, turned=True),
        Later(ReduceCross(up_grad)),
    )
    out_grad = turned_grad(branch_all, attn_low)
    attn_grad = multiply_arrays(branch_all, out_full).astype(jnp.bfloat16)
    qkv_low = attend_back(qkv_out, attn_grad, log_total, seq_ids, bounds)
    qkv_grad = turned_grad(first_moment_all, qkv_low)
    first_back = jnp.einsum(
        "tc,dc->td", qkv_low, qkv_full, preferred_element_type=jnp.float32
    ).astype(jnp.bfloat16)
    cols_grad, side_a, up_sum, up_squares, _, out_sum, out_squares, _, qkv_sum, qkv_squares = exchange(
        13,
        FoldPullSwap(first_back, grad_first, emb_rows, row_params),
        ReduceLine(up_half),
        reduce_grid(out_grad, turned=True),
        reduce_grid(qkv_grad, slabs=3),
    )
    qkv_cols = jnp.sum(qkv_low.astype(jnp.float32), axis=0).reshape(3, col_width)
    up_cols = jnp.sum(up_low.astype(jnp.float32), axis=0).reshape(-1, col_width)
    col_grad = jnp.concatenate([qkv_cols[0:1], qkv_cols[2:3], up_cols], axis=0)
    row_grad = jnp.concatenate(
        [
            side_a[0:1],
            side_b[0:1],
            side_c[0:1],
            side_a[1:2],
            side_b[1:2],
            side_c[1:2],
            side_b[2:3],
            side_c[2:3],
        ]
    )
    return (
        cols_grad,
        (qkv_sum, out_sum, up_sum, down_sum),
        (qkv_squares, out_squares, up_squares + down_squares),
        col_grad,
        row_grad,
    )


def plan_kernel(capacity, vocab_local, groups, perm_ref, low_ref, high_ref, pair_ref, slot_ref, ask_ref, id_buf, own_buf):
    slots = perm_ref.shape[1]
    table_rows = low_ref.shape[1]
    block = 128
    blocks = slots // block
    perm = perm_ref[...]
    high_part = perm // 128
    low_part = perm - high_part * 128
    chooser = (lax.broadcasted_iota(jnp.int32, (table_rows, slots), 0) == high_part).astype(
        jnp.float32
    ).astype(jnp.bfloat16)
    value = multiply_arrays(low_ref[...], chooser) + 256.0 * multiply_arrays(high_ref[...], chooser)
    lane_match = lax.broadcasted_iota(jnp.int32, (128, slots), 0) == low_part
    ids = jnp.sum(jnp.where(lane_match, value, 0.0), axis=0, keepdims=True)
    for b in range(blocks):
        id_buf[pl.ds(b * block, block), :] = jnp.broadcast_to(
            ids[:, b * block : (b + 1) * block], (block, block)
        ).T
    place = lax.broadcasted_iota(jnp.int32, (1, slots), 1).astype(jnp.float32)
    rows = lax.broadcasted_iota(jnp.int32, (block, 1), 0).astype(jnp.float32)

    def earliest(b, best):
        column = id_buf[pl.ds(pl.multiple_of(b * block, block), block), 0:1]
        index = rows + (b * block).astype(jnp.float32)
        found = jnp.where(column == ids, index, 1e9)
        return jnp.minimum(best, jnp.min(found, axis=0, keepdims=True))

    least = lax.fori_loop(0, blocks, earliest, jnp.full((1, slots), 1e9, jnp.float32))
    first = least == place
    owner = jnp.zeros((1, slots), jnp.float32)
    for index in range(1, groups):
        owner = owner + jnp.where(ids >= float(index * vocab_local), 1.0, 0.0)
    owner_rows = lax.broadcasted_iota(jnp.int32, (groups, slots), 0).astype(jnp.float32)
    marks = jnp.where(first & (owner == owner_rows), 1.0, 0.0)
    upper = jnp.where(
        lax.broadcasted_iota(jnp.int32, (block, block), 0)
        < lax.broadcasted_iota(jnp.int32, (block, block), 1),
        1.0,
        0.0,
    ).astype(jnp.bfloat16)
    running = jnp.zeros((groups, 1), jnp.float32)
    pieces = []
    for b in range(blocks):
        part = marks[:, b * block : (b + 1) * block]
        pieces.append(multiply_arrays(part.astype(jnp.bfloat16), upper) + running)
        running = running + jnp.sum(part, axis=1, keepdims=True)
    before = jnp.concatenate(pieces, axis=1)
    rank = jnp.sum(marks * before, axis=0, keepdims=True)
    own_slot = jnp.where(first & (rank < float(capacity)), owner * float(capacity) + rank, -1.0)
    for b in range(blocks):
        own_buf[pl.ds(b * block, block), :] = jnp.broadcast_to(
            own_slot[:, b * block : (b + 1) * block], (block, block)
        ).T
    list_rows = -(-capacity // 128)
    stride = list_rows * 128
    width = groups * stride
    index = lax.broadcasted_iota(jnp.int32, (1, width), 1)
    target = (index // stride * capacity + lax.rem(index, stride)).astype(jnp.float32)
    target = jnp.where(lax.rem(index, stride) < capacity, target, -2.0)

    def settle(b, carry):
        slot, listed = carry
        window = pl.ds(pl.multiple_of(b * block, block), block)
        column, slot_column = id_buf[window, 0:1], own_buf[window, 0:1]
        slot = jnp.maximum(
            slot, jnp.max(jnp.where(column == ids, slot_column, -1.0), axis=0, keepdims=True)
        )
        listed = jnp.maximum(
            listed, jnp.max(jnp.where(slot_column == target, column, -1.0), axis=0, keepdims=True)
        )
        return (slot, listed)

    slot, listed = lax.fori_loop(
        0,
        blocks,
        settle,
        (jnp.full((1, slots), -1.0, jnp.float32), jnp.full((1, width), -1.0, jnp.float32)),
    )
    slot_ref[...] = slot.astype(jnp.int32)
    listed = listed.astype(jnp.int32)
    most = jnp.max(running, axis=0, keepdims=True).astype(jnp.int32)
    for group in range(groups):
        for row in range(list_rows):
            first_lane = group * stride + row * 128
            ask_ref[group, row : row + 1] = listed[:, first_lane : first_lane + 128]
        ask_ref[group, list_rows : list_rows + 1] = pair_ref[...]
        ask_ref[group, list_rows + 1 :] = jnp.broadcast_to(most, (7 - list_rows, 128))


def make_plan(perm, all_ids, pair_row, capacity, vocab_local, groups):
    slots = perm.shape[0]
    table = all_ids.reshape(-1, 128).T
    high = table // 256
    low = table - high * 256
    return pl.pallas_call(
        partial(plan_kernel, capacity, vocab_local, groups),
        out_shape=[
            jax.ShapeDtypeStruct((1, slots), jnp.int32),
            jax.ShapeDtypeStruct((groups, 8, 128), jnp.int32),
        ],
        in_specs=[in_vmem()] * 4,
        out_specs=[in_vmem()] * 2,
        scratch_shapes=[pltpu.VMEM((slots, 128), jnp.float32), pltpu.VMEM((slots, 128), jnp.float32)],
        compiler_params=pltpu.CompilerParams(vmem_limit_bytes=20 * 1024 * 1024),
    )(perm[None], low.astype(jnp.bfloat16), high.astype(jnp.bfloat16), pair_row)


def loss_kernel(pooled_ref, head_ref, pair_ref, loss_ref, low_ref, grad_ref, back_ref):
    total = pooled_ref.shape[0]
    low = pooled_ref[...].astype(jnp.bfloat16)
    low_ref[...] = low
    head_low = head_ref[...].astype(jnp.bfloat16)
    vectors = multiply_arrays(low, head_low)
    depth = vectors.shape[1]
    lane = lax.broadcasted_iota(jnp.int32, vectors.shape, 1)
    across = lax.broadcasted_iota(jnp.int32, (total, total), 1)
    diagonal = lax.broadcasted_iota(jnp.int32, (total, total), 0) == across
    chosen = across == pair_ref[...]
    loss = jnp.zeros((1, 1), jnp.float32)
    grads = jnp.zeros(vectors.shape, jnp.float32)

    def exact(left, right, dims):
        return lax.dot_general(
            left, right, (dims, ((), ())), precision=HIGHEST_MODE, preferred_element_type=jnp.float32
        )

    for fraction in (16, 4, 1):
        prefix = jnp.where(lane < depth // fraction, vectors, 0.0)
        inverse = lax.rsqrt(jnp.sum(prefix * prefix, axis=1, keepdims=True) + 1e-06)
        unit = prefix * inverse
        logits = exact(unit, unit, ((1,), (1,))) / LOGIT_DIVISOR
        logits = jnp.where(diagonal, MASK_FILL, logits)
        top = jnp.max(logits, axis=1, keepdims=True)
        weights = jnp.exp(logits - top)
        weight_sum = jnp.sum(weights, axis=1, keepdims=True)
        positive = jnp.sum(jnp.where(chosen, logits, 0.0), axis=1, keepdims=True)
        loss = loss + jnp.sum(jnp.log(weight_sum) + top - positive, keepdims=True)
        pull = weights / weight_sum - jnp.where(chosen, 1.0, 0.0)
        unit_grad = (exact(pull, unit, ((1,), (0,))) + exact(pull, unit, ((0,), (0,)))) / LOGIT_DIVISOR
        unit_grad = jnp.where(lane < depth // fraction, unit_grad, 0.0)
        inner = jnp.sum(unit_grad * prefix, axis=1, keepdims=True)
        grads = grads + inverse * unit_grad - prefix * (inverse * inverse * inverse * inner)
    low_wide = low.astype(jnp.float32)
    head_squares = jnp.sum(
        exact(low_wide, low_wide, ((1,), (1,))) * exact(grads, grads, ((1,), (1,))), keepdims=True
    )
    line = lax.broadcasted_iota(jnp.int32, loss_ref.shape, 0)
    loss_ref[...] = jnp.where(line == 0, loss, head_squares)
    grad_ref[...] = grads
    pieces, rest = [], grads
    for _ in range(3):
        pieces.append(rest.astype(jnp.bfloat16))
        rest = rest - pieces[-1].astype(jnp.float32)
    product = lax.dot_general(
        jnp.concatenate(pieces, axis=0),
        head_low,
        (((1,), (1,)), ((), ())),
        preferred_element_type=jnp.float32,
    )
    back_ref[...] = product[:total] + product[total : 2 * total] + product[2 * total :]


def contrast_step(pooled, head_weight, pairs):
    total, depth = pooled.shape
    return pl.pallas_call(
        loss_kernel,
        out_shape=[
            jax.ShapeDtypeStruct((8, 128), jnp.float32),
            jax.ShapeDtypeStruct((total, depth), jnp.bfloat16),
            jax.ShapeDtypeStruct((total, depth), jnp.float32),
            jax.ShapeDtypeStruct((total, depth), jnp.float32),
        ],
        in_specs=[in_vmem()] * 3,
        out_specs=[in_vmem()] * 4,
        compiler_params=pltpu.CompilerParams(vmem_limit_bytes=20 * 1024 * 1024),
    )(pooled, head_weight, pairs[:, None])


CAPACITY = 192


def body(
    token_ids,
    slot_perm,
    seq_lengths,
    pair_index,
    tok_table,
    tok_first,
    tok_second,
    pos_table,
    pos_first,
    pos_second,
    query_key_value_weight,
    qkv_first,
    qkv_second,
    out_weight,
    out_first,
    out_second,
    up_weight,
    up_first,
    up_second,
    down_weight,
    down_first,
    down_second,
    head_weight,
    head_first,
    head_second,
    col_bias,
    col_first,
    col_second,
    row_params,
    row_first,
    row_second,
):
    groups = lax.axis_size("dp")
    tensor_count = lax.axis_size("tensor")
    group_index = lax.axis_index("dp")
    tensor_index = lax.axis_index("tensor")
    tok_dev = token_ids.shape[0]
    tok_grp = tok_dev * tensor_count
    col_width = pos_table.shape[1]
    vocab_local = tok_table.shape[0]
    column_start = tensor_index * col_width
    anchors = pair_index.shape[0]
    id_rows = tok_dev // 128
    pair_row = jnp.pad(pair_index, (0, 128 - anchors))[None]
    qkv_low = jnp.concatenate(
        [query_key_value_weight[:, third] for third in range(3)], axis=1
    ).astype(jnp.bfloat16)
    out_low = out_weight.T.astype(jnp.bfloat16)
    up_low = up_weight.astype(jnp.bfloat16).reshape(qkv_low.shape[0], -1)
    down_low = down_weight.reshape(-1, down_weight.shape[2]).T.astype(jnp.bfloat16)
    half = qkv_low.shape[0] // 2
    gathered, perms, qkv_first_half = exchange(
        1,
        GatherAll(token_ids.reshape(id_rows, 128)),
        Gather(slot_perm.reshape(id_rows, 128), "tensor"),
        SpreadLine(qkv_low[:half]),
    )
    all_ids = gathered.reshape(-1)
    own_perm = perms.reshape(-1)
    slot, request = make_plan(own_perm, all_ids, pair_row, CAPACITY, vocab_local, groups)
    slot = slot[0]
    list_rows = -(-CAPACITY // 128)
    asked = exchange(2, Swap(request, "dp"))
    pairs = asked[:, list_rows, :anchors].reshape(-1)
    overflow = jnp.max(asked[:, list_rows + 1]) > CAPACITY
    offset = group_index * vocab_local
    asked_rows = asked[:, :list_rows].reshape(groups, -1)[:, :CAPACITY].reshape(-1) - offset
    asked_safe = jnp.clip(asked_rows, 0, vocab_local - 1)
    sent_rows = jnp.take(tok_table, asked_safe, axis=0).astype(jnp.bfloat16)
    got_rows, pos_full, qkv_second_half = exchange(
        3,
        Swap(sent_rows.reshape(groups, CAPACITY, col_width), "dp"),
        Spread(pos_table, columns=True, chunks=1),
        SpreadLine(qkv_low[half:]),
    )
    got_rows = got_rows.reshape(-1, col_width)

    def chooser(slots):
        places = jnp.arange(groups * CAPACITY, dtype=jnp.int32)
        return (slots[:, None] == places[None, :]).astype(jnp.bfloat16)

    lengths = seq_lengths[0]
    seq_ids, positions, member = seq_layout(lengths, tok_grp)
    bounds = block_bounds(lengths, tok_grp)

    def every_slot_id():
        every_perm = lax.all_gather(slot_perm, ("dp", "tensor"), axis=0, tiled=True)
        return jnp.take(all_ids, every_perm, axis=0)

    def spread_wide():
        wanted = every_slot_id() - offset
        inside = (wanted >= 0) & (wanted < vocab_local)
        picked = jnp.take(
            tok_table.astype(jnp.bfloat16), jnp.clip(wanted, 0, vocab_local - 1), axis=0
        )
        return lax.psum_scatter(
            jnp.where(inside[:, None], picked, jnp.zeros((), jnp.bfloat16)),
            "dp",
            scatter_dimension=0,
            tiled=True,
        )

    tok_cols = lax.cond(
        overflow,
        spread_wide,
        lambda: multiply_arrays(chooser(slot), got_rows).astype(jnp.bfloat16),
    )
    tok_all, _, out_full, qkv_full, up_half = exchange(
        4,
        Spread(tok_cols, columns=True),
        spread_grid(out_low),
        SpreadCross(qkv_first_half, qkv_second_half),
        SpreadLine(up_low),
    )
    layer_mats = (qkv_full.reshape(D, -1), out_full.reshape(D, -1), up_half, down_low)
    embedded = embed(tok_all, pos_full, seq_ids, lengths, row_params)
    members = lax.dynamic_slice_in_dim(member, tensor_index * tok_dev, tok_dev, 0).T.astype(
        jnp.bfloat16
    )
    counts = lengths.astype(jnp.float32)[:, None]
    pooled, saved_vals, layer_mats = layer_forward(
        embedded, seq_ids, bounds, members, counts, row_params, col_bias, layer_mats
    )
    loss_out, pooled_low, vec_grad, pooled_grad = contrast_step(
        pooled.reshape(-1, D), head_weight, pairs
    )
    head_sum = exact_multiply(pooled_low.astype(jnp.float32).T, vec_grad)
    cols_grad, sums, grid_squares, col_grad, row_grad = layer_backward(
        pooled_grad, counts, members, seq_ids, bounds, row_params, layer_mats, saved_vals
    )
    qkv_sum, out_sum, up_sum, down_sum = sums
    qkv_squares, out_squares, wide_squares = grid_squares
    cols_grad = cols_grad.reshape(tok_grp, col_width)
    pos_pick = (
        jnp.arange(pos_table.shape[0], dtype=jnp.int32)[:, None] == positions[None, :]
    ).astype(jnp.bfloat16)
    pos_grad = multiply_arrays(pos_pick, cols_grad)
    shared = jnp.concatenate([pos_grad, col_grad], axis=0)
    shared_rows = -(-shared.shape[0] // (16 * groups)) * 16
    shared = jnp.pad(shared, ((0, shared_rows * groups - shared.shape[0]), (0, 0)))
    merged = jnp.einsum(
        "kn,kc->nc",
        chooser(lax.optimization_barrier(slot)),
        cols_grad,
        preferred_element_type=jnp.float32,
    )
    back_rows, _, shared_own, shared_squares = exchange(
        15,
        Swap(merged.astype(jnp.bfloat16).reshape(groups, CAPACITY, col_width), "dp"),
        reduce_grid(shared.astype(jnp.bfloat16).reshape(groups, shared_rows, col_width)),
    )

    def add_wide():
        wanted = every_slot_id() - offset
        inside = (wanted >= 0) & (wanted < vocab_local)
        grad = (
            jnp.zeros(tok_table.shape, jnp.float32)
            .at[jnp.clip(wanted, 0, vocab_local - 1)]
            .add(
                jnp.where(
                    inside[:, None],
                    lax.all_gather(cols_grad, "dp", axis=0, tiled=True).astype(jnp.float32),
                    0.0,
                )
            )
        )
        squares = jnp.sum(grad * grad, axis=0, keepdims=True)
        return (grad, jnp.pad(squares, ((0, 7), (0, 0))))

    tok_grad, tok_squares = lax.cond(
        overflow,
        add_wide,
        lambda: tuple(scatter_rows(asked_rows, back_rows.reshape(-1, col_width), vocab_local)),
    )
    up_grad = up_sum.reshape(up_weight.shape)
    down_grad = down_sum.reshape(down_weight.shape)

    def widen(*parts):
        joined = jnp.concatenate(parts, axis=1)
        return jnp.pad(joined, ((0, 0), (0, D - joined.shape[1])))

    square_rows = (
        widen(wide_squares)
        + widen(qkv_squares, out_squares)
        + widen(tok_squares, shared_squares)
    )
    row_block = jnp.concatenate([row_grad, square_rows], axis=0)
    row_total, shared_sum = exchange(16, SumAll(row_block, False), GatherGrid(shared_own.astype(jnp.bfloat16)))
    row_total = row_total[0]
    shared_sum = shared_sum.reshape(-1, col_width).astype(jnp.float32)
    pos_own = shared_sum[: pos_table.shape[0]]
    col_own = shared_sum[pos_table.shape[0] : pos_table.shape[0] + col_bias.shape[0]]
    row_sum = row_total[:8]
    squares = jnp.sum(row_total[8:]) + jnp.sum(row_sum * row_sum) + loss_out[1, 0]
    grad_norm = jnp.sqrt(squares)
    clip_scale = jnp.minimum(1.0, CLIP_NORM / (grad_norm + 1e-06))
    tok_new = adam_step(
        tok_table, tok_first, tok_second, tok_grad * clip_scale, RATE_MATRIX, DECAY_RATE
    )
    pos_new = adam_step(
        pos_table, pos_first, pos_second, pos_own * clip_scale, RATE_MATRIX, DECAY_RATE
    )
    qkv_new = adam_step(
        query_key_value_weight.swapaxes(0, 1),
        qkv_first.swapaxes(0, 1),
        qkv_second.swapaxes(0, 1),
        qkv_sum * clip_scale,
        RATE_MATRIX,
        DECAY_RATE,
    )
    qkv_new = tuple(item.swapaxes(0, 1) for item in qkv_new)
    out_new = adam_step(
        out_weight, out_first, out_second, out_sum * clip_scale, RATE_MATRIX, DECAY_RATE
    )
    up_new = adam_step(
        up_weight, up_first, up_second, up_grad * clip_scale, RATE_MATRIX, DECAY_RATE
    )
    down_new = adam_step(
        down_weight, down_first, down_second, down_grad * clip_scale, RATE_MATRIX, DECAY_RATE
    )
    head_new = adam_step(
        head_weight, head_first, head_second, head_sum * clip_scale, RATE_MATRIX, DECAY_RATE
    )
    col_new = adam_step(col_bias, col_first, col_second, col_own * clip_scale, RATE_VECTOR, 0.0)
    row_new = adam_step(row_params, row_first, row_second, row_sum * clip_scale, RATE_VECTOR, 0.0)
    return (loss_out[0, 0], grad_norm) + tok_new + pos_new + qkv_new + out_new + up_new + down_new + head_new + col_new + row_new


def solution(mesh):
    placed = (
        P(("dp", "tensor")),
        P(("dp", "tensor")),
        P("dp", None),
        P("dp"),
        P("dp", "tensor"),
        P("dp", "tensor"),
        P("dp", "tensor"),
        P(None, "tensor"),
        P(None, "tensor"),
        P(None, "tensor"),
        P("dp", None, "tensor"),
        P("dp", None, "tensor"),
        P("dp", None, "tensor"),
        P("tensor", "dp"),
        P("tensor", "dp"),
        P("tensor", "dp"),
        P("dp", None, "tensor"),
        P("dp", None, "tensor"),
        P("dp", None, "tensor"),
        P(None, "tensor", "dp"),
        P(None, "tensor", "dp"),
        P(None, "tensor", "dp"),
        P(),
        P(),
        P(),
        P(None, "tensor"),
        P(None, "tensor"),
        P(None, "tensor"),
        P(),
        P(),
        P(),
    )
    return jax.shard_map(
        body,
        mesh=mesh,
        in_specs=placed,
        out_specs=(
            P(),
            P(),
            P("dp", "tensor"),
            P("dp", "tensor"),
            P("dp", "tensor"),
            P(None, "tensor"),
            P(None, "tensor"),
            P(None, "tensor"),
            P("dp", None, "tensor"),
            P("dp", None, "tensor"),
            P("dp", None, "tensor"),
            P("tensor", "dp"),
            P("tensor", "dp"),
            P("tensor", "dp"),
            P("dp", None, "tensor"),
            P("dp", None, "tensor"),
            P("dp", None, "tensor"),
            P(None, "tensor", "dp"),
            P(None, "tensor", "dp"),
            P(None, "tensor", "dp"),
            P(),
            P(),
            P(),
            P(None, "tensor"),
            P(None, "tensor"),
            P(None, "tensor"),
            P(),
            P(),
            P(),
        ),
        check_vma=False,
    )
```

```python
from functools import partial

import jax
import jax.numpy as jnp
from jax import lax
from jax.experimental import pallas as pl
from jax.experimental.pallas import tpu as pltpu
from jax.sharding import PartitionSpec as P

D = 1024
HEAD = 64
MAXLEN = 512
STEP = 10


HIGHEST_MODE = lax.Precision.HIGHEST
LN_EPS = 1e-05
LOGIT_DIVISOR = 0.05
CLIP_NORM = 0.25
BETA_FIRST = 0.9
BETA_SECOND = 0.999
ADAM_EPS = 1e-08
RATE_MATRIX = 0.05
RATE_VECTOR = 0.5
DECAY_RATE = 0.01
MASK_FILL = -1e30


def multiply_arrays(left_mat, right_mat):
    return jnp.dot(left_mat, right_mat, preferred_element_type=jnp.float32)


def exact_multiply(left_mat, right_mat):
    return jnp.dot(left_mat, right_mat, precision=HIGHEST_MODE, preferred_element_type=jnp.float32)


def norm_rows(values, gain_row, bias_row):
    center = values - jnp.mean(values, axis=1, keepdims=True)
    inverse = lax.rsqrt(jnp.mean(center * center, axis=1, keepdims=True) + LN_EPS)
    return center * inverse * gain_row + bias_row


def seq_layout(lengths, slot_total):
    seq_ends = jnp.cumsum(lengths)
    starts = seq_ends - lengths
    slot_index = jnp.arange(slot_total, dtype=jnp.int32)
    member = (slot_index[:, None] >= starts[None, :]) & (slot_index[:, None] < seq_ends[None, :])
    seq_count = jnp.arange(lengths.shape[0], dtype=jnp.int32)
    seq_ids = jnp.sum(jnp.where(member, seq_count[None, :], 0), axis=1)
    positions = slot_index - jnp.sum(jnp.where(member, starts[None, :], 0), axis=1) + 2
    return (seq_ids, positions, member)


def adam_step(weight, first_old, second_old, clipped, step_rate, decay_rate):
    first_new = BETA_FIRST * first_old + (1.0 - BETA_FIRST) * clipped
    second_new = BETA_SECOND * second_old + (1.0 - BETA_SECOND) * clipped * clipped
    first_hat = first_new / (1.0 - BETA_FIRST**STEP)
    second_hat = second_new / (1.0 - BETA_SECOND**STEP)
    weight_new = weight - step_rate * (
        first_hat / (jnp.sqrt(second_hat) + ADAM_EPS) + decay_rate * weight
    )
    return (weight_new, first_new, second_new)


MESH_IDS = pl.DeviceIdType.MESH
SPARE_BYTES = 6 * 1024 * 1024
CHUNKS = 4
LINE = 4


def in_vmem():
    return pl.BlockSpec(memory_space=pltpu.VMEM)


def shaped(shape, dtype):
    return jax.ShapeDtypeStruct(tuple(shape), dtype)


def dma(*shape):
    return pltpu.SemaphoreType.DMA(shape)


def remote(src, dst, send_sem, recv_sem, target):
    return pltpu.make_async_remote_copy(
        src_ref=src,
        dst_ref=dst,
        send_sem=send_sem,
        recv_sem=recv_sem,
        device_id=target,
        device_id_type=MESH_IDS,
    )


def room(*items):
    total = 0
    for item in items:
        size = 0
        if item.dtype == jnp.bfloat16:
            size = 2
        elif item.dtype == jnp.float32 or item.dtype == jnp.int32:
            size = 4
        for extent in item.shape[:-1]:
            size = size * extent
        total = total + size * (-(-item.shape[-1] // 128) * 128)
    return total + SPARE_BYTES


def comm_params(collective, limit):
    return pltpu.CompilerParams(
        collective_id=collective, has_side_effects=True, vmem_limit_bytes=limit
    )


def exchange(collective, *tasks):
    def kernel(*refs):
        at = 0
        for attribute in ("ins", "outs", "scratch"):
            for task in tasks:
                size = len(getattr(task, attribute))
                setattr(task, attribute + "_refs", refs[at : at + size])
                at += size
        barrier = pltpu.get_barrier_semaphore()
        pl.semaphore_wait(barrier, sum(task.hello(barrier) for task in tasks))
        for task in tasks:
            task.begin()
        for task in tasks:
            task.middle()
        for task in tasks:
            task.late()
        for task in tasks[1:]:
            task.end()
        tasks[0].end()

    results = pl.pallas_call(
        kernel,
        out_shape=[out for task in tasks for out in task.outs],
        in_specs=[in_vmem() for task in tasks for _ in task.ins],
        out_specs=[in_vmem() for task in tasks for _ in task.outs],
        scratch_shapes=[item for task in tasks for item in task.scratch],
        compiler_params=comm_params(
            collective,
            room(*[item for task in tasks for item in task.ins + task.outs + task.scratch]),
        ),
    )(*[array for task in tasks for array in task.ins])
    return results[0] if len(results) == 1 else results


def tensor_place(width):
    me = lax.axis_index("tensor")
    core = lax.rem(me, 2)
    row = me // 2
    mate = me + 1 - 2 * core
    return (me, core, row, mate)


class Task:
    def hello(self, barrier):
        partners = self.partners()
        for partner in partners:
            pl.semaphore_signal(barrier, inc=1, device_id=partner, device_id_type=MESH_IDS)
        return len(partners)

    def begin(self):
        pass

    def middle(self):
        pass

    def late(self):
        pass

    def end(self):
        pass


class Pair(Task):
    def __init__(self):
        self.width = lax.axis_size("tensor")
        self.rows = self.width // 2

    def partners(self):
        me, core, row, mate = tensor_place(self.width)
        return [{"tensor": mate}] + [
            {"tensor": lax.rem(row + step, self.rows) * 2 + core} for step in range(1, self.rows)
        ]


class Spread(Pair):
    def __init__(self, block, columns=False, chunks=CHUNKS):
        super().__init__()
        height, depth = block.shape
        self.columns, self.chunks = columns, chunks
        self.ins = (block,)
        whole = (height, self.width * depth) if columns else (self.width * height, depth)
        self.outs = (shaped(whole, block.dtype),)
        self.scratch = tuple(dma(self.rows, chunks) for _ in range(4))

    def window(self, owner, part=None):
        (x_ref,), (o_ref,) = self.ins_refs, self.outs_refs
        height, depth = x_ref.shape
        size = height // self.chunks
        if self.columns:
            lanes = pl.ds(pl.multiple_of(owner * depth, depth), depth)
            if part is None or self.chunks == 1:
                return o_ref.at[:, lanes]
            return o_ref.at[pl.ds(part * size, size), lanes]
        if part is None:
            return o_ref.at[pl.ds(pl.multiple_of(owner * height, height), height)]
        return o_ref.at[pl.ds(pl.multiple_of(owner * height + part * size, size), size)]

    def begin(self):
        (x_ref,) = self.ins_refs
        far_send, far_recv, near_send, near_recv = self.scratch_refs
        me, core, row, mate = tensor_place(self.width)
        size = x_ref.shape[0] // self.chunks
        self.far = {}
        for part in range(self.chunks):
            source = x_ref if self.chunks == 1 else x_ref.at[pl.ds(part * size, size)]
            for step in range(1, self.rows):
                copy = remote(
                    source,
                    self.window(me, part),
                    far_send.at[step, part],
                    far_recv.at[step, part],
                    {"tensor": lax.rem(row + step, self.rows) * 2 + core},
                )
                copy.start()
                self.far[step, part] = copy
        copy = remote(
            x_ref, self.window(me), near_send.at[0, 0], near_recv.at[0, 0], {"tensor": mate}
        )
        copy.start()
        self.near = [copy]
        self.window(me)[...] = x_ref[...]

    def middle(self):
        far_send, far_recv, near_send, near_recv = self.scratch_refs
        me, core, row, mate = tensor_place(self.width)
        for part in range(self.chunks):
            for step in range(1, self.rows):
                self.far[step, part].wait_recv()
                source = lax.rem(row + self.rows - step, self.rows) * 2 + core
                onward = remote(
                    self.window(source, part),
                    self.window(source, part),
                    near_send.at[step, part],
                    near_recv.at[step, part],
                    {"tensor": mate},
                )
                onward.start()
                self.near.append(onward)

    def end(self):
        for copy in self.near:
            copy.wait()
        for copy in self.far.values():
            copy.wait_send()


class Fold(Pair):
    def __init__(self, parts, chunks=CHUNKS):
        super().__init__()
        height, depth = parts.shape[0] // self.width, parts.shape[1]
        far_rows = max(self.rows - 1, 1)
        self.chunks, self.height, self.depth = chunks, height, depth
        self.parts = parts
        self.fold_scratch = (
            pltpu.VMEM((self.rows, height, depth), jnp.bfloat16),
            pltpu.VMEM((far_rows, height, depth), jnp.bfloat16),
            pltpu.VMEM((far_rows, height, depth), jnp.bfloat16),
            pltpu.VMEM((height, depth), jnp.float32),
        ) + tuple(dma(self.rows, chunks) for _ in range(4))

    def span(self, owner, part):
        size = self.height // self.chunks
        return pl.ds(pl.multiple_of(owner * self.height + part * size, size), size)

    def local(self, part):
        size = self.height // self.chunks
        return pl.ds(part * size, size)

    def begin(self):
        p_ref = self.ins_refs[0]
        near_buf, near_send, near_recv = self.scratch_refs[0], *self.scratch_refs[4:6]
        me, core, row, mate = tensor_place(self.width)
        self.near = {}
        for step in list(range(1, self.rows)) + [0]:
            dest_row = lax.rem(row + step, self.rows)
            for part in range(self.chunks):
                copy = remote(
                    p_ref.at[self.span(dest_row * 2 + 1 - core, part)],
                    near_buf.at[step, self.local(part)],
                    near_send.at[step, part],
                    near_recv.at[step, part],
                    {"tensor": mate},
                )
                copy.start()
                self.near[step, part] = copy

    def middle(self):
        p_ref = self.ins_refs[0]
        near_buf, sum_buf, far_buf, total_buf = self.scratch_refs[:4]
        far_send, far_recv = self.scratch_refs[6:8]
        me, core, row, mate = tensor_place(self.width)
        self.far = {}
        for step in range(1, self.rows):
            dest = lax.rem(row + step, self.rows) * 2 + core
            for part in range(self.chunks):
                local = self.local(part)
                self.near[step, part].wait_recv()
                sum_buf[step - 1, local] = (
                    p_ref[self.span(dest, part)].astype(jnp.float32)
                    + near_buf[step, local].astype(jnp.float32)
                ).astype(jnp.bfloat16)
                copy = remote(
                    sum_buf.at[step - 1, local],
                    far_buf.at[step - 1, local],
                    far_send.at[step - 1, part],
                    far_recv.at[step - 1, part],
                    {"tensor": dest},
                )
                copy.start()
                self.far[step, part] = copy
        for part in range(self.chunks):
            local = self.local(part)
            self.near[0, part].wait_recv()
            total_buf[local] = p_ref[self.span(me, part)].astype(jnp.float32) + near_buf[
                0, local
            ].astype(jnp.float32)

    def folded(self, part):
        far_buf, total_buf = self.scratch_refs[2:4]
        local = self.local(part)
        total = total_buf[local]
        for step in range(1, self.rows):
            self.far[step, part].wait_recv()
            total = total + far_buf[step - 1, local].astype(jnp.float32)
        return total

    def settle_fold(self):
        for copy in list(self.near.values()) + list(self.far.values()):
            copy.wait_send()


class Relay:
    def relay_scratch(self):
        return (pltpu.VMEM((self.height, self.depth), jnp.bfloat16),) + tuple(
            dma(self.rows, self.chunks) for _ in range(4)
        )

    def relay_open(self, part, low):
        buf, far_send, far_recv, near_send, near_recv = self.scratch_refs[-5:]
        all_ref = self.outs_refs[0]
        me, core, row, mate = tensor_place(self.width)
        local = self.local(part)
        buf[local] = low
        if part == 0:
            self.sent, self.relay_near = {}, []
        for step in range(1, self.rows):
            copy = remote(
                buf.at[local],
                all_ref.at[self.span(me, part)],
                far_send.at[step, part],
                far_recv.at[step, part],
                {"tensor": lax.rem(row + step, self.rows) * 2 + core},
            )
            copy.start()
            self.sent[step, part] = copy
        copy = remote(
            buf.at[local],
            all_ref.at[self.span(me, part)],
            near_send.at[0, part],
            near_recv.at[0, part],
            {"tensor": mate},
        )
        copy.start()
        self.relay_near.append(copy)
        all_ref[self.span(me, part)] = low

    def relay_close(self):
        buf, far_send, far_recv, near_send, near_recv = self.scratch_refs[-5:]
        all_ref = self.outs_refs[0]
        me, core, row, mate = tensor_place(self.width)
        for part in range(self.chunks):
            for step in range(1, self.rows):
                self.sent[step, part].wait_recv()
                source = lax.rem(row + self.rows - step, self.rows) * 2 + core
                window = all_ref.at[self.span(source, part)]
                copy = remote(
                    window, window, near_send.at[step, part], near_recv.at[step, part], {"tensor": mate}
                )
                copy.start()
                self.relay_near.append(copy)
        for copy in self.relay_near:
            copy.wait()
        for copy in self.sent.values():
            copy.wait_send()


def split_three(values):
    pieces, rest = [], values
    for _ in range(3):
        pieces.append(rest.astype(jnp.bfloat16))
        rest = rest - pieces[-1].astype(jnp.float32)
    return pieces


def norm_pull(values, gain, grads):
    center = values - jnp.mean(values, axis=1, keepdims=True)
    inverse = lax.rsqrt(jnp.mean(center * center, axis=1, keepdims=True) + LN_EPS)
    unit = center * inverse
    scaled = grads * gain
    pull = inverse * (
        scaled
        - jnp.mean(scaled, axis=1, keepdims=True)
        - unit * jnp.mean(scaled * unit, axis=1, keepdims=True)
    )
    return (
        pull,
        jnp.sum(grads * unit, axis=0, keepdims=True),
        jnp.sum(grads, axis=0, keepdims=True),
    )


class FoldNormSpread(Relay, Fold):
    def __init__(self, parts, residual, row_params):
        super().__init__(parts)
        own = shaped((self.height, self.depth), jnp.float32)
        self.ins = (parts, residual, row_params)
        self.outs = (shaped(parts.shape, jnp.bfloat16), own, own)
        self.scratch = self.fold_scratch + self.relay_scratch()

    def late(self):
        p_ref, residual_ref, row_ref = self.ins_refs
        all_ref, sum_ref, norm_ref = self.outs_refs
        for part in range(self.chunks):
            local = self.local(part)
            total = residual_ref[local] + self.folded(part) + row_ref[6:7]
            sum_ref[local] = total
            norm = norm_rows(total, row_ref[1:2], row_ref[4:5])
            norm_ref[local] = norm
            self.relay_open(part, norm.astype(jnp.bfloat16))

    def end(self):
        self.relay_close()
        self.settle_fold()


class FoldPullSpread(Relay, Fold):
    def __init__(self, parts, residual, values, row_params):
        super().__init__(parts)
        own = shaped((self.height, self.depth), jnp.float32)
        self.ins = (parts, residual, values, row_params)
        self.outs = (shaped(parts.shape, jnp.bfloat16), own, shaped((8, self.depth), jnp.float32))
        self.scratch = self.fold_scratch + self.relay_scratch()

    def late(self):
        p_ref, residual_ref, value_ref, row_ref = self.ins_refs
        all_ref, grad_ref, side_ref = self.outs_refs
        side_ref[...] = jnp.zeros_like(side_ref)
        for part in range(self.chunks):
            local = self.local(part)
            pull, gain, shift = norm_pull(
                value_ref[local], row_ref[1:2], residual_ref[local] + self.folded(part)
            )
            grad_ref[local] = pull
            low = pull.astype(jnp.bfloat16)
            self.relay_open(part, low)
            side_ref[0:1] += gain
            side_ref[1:2] += shift
            side_ref[2:3] += jnp.sum(low.astype(jnp.float32), axis=0, keepdims=True)

    def end(self):
        self.relay_close()
        self.settle_fold()


class PullSpread(Relay, Pair):
    def __init__(self, pooled_grad, counts, members, values, row_params):
        super().__init__()
        self.height, self.depth = values.shape
        self.chunks = CHUNKS
        own = shaped(values.shape, jnp.float32)
        self.ins = (pooled_grad, counts, members, values, row_params)
        self.outs = (
            shaped((self.width * self.height, self.depth), jnp.bfloat16),
            own,
            shaped((8, self.depth), jnp.float32),
        )
        self.scratch = self.relay_scratch()

    span, local = Fold.span, Fold.local

    def begin(self):
        pooled_ref, count_ref, member_ref, value_ref, row_ref = self.ins_refs
        all_ref, grad_ref, side_ref = self.outs_refs
        side_ref[...] = jnp.zeros_like(side_ref)
        anchors = count_ref.shape[0]
        rows = block_span(lax.axis_index("dp"), anchors)
        pieces = jnp.concatenate(split_three(pooled_ref[rows] / count_ref[...]), axis=0)
        for part in range(self.chunks):
            local = self.local(part)
            grads = multiply_arrays(member_ref[local], pieces)
            pull, gain, shift = norm_pull(value_ref[local], row_ref[2:3], grads)
            grad_ref[local] = pull
            low = pull.astype(jnp.bfloat16)
            self.relay_open(part, low)
            side_ref[0:1] += gain
            side_ref[1:2] += shift
            side_ref[2:3] += jnp.sum(low.astype(jnp.float32), axis=0, keepdims=True)

    def end(self):
        self.relay_close()


class Swap(Task):
    def __init__(self, blocks, axis):
        self.axis, self.count = axis, lax.axis_size(axis)
        self.ins = (blocks,)
        self.outs = (shaped(blocks.shape, blocks.dtype),)
        self.scratch = (dma(self.count), dma(self.count))

    def others(self):
        me = lax.axis_index(self.axis)
        return [lax.rem(me + step, self.count) for step in range(1, self.count)]

    def partners(self):
        return [{self.axis: other} for other in self.others()]

    def begin(self):
        (x_ref,), (o_ref,), (send, recv) = self.ins_refs, self.outs_refs, self.scratch_refs
        me = lax.axis_index(self.axis)
        self.copies = [
            remote(x_ref.at[other], o_ref.at[me], send.at[i], recv.at[i], {self.axis: other})
            for i, other in enumerate(self.others())
        ]
        for copy in self.copies:
            copy.start()
        o_ref[me] = x_ref[me]

    def end(self):
        for copy in self.copies:
            copy.wait()


class Gather(Swap):
    def __init__(self, block, axis):
        super().__init__(block, axis)
        self.outs = (shaped((self.count,) + block.shape, block.dtype),)

    def begin(self):
        (x_ref,), (o_ref,), (send, recv) = self.ins_refs, self.outs_refs, self.scratch_refs
        me = lax.axis_index(self.axis)
        self.copies = [
            remote(x_ref, o_ref.at[me], send.at[i], recv.at[i], {self.axis: other})
            for i, other in enumerate(self.others())
        ]
        for copy in self.copies:
            copy.start()
        o_ref[me] = x_ref[...]


class GatherAll(Task):
    def __init__(self, block):
        self.width = lax.axis_size("tensor")
        self.total = total = lax.axis_size("dp") * self.width
        self.ins = (block,)
        self.outs = (shaped((total,) + block.shape, block.dtype),)
        self.scratch = (dma(total), dma(total))

    def me(self):
        return lax.axis_index("dp") * self.width + lax.axis_index("tensor")

    def place(self, step):
        other = lax.rem(self.me() + step, self.total)
        return (other // self.width, lax.rem(other, self.width))

    def copy(self, step):
        (x_ref,), (o_ref,), (send, recv) = self.ins_refs, self.outs_refs, self.scratch_refs
        return remote(x_ref, o_ref.at[self.me()], send.at[step], recv.at[step], self.place(step))

    def hello(self, barrier):
        def one(step, carry):
            pl.semaphore_signal(
                barrier, inc=1, device_id=self.place(step), device_id_type=MESH_IDS
            )
            return carry

        lax.fori_loop(1, self.total, one, 0)
        return self.total - 1

    def begin(self):
        def one(step, carry):
            self.copy(step).start()
            return carry

        lax.fori_loop(1, self.total, one, 0)
        self.outs_refs[0][self.me()] = self.ins_refs[0][...]

    def end(self):
        def one(step, carry):
            self.copy(step).wait()
            return carry

        lax.fori_loop(1, self.total, one, 0)


class FoldPool(Fold):
    def __init__(self, parts, residual, members, counts, row_params):
        super().__init__(parts)
        anchors = members.shape[0]
        self.total = SumAll(shaped((anchors, self.depth), jnp.float32), True)
        self.ins = (parts, residual, members, counts, row_params)
        self.outs = (shaped((self.height, self.depth), jnp.float32),) + self.total.outs
        self.scratch = (
            self.fold_scratch
            + (pltpu.VMEM((anchors, self.depth), jnp.float32),)
            + self.total.scratch
        )

    def hello(self, barrier):
        return super().hello(barrier) + self.total.hello(barrier)

    def end(self):
        p_ref, residual_ref, member_ref, count_ref, row_ref = self.ins_refs
        sum_ref = self.outs_refs[0]
        at = len(self.fold_scratch)
        pooled = self.scratch_refs[at]
        size = self.height // self.chunks
        parts = []
        for part in range(self.chunks):
            local = self.local(part)
            total = residual_ref[local] + self.folded(part) + row_ref[7:8]
            sum_ref[local] = total
            norm = norm_rows(total, row_ref[2:3], row_ref[5:6])
            member = member_ref[:, part * size : (part + 1) * size]
            for piece in split_three(norm):
                parts.append(multiply_arrays(member, piece))
        pooled[...] = sum(parts[1:], parts[0]) / count_ref[...]
        total = self.total
        total.ins_refs, total.outs_refs = (pooled,), self.outs_refs[1:]
        total.scratch_refs = self.scratch_refs[at + 1 :]
        total.begin()
        total.middle()
        total.end()
        self.settle_fold()


class FoldPullSwap(Fold):
    def __init__(self, parts, residual, values, row_params):
        super().__init__(parts)
        self.narrow = self.depth // self.width
        self.ins = (parts, residual, values, row_params)
        self.outs = (
            shaped((self.width, self.height, self.narrow), jnp.bfloat16),
            shaped((8, self.depth), jnp.float32),
        )
        self.scratch = self.fold_scratch + (
            pltpu.VMEM((self.height, self.depth), jnp.bfloat16),
            dma(self.width, self.chunks),
            dma(self.width, self.chunks),
        )

    def partners(self):
        me = lax.axis_index("tensor")
        return [{"tensor": lax.rem(me + step, self.width)} for step in range(1, self.width)]

    def late(self):
        p_ref, residual_ref, value_ref, row_ref = self.ins_refs
        cols_ref, side_ref = self.outs_refs
        buf, send, recv = self.scratch_refs[-3:]
        side_ref[...] = jnp.zeros_like(side_ref)
        me = lax.axis_index("tensor")

        def lanes(owner):
            return pl.ds(pl.multiple_of(owner * self.narrow, self.narrow), self.narrow)

        copies = []
        for part in range(self.chunks):
            local = self.local(part)
            pull, gain, shift = norm_pull(
                value_ref[local], row_ref[0:1], residual_ref[local] + self.folded(part)
            )
            buf[local] = pull.astype(jnp.bfloat16)
            for step in range(1, self.width):
                other = lax.rem(me + step, self.width)
                copy = remote(
                    buf.at[local, lanes(other)],
                    cols_ref.at[me, local],
                    send.at[step, part],
                    recv.at[step, part],
                    {"tensor": other},
                )
                copy.start()
                copies.append(copy)
            cols_ref[me, local] = buf[local, lanes(me)]
            side_ref[0:1] += gain
            side_ref[1:2] += shift
        self.copies = copies

    def end(self):
        for copy in self.copies:
            copy.wait()
        self.settle_fold()


def eight_rows(values):
    return jnp.sum(values.reshape(values.shape[0] // 8, 8, values.shape[1]), axis=0)


class GridTask(Task):
    def __init__(self):
        self.cross = lax.axis_size("dp") // LINE

    def place(self):
        me = lax.axis_index("dp")
        return (me // self.cross, lax.rem(me, self.cross))


class ReduceCross(GridTask):
    def __init__(self, blocks):
        super().__init__()
        shape = blocks.shape[1:]
        self.blocks_shape = (LINE, self.cross) + shape
        self.ins = (blocks.reshape(self.blocks_shape),)
        self.outs = (shaped((LINE,) + shape, jnp.bfloat16),)
        others = max(self.cross - 1, 1)
        self.scratch = (
            pltpu.VMEM((others, LINE) + shape, jnp.bfloat16),
            dma(others, LINE),
            dma(others, LINE),
        )

    def targets(self):
        line, cross = self.place()
        return [lax.rem(cross + step, self.cross) for step in range(1, self.cross)]

    def partners(self):
        line, cross = self.place()
        return [{"dp": line * self.cross + other} for other in self.targets()]

    def begin(self):
        (x_ref,), (buf, send, recv) = self.ins_refs, self.scratch_refs
        line, cross = self.place()
        self.copies = []
        for i, other in enumerate(self.targets()):
            for z in range(LINE):
                copy = remote(
                    x_ref.at[z, other],
                    buf.at[i, z],
                    send.at[i, z],
                    recv.at[i, z],
                    {"dp": line * self.cross + other},
                )
                copy.start()
                self.copies.append(copy)

    def end(self):
        (x_ref,), (o_ref,), (buf, send, recv) = self.ins_refs, self.outs_refs, self.scratch_refs
        line, cross = self.place()
        for copy in self.copies:
            copy.wait()
        for z in range(LINE):
            total = x_ref[z, cross].astype(jnp.float32)
            for i in range(self.cross - 1):
                total = total + buf[i, z].astype(jnp.float32)
            o_ref[z] = total.astype(jnp.bfloat16)


class SpreadLine(GridTask):
    def __init__(self, block):
        super().__init__()
        self.ins = (block,)
        self.outs = (shaped((LINE,) + block.shape, block.dtype),)
        self.scratch = (dma(LINE - 1), dma(LINE - 1))

    def targets(self):
        line, cross = self.place()
        return [lax.rem(line + step, LINE) for step in range(1, LINE)]

    def partners(self):
        line, cross = self.place()
        return [{"dp": other * self.cross + cross} for other in self.targets()]

    def begin(self):
        (x_ref,), (o_ref,), (send, recv) = self.ins_refs, self.outs_refs, self.scratch_refs
        line, cross = self.place()
        self.copies = [
            remote(x_ref, o_ref.at[line], send.at[i], recv.at[i], partner)
            for i, partner in enumerate(self.partners())
        ]
        for copy in self.copies:
            copy.start()
        o_ref[line] = x_ref[...]

    def end(self):
        for copy in self.copies:
            copy.wait()


class Chain(Task):
    def __init__(self, first, second):
        self.first, self.second = first, second
        self.ins = first.ins
        self.outs = first.outs + second.outs
        self.scratch = first.scratch + second.scratch

    def hello(self, barrier):
        return self.first.hello(barrier) + self.second.hello(barrier)

    def begin(self):
        outs, scratch = len(self.first.outs), len(self.first.scratch)
        self.first.ins_refs, self.first.outs_refs = self.ins_refs, self.outs_refs[:outs]
        self.first.scratch_refs = self.scratch_refs[:scratch]
        self.second.ins_refs, self.second.outs_refs = self.outs_refs[:outs], self.outs_refs[outs:]
        self.second.scratch_refs = self.scratch_refs[scratch:]
        self.first.begin()

    def middle(self):
        self.first.end()
        self.second.begin()

    def end(self):
        self.second.end()


class Later(Task):
    def __init__(self, task):
        self.task = task
        self.ins, self.outs, self.scratch = task.ins, task.outs, task.scratch

    def hello(self, barrier):
        return self.task.hello(barrier)

    def middle(self):
        task = self.task
        task.ins_refs, task.outs_refs = self.ins_refs, self.outs_refs
        task.scratch_refs = self.scratch_refs
        task.begin()

    def end(self):
        self.task.end()


def reduce_grid(blocks, **form):
    first = ReduceCross(blocks)
    return Chain(first, ReduceLine(first.outs[0], **form))


def spread_grid(block):
    first = SpreadLine(block)
    return Chain(first, SpreadCross(first.outs[0]))


class SpreadCross(GridTask):
    def __init__(self, *pieces):
        super().__init__()
        self.ins = pieces
        self.tall, depth = pieces[0].shape[1:]
        count = len(pieces)
        self.outs = (shaped((LINE, self.cross, self.tall * count, depth), pieces[0].dtype),)
        others = max(self.cross - 1, 1)
        self.scratch = (dma(others, LINE, count), dma(others, LINE, count))

    def partners(self):
        line, cross = self.place()
        return [
            {"dp": line * self.cross + lax.rem(cross + step, self.cross)}
            for step in range(1, self.cross)
        ]

    def begin(self):
        (o_ref,), (send, recv) = self.outs_refs, self.scratch_refs
        line, cross = self.place()
        self.copies = []
        for p, x_ref in enumerate(self.ins_refs):
            rows = pl.ds(p * self.tall, self.tall)
            for i, partner in enumerate(self.partners()):
                for z in range(LINE):
                    copy = remote(
                        x_ref.at[z],
                        o_ref.at[z, cross, rows],
                        send.at[i, z, p],
                        recv.at[i, z, p],
                        partner,
                    )
                    copy.start()
                    self.copies.append(copy)
            for z in range(LINE):
                o_ref[z, cross, rows] = x_ref[z]

    def end(self):
        for copy in self.copies:
            copy.wait()


class GatherGrid(GridTask):
    def __init__(self, block):
        super().__init__()
        self.ins = (block,)
        self.outs = (shaped((LINE, self.cross) + block.shape, block.dtype),)
        others = max(self.cross - 1, 1)
        self.scratch = (dma(LINE - 1), dma(LINE - 1), dma(others, LINE), dma(others, LINE))

    def lines(self):
        line, cross = self.place()
        return [
            {"dp": lax.rem(line + step, LINE) * self.cross + cross} for step in range(1, LINE)
        ]

    def crosses(self):
        line, cross = self.place()
        return [
            {"dp": line * self.cross + lax.rem(cross + step, self.cross)}
            for step in range(1, self.cross)
        ]

    def partners(self):
        return self.lines() + self.crosses()

    def begin(self):
        (x_ref,), (o_ref,), sems = self.ins_refs, self.outs_refs, self.scratch_refs
        line, cross = self.place()
        self.copies = [
            remote(x_ref, o_ref.at[line, cross], sems[0].at[i], sems[1].at[i], partner)
            for i, partner in enumerate(self.lines())
        ]
        for copy in self.copies:
            copy.start()
        o_ref[line, cross] = x_ref[...]

    def middle(self):
        (o_ref,), sems = self.outs_refs, self.scratch_refs
        line, cross = self.place()
        for copy in self.copies:
            copy.wait()
        self.copies = []
        for i, partner in enumerate(self.crosses()):
            for z in range(LINE):
                window = o_ref.at[z, cross]
                copy = remote(window, window, sems[2].at[i, z], sems[3].at[i, z], partner)
                copy.start()
                self.copies.append(copy)

    def end(self):
        for copy in self.copies:
            copy.wait()


class ReduceLine(GridTask):
    def __init__(self, blocks, slabs=1, turned=False):
        super().__init__()
        shape = blocks.shape[1:]
        self.slabs, self.turned = slabs, turned
        self.ins = (blocks,)
        result = shape[::-1] if turned else shape
        if slabs > 1:
            result = (slabs, shape[0], shape[1] // slabs)
        self.outs = (shaped(result, jnp.float32), shaped((8, shape[1]), jnp.float32))
        self.scratch = (pltpu.VMEM((LINE - 1,) + shape, jnp.bfloat16), dma(LINE - 1), dma(LINE - 1))

    def targets(self):
        line, cross = self.place()
        return [lax.rem(line + step, LINE) for step in range(1, LINE)]

    def partners(self):
        line, cross = self.place()
        return [{"dp": other * self.cross + cross} for other in self.targets()]

    def begin(self):
        (x_ref,), (buf, send, recv) = self.ins_refs, self.scratch_refs
        line, cross = self.place()
        self.copies = [
            remote(
                x_ref.at[other], buf.at[i], send.at[i], recv.at[i], {"dp": other * self.cross + cross}
            )
            for i, other in enumerate(self.targets())
        ]
        for copy in self.copies:
            copy.start()

    def end(self):
        (x_ref,), (o_ref, square_ref) = self.ins_refs, self.outs_refs
        buf = self.scratch_refs[0]
        line, cross = self.place()
        for copy in self.copies:
            copy.wait()
        total = x_ref[line].astype(jnp.float32)
        for i in range(LINE - 1):
            total = total + buf[i].astype(jnp.float32)
        square_ref[...] = eight_rows(total * total)
        if self.turned:
            o_ref[...] = total.T
        elif self.slabs > 1:
            narrow = total.shape[1] // self.slabs
            for slab in range(self.slabs):
                o_ref[slab] = total[:, slab * narrow : (slab + 1) * narrow]
        else:
            o_ref[...] = total


class SumAll(Task):
    def __init__(self, block, keep):
        self.groups, self.width, self.keep = lax.axis_size("dp"), lax.axis_size("tensor"), keep
        rows, depth = block.shape
        self.narrow = narrow = depth // self.width
        kept = self.groups if keep else 1
        self.ins = (block,)
        self.outs = (shaped((kept, rows, depth), block.dtype),)
        near, far = dma(self.width), dma(self.groups)
        self.scratch = (
            pltpu.VMEM((self.width, rows, narrow), block.dtype),
            pltpu.VMEM((rows, narrow), block.dtype),
            pltpu.VMEM((self.groups, rows, narrow), block.dtype),
            pltpu.VMEM((kept, rows, narrow), block.dtype),
            near, near, far, far, near, near,
        )

    def mates(self):
        me = lax.axis_index("tensor")
        return [lax.rem(me + step, self.width) for step in range(1, self.width)]

    def peers(self):
        me = lax.axis_index("dp")
        return [lax.rem(me + step, self.groups) for step in range(1, self.groups)]

    def partners(self):
        return [{"tensor": mate} for mate in self.mates()] + [{"dp": peer} for peer in self.peers()]

    def lanes(self, owner):
        return pl.ds(pl.multiple_of(owner * self.narrow, self.narrow), self.narrow)

    def launch(self, copies):
        for copy in copies:
            copy.start()
        self.copies = copies

    def settle(self):
        for copy in self.copies:
            copy.wait()

    def begin(self):
        (x_ref,) = self.ins_refs
        part_buf, sems = self.scratch_refs[0], self.scratch_refs[4:]
        me = lax.axis_index("tensor")
        self.launch(
            [
                remote(
                    x_ref.at[:, self.lanes(mate)],
                    part_buf.at[me],
                    sems[0].at[i],
                    sems[1].at[i],
                    {"tensor": mate},
                )
                for i, mate in enumerate(self.mates())
            ]
        )
        part_buf[me] = x_ref[:, self.lanes(me)]

    def middle(self):
        (o_ref,) = self.outs_refs
        part_buf, sum_buf, all_buf, out_buf = self.scratch_refs[:4]
        sems = self.scratch_refs[4:]
        dp_me, me = lax.axis_index("dp"), lax.axis_index("tensor")
        self.settle()
        sum_buf[...] = jnp.sum(part_buf[...], axis=0)
        self.launch(
            [
                remote(sum_buf, all_buf.at[dp_me], sems[2].at[i], sems[3].at[i], {"dp": peer})
                for i, peer in enumerate(self.peers())
            ]
        )
        all_buf[dp_me] = sum_buf[...]
        self.settle()
        if self.keep:
            out_buf[...] = all_buf[...]
        else:
            out_buf[0] = jnp.sum(all_buf[...], axis=0)
        self.launch(
            [
                remote(
                    out_buf,
                    o_ref.at[:, :, self.lanes(me)],
                    sems[4].at[i],
                    sems[5].at[i],
                    {"tensor": mate},
                )
                for i, mate in enumerate(self.mates())
            ]
        )
        o_ref[:, :, self.lanes(me)] = out_buf[...]

    def end(self):
        self.settle()


Q_BLOCK = 256
K_BLOCK = 512


def split_pair(wide):
    half = wide.shape[0] // 2
    upper = lax.broadcasted_iota(jnp.int32, wide.shape, 0) < half
    zero = jnp.zeros_like(wide)
    return jnp.concatenate([jnp.where(upper, wide, zero), jnp.where(upper, zero, wide)], axis=1)


def stack_pair(tall):
    half = tall.shape[1] // 2
    left = lax.broadcasted_iota(jnp.int32, tall.shape, 1) < half
    zero = jnp.zeros_like(tall)
    return jnp.concatenate([jnp.where(left, tall, zero), jnp.where(left, zero, tall)], axis=0)


def join_pair(wide):
    depth, columns = wide.shape
    upper = lax.broadcasted_iota(jnp.int32, (depth, columns // 2), 0) < depth // 2
    return jnp.where(upper, wide[:, : columns // 2], wide[:, columns // 2 :])


def turn(tile):
    return tile.astype(jnp.float32).T.astype(jnp.bfloat16)


def block_span(index, size):
    return pl.ds(pl.multiple_of(index * size, size), size)


def attend_kernel(low_ref, high_ref, qkv_ref, seq_col_ref, seq_row_ref, out_ref, log_ref, value_turned, scores):
    slots, columns = out_ref.shape
    pairs = columns // 128
    q_blocks, k_blocks = slots // Q_BLOCK, slots // K_BLOCK

    def turn_values(b, carry):
        rows = block_span(b, K_BLOCK)
        for pair in range(pairs):
            value_turned[pl.ds(pair * 128, 128), rows] = turn(
                qkv_ref[rows, pl.ds(2 * columns + pair * 128, 128)]
            )
        return carry

    lax.fori_loop(0, k_blocks, turn_values, 0)

    def one_block(q_index, carry):
        q_rows = block_span(q_index, Q_BLOCK)
        lowest, highest = low_ref[q_index], high_ref[q_index]
        seq_row = seq_row_ref[0:1, q_rows]
        seq_pair = jnp.concatenate([seq_row, seq_row], axis=1)
        queries = [
            split_pair(
                (qkv_ref[q_rows, pl.ds(pair * 128, 128)].astype(jnp.float32) * HEAD ** (-0.5))
                .T.astype(jnp.bfloat16)
            )
            for pair in range(pairs)
        ]

        def score(k_index, tops):
            k_rows = block_span(k_index, K_BLOCK)
            same = seq_col_ref[k_rows, 0:1] == seq_pair
            later = []
            for pair in range(pairs):
                keys = qkv_ref[k_rows, pl.ds(columns + pair * 128, 128)]
                value = jnp.where(same, multiply_arrays(keys, queries[pair]), MASK_FILL)
                scores[pair, k_index - lowest] = value
                later.append(jnp.maximum(tops[pair], jnp.max(value, axis=0, keepdims=True)))
            return tuple(later)

        start = tuple(jnp.full((1, 2 * Q_BLOCK), MASK_FILL, jnp.float32) for _ in range(pairs))
        tops = lax.fori_loop(lowest, highest, score, start)

        def mix(k_index, state):
            k_rows = block_span(k_index, K_BLOCK)
            later = []
            for pair in range(pairs):
                total, mixed = state[pair]
                weights = jnp.exp(scores[pair, k_index - lowest] - tops[pair])
                total = total + jnp.sum(weights, axis=0, keepdims=True)
                mixed = mixed + multiply_arrays(
                    value_turned[pl.ds(pair * 128, 128), k_rows], weights.astype(jnp.bfloat16)
                )
                later.append((total, mixed))
            return tuple(later)

        blank = tuple(
            (jnp.zeros((1, 2 * Q_BLOCK), jnp.float32), jnp.zeros((128, 2 * Q_BLOCK), jnp.float32))
            for _ in range(pairs)
        )
        final = lax.fori_loop(lowest, highest, mix, blank)
        for pair in range(pairs):
            total, mixed = final[pair]
            out_ref[q_rows, pl.ds(pair * 128, 128)] = join_pair(mixed / total).T.astype(jnp.bfloat16)
            logs = tops[pair] + jnp.log(total)
            log_ref[pl.ds(2 * pair, 1), q_rows] = logs[:, :Q_BLOCK]
            log_ref[pl.ds(2 * pair + 1, 1), q_rows] = logs[:, Q_BLOCK:]
        return carry

    lax.fori_loop(0, q_blocks, one_block, 0)


def block_bounds(lengths, slots):
    ends = jnp.cumsum(lengths)
    starts = ends - lengths
    first = jnp.arange(slots // Q_BLOCK, dtype=jnp.int32) * Q_BLOCK
    last = first + Q_BLOCK - 1
    lowest = jnp.max(
        jnp.where(starts[None, :] <= first[:, None], starts[None, :], 0), axis=1
    )
    highest = jnp.min(jnp.where(ends[None, :] > last[:, None], ends[None, :], slots), axis=1)
    return (lowest // K_BLOCK, (highest + K_BLOCK - 1) // K_BLOCK)


REACH = (2 * MAXLEN - 2 + Q_BLOCK) // K_BLOCK + 1


def in_scalars():
    return pl.BlockSpec(memory_space=pltpu.SMEM)


def attend(qkv_out, seq_ids, bounds):
    slots, columns = qkv_out.shape[0], qkv_out.shape[1] // 3
    pairs = columns // 128
    return pl.pallas_call(
        attend_kernel,
        out_shape=[
            jax.ShapeDtypeStruct((slots, columns), jnp.bfloat16),
            jax.ShapeDtypeStruct((8, slots), jnp.float32),
        ],
        in_specs=[in_scalars(), in_scalars()] + [in_vmem()] * 3,
        out_specs=[in_vmem()] * 2,
        scratch_shapes=[
            pltpu.VMEM((columns, slots), jnp.bfloat16),
            pltpu.VMEM((pairs, REACH, K_BLOCK, 2 * Q_BLOCK), jnp.float32),
        ],
        compiler_params=pltpu.CompilerParams(vmem_limit_bytes=20 * 1024 * 1024),
    )(bounds[0], bounds[1], qkv_out, seq_ids[:, None], jnp.broadcast_to(seq_ids[None], (8, slots)))


def attend_back_kernel(
    low_ref, high_ref, qkv_ref, grad_ref, log_ref, seq_col_ref, seq_row_ref, out_ref,
    key_turned, probs, prob_grads, key_sum, value_sum,
):
    slots, columns = grad_ref.shape
    pairs = columns // 128
    q_blocks, k_blocks = slots // Q_BLOCK, slots // K_BLOCK

    def turn_keys(b, carry):
        rows = block_span(b, K_BLOCK)
        for pair in range(pairs):
            key_turned[pl.ds(pair * 128, 128), rows] = turn(
                qkv_ref[rows, pl.ds(columns + pair * 128, 128)]
            )
        key_sum[rows] = jnp.zeros((K_BLOCK, columns), jnp.float32)
        value_sum[rows] = jnp.zeros((K_BLOCK, columns), jnp.float32)
        return carry

    lax.fori_loop(0, k_blocks, turn_keys, 0)

    def one_block(q_index, carry):
        q_rows = block_span(q_index, Q_BLOCK)
        lowest, highest = low_ref[q_index], high_ref[q_index]
        seq_row = seq_row_ref[0:1, q_rows]
        seq_pair = jnp.concatenate([seq_row, seq_row], axis=1)
        scaled, queries, grads, turned, logs = [], [], [], [], []
        for pair in range(pairs):
            plain = qkv_ref[q_rows, pl.ds(pair * 128, 128)].astype(jnp.float32) * HEAD ** (-0.5)
            scaled.append(stack_pair(plain.astype(jnp.bfloat16)))
            queries.append(split_pair(plain.T.astype(jnp.bfloat16)))
            grad = grad_ref[q_rows, pl.ds(pair * 128, 128)]
            grads.append(stack_pair(grad))
            turned.append(split_pair(turn(grad)))
            logs.append(
                jnp.concatenate(
                    [log_ref[pl.ds(2 * pair, 1), q_rows], log_ref[pl.ds(2 * pair + 1, 1), q_rows]],
                    axis=1,
                )
            )

        def look(k_index, inners):
            k_rows = block_span(k_index, K_BLOCK)
            same = seq_col_ref[k_rows, 0:1] == seq_pair
            later = []
            for pair in range(pairs):
                keys = qkv_ref[k_rows, pl.ds(columns + pair * 128, 128)]
                values = qkv_ref[k_rows, pl.ds(2 * columns + pair * 128, 128)]
                logits = jnp.where(same, multiply_arrays(keys, queries[pair]), MASK_FILL)
                weights = jnp.exp(logits - logs[pair])
                weight_grad = multiply_arrays(values, turned[pair])
                probs[pair, k_index - lowest] = weights
                prob_grads[pair, k_index - lowest] = weight_grad
                value_sum[k_rows, pl.ds(pair * 128, 128)] += multiply_arrays(
                    weights.astype(jnp.bfloat16), grads[pair]
                )
                later.append(
                    inners[pair] + jnp.sum(weights * weight_grad, axis=0, keepdims=True)
                )
            return tuple(later)

        start = tuple(jnp.zeros((1, 2 * Q_BLOCK), jnp.float32) for _ in range(pairs))
        inners = lax.fori_loop(lowest, highest, look, start)

        def push(k_index, sums):
            k_rows = block_span(k_index, K_BLOCK)
            later = []
            for pair in range(pairs):
                slope = (
                    probs[pair, k_index - lowest]
                    * (prob_grads[pair, k_index - lowest] - inners[pair])
                ).astype(jnp.bfloat16)
                key_sum[k_rows, pl.ds(pair * 128, 128)] += multiply_arrays(slope, scaled[pair])
                later.append(
                    sums[pair] + multiply_arrays(key_turned[pl.ds(pair * 128, 128), k_rows], slope)
                )
            return tuple(later)

        blank = tuple(jnp.zeros((128, 2 * Q_BLOCK), jnp.float32) for _ in range(pairs))
        sums = lax.fori_loop(lowest, highest, push, blank)
        for pair in range(pairs):
            out_ref[q_rows, pl.ds(pair * 128, 128)] = (
                (join_pair(sums[pair]) * HEAD ** (-0.5)).T.astype(jnp.bfloat16)
            )
        return carry

    lax.fori_loop(0, q_blocks, one_block, 0)
    out_ref[:, columns : 2 * columns] = key_sum[...].astype(jnp.bfloat16)
    out_ref[:, 2 * columns :] = value_sum[...].astype(jnp.bfloat16)


def attend_back(qkv_out, attn_grad, log_total, seq_ids, bounds):
    slots, columns = attn_grad.shape
    pairs = columns // 128
    window = pltpu.VMEM((pairs, REACH, K_BLOCK, 2 * Q_BLOCK), jnp.float32)
    return pl.pallas_call(
        attend_back_kernel,
        out_shape=jax.ShapeDtypeStruct(qkv_out.shape, jnp.bfloat16),
        in_specs=[in_scalars(), in_scalars()] + [in_vmem()] * 5,
        out_specs=in_vmem(),
        scratch_shapes=[
            pltpu.VMEM((columns, slots), jnp.bfloat16),
            window,
            window,
            pltpu.VMEM((slots, columns), jnp.float32),
            pltpu.VMEM((slots, columns), jnp.float32),
        ],
        compiler_params=pltpu.CompilerParams(vmem_limit_bytes=36 * 1024 * 1024),
    )(
        bounds[0],
        bounds[1],
        qkv_out,
        attn_grad,
        log_total,
        seq_ids[:, None],
        jnp.broadcast_to(seq_ids[None], (8, slots)),
    )


def gelu_parts(upper):
    distance = jnp.abs(upper) * 0.7071067811865476
    step = 1.0 / (1.0 + 0.3275911 * distance)
    bell = jnp.exp(-distance * distance)
    series = step * (
        0.254829592
        + step * (-0.284496736 + step * (1.421413741 + step * (-1.453152027 + step * 1.061405429)))
    )
    tail = 0.5 * series * bell
    share = jnp.where(upper >= 0.0, 1.0 - tail, tail)
    return (upper * share, share + upper * (bell * 0.3989422804014327))


def expand_kernel(rows_ref, weight_ref, bias_ref, hidden_ref, slope_ref):
    units = weight_ref.shape[1]
    rows = rows_ref[...]
    for first in range(0, units, 256):
        lanes = pl.ds(first, 256)
        upper = multiply_arrays(rows, weight_ref[:, lanes]) + bias_ref[:, lanes]
        hidden, slope = gelu_parts(upper)
        hidden_ref[:, lanes] = hidden.astype(jnp.bfloat16)
        slope_ref[:, lanes] = slope


def expand(rows, weight, bias):
    slots, depth = rows.shape
    units = weight.shape[1]
    tall = 512
    return pl.pallas_call(
        expand_kernel,
        grid=(slots // tall,),
        out_shape=[shaped((slots, units), jnp.bfloat16), shaped((slots, units), jnp.float32)],
        in_specs=[
            pl.BlockSpec((tall, depth), lambda i: (i, 0)),
            pl.BlockSpec((depth, units), lambda i: (0, 0)),
            pl.BlockSpec((1, units), lambda i: (0, 0)),
        ],
        out_specs=[
            pl.BlockSpec((tall, units), lambda i: (i, 0)),
            pl.BlockSpec((tall, units), lambda i: (i, 0)),
        ],
        compiler_params=pltpu.CompilerParams(vmem_limit_bytes=20 * 1024 * 1024),
    )(rows, weight, bias)


EMBED_ROWS = 128
EMBED_PART = 16
MARGIN = 256


def embed_kernel(
    start_ref, span_ref, own_ref, tok_ref, pos_ref, seq_ref, row_ref, low_ref, emb_ref, norm_ref,
    padded, placed, normed,
):
    slots = tok_ref.shape[0]
    blocks, own_blocks = slots // EMBED_ROWS, emb_ref.shape[0] // EMBED_ROWS
    padded[pl.ds(MARGIN, pos_ref.shape[0])] = pos_ref[...]
    gain, shift = row_ref[0:1], row_ref[3:4]

    def one_block(b, carry):
        rows = block_span(b, EMBED_ROWS)
        seq = seq_ref[rows, 0:1]

        def pick(s, state):
            first = MARGIN + 2 + b * EMBED_ROWS - start_ref[s]
            base = first // 8
            shift = EMBED_PART + 8 - (first - base * 8)
            for at in range(0, EMBED_ROWS, EMBED_PART):
                window = padded[pl.ds(pl.multiple_of(base * 8 + at, 8), EMBED_PART + 8)]
                window = pltpu.roll(window, shift, 0)[:EMBED_PART]
                local = pl.ds(at, EMBED_PART)
                placed[local] = jnp.where(seq[at : at + EMBED_PART] == s, window, placed[local])
            return state

        lax.fori_loop(span_ref[0, b], span_ref[1, b], pick, 0)
        own = b - own_ref[0] * own_blocks
        kept = (own >= 0) & (own < own_blocks)
        own_first = jnp.where(kept, own, 0) * EMBED_ROWS
        for at in range(0, EMBED_ROWS, EMBED_PART):
            local = pl.ds(pl.multiple_of(b * EMBED_ROWS + at, EMBED_PART), EMBED_PART)
            emb = tok_ref[local].astype(jnp.float32) + placed[pl.ds(at, EMBED_PART)]
            norm = norm_rows(emb, gain, shift)
            low_ref[local] = norm.astype(jnp.bfloat16)
            placed[pl.ds(at, EMBED_PART)] = emb
            normed[pl.ds(at, EMBED_PART)] = norm

        @pl.when(kept)
        def _():
            own_rows = pl.ds(pl.multiple_of(own_first, EMBED_ROWS), EMBED_ROWS)
            emb_ref[own_rows] = placed[...]
            norm_ref[own_rows] = normed[...]

        return carry

    lax.fori_loop(0, blocks, one_block, 0)


def embed(tok_all, pos_full, seq_ids, lengths, row_params):
    slots, depth = tok_all.shape
    own = slots // lax.axis_size("tensor")
    ends = jnp.cumsum(lengths)
    starts = ends - lengths
    first = jnp.arange(slots // EMBED_ROWS, dtype=jnp.int32) * EMBED_ROWS
    spans = jnp.stack(
        [
            jnp.sum((ends[None, :] <= first[:, None]).astype(jnp.int32), axis=1),
            jnp.sum((starts[None, :] < first[:, None] + EMBED_ROWS).astype(jnp.int32), axis=1),
        ]
    )
    return pl.pallas_call(
        embed_kernel,
        out_shape=[
            shaped((slots, depth), jnp.bfloat16),
            shaped((own, depth), jnp.float32),
            shaped((own, depth), jnp.float32),
        ],
        in_specs=[in_scalars()] * 3 + [in_vmem()] * 4,
        out_specs=[in_vmem()] * 3,
        scratch_shapes=[
            pltpu.VMEM((MARGIN + MAXLEN + EMBED_ROWS + 24, depth), jnp.float32),
            pltpu.VMEM((EMBED_ROWS, depth), jnp.float32),
            pltpu.VMEM((EMBED_ROWS, depth), jnp.float32),
        ],
        compiler_params=pltpu.CompilerParams(vmem_limit_bytes=28 * 1024 * 1024),
    )(
        starts,
        spans,
        lax.axis_index("tensor").astype(jnp.int32)[None],
        tok_all,
        pos_full,
        seq_ids[:, None],
        row_params,
    )


SCATTER_ROWS = 512


def scatter_kernel(index_ref, rows_ref, grad_ref, square_ref):
    first = pl.program_id(0) * SCATTER_ROWS
    slots = index_ref.shape[1]
    here = (
        lax.broadcasted_iota(jnp.int32, (SCATTER_ROWS, slots), 0) + first == index_ref[...]
    ).astype(jnp.float32)
    grad = multiply_arrays(here.astype(jnp.bfloat16), rows_ref[...])
    grad_ref[...] = grad

    @pl.when(pl.program_id(0) == 0)
    def _():
        square_ref[...] = jnp.zeros_like(square_ref)

    square_ref[...] += eight_rows(grad * grad)


def scatter_rows(index, rows, height):
    slots, width = rows.shape
    return pl.pallas_call(
        scatter_kernel,
        grid=(pl.cdiv(height, SCATTER_ROWS),),
        out_shape=[shaped((height, width), jnp.float32), shaped((8, width), jnp.float32)],
        in_specs=[
            pl.BlockSpec((1, slots), lambda i: (0, 0)),
            pl.BlockSpec((slots, width), lambda i: (0, 0)),
        ],
        out_specs=[
            pl.BlockSpec((SCATTER_ROWS, width), lambda i: (i, 0)),
            pl.BlockSpec((8, width), lambda i: (0, 0)),
        ],
        compiler_params=pltpu.CompilerParams(vmem_limit_bytes=20 * 1024 * 1024),
    )(index[None], rows)


def layer_forward(embedded, seq_ids, bounds, members, counts, row_params, col_local, layer_mats):
    first_moment_all, emb_rows, norm_first = embedded
    qkv_full, out_full, up_half, down_low = layer_mats
    col_width = col_local.shape[1]
    qkv_bias = jnp.concatenate([col_local[0], jnp.zeros_like(col_local[0]), col_local[1]])
    qkv_out = (multiply_arrays(first_moment_all, qkv_full) + qkv_bias).astype(jnp.bfloat16)
    attn_low, log_total = attend(qkv_out, seq_ids, bounds)
    first_back = jnp.einsum("tc,dc->td", attn_low, out_full, preferred_element_type=jnp.float32)
    second_all, first_sum, norm_second, up_full, _, down_full = exchange(
        5,
        FoldNormSpread(first_back.astype(jnp.bfloat16), norm_first, row_params),
        SpreadCross(up_half),
        spread_grid(down_low),
    )
    up_full = up_full.reshape(D, -1)
    down_full = down_full.reshape(D, -1)
    hidden_low, slope = expand(second_all, up_full, col_local[2:].reshape(1, -1))
    second_back = jnp.einsum("tf,df->td", hidden_low, down_full, preferred_element_type=jnp.float32)
    second_sum, pooled = exchange(
        7, FoldPool(second_back.astype(jnp.bfloat16), norm_second, members, counts, row_params)
    )
    saved_vals = (
        emb_rows,
        first_moment_all,
        qkv_out,
        log_total,
        attn_low,
        first_sum,
        second_all,
        slope,
        hidden_low,
        second_sum,
    )
    return (pooled, saved_vals, (qkv_full, out_full, up_full, down_full))


def turned_grad(left_all, right_all):
    grad = jnp.einsum("td,tc->dc", left_all, right_all, preferred_element_type=jnp.float32)
    groups = lax.axis_size("dp")
    return grad.astype(jnp.bfloat16).reshape(groups, grad.shape[0] // groups, grad.shape[1])


def layer_backward(pooled_grad, counts, members, seq_ids, bounds, row_params, layer_mats, saved_vals):
    qkv_full, out_full, up_full, down_full = layer_mats
    (
        emb_rows,
        first_moment_all,
        qkv_out,
        log_total,
        attn_low,
        first_sum,
        second_all,
        slope,
        hidden_low,
        second_sum,
    ) = saved_vals
    col_width = out_full.shape[1]
    mixed_all, grad_second, side_c = exchange(
        10, PullSpread(pooled_grad, counts, jnp.tile(members.T, (1, 3)), second_sum, row_params)
    )
    down_grad = turned_grad(mixed_all, hidden_low)
    up_low = (multiply_arrays(mixed_all, down_full) * slope).astype(jnp.bfloat16)
    up_grad = turned_grad(second_all, up_low)
    second_back = jnp.einsum(
        "tf,df->td", up_low, up_full, preferred_element_type=jnp.float32
    ).astype(jnp.bfloat16)
    branch_all, grad_first, side_b, _, down_sum, down_squares, up_half = exchange(
        11,
        FoldPullSpread(second_back, grad_second, first_sum, row_params),
        reduce_grid(down_grad, turned=True),
        Later(ReduceCross(up_grad)),
    )
    out_grad = turned_grad(branch_all, attn_low)
    attn_grad = multiply_arrays(branch_all, out_full).astype(jnp.bfloat16)
    qkv_low = attend_back(qkv_out, attn_grad, log_total, seq_ids, bounds)
    qkv_grad = turned_grad(first_moment_all, qkv_low)
    first_back = jnp.einsum(
        "tc,dc->td", qkv_low, qkv_full, preferred_element_type=jnp.float32
    ).astype(jnp.bfloat16)
    cols_grad, side_a, up_sum, up_squares, _, out_sum, out_squares, _, qkv_sum, qkv_squares = exchange(
        13,
        FoldPullSwap(first_back, grad_first, emb_rows, row_params),
        ReduceLine(up_half),
        reduce_grid(out_grad, turned=True),
        reduce_grid(qkv_grad, slabs=3),
    )
    qkv_cols = jnp.sum(qkv_low.astype(jnp.float32), axis=0).reshape(3, col_width)
    up_cols = jnp.sum(up_low.astype(jnp.float32), axis=0).reshape(-1, col_width)
    col_grad = jnp.concatenate([qkv_cols[0:1], qkv_cols[2:3], up_cols], axis=0)
    row_grad = jnp.concatenate(
        [
            side_a[0:1],
            side_b[0:1],
            side_c[0:1],
            side_a[1:2],
            side_b[1:2],
            side_c[1:2],
            side_b[2:3],
            side_c[2:3],
        ]
    )
    return (
        cols_grad,
        (qkv_sum, out_sum, up_sum, down_sum),
        (qkv_squares, out_squares, up_squares + down_squares),
        col_grad,
        row_grad,
    )


def plan_kernel(capacity, vocab_local, groups, perm_ref, low_ref, high_ref, pair_ref, slot_ref, ask_ref, id_buf, own_buf):
    slots = perm_ref.shape[1]
    table_rows = low_ref.shape[1]
    block = 128
    blocks = slots // block
    perm = perm_ref[...]
    high_part = perm // 128
    low_part = perm - high_part * 128
    chooser = (lax.broadcasted_iota(jnp.int32, (table_rows, slots), 0) == high_part).astype(
        jnp.float32
    ).astype(jnp.bfloat16)
    value = multiply_arrays(low_ref[...], chooser) + 256.0 * multiply_arrays(high_ref[...], chooser)
    lane_match = lax.broadcasted_iota(jnp.int32, (128, slots), 0) == low_part
    ids = jnp.sum(jnp.where(lane_match, value, 0.0), axis=0, keepdims=True)
    for b in range(blocks):
        id_buf[pl.ds(b * block, block), :] = jnp.broadcast_to(
            ids[:, b * block : (b + 1) * block], (block, block)
        ).T
    place = lax.broadcasted_iota(jnp.int32, (1, slots), 1).astype(jnp.float32)
    rows = lax.broadcasted_iota(jnp.int32, (block, 1), 0).astype(jnp.float32)

    def earliest(b, best):
        column = id_buf[pl.ds(pl.multiple_of(b * block, block), block), 0:1]
        index = rows + (b * block).astype(jnp.float32)
        found = jnp.where(column == ids, index, 1e9)
        return jnp.minimum(best, jnp.min(found, axis=0, keepdims=True))

    least = lax.fori_loop(0, blocks, earliest, jnp.full((1, slots), 1e9, jnp.float32))
    first = least == place
    owner = jnp.zeros((1, slots), jnp.float32)
    for index in range(1, groups):
        owner = owner + jnp.where(ids >= float(index * vocab_local), 1.0, 0.0)
    owner_rows = lax.broadcasted_iota(jnp.int32, (groups, slots), 0).astype(jnp.float32)
    marks = jnp.where(first & (owner == owner_rows), 1.0, 0.0)
    upper = jnp.where(
        lax.broadcasted_iota(jnp.int32, (block, block), 0)
        < lax.broadcasted_iota(jnp.int32, (block, block), 1),
        1.0,
        0.0,
    ).astype(jnp.bfloat16)
    running = jnp.zeros((groups, 1), jnp.float32)
    pieces = []
    for b in range(blocks):
        part = marks[:, b * block : (b + 1) * block]
        pieces.append(multiply_arrays(part.astype(jnp.bfloat16), upper) + running)
        running = running + jnp.sum(part, axis=1, keepdims=True)
    before = jnp.concatenate(pieces, axis=1)
    rank = jnp.sum(marks * before, axis=0, keepdims=True)
    own_slot = jnp.where(first & (rank < float(capacity)), owner * float(capacity) + rank, -1.0)
    for b in range(blocks):
        own_buf[pl.ds(b * block, block), :] = jnp.broadcast_to(
            own_slot[:, b * block : (b + 1) * block], (block, block)
        ).T
    list_rows = -(-capacity // 128)
    stride = list_rows * 128
    width = groups * stride
    index = lax.broadcasted_iota(jnp.int32, (1, width), 1)
    target = (index // stride * capacity + lax.rem(index, stride)).astype(jnp.float32)
    target = jnp.where(lax.rem(index, stride) < capacity, target, -2.0)

    def settle(b, carry):
        slot, listed = carry
        window = pl.ds(pl.multiple_of(b * block, block), block)
        column, slot_column = id_buf[window, 0:1], own_buf[window, 0:1]
        slot = jnp.maximum(
            slot, jnp.max(jnp.where(column == ids, slot_column, -1.0), axis=0, keepdims=True)
        )
        listed = jnp.maximum(
            listed, jnp.max(jnp.where(slot_column == target, column, -1.0), axis=0, keepdims=True)
        )
        return (slot, listed)

    slot, listed = lax.fori_loop(
        0,
        blocks,
        settle,
        (jnp.full((1, slots), -1.0, jnp.float32), jnp.full((1, width), -1.0, jnp.float32)),
    )
    slot_ref[...] = slot.astype(jnp.int32)
    listed = listed.astype(jnp.int32)
    most = jnp.max(running, axis=0, keepdims=True).astype(jnp.int32)
    for group in range(groups):
        for row in range(list_rows):
            first_lane = group * stride + row * 128
            ask_ref[group, row : row + 1] = listed[:, first_lane : first_lane + 128]
        ask_ref[group, list_rows : list_rows + 1] = pair_ref[...]
        ask_ref[group, list_rows + 1 :] = jnp.broadcast_to(most, (7 - list_rows, 128))


def make_plan(perm, all_ids, pair_row, capacity, vocab_local, groups):
    slots = perm.shape[0]
    table = all_ids.reshape(-1, 128).T
    high = table // 256
    low = table - high * 256
    return pl.pallas_call(
        partial(plan_kernel, capacity, vocab_local, groups),
        out_shape=[
            jax.ShapeDtypeStruct((1, slots), jnp.int32),
            jax.ShapeDtypeStruct((groups, 8, 128), jnp.int32),
        ],
        in_specs=[in_vmem()] * 4,
        out_specs=[in_vmem()] * 2,
        scratch_shapes=[pltpu.VMEM((slots, 128), jnp.float32), pltpu.VMEM((slots, 128), jnp.float32)],
        compiler_params=pltpu.CompilerParams(vmem_limit_bytes=20 * 1024 * 1024),
    )(perm[None], low.astype(jnp.bfloat16), high.astype(jnp.bfloat16), pair_row)


def loss_kernel(pooled_ref, head_ref, pair_ref, loss_ref, low_ref, grad_ref, back_ref):
    total = pooled_ref.shape[0]
    low = pooled_ref[...].astype(jnp.bfloat16)
    low_ref[...] = low
    head_low = head_ref[...].astype(jnp.bfloat16)
    vectors = multiply_arrays(low, head_low)
    depth = vectors.shape[1]
    lane = lax.broadcasted_iota(jnp.int32, vectors.shape, 1)
    across = lax.broadcasted_iota(jnp.int32, (total, total), 1)
    diagonal = lax.broadcasted_iota(jnp.int32, (total, total), 0) == across
    chosen = across == pair_ref[...]
    loss = jnp.zeros((1, 1), jnp.float32)
    grads = jnp.zeros(vectors.shape, jnp.float32)

    def exact(left, right, dims):
        return lax.dot_general(
            left, right, (dims, ((), ())), precision=HIGHEST_MODE, preferred_element_type=jnp.float32
        )

    for fraction in (16, 4, 1):
        prefix = jnp.where(lane < depth // fraction, vectors, 0.0)
        inverse = lax.rsqrt(jnp.sum(prefix * prefix, axis=1, keepdims=True) + 1e-06)
        unit = prefix * inverse
        logits = exact(unit, unit, ((1,), (1,))) / LOGIT_DIVISOR
        logits = jnp.where(diagonal, MASK_FILL, logits)
        top = jnp.max(logits, axis=1, keepdims=True)
        weights = jnp.exp(logits - top)
        weight_sum = jnp.sum(weights, axis=1, keepdims=True)
        positive = jnp.sum(jnp.where(chosen, logits, 0.0), axis=1, keepdims=True)
        loss = loss + jnp.sum(jnp.log(weight_sum) + top - positive, keepdims=True)
        pull = weights / weight_sum - jnp.where(chosen, 1.0, 0.0)
        unit_grad = (exact(pull, unit, ((1,), (0,))) + exact(pull, unit, ((0,), (0,)))) / LOGIT_DIVISOR
        unit_grad = jnp.where(lane < depth // fraction, unit_grad, 0.0)
        inner = jnp.sum(unit_grad * prefix, axis=1, keepdims=True)
        grads = grads + inverse * unit_grad - prefix * (inverse * inverse * inverse * inner)
    low_wide = low.astype(jnp.float32)
    head_squares = jnp.sum(
        exact(low_wide, low_wide, ((1,), (1,))) * exact(grads, grads, ((1,), (1,))), keepdims=True
    )
    line = lax.broadcasted_iota(jnp.int32, loss_ref.shape, 0)
    loss_ref[...] = jnp.where(line == 0, loss, head_squares)
    grad_ref[...] = grads
    pieces, rest = [], grads
    for _ in range(3):
        pieces.append(rest.astype(jnp.bfloat16))
        rest = rest - pieces[-1].astype(jnp.float32)
    product = lax.dot_general(
        jnp.concatenate(pieces, axis=0),
        head_low,
        (((1,), (1,)), ((), ())),
        preferred_element_type=jnp.float32,
    )
    back_ref[...] = product[:total] + product[total : 2 * total] + product[2 * total :]


def contrast_step(pooled, head_weight, pairs):
    total, depth = pooled.shape
    return pl.pallas_call(
        loss_kernel,
        out_shape=[
            jax.ShapeDtypeStruct((8, 128), jnp.float32),
            jax.ShapeDtypeStruct((total, depth), jnp.bfloat16),
            jax.ShapeDtypeStruct((total, depth), jnp.float32),
            jax.ShapeDtypeStruct((total, depth), jnp.float32),
        ],
        in_specs=[in_vmem()] * 3,
        out_specs=[in_vmem()] * 4,
        compiler_params=pltpu.CompilerParams(vmem_limit_bytes=20 * 1024 * 1024),
    )(pooled, head_weight, pairs[:, None])


CAPACITY = 192


def body(
    token_ids,
    slot_perm,
    seq_lengths,
    pair_index,
    tok_table,
    tok_first,
    tok_second,
    pos_table,
    pos_first,
    pos_second,
    query_key_value_weight,
    qkv_first,
    qkv_second,
    out_weight,
    out_first,
    out_second,
    up_weight,
    up_first,
    up_second,
    down_weight,
    down_first,
    down_second,
    head_weight,
    head_first,
    head_second,
    col_bias,
    col_first,
    col_second,
    row_params,
    row_first,
    row_second,
):
    groups = lax.axis_size("dp")
    tensor_count = lax.axis_size("tensor")
    group_index = lax.axis_index("dp")
    tensor_index = lax.axis_index("tensor")
    tok_dev = token_ids.shape[0]
    tok_grp = tok_dev * tensor_count
    col_width = pos_table.shape[1]
    vocab_local = tok_table.shape[0]
    column_start = tensor_index * col_width
    anchors = pair_index.shape[0]
    id_rows = tok_dev // 128
    pair_row = jnp.pad(pair_index, (0, 128 - anchors))[None]
    qkv_low = jnp.concatenate(
        [query_key_value_weight[:, third] for third in range(3)], axis=1
    ).astype(jnp.bfloat16)
    out_low = out_weight.T.astype(jnp.bfloat16)
    up_low = up_weight.astype(jnp.bfloat16).reshape(qkv_low.shape[0], -1)
    down_low = down_weight.reshape(-1, down_weight.shape[2]).T.astype(jnp.bfloat16)
    half = qkv_low.shape[0] // 2
    gathered, perms, qkv_first_half = exchange(
        1,
        GatherAll(token_ids.reshape(id_rows, 128)),
        Gather(slot_perm.reshape(id_rows, 128), "tensor"),
        SpreadLine(qkv_low[:half]),
    )
    all_ids = gathered.reshape(-1)
    own_perm = perms.reshape(-1)
    slot, request = make_plan(own_perm, all_ids, pair_row, CAPACITY, vocab_local, groups)
    slot = slot[0]
    list_rows = -(-CAPACITY // 128)
    asked = exchange(2, Swap(request, "dp"))
    pairs = asked[:, list_rows, :anchors].reshape(-1)
    overflow = jnp.max(asked[:, list_rows + 1]) > CAPACITY
    offset = group_index * vocab_local
    asked_rows = asked[:, :list_rows].reshape(groups, -1)[:, :CAPACITY].reshape(-1) - offset
    asked_safe = jnp.clip(asked_rows, 0, vocab_local - 1)
    sent_rows = jnp.take(tok_table, asked_safe, axis=0).astype(jnp.bfloat16)
    got_rows, pos_full, qkv_second_half = exchange(
        3,
        Swap(sent_rows.reshape(groups, CAPACITY, col_width), "dp"),
        Spread(pos_table, columns=True, chunks=1),
        SpreadLine(qkv_low[half:]),
    )
    got_rows = got_rows.reshape(-1, col_width)

    def chooser(slots):
        places = jnp.arange(groups * CAPACITY, dtype=jnp.int32)
        return (slots[:, None] == places[None, :]).astype(jnp.bfloat16)

    lengths = seq_lengths[0]
    seq_ids, positions, member = seq_layout(lengths, tok_grp)
    bounds = block_bounds(lengths, tok_grp)

    def every_slot_id():
        every_perm = lax.all_gather(slot_perm, ("dp", "tensor"), axis=0, tiled=True)
        return jnp.take(all_ids, every_perm, axis=0)

    def spread_wide():
        wanted = every_slot_id() - offset
        inside = (wanted >= 0) & (wanted < vocab_local)
        picked = jnp.take(
            tok_table.astype(jnp.bfloat16), jnp.clip(wanted, 0, vocab_local - 1), axis=0
        )
        return lax.psum_scatter(
            jnp.where(inside[:, None], picked, jnp.zeros((), jnp.bfloat16)),
            "dp",
            scatter_dimension=0,
            tiled=True,
        )

    tok_cols = lax.cond(
        overflow,
        spread_wide,
        lambda: multiply_arrays(chooser(slot), got_rows).astype(jnp.bfloat16),
    )
    tok_all, _, out_full, qkv_full, up_half = exchange(
        4,
        Spread(tok_cols, columns=True),
        spread_grid(out_low),
        SpreadCross(qkv_first_half, qkv_second_half),
        SpreadLine(up_low),
    )
    layer_mats = (qkv_full.reshape(D, -1), out_full.reshape(D, -1), up_half, down_low)
    embedded = embed(tok_all, pos_full, seq_ids, lengths, row_params)
    members = lax.dynamic_slice_in_dim(member, tensor_index * tok_dev, tok_dev, 0).T.astype(
        jnp.bfloat16
    )
    counts = lengths.astype(jnp.float32)[:, None]
    pooled, saved_vals, layer_mats = layer_forward(
        embedded, seq_ids, bounds, members, counts, row_params, col_bias, layer_mats
    )
    loss_out, pooled_low, vec_grad, pooled_grad = contrast_step(
        pooled.reshape(-1, D), head_weight, pairs
    )
    head_sum = exact_multiply(pooled_low.astype(jnp.float32).T, vec_grad)
    cols_grad, sums, grid_squares, col_grad, row_grad = layer_backward(
        pooled_grad, counts, members, seq_ids, bounds, row_params, layer_mats, saved_vals
    )
    qkv_sum, out_sum, up_sum, down_sum = sums
    qkv_squares, out_squares, wide_squares = grid_squares
    cols_grad = cols_grad.reshape(tok_grp, col_width)
    pos_pick = (
        jnp.arange(pos_table.shape[0], dtype=jnp.int32)[:, None] == positions[None, :]
    ).astype(jnp.bfloat16)
    pos_grad = multiply_arrays(pos_pick, cols_grad)
    shared = jnp.concatenate([pos_grad, col_grad], axis=0)
    shared_rows = -(-shared.shape[0] // (16 * groups)) * 16
    shared = jnp.pad(shared, ((0, shared_rows * groups - shared.shape[0]), (0, 0)))
    merged = jnp.einsum(
        "kn,kc->nc",
        chooser(lax.optimization_barrier(slot)),
        cols_grad,
        preferred_element_type=jnp.float32,
    )
    back_rows, _, shared_own, shared_squares = exchange(
        15,
        Swap(merged.astype(jnp.bfloat16).reshape(groups, CAPACITY, col_width), "dp"),
        reduce_grid(shared.astype(jnp.bfloat16).reshape(groups, shared_rows, col_width)),
    )

    def add_wide():
        wanted = every_slot_id() - offset
        inside = (wanted >= 0) & (wanted < vocab_local)
        grad = (
            jnp.zeros(tok_table.shape, jnp.float32)
            .at[jnp.clip(wanted, 0, vocab_local - 1)]
            .add(
                jnp.where(
                    inside[:, None],
                    lax.all_gather(cols_grad, "dp", axis=0, tiled=True).astype(jnp.float32),
                    0.0,
                )
            )
        )
        squares = jnp.sum(grad * grad, axis=0, keepdims=True)
        return (grad, jnp.pad(squares, ((0, 7), (0, 0))))

    tok_grad, tok_squares = lax.cond(
        overflow,
        add_wide,
        lambda: tuple(scatter_rows(asked_rows, back_rows.reshape(-1, col_width), vocab_local)),
    )
    up_grad = up_sum.reshape(up_weight.shape)
    down_grad = down_sum.reshape(down_weight.shape)

    def widen(*parts):
        joined = jnp.concatenate(parts, axis=1)
        return jnp.pad(joined, ((0, 0), (0, D - joined.shape[1])))

    square_rows = (
        widen(wide_squares)
        + widen(qkv_squares, out_squares)
        + widen(tok_squares, shared_squares)
    )
    row_block = jnp.concatenate([row_grad, square_rows], axis=0)
    row_total, shared_sum = exchange(16, SumAll(row_block, False), GatherGrid(shared_own.astype(jnp.bfloat16)))
    row_total = row_total[0]
    shared_sum = shared_sum.reshape(-1, col_width).astype(jnp.float32)
    pos_own = shared_sum[: pos_table.shape[0]]
    col_own = shared_sum[pos_table.shape[0] : pos_table.shape[0] + col_bias.shape[0]]
    row_sum = row_total[:8]
    squares = jnp.sum(row_total[8:]) + jnp.sum(row_sum * row_sum) + loss_out[1, 0]
    grad_norm = jnp.sqrt(squares)
    clip_scale = jnp.minimum(1.0, CLIP_NORM / (grad_norm + 1e-06))
    tok_new = adam_step(
        tok_table, tok_first, tok_second, tok_grad * clip_scale, RATE_MATRIX, DECAY_RATE
    )
    pos_new = adam_step(
        pos_table, pos_first, pos_second, pos_own * clip_scale, RATE_MATRIX, DECAY_RATE
    )
    qkv_new = adam_step(
        query_key_value_weight.swapaxes(0, 1),
        qkv_first.swapaxes(0, 1),
        qkv_second.swapaxes(0, 1),
        qkv_sum * clip_scale,
        RATE_MATRIX,
        DECAY_RATE,
    )
    qkv_new = tuple(item.swapaxes(0, 1) for item in qkv_new)
    out_new = adam_step(
        out_weight, out_first, out_second, out_sum * clip_scale, RATE_MATRIX, DECAY_RATE
    )
    up_new = adam_step(
        up_weight, up_first, up_second, up_grad * clip_scale, RATE_MATRIX, DECAY_RATE
    )
    down_new = adam_step(
        down_weight, down_first, down_second, down_grad * clip_scale, RATE_MATRIX, DECAY_RATE
    )
    head_new = adam_step(
        head_weight, head_first, head_second, head_sum * clip_scale, RATE_MATRIX, DECAY_RATE
    )
    col_new = adam_step(col_bias, col_first, col_second, col_own * clip_scale, RATE_VECTOR, 0.0)
    row_new = adam_step(row_params, row_first, row_second, row_sum * clip_scale, RATE_VECTOR, 0.0)
    return (loss_out[0, 0], grad_norm) + tok_new + pos_new + qkv_new + out_new + up_new + down_new + head_new + col_new + row_new


def solution(mesh):
    placed = (
        P(("dp", "tensor")),
        P(("dp", "tensor")),
        P("dp", None),
        P("dp"),
        P("dp", "tensor"),
        P("dp", "tensor"),
        P("dp", "tensor"),
        P(None, "tensor"),
        P(None, "tensor"),
        P(None, "tensor"),
        P("dp", None, "tensor"),
        P("dp", None, "tensor"),
        P("dp", None, "tensor"),
        P("tensor", "dp"),
        P("tensor", "dp"),
        P("tensor", "dp"),
        P("dp", None, "tensor"),
        P("dp", None, "tensor"),
        P("dp", None, "tensor"),
        P(None, "tensor", "dp"),
        P(None, "tensor", "dp"),
        P(None, "tensor", "dp"),
        P(),
        P(),
        P(),
        P(None, "tensor"),
        P(None, "tensor"),
        P(None, "tensor"),
        P(),
        P(),
        P(),
    )
    return jax.shard_map(
        body,
        mesh=mesh,
        in_specs=placed,
        out_specs=(
            P(),
            P(),
            P("dp", "tensor"),
            P("dp", "tensor"),
            P("dp", "tensor"),
            P(None, "tensor"),
            P(None, "tensor"),
            P(None, "tensor"),
            P("dp", None, "tensor"),
            P("dp", None, "tensor"),
            P("dp", None, "tensor"),
            P("tensor", "dp"),
            P("tensor", "dp"),
            P("tensor", "dp"),
            P("dp", None, "tensor"),
            P("dp", None, "tensor"),
            P("dp", None, "tensor"),
            P(None, "tensor", "dp"),
            P(None, "tensor", "dp"),
            P(None, "tensor", "dp"),
            P(),
            P(),
            P(),
            P(None, "tensor"),
            P(None, "tensor"),
            P(None, "tensor"),
            P(),
            P(),
            P(),
        ),
        check_vma=False,
    )
```
